32 devices in a mesh: items: 4 (over y, x), seq: 8 (over z, core).
Axes of the slice: x: 2, y: 2, z: 4, core: 2. Of those that a mesh axis runs over, the one named last changes fastest.
Arguments:
- dec_in: bfloat16 [8, 512, 1024], P('items', 'seq'), may hold values from -6 to 6
- memory: bfloat16 [8, 384, 1024], P('items', 'seq'), may hold values from -6 to 6
- dec_len: int32 [8], P('items'), may hold values from 64 to 512, as said below
- mem_len: int32 [8], P('items'), may hold values from 25 to 384, as said below
- cell_mask: int32 [8, 384], P('items', 'seq'), may hold values 0 or 1
- self_query: bfloat16 [1024, 1024], P('seq'), may hold values from -0.1875 to 0.1875
- self_key: bfloat16 [1024, 1024], P('seq'), may hold values from -0.1875 to 0.1875
- self_value: bfloat16 [1024, 1024], P('seq'), may hold values from -0.1875 to 0.1875
- self_out: bfloat16 [1024, 1024], P('seq'), may hold values from -1.5 to 1.5
- cross_query: bfloat16 [1024, 1024], P('seq'), may hold values from -0.1875 to 0.1875
- cross_key: bfloat16 [1024, 1024], P('seq'), may hold values from -0.1875 to 0.1875
- cross_value: bfloat16 [1024, 1024], P('seq'), may hold values from -0.1875 to 0.1875
- cross_out: bfloat16 [1024, 1024], P('seq'), may hold values from -1.5 to 1.5
- ffn_in: bfloat16 [1024, 4096], P(None, 'seq'), may hold values from -0.1875 to 0.1875
- ffn_out: bfloat16 [4096, 1024], P('seq'), may hold values from -0.1875 to 0.1875
- norm_gain: float32 [3, 1024], replicated, may hold values from 0.5 to 1.5
- norm_bias: float32 [3, 1024], replicated, may hold values from -1 to 1
- cotangent: bfloat16 [8, 512, 1024], P('items', 'seq'), may hold values from -6 to 6
Outputs:
- layer_out: bfloat16 [8, 512, 1024], P('items', 'seq')
- grad_dec: float32 [8, 512, 1024], P('items', 'seq')
- grad_memory: float32 [8, 384, 1024], P('items', 'seq')
- grad_self_query: float32 [1024, 1024], P('seq')
- grad_self_key: float32 [1024, 1024], P('seq')
- grad_self_value: float32 [1024, 1024], P('seq')
- grad_self_out: float32 [1024, 1024], P('seq')
- grad_cross_query: float32 [1024, 1024], P('seq')
- grad_cross_key: float32 [1024, 1024], P('seq')
- grad_cross_value: float32 [1024, 1024], P('seq')
- grad_cross_out: float32 [1024, 1024], P('seq')
- grad_ffn_in: float32 [1024, 4096], P(None, 'seq')
- grad_ffn_out: float32 [4096, 1024], P('seq')
- grad_norm_gain: float32 [3, 1024], replicated
- grad_norm_bias: float32 [3, 1024], replicated
The draws below stay inside these ranges and needn't reach their ends.
Inputs may be any that keep to these rules, and one draw needn't show every extreme that they name: `dec_len`: among the 2 consecutive items of each index of items, one has decoder length 512. `mem_len`: among the 2 consecutive items of each index of items, one has memory length 384.
All inputs are finite; a program needn't handle non-finite values. No bound on the sum of `cell_mask` on one device may be relied on, other than what follows from the above.
Results may differ from the reference program's by a relative error of at most 0.03.
Values may be sent and summed in bfloat16 or wider, within the bound.
A program may use at most 256 MiB of HBM per device.

```python
import jax
import jax.numpy as jnp
from jax import lax

D = 1024
FF = 4096
HEAD_DIM = 64
ITEMS_DEV = 2
ITEMS = 8
DEC = 512
MEM = 384


def ragged_lengths(key, count, group, least, top):
    first_key, second_key = jax.random.split(key)
    blocks = count // group
    lengths = jax.random.randint(first_key, (blocks, group), least, top + 1)
    chosen = jax.random.randint(second_key, (blocks, 1), 0, group)
    slots = lax.broadcasted_iota(jnp.int32, (blocks, group), 1)
    return jnp.where(slots == chosen, top, lengths).reshape(count).astype(jnp.int32)


def draw_dec_len(key, part):
    key = jax.random.fold_in(key, 11)
    return ragged_lengths(key, ITEMS, ITEMS_DEV, max(1, DEC // 8), DEC)


def draw_mem_len(key, part):
    key = jax.random.fold_in(key, 23)
    return ragged_lengths(key, ITEMS, ITEMS_DEV, max(1, MEM * 50 // 768), MEM)


def set_ends(drawn, own_key, low, high):
    longest = drawn.shape.index(max(drawn.shape))
    spots = []
    for shift in (0, 1):
        where = [jax.random.randint(jax.random.fold_in(own_key, axis), (), 0, length) for axis, length in enumerate(drawn.shape)]
        where[longest] = (where[longest] + shift) % drawn.shape[longest]
        spots.append(tuple(where))
    return drawn.at[spots[0]].set(low).at[spots[1]].set(high)


def level_of(stream_key, shape, shards, low, largest):
    factor_of, own = 1.0, jax.random.fold_in(stream_key, 6)
    for position, shards_of in shards:
        steps = jnp.exp(jax.random.uniform(jax.random.fold_in(own, position), (shards_of,), jnp.float32, low / len(shards), largest / len(shards)))
        factor_of = factor_of * jnp.repeat(steps, shape[position] // shards_of).reshape([-1 if axis == position else 1 for axis in range(len(shape))])
    return factor_of


def gaussian(stream_key, dims, scale, most, shards=(), kind=jnp.bfloat16):
    values = scale * jax.random.normal(stream_key, dims, jnp.float32)
    if shards:
        values = values * level_of(stream_key, dims, shards, -0.22, 0.18)
    return jnp.clip(values, -most, most).astype(kind)


def setup_inputs(seed: int = 0) -> dict:
    seeds = jax.random.split(jax.random.key(seed), 19)
    return {
        "dec_in": gaussian(seeds[0], (ITEMS, DEC, D), 1.0, 6.0, ((0, 4), (1, 8))),
        "memory": gaussian(seeds[1], (ITEMS, MEM, D), 1.0, 6.0, ((0, 4), (1, 8))),
        "dec_len": draw_dec_len(jax.random.fold_in(seeds[18], 71), 0),
        "mem_len": draw_mem_len(jax.random.fold_in(seeds[18], 71), 0),
        "cell_mask": set_ends((jax.random.randint(seeds[4], (ITEMS, MEM), 0, 8) < 7).astype(jnp.int32), jax.random.fold_in(seeds[4], 1), 0, 1),
        "self_query": gaussian(seeds[5], (D, D), D ** -0.5, 0.1875, ((0, 8),)),
        "self_key": gaussian(seeds[6], (D, D), D ** -0.5, 0.1875, ((0, 8),)),
        "self_value": gaussian(seeds[7], (D, D), D ** -0.5, 0.1875, ((0, 8),)),
        "self_out": gaussian(seeds[8], (D, D), (D // 64) ** -0.5, 1.5, ((0, 8),)),
        "cross_query": gaussian(seeds[9], (D, D), D ** -0.5, 0.1875, ((0, 8),)),
        "cross_key": gaussian(seeds[10], (D, D), D ** -0.5, 0.1875, ((0, 8),)),
        "cross_value": gaussian(seeds[11], (D, D), D ** -0.5, 0.1875, ((0, 8),)),
        "cross_out": gaussian(seeds[12], (D, D), (D // 64) ** -0.5, 1.5, ((0, 8),)),
        "ffn_in": gaussian(seeds[13], (D, FF), D ** -0.5, 0.1875, ((1, 8),)),
        "ffn_out": gaussian(seeds[14], (FF, D), (FF // 4) ** -0.5, 0.1875, ((0, 8),)),
        "norm_gain": jnp.clip(1.0 + 0.1 * jax.random.normal(seeds[15], (3, D), jnp.float32), 0.5, 1.5),
        "norm_bias": gaussian(seeds[16], (3, D), 0.2, 1.0, (), jnp.float32),
        "cotangent": gaussian(seeds[17], (ITEMS, DEC, D), 1.0, 6.0, ((0, 4), (1, 8))),
    }


@jax.custom_vjp
def low(v):
    return lax.optimization_barrier(v.astype(jnp.bfloat16)).astype(jnp.float32)

@jax.custom_vjp
def low_back(v):
    return v

def low_keep(v):
    return (low(v), None)

def low_pass(kept, grad):
    return (grad,)

def back_keep(v):
    return (v, None)

def back_low(kept, grad):
    return (low(grad),)
low.defvjp(low_keep, low_pass)
low_back.defvjp(back_keep, back_low)
EPS = 1e-05
NEG = -1e+30
HIGH = lax.Precision.HIGHEST

def rounded(value):
    return low_back(low(value))

def matmul(left, right):
    return jnp.dot(left, right, precision=HIGH)

def norm_rows(value, gain, bias):
    mean = lax.optimization_barrier(jnp.mean(value, axis=-1, keepdims=True))
    centered = value - mean
    scaled = centered * lax.rsqrt(lax.optimization_barrier(jnp.mean(centered * centered, axis=-1, keepdims=True)) + EPS)
    return scaled * gain + bias

def attend(query, keys, values, valid):
    q_heads = query.reshape(query.shape[0], -1, HEAD_DIM)
    k_heads = keys.reshape(keys.shape[0], -1, HEAD_DIM)
    v_heads = values.reshape(values.shape[0], -1, HEAD_DIM)
    scores = jnp.einsum('rhe,khe->hrk', q_heads, k_heads, precision=HIGH) * HEAD_DIM ** (-0.5)
    scores = jnp.where(valid[None], low_back(scores), NEG)
    probs = jax.nn.softmax(scores, axis=-1)
    mixed = jnp.einsum('hrk,khe->rhe', low(probs), v_heads, precision=HIGH)
    return rounded(mixed.reshape(query.shape))

def item_layer(tokens, mems, dec_length, mem_length, cells, weights, gains, biases):
    w_sq, w_sk, w_sv, w_so, w_cq, w_ck, w_cv, w_co, w_in, w_out = weights
    total_dec = tokens.shape[0]
    total_mem = mems.shape[0]
    rows = lax.broadcasted_iota(jnp.int32, (total_dec, total_dec), 0)
    cols = lax.broadcasted_iota(jnp.int32, (total_dec, total_dec), 1)
    self_ok = (cols <= rows) & (cols < dec_length)
    self_mixed = attend(rounded(matmul(tokens, w_sq)), rounded(matmul(tokens, w_sk)), rounded(matmul(tokens, w_sv)), self_ok)
    first = norm_rows(tokens + low_back(matmul(self_mixed, w_so)), gains[0], biases[0])
    places = jnp.arange(total_mem, dtype=jnp.int32)
    keep = (places < mem_length) & ((cells == 1) | (places == 0))
    cross_ok = jnp.broadcast_to(keep[None], (total_dec, total_mem))
    cross_mixed = attend(rounded(matmul(low(first), w_cq)), rounded(matmul(mems, w_ck)), rounded(matmul(mems, w_cv)), cross_ok)
    second = norm_rows(first + low_back(matmul(cross_mixed, w_co)), gains[1], biases[1])
    pre = low_back(matmul(low(second), w_in))
    act = low(jax.nn.gelu(pre, approximate=False))
    third = norm_rows(second + low_back(matmul(act, w_out)), gains[2], biases[2])
    row_ok = jnp.arange(total_dec, dtype=jnp.int32) < dec_length
    return jnp.where(row_ok[:, None], third, 0.0)

def reference(dec_in, memory, dec_len, mem_len, cell_mask, self_query, self_key, self_value, self_out, cross_query, cross_key, cross_value, cross_out, ffn_in, ffn_out, norm_gain, norm_bias, cotangent):
    weights = tuple((w.astype(jnp.float32) for w in (self_query, self_key, self_value, self_out, cross_query, cross_key, cross_value, cross_out, ffn_in, ffn_out)))

    def forward(all_tokens, all_mems, weight_set, gains, biases):

        def one_item(pieces):
            tokens, mems, dec_length, mem_length, cells = pieces
            return item_layer(tokens, mems, dec_length, mem_length, cells, weight_set, gains, biases)
        return lax.map(jax.checkpoint(one_item), (all_tokens, all_mems, dec_len, mem_len, cell_mask))
    result, backward = jax.vjp(forward, dec_in.astype(jnp.float32), memory.astype(jnp.float32), weights, norm_gain, norm_bias)
    grad_dec, grad_memory, grad_weights, grad_gain, grad_bias = backward(cotangent.astype(jnp.float32))
    return (result.astype(jnp.bfloat16), grad_dec, grad_memory, grad_weights[0], grad_weights[1], grad_weights[2], grad_weights[3], grad_weights[4], grad_weights[5], grad_weights[6], grad_weights[7], grad_weights[8], grad_weights[9], grad_gain, grad_bias)
```

```python
import functools

import jax
import jax.numpy as jnp
from jax import lax
from jax.experimental import pallas as pl
from jax.experimental.pallas import tpu as pltpu
from jax.sharding import PartitionSpec as P

HEAD_DIM = 64
EPS = 1e-05
NEG = -1e30
SCALE = HEAD_DIM ** (-0.5)
BF = jnp.bfloat16
F32 = jnp.float32
VMEM_BYTES = 58 * 1024 * 1024
MESH = pl.DeviceIdType.MESH
VM = pl.BlockSpec(memory_space=pltpu.VMEM)
HBM = pl.BlockSpec(memory_space=pl.ANY)
SM = pl.BlockSpec(memory_space=pltpu.SMEM)


def nn(left, right):
    return lax.dot_general(left, right, (((1,), (0,)), ((), ())), preferred_element_type=F32)


def nt(left, right):
    return lax.dot_general(left, right, (((1,), (1,)), ((), ())), preferred_element_type=F32)


def tn(left, right):
    return lax.dot_general(left, right, (((0,), (0,)), ((), ())), preferred_element_type=F32)


class Link:
    def __init__(self, send_sems, recv_sems):
        self.send_sems, self.recv_sems, self.count, self.open = send_sems, recv_sems, 0, []

    def make(self, src, dst, device):
        index = self.count
        self.count += 1
        return pltpu.make_async_remote_copy(
            src_ref=src,
            dst_ref=dst,
            send_sem=self.send_sems.at[index],
            recv_sem=self.recv_sems.at[index],
            device_id=device,
            device_id_type=MESH,
        )

    def send(self, src, dst, device):
        copy = self.make(src, dst, device)
        copy.start()
        self.open.append(copy)
        return copy

    def local(self, src, dst):
        index = self.count
        self.count += 1
        copy = pltpu.make_async_copy(src, dst, self.send_sems.at[index])
        copy.start()
        return copy

    def finish(self):
        for copy in self.open:
            copy.wait_send()


def greet(devices):
    barrier = pltpu.get_barrier_semaphore()
    for device in devices:
        pl.semaphore_signal(barrier, inc=1, device_id=device, device_id_type=MESH)
    pl.semaphore_wait(barrier, len(devices))


class Place:
    def __init__(self, dims):
        self.dims = dims
        group, share = dims["group"], dims["share"]
        self.me = lax.axis_index("seq")
        self.h = self.me // group
        self.q = self.me % group
        self.b0 = self.q % 2
        self.b1 = (self.q // 2) % 2
        self.c = self.q // 4
        it = lax.axis_index("items")
        self.base = (it // share) * share
        self.t = it % share

    def across(self, bit):
        value = (self.q // (1 << bit)) % 2
        return {"seq": self.me + (1 - 2 * value) * (1 << bit)}

    def partner(self):
        return {"seq": (1 - self.h) * self.dims["group"] + self.q}

    def seq_shift(self, d):
        return lax.rem(self.me + d, self.dims["seq"])

    def share_shift(self, e):
        return lax.rem(self.t + e, self.dims["share"])

    def group_peers(self):
        return [self.across(bit) for bit in range(self.dims["bits"])]

    def seq_peers(self):
        return [{"seq": self.seq_shift(d)} for d in range(1, self.dims["seq"])]

    def share_peers(self):
        return [
            {"items": self.base + self.share_shift(e)} for e in range(1, self.dims["share"])
        ]


def spread_start(link, place, out, k):
    bits = place.dims["bits"]
    c, b1, b0 = place.c, place.b1, place.b0
    if bits == 3:
        step = link.send(out.at[k, c, b1, b0], out.at[k, c, b1, b0], place.across(2))
        step.wait_recv()
    waits = []
    high = link.send(out.at[k, :, b1, b0], out.at[k, :, b1, b0], place.across(1))
    waits.append(link.send(out.at[k, :, b1, b0], out.at[k, :, b1, b0], place.across(0)))
    return high, waits


def spread_end(link, place, out, k, started):
    high, waits = started
    b1, b0 = place.b1, place.b0
    high.wait_recv()
    waits.append(link.send(out.at[k, :, 1 - b1, b0], out.at[k, :, 1 - b1, b0], place.across(0)))
    return waits


def comm_call(body, name, cid, args, in_specs, out_shape, out_specs, scratch, copies):
    return pl.pallas_call(
        body,
        name=name,
        out_shape=out_shape,
        in_specs=in_specs,
        out_specs=out_specs,
        scratch_shapes=list(scratch)
        + [pltpu.SemaphoreType.DMA((copies,)), pltpu.SemaphoreType.DMA((copies,))],
        compiler_params=pltpu.CompilerParams(
            collective_id=cid, has_side_effects=True, vmem_limit_bytes=VMEM_BYTES
        ),
    )(*args)


def columns_out(link, place, src, dst, width):
    seq, group = place.dims["seq"], place.dims["group"]
    steps = []
    for d in range(1, seq):
        target = place.seq_shift(d)
        cols = pl.ds(pl.multiple_of(lax.rem(target, group) * width, width), width)
        steps.append(
            link.send(src.at[:, :, cols], dst.at[:, place.me, place.t], {"seq": target})
        )
    cols = pl.ds(pl.multiple_of(place.q * width, width), width)
    own = link.local(src.at[:, :, cols], dst.at[:, place.me, place.t])
    return steps, own


def rows_out(link, place, src, dst):
    dims, me = place.dims, place.me
    slot = lax.rem(me, dims["items_dev"])
    base = link.count
    link.count += dims["items_dev"] + 1
    copies = []
    for half in range(dims["items_dev"]):
        target = half * dims["group"] + me // dims["items_dev"]
        copy = pltpu.make_async_remote_copy(
            src_ref=src,
            dst_ref=dst.at[slot, place.t],
            send_sem=link.send_sems.at[base + half],
            recv_sem=link.recv_sems.at[base + slot],
            device_id={"seq": target},
            device_id_type=MESH,
        )
        copies.append((target != me, copy))
        pl.when(target != me)(copy.start)
    own = pltpu.make_async_copy(
        src, dst.at[slot, place.t], link.send_sems.at[base + dims["items_dev"]]
    )
    mine = me // dims["items_dev"] == place.q
    pl.when(mine)(own.start)

    def arrived():
        pl.when(mine)(own.wait)
        for block in range(dims["items_dev"]):
            copy = pltpu.make_async_remote_copy(
                src_ref=src,
                dst_ref=dst.at[block, place.t],
                send_sem=link.send_sems.at[base],
                recv_sem=link.recv_sems.at[base + block],
                device_id={"seq": me},
                device_id_type=MESH,
            )
            pl.when(place.q * dims["items_dev"] + block != me)(copy.wait_recv)

    def sent():
        for other, copy in copies:
            pl.when(other)(copy.wait_send)

    return arrived, sent


def to_share(link, place, src, dst):
    steps = []
    for e in range(1, place.dims["share"]):
        other = place.share_shift(e)
        steps.append(link.send(src(other), dst, {"items": place.base + other}))
    return steps


def arrive(steps):
    for step in steps:
        step.wait_recv()


def start_kernel(
    dims, dec, mem, cot, w_self, w_cross, w_rows, f_in, f_out,
    x_all, m_all, x_own, c_own, o_self, o_cross, o_so, o_co, o_fin, o_fout,
    send_sems, recv_sems,
):
    place = Place(dims)
    link = Link(send_sems, recv_sems)
    width = dims["width"]
    h, t = place.h, place.t
    c, b1, b0 = place.c, place.b1, place.b0
    partner = place.partner()
    greet(place.seq_peers() + place.share_peers())
    swap_x = link.send(dec.at[1 - h], x_all.at[h, c, b1, b0], partner)
    steps_self, own_self = columns_out(link, place, w_self, o_self, width)
    x_all[h, c, b1, b0] = dec[h]
    m_all[h, c, b1, b0] = mem[h]
    x_own[h] = dec[h]
    c_own[h] = cot[h]
    first_x = spread_start(link, place, x_all, h)
    so_arrived, so_sent = rows_out(link, place, w_rows.at[0], o_so)
    waits = spread_end(link, place, x_all, h, first_x)
    swap_x.wait_recv()
    x_own[1 - h] = x_all[1 - h, c, b1, b0]
    second_x = spread_start(link, place, x_all, 1 - h)
    arrive(steps_self)
    own_self.wait()
    waits += to_share(link, place, lambda _: o_self.at[:, :, t], o_self.at[:, :, t])
    so_arrived()
    waits += to_share(link, place, lambda _: o_so.at[:, t], o_so.at[:, t])
    waits += spread_end(link, place, x_all, 1 - h, second_x)
    swap_m = link.send(mem.at[1 - h], m_all.at[h, c, b1, b0], partner)
    swap_c = link.send(cot.at[1 - h], c_own.at[h], partner)
    first_m = spread_start(link, place, m_all, h)
    steps_cross, own_cross = columns_out(link, place, w_cross, o_cross, width)
    co_arrived, co_sent = rows_out(link, place, w_rows.at[1], o_co)
    step_fin = link.send(f_in, o_fin.at[t], partner)
    step_fout = link.send(f_out, o_fout.at[t], partner)
    waits += spread_end(link, place, m_all, h, first_m)
    swap_m.wait_recv()
    second_m = spread_start(link, place, m_all, 1 - h)
    waits += spread_end(link, place, m_all, 1 - h, second_m)
    arrive(steps_cross)
    own_cross.wait()
    waits += to_share(link, place, lambda _: o_cross.at[:, :, t], o_cross.at[:, :, t])
    co_arrived()
    waits += to_share(link, place, lambda _: o_co.at[:, t], o_co.at[:, t])
    step_fin.wait_recv()
    waits += to_share(link, place, lambda _: o_fin.at[t], o_fin.at[t])
    step_fout.wait_recv()
    waits += to_share(link, place, lambda _: o_fout.at[t], o_fout.at[t])
    swap_c.wait_recv()
    arrive(waits)
    so_sent()
    co_sent()
    link.finish()


class Reduce:
    def __init__(self, link, place, part, bufs):
        self.link, self.place, self.part, self.bufs = link, place, part, bufs
        self.zero, self.one = {}, {}

    def start(self, index, k):
        place = self.place
        self.zero[index] = self.link.send(
            self.part.at[k, :, :, 1 - place.b0], self.bufs[0].at[index], place.across(0)
        )

    def middle(self, index, k):
        place, part = self.place, self.part
        recv0, send1, recv1, keep1 = self.bufs[:4]
        self.zero[index].wait_recv()
        b1, b0 = place.b1, place.b0
        for c in range(part.shape[1]):
            value = part[k, c, 1 - b1, b0].astype(F32) + recv0[index, c, 1 - b1].astype(F32)
            send1[index, c] = value.astype(BF)
        self.one[index] = self.link.send(send1.at[index], recv1.at[index], place.across(1))
        for c in range(part.shape[1]):
            keep1[index, c] = part[k, c, b1, b0].astype(F32) + recv0[index, c, b1].astype(F32)

    def end(self, index):
        place = self.place
        recv1, keep1 = self.bufs[2:4]
        self.one[index].wait_recv()
        if place.dims["bits"] == 2:
            return keep1[index, 0] + recv1[index, 0].astype(F32)
        send2, recv2 = self.bufs[4:6]
        c = place.c
        send2[index] = (keep1[index, 1 - c] + recv1[index, 1 - c].astype(F32)).astype(BF)
        step = self.link.send(send2.at[index], recv2.at[index], place.across(2))
        kept = keep1[index, c] + recv1[index, c].astype(F32)
        step.wait_recv()
        return kept + recv2[index].astype(F32)


def reduce_bufs(dims, rows):
    items_dev, width, chips = dims["items_dev"], dims["model"], dims["chips"]
    bufs = [
        pltpu.VMEM((items_dev, chips, 2, rows, width), BF),
        pltpu.VMEM((items_dev, chips, rows, width), BF),
        pltpu.VMEM((items_dev, chips, rows, width), BF),
        pltpu.VMEM((items_dev, chips, rows, width), F32),
    ]
    if dims["bits"] == 3:
        bufs += [pltpu.VMEM((items_dev, rows, width), BF) for _ in range(2)]
    return bufs


def moments(value):
    mean = jnp.mean(value, axis=-1, keepdims=True)
    centered = value - mean
    inv = lax.rsqrt(jnp.mean(centered * centered, axis=-1, keepdims=True) + EPS)
    return centered * inv, inv


def norm_back(normed, inv, gain, grad):
    scaled = grad * gain
    mean = jnp.mean(scaled, axis=-1, keepdims=True)
    cross = jnp.mean(scaled * normed, axis=-1, keepdims=True)
    return inv * (scaled - mean - normed * cross)


def stage_kernel(dims, n_in, n_out, mid, *refs):
    part, ins = refs[0], refs[1 : 1 + n_in]
    outs = refs[1 + n_in : 1 + n_in + n_out]
    spread = outs[0]
    bufs = refs[1 + n_in + n_out : -2]
    place = Place(dims)
    link = Link(*refs[-2:])
    greet(place.group_peers())
    reduce = Reduce(link, place, part, bufs)
    count = dims["items_dev"]
    for k in range(count):
        reduce.start(k, k)
    for k in range(count):
        reduce.middle(k, k)
    started, waits = [], []
    for k in range(count):
        spread[k, place.c, place.b1, place.b0] = mid(k, reduce.end(k), ins, outs[1:])
        started.append(spread_start(link, place, spread, k))
    for k in range(count):
        waits += spread_end(link, place, spread, k, started[k])
    arrive(waits)
    link.finish()


def mid_forward(k, total, ins, outs):
    res, gain, bias = ins
    summed, out = outs
    value = res[k].astype(F32) + total
    summed[k] = value
    normed, _ = moments(value)
    result = normed * gain[...] + bias[...]
    out[k] = result
    return result.astype(BF)


def add_sums(k, sums, normed, grad):
    new = jnp.concatenate(
        [jnp.sum(grad * normed, axis=0, keepdims=True), jnp.sum(grad, axis=0, keepdims=True)], axis=0
    )
    sums[...] = new if k == 0 else sums[...] + new


def mid_turn(k, total, ins, outs):
    res, gain, bias, keep, cot = ins
    layer, grad_out, sums = outs
    normed, inv = moments(res[k] + total)
    kept = keep[k, :, 0:1] > 0.5
    layer[k] = jnp.where(kept, normed * gain[...] + bias[...], 0.0).astype(BF)
    grad = jnp.where(kept, cot[k].astype(F32), 0.0)
    add_sums(k, sums, normed, grad)
    result = norm_back(normed, inv, gain[...], grad)
    grad_out[k] = result
    return result.astype(BF)


def mid_backward(k, total, ins, outs):
    res, summed, gain = ins
    grad_out, sums = outs
    normed, inv = moments(summed[k])
    grad = res[k] + total
    add_sums(k, sums, normed, grad)
    result = norm_back(normed, inv, gain[...], grad)
    grad_out[k] = result
    return result.astype(BF)


def last_kernel(dims, part_x, part_m, res, layer, grad_dec, grad_mem, layer_out, *refs):
    place = Place(dims)
    link = Link(*refs[-2:])
    many = len(refs[:-2]) // 2
    bufs_x, send_x, recv_x = refs[: many - 2], refs[many - 2], refs[many - 1]
    bufs_m, send_m, recv_m = refs[many : 2 * many - 2], refs[2 * many - 2], refs[2 * many - 1]
    h, partner = place.h, place.partner()
    greet(place.group_peers() + [partner])
    red_x = Reduce(link, place, part_x, bufs_x)
    red_m = Reduce(link, place, part_m, bufs_m)
    ks = (1 - h, h)
    for red in (red_x, red_m):
        for index in range(2):
            red.start(index, ks[index])
    for red in (red_x, red_m):
        for index in range(2):
            red.middle(index, ks[index])
    swap_l = link.send(layer.at[1 - h], layer_out.at[h], partner)
    layer_out[h] = layer[h]
    send_x[...] = (red_x.end(0) + res[1 - h]).astype(BF)
    swap_x = link.send(send_x, recv_x, partner)
    grad_dec[h] = red_x.end(1) + res[h]
    send_m[...] = red_m.end(0).astype(BF)
    swap_m = link.send(send_m, recv_m, partner)
    grad_mem[h] = red_m.end(1)
    swap_x.wait_recv()
    grad_dec[1 - h] = recv_x[...].astype(F32)
    swap_m.wait_recv()
    grad_mem[1 - h] = recv_m[...].astype(F32)
    swap_l.wait_recv()
    link.finish()


def grads_items_kernel(
    dims, g_cross, g_self, g_co, g_so, g_fin, g_fout, sums,
    r_cross, r_self, r_co, r_so, r_fin, r_fout, r_sums, send_sems, recv_sems,
):
    place = Place(dims)
    link = Link(send_sems, recv_sems)
    t = place.t
    greet(place.seq_peers() + place.share_peers())
    waits, own = [], []
    for src, dst in (
        (g_fin, r_fin), (g_fout, r_fout), (g_co, r_co), (g_so, r_so),
    ):
        waits += to_share(link, place, lambda p, s=src: s.at[:, p], dst.at[t])
        own.append(link.local(src.at[:, t], dst.at[t]))
    for src, dst in ((g_cross, r_cross), (g_self, r_self)):
        waits += to_share(link, place, lambda p, s=src: s.at[:, :, p], dst.at[t])
        own.append(link.local(src.at[:, :, t], dst.at[t]))
    for d in range(1, dims["seq"]):
        target = {"seq": place.seq_shift(d)}
        waits.append(link.send(sums, r_sums.at[place.me], target))
    own.append(link.local(sums, r_sums.at[place.me]))
    arrive(waits)
    for copy in own:
        copy.wait()
    link.finish()


def rows_back(link, place, src, dst):
    dims, me, h = place.dims, place.me, place.h
    count = dims["items_dev"]
    base = link.count
    link.count += count + 1
    copies = []
    for k in range(count):
        target = place.q * count + k
        copy = pltpu.make_async_remote_copy(
            src_ref=src.at[k],
            dst_ref=dst.at[h],
            send_sem=link.send_sems.at[base + k],
            recv_sem=link.recv_sems.at[base + h],
            device_id={"seq": target},
            device_id_type=MESH,
        )
        copies.append((target != me, copy))
        pl.when(target != me)(copy.start)
    own = pltpu.make_async_copy(
        src.at[lax.rem(me, count)], dst.at[h], link.send_sems.at[base + count]
    )
    mine = me // count == place.q
    pl.when(mine)(own.start)

    def done():
        pl.when(mine)(own.wait)
        for half in range(count):
            copy = pltpu.make_async_remote_copy(
                src_ref=src.at[0],
                dst_ref=dst.at[half],
                send_sem=link.send_sems.at[base],
                recv_sem=link.recv_sems.at[base + half],
                device_id={"seq": me},
                device_id_type=MESH,
            )
            pl.when(half * dims["group"] + me // count != me)(copy.wait_recv)
        for other, copy in copies:
            pl.when(other)(copy.wait_send)

    return done


def grads_seq_kernel(
    dims, s_cross, s_self, s_co, s_so, s_fin, s_fout, sums,
    z_cross, z_self, z_co, z_so, z_fin, z_fout, z_sums, send_sems, recv_sems,
):
    place = Place(dims)
    link = Link(send_sems, recv_sems)
    me = place.me
    greet(place.seq_peers() + place.share_peers())
    waits, own = [], []
    for src, dst in ((s_fin, z_fin), (s_fout, z_fout)):
        waits.append(link.send(src.at[1], dst, place.partner()))
    for src, dst in ((s_cross, z_cross), (s_self, z_self)):
        for d in range(1, dims["seq"]):
            target = place.seq_shift(d)
            waits.append(link.send(src.at[:, target], dst.at[me], {"seq": target}))
        own.append(link.local(src.at[:, me], dst.at[me]))
    done = [rows_back(link, place, s_co, z_co), rows_back(link, place, s_so, z_so)]
    waits += to_share(link, place, lambda p: sums, z_sums.at[place.t])
    own.append(link.local(sums, z_sums.at[place.t]))
    arrive(waits)
    for copy in own:
        copy.wait()
    for wait in done:
        wait()
    link.finish()


def grads_gather_kernel(dims, count, *refs):
    place = Place(dims)
    link = Link(*refs[-2:])
    greet(place.share_peers())
    waits, own = [], []
    for src, dst in zip(refs[:count], refs[count : 2 * count]):
        waits += to_share(link, place, lambda p, s=src: s, dst.at[place.t])
        own.append(link.local(src, dst.at[place.t]))
    arrive(waits)
    for copy in own:
        copy.wait()
    link.finish()


def call(body, name, args, in_specs, out_shape, scratch=()):
    return pl.pallas_call(
        body,
        name=name,
        out_shape=out_shape,
        in_specs=in_specs,
        out_specs=[VM] * len(out_shape),
        scratch_shapes=list(scratch),
        compiler_params=pltpu.CompilerParams(vmem_limit_bytes=VMEM_BYTES),
    )(*args)


def shape(dims, dtype):
    return jax.ShapeDtypeStruct(tuple(dims), dtype)


def half_mask(rows, half):
    return (lax.broadcasted_iota(jnp.int32, (rows, 128), 1) // HEAD_DIM) == half


def attend(q_ref, k_ref, v_ref, valid, p_ref, mix_ref, causal, block):
    rows, keys = q_ref.shape[0], k_ref.shape[0]
    for pair in range(q_ref.shape[1] // 128):
        lanes = slice(pair * 128, pair * 128 + 128)
        for start in range(0, rows, block):
            stop = start + block if causal else keys
            halves = []
            for half in range(2):
                query = q_ref[start : start + block, lanes]
                query = jnp.where(half_mask(block, half), query, jnp.zeros_like(query))
                scores = nt(k_ref[:stop, lanes], query) * SCALE
                scores = jnp.where(valid(start, stop), scores, NEG)
                top = jnp.max(scores, axis=0, keepdims=True)
                grown = jnp.exp(scores - top)
                probs = (grown * (1.0 / jnp.sum(grown, axis=0, keepdims=True))).astype(BF)
                p_ref[2 * pair + half, :stop, start : start + block] = probs
                mixed = tn(v_ref[:stop, lanes], probs)
                halves.append(mixed[half * HEAD_DIM : (half + 1) * HEAD_DIM])
            mix_ref[start : start + block, lanes] = jnp.concatenate(halves, axis=0).T.astype(BF)


def attend_back(q_ref, k_ref, v_ref, p_ref, grad_ref, dq_ref, dk_ref, dv_ref, causal, block):
    rows, keys = q_ref.shape[0], k_ref.shape[0]
    for pair in range(q_ref.shape[1] // 128):
        lanes = slice(pair * 128, pair * 128 + 128)
        dk = jnp.zeros((keys, 128), F32)
        dv = jnp.zeros((keys, 128), F32)
        for start in range(0, rows, block):
            stop = start + block if causal else keys
            halves = []
            for half in range(2):
                mask = half_mask(block, half)
                query = q_ref[start : start + block, lanes]
                query = jnp.where(mask, query, jnp.zeros_like(query))
                grad = grad_ref[start : start + block, lanes]
                grad = jnp.where(mask, grad, jnp.zeros_like(grad))
                low = p_ref[2 * pair + half, :stop, start : start + block]
                probs = low.astype(F32)
                grad_probs = nt(v_ref[:stop, lanes], grad)
                delta = jnp.sum(probs * grad_probs, axis=0, keepdims=True)
                grad_scores = (probs * (grad_probs - delta)).astype(BF)
                turned = tn(k_ref[:stop, lanes], grad_scores) * SCALE
                halves.append(turned[half * HEAD_DIM : (half + 1) * HEAD_DIM])
                new_k, new_v = nn(grad_scores, query), nn(low, grad)
                if stop < keys:
                    rest = jnp.zeros((keys - stop, 128), F32)
                    new_k = jnp.concatenate([new_k, rest], axis=0)
                    new_v = jnp.concatenate([new_v, rest], axis=0)
                dk, dv = dk + new_k, dv + new_v
            dq_ref[start : start + block, lanes] = jnp.concatenate(halves, axis=0).T.astype(BF)
        dk_ref[:, lanes] = (dk * SCALE).astype(BF)
        dv_ref[:, lanes] = dv.astype(BF)


def self_valid(length):
    def valid(start, stop, block):
        keys = lax.broadcasted_iota(jnp.int32, (stop, block), 0)
        rows = lax.broadcasted_iota(jnp.int32, (stop, block), 1) + start
        return (keys <= rows) & (keys < length)

    return valid


def self_forward(block, length, x, w, so, q, k, v, p, mix, part):
    rows = x[...]
    q[...] = nn(rows, w[0]).astype(BF)
    k[...] = nn(rows, w[1]).astype(BF)
    v[...] = nn(rows, w[2]).astype(BF)
    check = self_valid(length[0])
    attend(q, k, v, lambda a, b: check(a, b, block), p, mix, True, block)
    part[...] = nn(mix[...], so[...]).astype(BF)


def cross_forward(block, x, m, keep, w, co, q, k, v, p, mix, part):
    q[...] = nn(x[...], w[0]).astype(BF)
    k[...] = nn(m[...], w[1]).astype(BF)
    v[...] = nn(m[...], w[2]).astype(BF)
    attend(q, k, v, lambda a, b: keep[:, 0:1] > 0.5, p, mix, False, block)
    part[...] = nn(mix[...], co[...]).astype(BF)


def ffn_forward(x, w_in0, w_in1, w_out0, w_out1, act, slope, part):
    rows = x[...]
    width = w_in0.shape[1]
    for index, w_in in enumerate((w_in0, w_in1)):
        pre = nn(rows, w_in[...])
        cdf = 0.5 * (1.0 + lax.erf(pre * (0.5**0.5)))
        cols = slice(index * width, (index + 1) * width)
        act[:, cols] = (pre * cdf).astype(BF)
        slope[:, cols] = (
            cdf + pre * (jnp.exp(-0.5 * pre * pre) * 0.3989422804014327)
        ).astype(BF)
    part[...] = (nn(act[:, :width], w_out0[...]) + nn(act[:, width:], w_out1[...])).astype(BF)


def ffn_backward(x, gy, w_in0, w_in1, w_out0, w_out1, act, slope, part, g_in, g_out):
    rows, grad = x[...], gy[...]
    width = w_in0.shape[1]
    total = None
    for index, (w_in, w_out) in enumerate(((w_in0, w_out0), (w_in1, w_out1))):
        cols = slice(index * width, (index + 1) * width)
        grad_pre = (nt(grad, w_out[...]) * slope[:, cols].astype(F32)).astype(BF)
        term = nt(grad_pre, w_in[...])
        total = term if total is None else total + term
        g_in[index] = tn(rows, grad_pre).astype(BF)
        g_out[index] = tn(act[:, cols], grad).astype(BF)
    part[...] = total.astype(BF)


def cross_backward(
    block, gc, x, m, w, co, q, k, v, p, mix, part_x, part_m, g_w, g_co, dmix, dq, dk, dv
):
    grad = gc[...]
    dmix[...] = nt(grad, co[...]).astype(BF)
    attend_back(q, k, v, p, dmix, dq, dk, dv, False, block)
    part_x[...] = nt(dq[...], w[0]).astype(BF)
    part_m[...] = (nt(dk[...], w[1]) + nt(dv[...], w[2])).astype(BF)
    g_w[0] = tn(x[...], dq[...]).astype(BF)
    g_w[1] = tn(m[...], dk[...]).astype(BF)
    g_w[2] = tn(m[...], dv[...]).astype(BF)
    g_co[...] = tn(mix[...], grad).astype(BF)


def self_backward(block, gc, x, w, so, q, k, v, p, mix, part_x, g_w, g_so, dmix, dq, dk, dv):
    grad = gc[...]
    dmix[...] = nt(grad, so[...]).astype(BF)
    attend_back(q, k, v, p, dmix, dq, dk, dv, True, block)
    part_x[...] = (nt(dq[...], w[0]) + nt(dk[...], w[1]) + nt(dv[...], w[2])).astype(BF)
    rows = x[...]
    g_w[0] = tn(rows, dq[...]).astype(BF)
    g_w[1] = tn(rows, dk[...]).astype(BF)
    g_w[2] = tn(rows, dv[...]).astype(BF)
    g_so[...] = tn(mix[...], grad).astype(BF)


def shards(
    mesh, dec_in, memory, dec_len, mem_len, cell_mask, self_query, self_key, self_value, self_out,
    cross_query, cross_key, cross_value, cross_out, ffn_in, ffn_out, norm_gain, norm_bias, cotangent,
):
    items_dev, rb, model = dec_in.shape
    mb = memory.shape[1]
    seq, items = mesh.shape["seq"], mesh.shape["items"]
    group = seq // items_dev
    share = 4
    bits = group.bit_length() - 1
    chips = group // 4
    width = model // group
    dims = {
        "items_dev": items_dev, "seq": seq, "group": group, "share": share, "bits": bits,
        "chips": chips, "width": width, "model": model,
    }
    me, it = lax.axis_index("seq"), lax.axis_index("items")
    h, q, t = me // group, me % group, it % share
    total_dec, total_mem = rb * seq, mb * seq
    heads = width // HEAD_DIM
    hidden = ffn_in.shape[1]
    wr = self_query.shape[0] // share
    block = 256

    length = lax.dynamic_index_in_dim(dec_len, h, 0, keepdims=True)
    cells = lax.all_gather(cell_mask.astype(BF), "seq", axis=1, tiled=True)
    cells = lax.dynamic_index_in_dim(cells, h, 0, keepdims=False)
    spots = jnp.arange(total_mem, dtype=jnp.int32)
    mem_length = lax.dynamic_index_in_dim(mem_len, h, 0, keepdims=False)
    keep_mem = (spots < mem_length) & ((cells == 1.0) | (spots == 0))
    keep_mem = jnp.broadcast_to(keep_mem.astype(F32)[:, None], (total_mem, 128))
    row_pos = (
        lax.broadcasted_iota(jnp.int32, (items_dev, rb, 128), 0) * group + q
    ) * rb + lax.broadcasted_iota(jnp.int32, (items_dev, rb, 128), 1)
    keep_row = (row_pos < length[0]).astype(F32)

    def quarter(value, rows):
        return lax.dynamic_slice_in_dim(value, t * rows, rows, axis=0)

    w_self_q = jnp.stack([quarter(w, wr) for w in (self_query, self_key, self_value)])
    w_cross_q = jnp.stack([quarter(w, wr) for w in (cross_query, cross_key, cross_value)])
    w_rows_q = jnp.stack([quarter(w, wr) for w in (self_out, cross_out)])
    fr, gr = model // share, hidden // share
    f_in_q, f_out_q = quarter(ffn_in, fr), quarter(ffn_out, gr)

    grid = (items_dev, chips, 2, 2)
    (
        x_all, m_all, x_own, c_own, w_self, w_cross, w_so, w_co, p_fin, p_fout,
    ) = comm_call(
        functools.partial(start_kernel, dims),
        "start", 0,
        (dec_in, memory, cotangent, w_self_q, w_cross_q, w_rows_q, f_in_q, f_out_q),
        [VM, VM, VM, HBM, HBM, HBM, HBM, HBM],
        [
            shape(grid + (rb, model), BF),
            shape(grid + (mb, model), BF),
            shape((items_dev, rb, model), BF),
            shape((items_dev, rb, model), BF),
            shape((3, seq, share, wr, width), BF),
            shape((3, seq, share, wr, width), BF),
            shape((items_dev, share, wr, model), BF),
            shape((items_dev, share, wr, model), BF),
            shape((share, fr, hidden), BF),
            shape((share, gr, model), BF),
        ],
        [VM, VM, VM, VM] + [HBM] * 6,
        [], 112,
    )
    x_rows = x_all.reshape(total_dec, model)
    m_rows = m_all.reshape(total_mem, model)
    w_self = w_self.reshape(3, model, width)
    w_cross = w_cross.reshape(3, model, width)
    w_so, w_co = w_so.reshape(width, model), w_co.reshape(width, model)
    p_fin, p_fout = p_fin.reshape(model, hidden), p_fout.reshape(hidden, model)
    gains = [norm_gain[k : k + 1] for k in range(3)]
    biases = [norm_bias[k : k + 1] for k in range(3)]
    own = (items_dev, rb, model)

    def stage(name, cid, part, mid, ins, outs):
        return comm_call(
            functools.partial(stage_kernel, dims, len(ins), 1 + len(outs), mid),
            name, cid, (part.reshape(grid + (rb, model)),) + tuple(ins),
            [VM] * (1 + len(ins)),
            [shape(grid + (rb, model), BF)] + list(outs),
            [VM] * (1 + len(outs)),
            reduce_bufs(dims, rb), 24,
        )

    sq, sk, sv, sp, smix, part = call(
        functools.partial(self_forward, block), "self_forward",
        (length, x_rows, w_self, w_so), [SM, VM, VM, VM],
        [shape((total_dec, width), BF)] * 3
        + [shape((heads, total_dec, total_dec), BF), shape((total_dec, width), BF),
           shape((total_dec, model), BF)],
    )
    first_all, sum_one, first = stage(
        "first", 1, part, mid_forward, (x_own, gains[0], biases[0]), [shape(own, F32)] * 2
    )
    first_all = first_all.reshape(total_dec, model)
    cq, ck, cv, cp, cmix, part = call(
        functools.partial(cross_forward, block), "cross_forward",
        (first_all, m_rows, keep_mem, w_cross, w_co), [VM] * 5,
        [shape((total_dec, width), BF)] + [shape((total_mem, width), BF)] * 2
        + [shape((heads, total_mem, total_dec), BF), shape((total_dec, width), BF),
           shape((total_dec, model), BF)],
    )
    second_all, sum_two, second = stage(
        "second", 2, part, mid_forward, (first, gains[1], biases[1]), [shape(own, F32)] * 2
    )
    second_all = second_all.reshape(total_dec, model)
    act, slope, part = call(
        ffn_forward, "ffn_forward", (second_all, ffn_in, p_fin, ffn_out, p_fout), [VM] * 5,
        [shape((total_dec, 2 * hidden), BF)] * 2 + [shape((total_dec, model), BF)],
    )
    gy_all, layer, grad_third, sums_three = stage(
        "turn", 3, part, mid_turn, (second, gains[2], biases[2], keep_row, c_own),
        [shape(own, BF), shape(own, F32), shape((2, model), F32)],
    )
    part, g_fin, g_fout = call(
        ffn_backward, "ffn_backward",
        (second_all, gy_all.reshape(total_dec, model), ffn_in, p_fin, ffn_out, p_fout, act, slope),
        [VM] * 8,
        [shape((total_dec, model), BF), shape((2, model, hidden), BF), shape((2, hidden, model), BF)],
    )
    gc_all, grad_r2, sums_two = stage(
        "back_second", 4, part, mid_backward, (grad_third, sum_two, gains[1]),
        [shape(own, F32), shape((2, model), F32)],
    )
    part, part_m, g_cross, g_co = call(
        functools.partial(cross_backward, block), "cross_backward",
        (gc_all.reshape(total_dec, model), first_all, m_rows, w_cross, w_co, cq, ck, cv, cp, cmix),
        [VM] * 10,
        [shape((total_dec, model), BF), shape((total_mem, model), BF),
         shape((3, model, width), BF), shape((width, model), BF)],
        [pltpu.VMEM((total_dec, width), BF)] * 2 + [pltpu.VMEM((total_mem, width), BF)] * 2,
    )
    gc_all, grad_r1, sums_one = stage(
        "back_first", 5, part, mid_backward, (grad_r2, sum_one, gains[0]),
        [shape(own, F32), shape((2, model), F32)],
    )
    part, g_self, g_so = call(
        functools.partial(self_backward, block), "self_backward",
        (gc_all.reshape(total_dec, model), x_rows, w_self, w_so, sq, sk, sv, sp, smix),
        [VM] * 9,
        [shape((total_dec, model), BF), shape((3, model, width), BF), shape((width, model), BF)],
        [pltpu.VMEM((total_dec, width), BF)] * 4,
    )
    swap = [pltpu.VMEM((rb, model), BF)] * 2, [pltpu.VMEM((mb, model), BF)] * 2
    grad_dec, grad_memory, layer_out = comm_call(
        functools.partial(last_kernel, dims), "last", 6,
        (part.reshape(grid + (rb, model)), part_m.reshape(grid + (mb, model)), grad_r1, layer),
        [VM] * 4,
        [shape(own, F32), shape((items_dev, mb, model), F32), shape(own, BF)],
        [VM] * 3,
        reduce_bufs(dims, rb) + swap[0] + reduce_bufs(dims, mb) + swap[1], 24,
    )
    sums = jnp.concatenate([sums_one, sums_two, sums_three, jnp.zeros((2, model), F32)], axis=0)
    received = comm_call(
        functools.partial(grads_items_kernel, dims), "grads_items", 7,
        (
            g_cross.reshape(3, seq, share, wr, width),
            g_self.reshape(3, seq, share, wr, width),
            g_co.reshape(items_dev, share, wr, model),
            g_so.reshape(items_dev, share, wr, model),
            g_fin.reshape(2, share, fr, hidden),
            g_fout.reshape(2, share, gr, model),
            sums,
        ),
        [HBM] * 7,
        [
            shape((share, 3, seq, wr, width), BF),
            shape((share, 3, seq, wr, width), BF),
            shape((share, items_dev, wr, model), BF),
            shape((share, items_dev, wr, model), BF),
            shape((share, 2, fr, hidden), BF),
            shape((share, 2, gr, model), BF),
            shape((seq, 8, model), F32),
        ],
        [HBM] * 7, [], 56,
    )

    def over_groups(value):
        if items == share:
            return value
        lines = [[a * share + b for a in range(items // share)] for b in range(share)]
        return lax.psum(value, "items", axis_index_groups=lines)

    quarters = [
        over_groups(jnp.sum(value.astype(F32), axis=0).astype(BF)) for value in received[:6]
    ]
    sums = over_groups(jnp.sum(received[6], axis=0))
    moved = comm_call(
        functools.partial(grads_seq_kernel, dims), "grads_seq", 8,
        tuple(quarters) + (sums,), [HBM] * 7,
        [
            shape((seq, 3, wr, width), BF),
            shape((seq, 3, wr, width), BF),
            shape((items_dev, wr, model), BF),
            shape((items_dev, wr, model), BF),
            shape((fr, hidden), BF),
            shape((gr, model), BF),
            shape((share, 8, model), F32),
        ],
        [HBM] * 7, [], 56,
    )

    def whole_rows(value):
        value = value.reshape(items_dev, group, 3, wr, width).astype(F32).sum(axis=0)
        return value.transpose(1, 2, 0, 3).reshape(3, wr, model).astype(BF)

    done = [
        whole_rows(moved[0]),
        whole_rows(moved[1]),
        moved[2].astype(F32).sum(axis=0).astype(BF),
        moved[3].astype(F32).sum(axis=0).astype(BF),
        (moved[4].astype(F32) + quarters[4][0].astype(F32)).astype(BF),
        (moved[5].astype(F32) + quarters[5][0].astype(F32)).astype(BF),
    ]
    sums = jnp.sum(moved[6], axis=0)
    final = comm_call(
        functools.partial(grads_gather_kernel, dims, 6), "grads_gather", 9,
        tuple(done), [HBM] * 6,
        [shape((share,) + value.shape, BF) for value in done],
        [HBM] * 6, [], 24,
    )
    f_cross = final[0].transpose(1, 0, 2, 3).reshape(3, share * wr, model).astype(F32)
    f_self = final[1].transpose(1, 0, 2, 3).reshape(3, share * wr, model).astype(F32)
    f_co = final[2].reshape(share * wr, model).astype(F32)
    f_so = final[3].reshape(share * wr, model).astype(F32)
    return (
        layer_out, grad_dec, grad_memory,
        f_self[0], f_self[1], f_self[2], f_so,
        f_cross[0], f_cross[1], f_cross[2], f_co,
        final[4].reshape(model, hidden).astype(F32),
        final[5].reshape(hidden, model).astype(F32),
        sums[0:6:2], sums[1:6:2],
    )


def solution(mesh):
    rows = P("seq", None)
    tokens = P("items", "seq", None)
    placed = (
        (tokens, tokens, P("items"), P("items"), P("items", "seq"))
        + (rows,) * 8
        + (P(None, "seq"), rows, P(), P(), tokens)
    )
    return jax.shard_map(
        functools.partial(shards, mesh),
        mesh=mesh,
        in_specs=placed,
        out_specs=(tokens,) * 3 + (rows,) * 8 + (P(None, "seq"), rows, P(), P()),
        check_vma=False,
    )
```

```python
import functools

import jax
import jax.numpy as jnp
from jax import lax
from jax.experimental import pallas as pl
from jax.experimental.pallas import tpu as pltpu
from jax.sharding import PartitionSpec as P

HEAD_DIM = 64
EPS = 1e-05
NEG = -1e30
SCALE = HEAD_DIM ** (-0.5)
BF = jnp.bfloat16
F32 = jnp.float32
VMEM_BYTES = 61 * 1024 * 1024
MESH = pl.DeviceIdType.MESH
VM = pl.BlockSpec(memory_space=pltpu.VMEM)
HBM = pl.BlockSpec(memory_space=pl.ANY)
SM = pl.BlockSpec(memory_space=pltpu.SMEM)


def nn(left, right):
    return lax.dot_general(left, right, (((1,), (0,)), ((), ())), preferred_element_type=F32)


def nt(left, right):
    return lax.dot_general(left, right, (((1,), (1,)), ((), ())), preferred_element_type=F32)


def tn(left, right):
    return lax.dot_general(left, right, (((0,), (0,)), ((), ())), preferred_element_type=F32)


class Link:
    def __init__(self, send_sems, recv_sems):
        self.send_sems, self.recv_sems, self.count, self.open = send_sems, recv_sems, 0, []

    def make(self, src, dst, device):
        index = self.count
        self.count += 1
        return pltpu.make_async_remote_copy(
            src_ref=src,
            dst_ref=dst,
            send_sem=self.send_sems.at[index],
            recv_sem=self.recv_sems.at[index],
            device_id=device,
            device_id_type=MESH,
        )

    def send(self, src, dst, device):
        copy = self.make(src, dst, device)
        copy.start()
        self.open.append(copy)
        return copy

    def local(self, src, dst):
        index = self.count
        self.count += 1
        copy = pltpu.make_async_copy(src, dst, self.send_sems.at[index])
        copy.start()
        return copy

    def finish(self):
        for copy in self.open:
            copy.wait_send()


def greet(devices):
    barrier = pltpu.get_barrier_semaphore()
    for device in devices:
        pl.semaphore_signal(barrier, inc=1, device_id=device, device_id_type=MESH)
    pl.semaphore_wait(barrier, len(devices))


class Place:
    def __init__(self, dims):
        self.dims = dims
        group, share = dims["group"], dims["share"]
        self.me = lax.axis_index("seq")
        self.h = self.me // group
        self.q = self.me % group
        self.b0 = self.q % 2
        self.b1 = (self.q // 2) % 2
        self.c = self.q // 4
        self.it = lax.axis_index("items")
        self.base = (self.it // share) * share
        self.t = self.it % share

    def across(self, bit):
        value = (self.q // (1 << bit)) % 2
        return {"seq": self.me + (1 - 2 * value) * (1 << bit)}

    def partner(self):
        return {"seq": (1 - self.h) * self.dims["group"] + self.q}

    def seq_shift(self, d):
        return lax.rem(self.me + d, self.dims["seq"])

    def share_shift(self, e):
        return lax.rem(self.t + e, self.dims["share"])

    def seq_peers(self):
        return [{"seq": self.seq_shift(d)} for d in range(1, self.dims["seq"])]

    def items_peers(self):
        count = self.dims["items"]
        return [{"items": lax.rem(self.it + e, count)} for e in range(1, count)]


def spread_start(link, place, out, k):
    bits = place.dims["bits"]
    c, b1, b0 = place.c, place.b1, place.b0
    if bits == 3:
        step = link.send(out.at[k, c, b1, b0], out.at[k, c, b1, b0], place.across(2))
        step.wait_recv()
    waits = []
    high = link.send(out.at[k, :, b1, b0], out.at[k, :, b1, b0], place.across(1))
    waits.append(link.send(out.at[k, :, b1, b0], out.at[k, :, b1, b0], place.across(0)))
    return high, waits


def spread_end(link, place, out, k, started):
    high, waits = started
    b1, b0 = place.b1, place.b0
    high.wait_recv()
    waits.append(link.send(out.at[k, :, 1 - b1, b0], out.at[k, :, 1 - b1, b0], place.across(0)))
    return waits


def columns_out(link, place, src, dst, width):
    seq, group = place.dims["seq"], place.dims["group"]
    steps = []
    for d in range(1, seq):
        target = place.seq_shift(d)
        cols = pl.ds(pl.multiple_of(lax.rem(target, group) * width, width), width)
        steps.append(link.send(src.at[:, cols], dst.at[place.me, place.t], {"seq": target}))
    cols = pl.ds(pl.multiple_of(place.q * width, width), width)
    return steps, link.local(src.at[:, cols], dst.at[place.me, place.t])


def rows_out(link, place, src, dst):
    dims, me = place.dims, place.me
    slot = lax.rem(me, dims["items_dev"])
    base = link.count
    link.count += dims["items_dev"] + 1
    copies = []
    for half in range(dims["items_dev"]):
        target = half * dims["group"] + me // dims["items_dev"]
        copy = pltpu.make_async_remote_copy(
            src_ref=src,
            dst_ref=dst.at[slot, place.t],
            send_sem=link.send_sems.at[base + half],
            recv_sem=link.recv_sems.at[base + slot],
            device_id={"seq": target},
            device_id_type=MESH,
        )
        copies.append((target != me, copy))
        pl.when(target != me)(copy.start)
    own = pltpu.make_async_copy(
        src, dst.at[slot, place.t], link.send_sems.at[base + dims["items_dev"]]
    )
    mine = me // dims["items_dev"] == place.q
    pl.when(mine)(own.start)

    def arrived():
        pl.when(mine)(own.wait)
        for block in range(dims["items_dev"]):
            copy = pltpu.make_async_remote_copy(
                src_ref=src,
                dst_ref=dst.at[block, place.t],
                send_sem=link.send_sems.at[base],
                recv_sem=link.recv_sems.at[base + block],
                device_id={"seq": me},
                device_id_type=MESH,
            )
            pl.when(place.q * dims["items_dev"] + block != me)(copy.wait_recv)

    def sent():
        for other, copy in copies:
            pl.when(other)(copy.wait_send)

    return arrived, sent


def to_share(link, place, src, dst):
    steps = []
    for e in range(1, place.dims["share"]):
        other = place.share_shift(e)
        steps.append(link.send(src(other), dst, {"items": place.base + other}))
    return steps


def arrive(steps):
    for step in steps:
        step.wait_recv()


class Reduce:
    def __init__(self, link, place, part, bufs):
        self.link, self.place, self.part, self.bufs = link, place, part, bufs
        self.zero, self.one = {}, {}

    def start(self, index, k):
        place = self.place
        self.zero[index] = self.link.send(
            self.part.at[k, :, :, 1 - place.b0], self.bufs[0].at[index], place.across(0)
        )

    def middle(self, index, k):
        place, part = self.place, self.part
        recv0, send1, recv1, keep1 = self.bufs[:4]
        self.zero[index].wait_recv()
        b1, b0 = place.b1, place.b0
        for c in range(part.shape[1]):
            value = part[k, c, 1 - b1, b0].astype(F32) + recv0[index, c, 1 - b1].astype(F32)
            send1[index, c] = value.astype(BF)
        self.one[index] = self.link.send(send1.at[index], recv1.at[index], place.across(1))
        for c in range(part.shape[1]):
            keep1[index, c] = part[k, c, b1, b0].astype(F32) + recv0[index, c, b1].astype(F32)

    def end(self, index):
        place = self.place
        recv1, keep1 = self.bufs[2:4]
        self.one[index].wait_recv()
        if place.dims["bits"] == 2:
            return keep1[index, 0] + recv1[index, 0].astype(F32)
        send2, recv2 = self.bufs[4:6]
        c = place.c
        send2[index] = (keep1[index, 1 - c] + recv1[index, 1 - c].astype(F32)).astype(BF)
        step = self.link.send(send2.at[index], recv2.at[index], place.across(2))
        kept = keep1[index, c] + recv1[index, c].astype(F32)
        step.wait_recv()
        return kept + recv2[index].astype(F32)


def reduce_bufs(dims, rows):
    items_dev, width, chips = dims["items_dev"], dims["model"], dims["chips"]
    bufs = [
        pltpu.VMEM((items_dev, chips, 2, rows, width), BF),
        pltpu.VMEM((items_dev, chips, rows, width), BF),
        pltpu.VMEM((items_dev, chips, rows, width), BF),
        pltpu.VMEM((items_dev, chips, rows, width), F32),
    ]
    if dims["bits"] == 3:
        bufs += [pltpu.VMEM((items_dev, rows, width), BF) for _ in range(2)]
    return bufs


def moments(value):
    mean = jnp.mean(value, axis=-1, keepdims=True)
    centered = value - mean
    inv = lax.rsqrt(jnp.mean(centered * centered, axis=-1, keepdims=True) + EPS)
    return centered * inv, inv


def norm_back(normed, inv, gain, grad):
    scaled = grad * gain
    mean = jnp.mean(scaled, axis=-1, keepdims=True)
    cross = jnp.mean(scaled * normed, axis=-1, keepdims=True)
    return inv * (scaled - mean - normed * cross)


def rows_back(link, place, src, dst):
    dims, me, h = place.dims, place.me, place.h
    count = dims["items_dev"]
    base = link.count
    link.count += count + 1
    copies = []
    for k in range(count):
        target = place.q * count + k
        copy = pltpu.make_async_remote_copy(
            src_ref=src.at[k],
            dst_ref=dst.at[h],
            send_sem=link.send_sems.at[base + k],
            recv_sem=link.recv_sems.at[base + h],
            device_id={"seq": target},
            device_id_type=MESH,
        )
        copies.append((target != me, copy))
        pl.when(target != me)(copy.start)
    own = pltpu.make_async_copy(
        src.at[lax.rem(me, count)], dst.at[h], link.send_sems.at[base + count]
    )
    mine = me // count == place.q
    pl.when(mine)(own.start)

    def done():
        pl.when(mine)(own.wait)
        for half in range(count):
            copy = pltpu.make_async_remote_copy(
                src_ref=src.at[0],
                dst_ref=dst.at[half],
                send_sem=link.send_sems.at[base],
                recv_sem=link.recv_sems.at[base + half],
                device_id={"seq": me},
                device_id_type=MESH,
            )
            pl.when(half * dims["group"] + me // count != me)(copy.wait_recv)
        for other, copy in copies:
            pl.when(other)(copy.wait_send)

    return done


def half_mask(rows, half):
    return (lax.broadcasted_iota(jnp.int32, (rows, 128), 1) // HEAD_DIM) == half


def attend(q_ref, k_ref, v_ref, valid, p_ref, mix_ref, causal, block, first, last):
    keys = k_ref.shape[0]
    for pair in range(q_ref.shape[1] // 128):
        lanes = slice(pair * 128, pair * 128 + 128)
        for start in range(first, last, block):
            stop = start + block if causal else keys
            halves = []
            for half in range(2):
                query = q_ref[start : start + block, lanes]
                query = jnp.where(half_mask(block, half), query, jnp.zeros_like(query))
                scores = nt(k_ref[:stop, lanes], query) * SCALE
                scores = jnp.where(valid(start, stop), scores, NEG)
                top = jnp.max(scores, axis=0, keepdims=True)
                grown = jnp.exp(scores - top)
                probs = (grown * (1.0 / jnp.sum(grown, axis=0, keepdims=True))).astype(BF)
                p_ref[2 * pair + half, :stop, start : start + block] = probs
                mixed = tn(v_ref[:stop, lanes], probs)
                halves.append(mixed[half * HEAD_DIM : (half + 1) * HEAD_DIM])
            mix_ref[start : start + block, lanes] = jnp.concatenate(halves, axis=0).T.astype(BF)


def attend_back(
    q_ref, k_ref, v_ref, p_ref, grad_ref, dq_ref, dk_ref, dv_ref, causal, block, first, last
):
    keys = k_ref.shape[0]
    for pair in range(q_ref.shape[1] // 128):
        lanes = slice(pair * 128, pair * 128 + 128)
        for start in range(first, last, block):
            stop = start + block if causal else keys
            halves = []
            sum_k, sum_v = None, None
            for half in range(2):
                mask = half_mask(block, half)
                query = q_ref[start : start + block, lanes]
                query = jnp.where(mask, query, jnp.zeros_like(query))
                grad = grad_ref[start : start + block, lanes]
                grad = jnp.where(mask, grad, jnp.zeros_like(grad))
                low = p_ref[2 * pair + half, :stop, start : start + block]
                probs = low.astype(F32)
                grad_probs = nt(v_ref[:stop, lanes], grad)
                delta = jnp.sum(probs * grad_probs, axis=0, keepdims=True)
                grad_scores = (probs * (grad_probs - delta)).astype(BF)
                turned = tn(k_ref[:stop, lanes], grad_scores) * SCALE
                halves.append(turned[half * HEAD_DIM : (half + 1) * HEAD_DIM])
                new_k, new_v = nn(grad_scores, query), nn(low, grad)
                sum_k = new_k if sum_k is None else sum_k + new_k
                sum_v = new_v if sum_v is None else sum_v + new_v
            old = start if causal else (keys if start else 0)
            for ref, value in ((dk_ref, sum_k), (dv_ref, sum_v)):
                if old:
                    ref[:old, lanes] = ref[:old, lanes] + value[:old]
                if old < stop:
                    ref[old:stop, lanes] = value[old:]
            dq_ref[start : start + block, lanes] = jnp.concatenate(halves, axis=0).T.astype(BF)


class Box:
    def __init__(self, names, refs):
        for name, ref in zip(names, refs):
            setattr(self, name, ref)


class Quarters:
    def __init__(self, link, place, grad, box_names, box):
        self.link, self.place, self.grad = link, place, grad
        self.recv, self.lines, self.total, self.moved, self.done, self.out = (
            getattr(box, name) if name else None for name in box_names
        )

    def send(self):
        place = self.place
        self.steps = []
        for e in range(1, place.dims["share"]):
            other = place.share_shift(e)
            self.steps.append(
                self.link.send(
                    self.pick(other), self.recv.at[e - 1], {"items": place.base + other}
                )
            )

    def add(self):
        place = self.place
        arrive(self.steps)
        value = self.mine().astype(F32)
        for e in range(1, place.dims["share"]):
            value = value + self.recv[e - 1].astype(F32)
        self.total[...] = value.astype(BF)
        if self.lines is not None:
            share, items = place.dims["share"], place.dims["items"]
            steps = []
            for a in range(1, items // share):
                target = {"items": lax.rem(place.it + a * share, items)}
                steps.append(self.link.send(self.total, self.lines.at[a - 1], target))
            arrive(steps)
            for step in steps:
                step.wait_send()
            del self.link.open[-len(steps) :]
            for a in range(1, items // share):
                value = value + self.lines[a - 1].astype(F32)
            self.total[...] = value.astype(BF)
        self.along()

    def gather(self):
        self.close()
        place = self.place
        self.steps = to_share(self.link, place, lambda p: self.done, self.out.at[place.t])
        self.own = self.link.local(self.done, self.out.at[place.t])

    def finish(self):
        arrive(self.steps)
        self.own.wait()


class Hidden(Quarters):
    def pick(self, other):
        return self.grad.at[:, other]

    def mine(self):
        return self.grad[:, self.place.t]

    def along(self):
        self.steps = [self.link.send(self.total.at[1], self.moved, self.place.partner())]

    def close(self):
        arrive(self.steps)
        self.done[...] = (self.total[0].astype(F32) + self.moved[...].astype(F32)).astype(BF)


class Columns(Quarters):
    def pick(self, other):
        return self.grad.at[:, :, other]

    def mine(self):
        return self.grad[:, :, self.place.t]

    def along(self):
        place = self.place
        self.steps = []
        for d in range(1, place.dims["seq"]):
            target = place.seq_shift(d)
            self.steps.append(
                self.link.send(
                    self.total.at[:, target], self.moved.at[place.me], {"seq": target}
                )
            )
        self.own = self.link.local(self.total.at[:, place.me], self.moved.at[place.me])

    def close(self):
        arrive(self.steps)
        self.own.wait()
        dims = self.place.dims
        group, width = dims["group"], dims["width"]
        for index in range(3):
            for q in range(group):
                value = self.moved[q, index].astype(F32)
                for half in range(1, dims["items_dev"]):
                    value = value + self.moved[half * group + q, index].astype(F32)
                self.done[index, :, q * width : (q + 1) * width] = value.astype(BF)


class Rows(Quarters):
    pick, mine = Hidden.pick, Hidden.mine

    def along(self):
        self.moved_done = rows_back(self.link, self.place, self.total, self.moved)

    def close(self):
        self.moved_done()
        value = self.moved[0].astype(F32)
        for half in range(1, self.place.dims["items_dev"]):
            value = value + self.moved[half].astype(F32)
        self.done[...] = value.astype(BF)


class Stage:
    def __init__(self, link, place, part, bufs, mid, spread):
        self.link, self.place, self.mid, self.spread = link, place, mid, spread
        self.reduce = Reduce(link, place, part, bufs)
        self.started, self.waits = {}, {}

    def start(self, k):
        self.reduce.start(k, k)

    def middle(self, k):
        self.reduce.middle(k, k)

    def end(self, k):
        place, spread = self.place, self.spread
        spread[k, place.c, place.b1, place.b0] = self.mid(k, self.reduce.end(k))
        self.started[k] = spread_start(self.link, place, spread, k)

    def forward(self, k):
        self.waits[k] = spread_end(self.link, self.place, self.spread, k, self.started[k])

    def arrive(self, k):
        arrive(self.waits[k])


def stage_steps(stage, compute, flight=None, ended=None):
    compute(0)
    stage.start(0)
    compute(1)
    stage.start(1)
    stage.middle(0)
    stage.middle(1)
    if flight:
        flight()
    stage.end(0)
    stage.end(1)
    if ended:
        ended()
    stage.forward(0)
    stage.forward(1)


def layer_kernel(dims, names, *refs):
    b = Box(names, refs)
    b.grad_third, b.grad_r2, b.grad_r1, b.gc1_all = b.first, b.second, b.first, b.gy_all
    place = Place(dims)
    link = Link(b.send_sems, b.recv_sems)
    width, block, items_dev = dims["width"], dims["block"], dims["items_dev"]
    h, t, q_place = place.h, place.t, place.q
    c, b1, b0 = place.c, place.b1, place.b0
    partner = place.partner()
    wr = b.w_sq.shape[0] // dims["share"]
    model = dims["model"]
    total_dec, total_mem = dims["total_dec"], dims["total_mem"]
    rb = b.dec.shape[1]

    def rows_of(ref, cols=model):
        return ref[...].reshape(-1, ref.shape[-1])[:, :cols]

    def chunk(ref, k):
        return ref[k].reshape(-1, model)

    half_rows = total_dec // 2

    def span(k):
        return slice(k * half_rows, (k + 1) * half_rows)

    def put(k, value):
        b.part[k] = value.astype(BF).reshape(b.part.shape[1:])

    def weight(ref, index):
        return ref[index].reshape(model, width)

    weights = (b.w_sq, b.w_sk, b.w_sv, b.w_so, b.w_ck, b.w_cv, b.w_cq, b.w_co)
    rows_t = pl.ds(pl.multiple_of(t * wr, wr), wr)
    staged = [link.local(w.at[rows_t], b.staged.at[i]) for i, w in enumerate(weights)]
    own_fin = link.local(b.f_in, b.own_fin)
    own_fout = link.local(b.f_out, b.own_fout)
    greet(place.seq_peers() + place.items_peers())

    swap_x = link.send(b.dec.at[1 - h], b.x_all.at[h, c, b1, b0], partner)
    b.x_all[h, c, b1, b0] = b.dec[h]
    first_x = spread_start(link, place, b.x_all, h)
    for copy in staged:
        copy.wait()
    self_steps = [columns_out(link, place, b.staged.at[i], b.o_self.at[i], width) for i in range(3)]
    waits = spread_end(link, place, b.x_all, h, first_x)
    swap_x.wait_recv()
    second_x = spread_start(link, place, b.x_all, 1 - h)
    so_arrived, so_sent = rows_out(link, place, b.staged.at[3], b.o_so)

    def share_columns(steps, dst):
        arrive(steps[0])
        steps[1].wait()
        return to_share(link, place, lambda _: dst.at[:, t], dst.at[:, t])

    self_share = [share_columns(self_steps[i], b.o_self.at[i]) for i in range(3)]
    waits += spread_end(link, place, b.x_all, 1 - h, second_x)
    so_arrived()
    so_share = to_share(link, place, lambda _: b.o_so.at[:, t], b.o_so.at[:, t])

    b.m_all[h, c, b1, b0] = b.mem[h]
    swap_m = link.send(b.mem.at[1 - h], b.m_all.at[h, c, b1, b0], partner)
    first_m = spread_start(link, place, b.m_all, h)
    cross_steps = [
        columns_out(link, place, b.staged.at[4 + i], b.o_cross.at[i], width) for i in range(3)
    ]
    co_arrived, co_sent = rows_out(link, place, b.staged.at[7], b.o_co)
    b.c_own[h] = b.cot[h]
    swap_c = link.send(b.cot.at[1 - h], b.c_own.at[h], partner)
    own_fin.wait()
    own_fout.wait()
    fr, gr = b.o_fin.shape[1], b.o_fout.shape[1]
    step_fin = link.send(b.own_fin.at[pl.ds(pl.multiple_of(t * fr, fr), fr)], b.o_fin.at[t], partner)
    step_fout = link.send(
        b.own_fout.at[pl.ds(pl.multiple_of(t * gr, gr), gr)], b.o_fout.at[t], partner
    )
    mem_waits = spread_end(link, place, b.m_all, h, first_m)
    swap_m.wait_recv()
    second_m = spread_start(link, place, b.m_all, 1 - h)
    mem_waits += spread_end(link, place, b.m_all, 1 - h, second_m)

    arrive(waits)
    rows = rows_of(b.x_all)
    for index, dst in enumerate((b.sq, b.sk, b.sv)):
        arrive(self_share[index])
        dst[...] = nn(rows, weight(b.o_self, index)).astype(BF)
    cross_share = [share_columns(cross_steps[i], b.o_cross.at[i]) for i in range(3)]
    co_arrived()
    co_share = to_share(link, place, lambda _: b.o_co.at[:, t], b.o_co.at[:, t])
    length, mem_length = b.dec_len[h], b.mem_len[h]

    def self_ok(start, stop):
        keys = lax.broadcasted_iota(jnp.int32, (stop, block), 0)
        spots = lax.broadcasted_iota(jnp.int32, (stop, block), 1) + start
        return (keys <= spots) & (keys < length)

    bufs = [b.recv0, b.send1, b.recv1, b.keep1]
    if dims["bits"] == 3:
        bufs += [b.send2, b.recv2]

    def forward(index, res, summed, out):
        def mid(k, total):
            value = res(k) + total
            summed[k] = value
            normed, _ = moments(value)
            result = normed * b.gain[index : index + 1] + b.bias[index : index + 1]
            out[k] = result
            return result.astype(BF)

        return mid

    def sent(kept=()):
        late = {id(copy) for copy in kept}
        for copy in link.open:
            if id(copy) not in late:
                copy.wait_send()
        link.open[:] = [copy for copy in link.open if id(copy) in late]

    def self_part(k):
        attend(
            b.sq, b.sk, b.sv, self_ok, b.sp, b.smix, True, block,
            k * half_rows, (k + 1) * half_rows,
        )
        if k == 0:
            arrive(so_share)
        put(k, nn(b.smix[span(k)], rows_of(b.o_so)))

    def memory_part():
        arrive(mem_waits)
        mems = rows_of(b.m_all)
        arrive(cross_share[0])
        b.ck[...] = nn(mems, weight(b.o_cross, 0)).astype(BF)
        arrive(cross_share[1])
        b.cv[...] = nn(mems, weight(b.o_cross, 1)).astype(BF)
        spots = lax.broadcasted_iota(jnp.int32, (total_mem, 128), 0)
        cells = b.m_all[...].reshape(-1, b.m_all.shape[-1])[:, model:].astype(F32)
        b.keep[...] = ((spots < mem_length) & ((cells > 0.5) | (spots == 0))).astype(F32)

    stage = Stage(
        link, place, b.part, bufs,
        forward(0, lambda k: b.x_all[k, c, b1, b0].astype(F32), b.sum_one, b.first), b.first_all,
    )
    stage_steps(stage, self_part)
    step_fin.wait_recv()
    step_fout.wait_recv()
    ffn_share = to_share(link, place, lambda _: b.o_fin.at[t], b.o_fin.at[t])
    ffn_share += to_share(link, place, lambda _: b.o_fout.at[t], b.o_fout.at[t])
    memory_part()

    def cross_part(k):
        last.arrive(k)
        if k == 0:
            sent(ffn_share)
            arrive(cross_share[2])
        b.cq[span(k)] = nn(chunk(b.first_all, k), weight(b.o_cross, 2)).astype(BF)
        attend(
            b.cq, b.ck, b.cv, lambda start, stop: b.keep[:, 0:1] > 0.5, b.cp, b.cmix, False, block,
            k * half_rows, (k + 1) * half_rows,
        )
        if k == 0:
            arrive(co_share)
        put(k, nn(b.cmix[span(k)], rows_of(b.o_co)))

    last = stage
    stage = Stage(
        link, place, b.part, bufs, forward(1, lambda k: b.first[k], b.sum_two, b.second),
        b.second_all,
    )
    stage_steps(stage, cross_part)

    w_ins = (lambda: b.own_fin[...], lambda: b.o_fin[...].reshape(model, -1))
    w_outs = (lambda: b.own_fout[...], lambda: b.o_fout[...].reshape(-1, model))
    hidden = b.own_fin.shape[1]
    last_second = stage

    def ffn_part(k):
        last_second.arrive(k)
        if k == 0:
            sent()
            arrive(ffn_share)
        rows = chunk(b.second_all, k)
        for index in range(2):
            pre = nn(rows, w_ins[index]())
            cdf = 0.5 * (1.0 + lax.erf(pre * (0.5**0.5)))
            cols = slice(index * hidden, (index + 1) * hidden)
            b.act[span(k), cols] = (pre * cdf).astype(BF)
            b.slope[span(k), cols] = (
                cdf + pre * (jnp.exp(-0.5 * pre * pre) * 0.3989422804014327)
            ).astype(BF)
        put(k, nn(b.act[span(k), :hidden], w_outs[0]()) + nn(b.act[span(k), hidden:], w_outs[1]()))

    swap_c.wait_recv()

    def add_sums(index, k, normed, grad):
        new = (jnp.sum(grad * normed, axis=0, keepdims=True), jnp.sum(grad, axis=0, keepdims=True))
        for row, value in zip((index, 3 + index), new):
            b.sums[row : row + 1] = value if k == 0 else b.sums[row : row + 1] + value

    def turn(k, total):
        gain = b.gain[2:3]
        normed, inv = moments(b.second[k] + total)
        spots = lax.broadcasted_iota(jnp.int32, (rb, model), 0) + (k * dims["group"] + q_place) * rb
        kept = spots < length
        b.layer[k] = jnp.where(kept, normed * gain + b.bias[2:3], 0.0).astype(BF)
        grad = jnp.where(kept, b.c_own[k].astype(F32), 0.0)
        add_sums(2, k, normed, grad)
        result = norm_back(normed, inv, gain, grad)
        b.grad_third[k] = result
        return result.astype(BF)

    stage = Stage(link, place, b.part, bufs, turn, b.gy_all)
    stage_steps(stage, ffn_part)

    last_turn = stage

    def ffn_back(k):
        last_turn.arrive(k)
        if k == 0:
            sent()
        grad = chunk(b.gy_all, k)
        total = None
        for index in range(2):
            cols = slice(index * hidden, (index + 1) * hidden)
            grad_pre = (nt(grad, w_outs[index]()) * b.slope[span(k), cols].astype(F32)).astype(BF)
            b.slope[span(k), cols] = grad_pre
            term = nt(grad_pre, w_ins[index]())
            total = term if total is None else total + term
        put(k, total)

    way_fout = Hidden(
        link, place, b.g_fout, ("q_fout", dims["lines"] and "l_fout", "s_fout", "z_fout", "d_fout", "r_fout"), b
    )
    way_fin = Hidden(
        link, place, b.g_fin, ("q_fin", dims["lines"] and "l_fin", "s_fin", "z_fin", "d_fin", "r_fin"), b
    )
    way_cross = Columns(
        link, place, b.g_cross, ("q_cross", dims["lines"] and "l_cross", "s_cross", "z_cross", "d_cross", "r_cross"), b
    )
    way_self = Columns(
        link, place, b.g_self, ("q_self", dims["lines"] and "l_self", "s_self", "z_self", "d_self", "r_self"), b
    )
    way_co = Rows(
        link, place, b.g_co, ("q_co", dims["lines"] and "l_co", "s_co", "z_co", "d_co", "r_co"), b
    )
    way_so = Rows(
        link, place, b.g_so, ("q_so", dims["lines"] and "l_so", "s_so", "z_so", "d_so", "r_so"), b
    )

    def backward(index, res, summed, out):
        def mid(k, total):
            normed, inv = moments(summed[k])
            grad = res[k] + total
            add_sums(index, k, normed, grad)
            result = norm_back(normed, inv, b.gain[index : index + 1], grad)
            out[k] = result
            return result.astype(BF)

        return mid

    def out_grads():
        grad = rows_of(b.gy_all)
        for index in range(2):
            cols = slice(index * hidden, (index + 1) * hidden)
            value = tn(b.act[:, cols], grad)
            b.g_fout[index] = value.astype(BF).reshape(b.g_fout.shape[1:])
        way_fout.send()

    def in_grads():
        rows = rows_of(b.second_all)
        for index in range(2):
            cols = slice(index * hidden, (index + 1) * hidden)
            value = tn(rows, b.slope[:, cols])
            b.g_fin[index] = value.astype(BF).reshape(b.g_fin.shape[1:])
        way_fin.send()

    stage = Stage(
        link, place, b.part, bufs, backward(1, b.grad_third, b.sum_two, b.grad_r2), b.gc2_all
    )
    stage_steps(stage, ffn_back, out_grads, in_grads)

    last_back = stage
    flying = way_fout.steps + way_fin.steps

    def cross_back(k):
        last_back.arrive(k)
        if k == 0:
            sent(flying)
        b.dmix[span(k)] = nt(chunk(b.gc2_all, k), rows_of(b.o_co)).astype(BF)
        attend_back(
            b.cq, b.ck, b.cv, b.cp, b.dmix, b.dq, b.sum_dk, b.sum_dv, False, block,
            k * half_rows, (k + 1) * half_rows,
        )
        put(k, nt(b.dq[span(k)], weight(b.o_cross, 2)))

    def cross_grads():
        mems = rows_of(b.m_all)
        shape = b.g_cross.shape[1:]
        b.dck[...] = (b.sum_dk[:total_mem] * SCALE).astype(BF)
        b.dcv[...] = b.sum_dv[:total_mem].astype(BF)
        b.g_cross[0] = tn(rows_of(b.first_all), b.dq[...]).astype(BF).reshape(shape)
        b.g_cross[1] = tn(mems, b.dck[...]).astype(BF).reshape(shape)
        b.g_cross[2] = tn(mems, b.dcv[...]).astype(BF).reshape(shape)
        way_cross.send()
        b.g_co[...] = tn(b.cmix[...], rows_of(b.gc2_all)).astype(BF).reshape(b.g_co.shape)
        way_co.send()

    def part_mem():
        value = nt(b.dck[...], weight(b.o_cross, 0)) + nt(b.dcv[...], weight(b.o_cross, 1))
        b.part_m[...] = value.astype(BF).reshape(b.part_m.shape)

    stage = Stage(
        link, place, b.part, bufs, backward(0, b.grad_r2, b.sum_one, b.grad_r1), b.gc1_all
    )
    stage_steps(stage, cross_back, cross_grads, part_mem)
    flying += way_cross.steps + way_co.steps

    for k in range(2):
        stage.arrive(k)
        b.dmix[span(k)] = nt(chunk(b.gc1_all, k), rows_of(b.o_so)).astype(BF)
        attend_back(
            b.sq, b.sk, b.sv, b.sp, b.dmix, b.dq, b.sum_dk, b.sum_dv, True, block,
            k * half_rows, (k + 1) * half_rows,
        )
    sent(flying)
    b.dsk[...] = (b.sum_dk[...] * SCALE).astype(BF)
    b.dsv[...] = b.sum_dv[...].astype(BF)
    for k in range(2):
        total = nt(b.dq[span(k)], weight(b.o_self, 0)) + nt(b.dsk[span(k)], weight(b.o_self, 1))
        put(k, total + nt(b.dsv[span(k)], weight(b.o_self, 2)))
    seq_sums = []
    for d in range(1, dims["seq"]):
        seq_sums.append(
            link.send(b.sums, b.sums_seq.at[d - 1], {"seq": place.seq_shift(d)})
        )
    ks = (1 - h, h)
    red_x = Reduce(link, place, b.part, bufs)
    mem_bufs = [b.recv0_m, b.send1_m, b.recv1_m, b.keep1_m]
    if dims["bits"] == 3:
        mem_bufs += [b.send2_m, b.recv2_m]
    red_m = Reduce(link, place, b.part_m, mem_bufs)
    for red in (red_x, red_m):
        for index in range(2):
            red.start(index, ks[index])
    for red in (red_x, red_m):
        for index in range(2):
            red.middle(index, ks[index])
    swap_l = link.send(b.layer.at[1 - h], b.layer_out.at[h], partner)
    b.layer_out[h] = b.layer[h]
    rows = rows_of(b.x_all)
    shape = b.g_self.shape[1:]
    b.g_self[0] = tn(rows, b.dq[...]).astype(BF).reshape(shape)
    b.g_self[1] = tn(rows, b.dsk[...]).astype(BF).reshape(shape)
    b.g_self[2] = tn(rows, b.dsv[...]).astype(BF).reshape(shape)
    way_self.send()
    b.g_so[...] = tn(b.smix[...], rows_of(b.gc1_all)).astype(BF).reshape(b.g_so.shape)
    way_so.send()
    way_fout.add()
    b.send_x[...] = (red_x.end(0) + b.grad_r1[1 - h]).astype(BF)
    swap_x = link.send(b.send_x, b.recv_x, partner)
    b.grad_dec[h] = red_x.end(1) + b.grad_r1[h]
    b.send_m[...] = red_m.end(0).astype(BF)
    swap_m = link.send(b.send_m, b.recv_m, partner)
    b.grad_mem[h] = red_m.end(1)
    arrive(seq_sums)
    value = b.sums[...]
    for d in range(1, dims["seq"]):
        value = value + b.sums_seq[d - 1]
    b.sums_line[...] = value
    item_sums = []
    for e in range(1, dims["items"]):
        target = {"items": lax.rem(place.it + e, dims["items"])}
        item_sums.append(link.send(b.sums_line, b.sums_items.at[e - 1], target))
    way_fin.add()
    swap_x.wait_recv()
    b.grad_dec[1 - h] = b.recv_x[...].astype(F32)
    swap_m.wait_recv()
    b.grad_mem[1 - h] = b.recv_m[...].astype(F32)
    swap_l.wait_recv()
    way_fout.gather()
    way_cross.add()
    way_co.add()
    way_fin.gather()
    way_self.add()
    way_so.add()
    way_cross.gather()
    way_co.gather()
    arrive(item_sums)
    value = b.sums_line[...]
    for e in range(1, dims["items"]):
        value = value + b.sums_items[e - 1]
    b.sums_out[...] = value
    way_self.gather()
    way_so.gather()
    for way in (way_fout, way_fin, way_cross, way_co, way_self, way_so):
        way.finish()
    so_sent()
    co_sent()
    link.finish()


def shape(dims, dtype):
    return jax.ShapeDtypeStruct(tuple(dims), dtype)


def shards(
    mesh, dec_in, memory, dec_len, mem_len, cell_mask, self_query, self_key, self_value, self_out,
    cross_query, cross_key, cross_value, cross_out, ffn_in, ffn_out, norm_gain, norm_bias, cotangent,
):
    items_dev, rb, model = dec_in.shape
    mb = memory.shape[1]
    seq, items = mesh.shape["seq"], mesh.shape["items"]
    group = seq // items_dev
    share = 4
    bits = group.bit_length() - 1
    chips = group // 4
    width = model // group
    total_dec, total_mem = rb * seq, mb * seq
    heads = width // HEAD_DIM
    hidden = ffn_in.shape[1]
    wr = self_query.shape[0] // share
    fr, gr = model // share, hidden // share
    lines = items // share - 1
    dims = {
        "items_dev": items_dev, "items": items, "seq": seq, "group": group, "share": share,
        "bits": bits, "chips": chips, "width": width, "model": model, "block": 256,
        "total_dec": total_dec, "total_mem": total_mem, "lines": lines,
    }
    cells = jnp.broadcast_to((cell_mask == 1).astype(BF)[:, :, None], (items_dev, mb, 128))
    mem_cells = jnp.concatenate([memory, cells], axis=2)

    ins = [
        ("dec", dec_in, VM), ("mem", mem_cells, VM), ("cot", cotangent, VM),
        ("dec_len", dec_len, SM), ("mem_len", mem_len, SM),
        ("w_sq", self_query, HBM), ("w_sk", self_key, HBM), ("w_sv", self_value, HBM),
        ("w_so", self_out, HBM), ("w_cq", cross_query, HBM), ("w_ck", cross_key, HBM),
        ("w_cv", cross_value, HBM), ("w_co", cross_out, HBM), ("f_in", ffn_in, HBM),
        ("f_out", ffn_out, HBM), ("gain", norm_gain, VM), ("bias", norm_bias, VM),
    ]
    own, own_m = (items_dev, rb, model), (items_dev, mb, model)
    grid = (items_dev, chips, 2, 2)
    outs = [
        ("layer_out", own, BF, VM), ("grad_dec", own, F32, VM), ("grad_mem", own_m, F32, VM),
        ("sums_out", (8, model), F32, VM),
        ("r_cross", (share, 3, wr, model), BF, HBM), ("r_self", (share, 3, wr, model), BF, HBM),
        ("r_co", (share, wr, model), BF, HBM), ("r_so", (share, wr, model), BF, HBM),
        ("r_fin", (share, fr, hidden), BF, HBM), ("r_fout", (share, gr, model), BF, HBM),
    ]
    cols = (3, seq, share, wr, width)
    scratch = [
        ("x_all", grid + (rb, model), BF), ("m_all", grid + (mb, model + 128), BF),
        ("c_own", own, BF), ("staged", (8, wr, model), BF),
        ("own_fin", (model, hidden), BF), ("own_fout", (hidden, model), BF),
        ("o_self", cols, BF), ("o_cross", cols, BF),
        ("o_so", (items_dev, share, wr, model), BF), ("o_co", (items_dev, share, wr, model), BF),
        ("o_fin", (share, fr, hidden), BF), ("o_fout", (share, gr, model), BF),
        ("sq", (total_dec, width), BF), ("sk", (total_dec, width), BF), ("sv", (total_dec, width), BF),
        ("cq", (total_dec, width), BF), ("ck", (total_mem, width), BF), ("cv", (total_mem, width), BF),
        ("sp", (heads, total_dec, total_dec), BF), ("cp", (heads, total_mem, total_dec), BF),
        ("smix", (total_dec, width), BF), ("cmix", (total_dec, width), BF),
        ("keep", (total_mem, 128), F32),
        ("part", grid + (rb, model), BF), ("part_m", grid + (mb, model), BF),
        ("first_all", grid + (rb, model), BF), ("second_all", grid + (rb, model), BF),
        ("gy_all", grid + (rb, model), BF), ("gc2_all", grid + (rb, model), BF),
        ("sum_one", own, F32), ("sum_two", own, F32), ("first", own, F32), ("second", own, F32),
        ("layer", own, BF), ("sum_dk", (total_dec, width), F32), ("sum_dv", (total_dec, width), F32),
        ("act", (total_dec, 2 * hidden), BF), ("slope", (total_dec, 2 * hidden), BF),
        ("dmix", (total_dec, width), BF), ("dq", (total_dec, width), BF),
        ("dsk", (total_dec, width), BF), ("dsv", (total_dec, width), BF),
        ("dck", (total_mem, width), BF), ("dcv", (total_mem, width), BF),
        ("send_x", (rb, model), BF), ("recv_x", (rb, model), BF),
        ("send_m", (mb, model), BF), ("recv_m", (mb, model), BF),
        ("sums", (8, model), F32), ("sums_line", (8, model), F32),
        ("sums_seq", (seq - 1, 8, model), F32), ("sums_items", (items - 1, 8, model), F32),
    ]
    for name, rows in (("", rb), ("_m", mb)):
        scratch += [
            ("recv0" + name, (items_dev, chips, 2, rows, model), BF),
            ("send1" + name, (items_dev, chips, rows, model), BF),
            ("recv1" + name, (items_dev, chips, rows, model), BF),
            ("keep1" + name, (items_dev, chips, rows, model), F32),
        ]
        if bits == 3:
            scratch += [
                ("send2" + name, (items_dev, rows, model), BF),
                ("recv2" + name, (items_dev, rows, model), BF),
            ]
    for name, grad, quarter, moved, done in (
        ("fin", (2, share, fr, hidden), (2, fr, hidden), (fr, hidden), (fr, hidden)),
        ("fout", (2, share, gr, model), (2, gr, model), (gr, model), (gr, model)),
        ("cross", cols, (3, seq, wr, width), (seq, 3, wr, width), (3, wr, model)),
        ("self", cols, (3, seq, wr, width), (seq, 3, wr, width), (3, wr, model)),
        ("co", (items_dev, share, wr, model), (items_dev, wr, model), (items_dev, wr, model), (wr, model)),
        ("so", (items_dev, share, wr, model), (items_dev, wr, model), (items_dev, wr, model), (wr, model)),
    ):
        scratch += [
            ("g_" + name, grad, BF), ("q_" + name, (share - 1,) + quarter, BF),
            ("s_" + name, quarter, BF), ("z_" + name, moved, BF), ("d_" + name, done, BF),
        ]
        if lines:
            scratch.append(("l_" + name, (lines,) + quarter, BF))
    copies = 320 + 16 * (seq - 8) + 12 * (bits - 2) + 12 * lines
    names = [x[0] for x in ins + outs + scratch] + ["send_sems", "recv_sems"]
    results = pl.pallas_call(
        functools.partial(layer_kernel, dims, names),
        name="layer",
        out_shape=[shape(x[1], x[2]) for x in outs],
        in_specs=[x[2] for x in ins],
        out_specs=[x[3] for x in outs],
        scratch_shapes=[pltpu.VMEM(x[1], x[2]) for x in scratch]
        + [pltpu.SemaphoreType.DMA((copies,)), pltpu.SemaphoreType.DMA((copies,))],
        compiler_params=pltpu.CompilerParams(
            collective_id=0, has_side_effects=True, vmem_limit_bytes=VMEM_BYTES
        ),
    )(*[x[1] for x in ins])
    layer_out, grad_dec, grad_memory, sums, r_cross, r_self, r_co, r_so, r_fin, r_fout = results
    f_cross = r_cross.transpose(1, 0, 2, 3).reshape(3, share * wr, model).astype(F32)
    f_self = r_self.transpose(1, 0, 2, 3).reshape(3, share * wr, model).astype(F32)
    return (
        layer_out, grad_dec, grad_memory,
        f_self[0], f_self[1], f_self[2], r_so.reshape(share * wr, model).astype(F32),
        f_cross[0], f_cross[1], f_cross[2], r_co.reshape(share * wr, model).astype(F32),
        r_fin.reshape(model, hidden).astype(F32), r_fout.reshape(hidden, model).astype(F32),
        sums[0:3], sums[3:6],
    )


def solution(mesh):
    rows = P("seq", None)
    tokens = P("items", "seq", None)
    placed = (
        (tokens, tokens, P("items"), P("items"), P("items", "seq"))
        + (rows,) * 8
        + (P(None, "seq"), rows, P(), P(), tokens)
    )
    return jax.shard_map(
        functools.partial(shards, mesh),
        mesh=mesh,
        in_specs=placed,
        out_specs=(tokens,) * 3 + (rows,) * 8 + (P(None, "seq"), rows, P(), P()),
        check_vma=False,
    )
```

```python
import functools

import jax
import jax.numpy as jnp
from jax import lax
from jax.experimental import pallas as pl
from jax.experimental.pallas import tpu as pltpu
from jax.sharding import PartitionSpec as P

HEAD_DIM = 64
EPS = 1e-05
NEG = -1e30
SCALE = HEAD_DIM ** (-0.5)
BF = jnp.bfloat16
F32 = jnp.float32
VMEM_BYTES = 63 * 1024 * 1024
MESH = pl.DeviceIdType.MESH
VM = pl.BlockSpec(memory_space=pltpu.VMEM)
HBM = pl.BlockSpec(memory_space=pl.ANY)
SM = pl.BlockSpec(memory_space=pltpu.SMEM)


def nn(left, right):
    return lax.dot_general(left, right, (((1,), (0,)), ((), ())), preferred_element_type=F32)


def nt(left, right):
    return lax.dot_general(left, right, (((1,), (1,)), ((), ())), preferred_element_type=F32)


def tn(left, right):
    return lax.dot_general(left, right, (((0,), (0,)), ((), ())), preferred_element_type=F32)


class Link:
    def __init__(self, send_sems, recv_sems, first=0):
        self.send_sems, self.recv_sems, self.count, self.open = send_sems, recv_sems, first, []

    def index(self):
        self.count += 1
        return self.count - 1

    def make(self, src, dst, device, index):
        return pltpu.make_async_remote_copy(
            src_ref=src,
            dst_ref=dst,
            send_sem=self.send_sems.at[index],
            recv_sem=self.recv_sems.at[index],
            device_id=device,
            device_id_type=MESH,
        )

    def send(self, src, dst, device):
        copy = self.make(src, dst, device, self.index())
        copy.start()
        self.open.append(copy)
        return copy

    def batch(self, copies, whole):
        index = self.index()
        for copy in copies:
            self.make(*copy, index).start()
        wait = self.make(whole, whole, copies[0][2], index)
        self.open.append(wait)
        return wait

    def local(self, src, dst):
        copy = pltpu.make_async_copy(src, dst, self.send_sems.at[self.index()])
        copy.start()
        return copy

    def finish(self, kept=()):
        late = {id(copy) for copy in kept}
        for copy in self.open:
            if id(copy) not in late:
                copy.wait_send()
        self.open = [copy for copy in self.open if id(copy) in late]


def greet(devices):
    barrier = pltpu.get_barrier_semaphore()
    for device in devices:
        pl.semaphore_signal(barrier, inc=1, device_id=device, device_id_type=MESH)
    pl.semaphore_wait(barrier, len(devices))


class Place:
    def __init__(self, dims):
        self.dims = dims
        group, share = dims["group"], dims["share"]
        self.me = lax.axis_index("seq")
        self.h = self.me // group
        self.q = self.me % group
        self.b0 = self.q % 2
        self.b1 = (self.q // 2) % 2
        self.c = self.q // 4
        self.it = lax.axis_index("items")
        self.base = (self.it // share) * share
        self.t = self.it % share
        x, y = self.t % 2, self.t // 2
        self.tx, self.ty, self.txy = y * 2 + 1 - x, (1 - y) * 2 + x, (1 - y) * 2 + 1 - x

    def across(self, bit):
        value = (self.q // (1 << bit)) % 2
        return {"seq": self.me + (1 - 2 * value) * (1 << bit)}

    def partner(self):
        return {"seq": (1 - self.h) * self.dims["group"] + self.q}

    def seq_shift(self, d):
        return lax.rem(self.me + d, self.dims["seq"])

    def line(self, t):
        return {"items": self.base + t}

    def seq_peers(self):
        return [{"seq": self.seq_shift(d)} for d in range(1, self.dims["seq"])]

    def items_peers(self):
        count = self.dims["items"]
        return [{"items": lax.rem(self.it + e, count)} for e in range(1, count)]


def spread_start(link, place, out, k):
    bits = place.dims["bits"]
    c, b1, b0 = place.c, place.b1, place.b0
    if bits == 3:
        step = link.send(out.at[k, c, b1, b0], out.at[k, c, b1, b0], place.across(2))
        step.wait_recv()
    waits = []
    high = link.send(out.at[k, :, b1, b0], out.at[k, :, b1, b0], place.across(1))
    waits.append(link.send(out.at[k, :, b1, b0], out.at[k, :, b1, b0], place.across(0)))
    return high, waits


def spread_end(link, place, out, k, started):
    high, waits = started
    b1, b0 = place.b1, place.b0
    high.wait_recv()
    waits.append(link.send(out.at[k, :, 1 - b1, b0], out.at[k, :, 1 - b1, b0], place.across(0)))
    return waits


def columns_out(link, place, src, dst, width):
    seq, group = place.dims["seq"], place.dims["group"]
    copies = []
    for d in range(1, seq):
        target = place.seq_shift(d)
        cols = pl.ds(pl.multiple_of(lax.rem(target, group) * width, width), width)
        copies.append((src.at[:, cols], dst.at[place.me, place.t], {"seq": target}))
    steps = [link.batch(copies, dst.at[0 : seq - 1, place.t])]
    cols = pl.ds(pl.multiple_of(place.q * width, width), width)
    return steps, link.local(src.at[:, cols], dst.at[place.me, place.t])


def rows_out(link, place, src, dst):
    dims, me = place.dims, place.me
    slot = lax.rem(me, dims["items_dev"])
    base = link.count
    link.count += dims["items_dev"] + 1
    copies = []
    for half in range(dims["items_dev"]):
        target = half * dims["group"] + me // dims["items_dev"]
        copy = pltpu.make_async_remote_copy(
            src_ref=src,
            dst_ref=dst.at[slot, place.t],
            send_sem=link.send_sems.at[base + half],
            recv_sem=link.recv_sems.at[base + slot],
            device_id={"seq": target},
            device_id_type=MESH,
        )
        copies.append((target != me, copy))
        pl.when(target != me)(copy.start)
    own = pltpu.make_async_copy(
        src, dst.at[slot, place.t], link.send_sems.at[base + dims["items_dev"]]
    )
    mine = me // dims["items_dev"] == place.q
    pl.when(mine)(own.start)

    def arrived():
        pl.when(mine)(own.wait)
        for block in range(dims["items_dev"]):
            copy = pltpu.make_async_remote_copy(
                src_ref=src,
                dst_ref=dst.at[block, place.t],
                send_sem=link.send_sems.at[base],
                recv_sem=link.recv_sems.at[base + block],
                device_id={"seq": me},
                device_id_type=MESH,
            )
            pl.when(place.q * dims["items_dev"] + block != me)(copy.wait_recv)

    def sent():
        for other, copy in copies:
            pl.when(other)(copy.wait_send)

    return arrived, sent


class Share:
    def __init__(self, link, place, slab, half):
        self.link, self.place, self.half = link, place, half
        t = place.t
        self.from_x = link.send(slab(t), slab(t), place.line(place.tx))
        self.from_y = link.send(slab(t), slab(t), place.line(place.ty))

    def forward(self):
        link, place, half = self.link, self.place, self.half
        self.from_y.wait_recv()
        part = half(place.ty, 0)
        self.steps = [link.send(part, part, place.line(place.tx))]
        self.from_x.wait_recv()
        part = half(place.tx, 1)
        self.steps.append(link.send(part, part, place.line(place.ty)))

    def wait(self):
        arrive(self.steps)


def arrive(steps):
    for step in steps:
        step.wait_recv()


class Reduce:
    def __init__(self, link, place, part, bufs):
        self.link, self.place, self.part, self.bufs = link, place, part, bufs
        self.zero, self.one = {}, {}

    def start(self, index, k):
        place = self.place
        self.zero[index] = self.link.send(
            self.part.at[k, :, :, 1 - place.b0], self.bufs[0].at[index], place.across(0)
        )

    def middle(self, index, k):
        place, part = self.place, self.part
        recv0, send1, recv1, keep1 = self.bufs[:4]
        self.zero[index].wait_recv()
        b1, b0 = place.b1, place.b0
        for c in range(part.shape[1]):
            value = part[k, c, 1 - b1, b0].astype(F32) + recv0[index, c, 1 - b1].astype(F32)
            send1[index, c] = value.astype(BF)
        self.one[index] = self.link.send(send1.at[index], recv1.at[index], place.across(1))
        for c in range(part.shape[1]):
            keep1[index, c] = part[k, c, b1, b0].astype(F32) + recv0[index, c, b1].astype(F32)

    def end(self, index):
        place = self.place
        recv1, keep1 = self.bufs[2:4]
        self.one[index].wait_recv()
        if place.dims["bits"] == 2:
            return keep1[index, 0] + recv1[index, 0].astype(F32)
        send2, recv2 = self.bufs[4:6]
        c = place.c
        send2[index] = (keep1[index, 1 - c] + recv1[index, 1 - c].astype(F32)).astype(BF)
        step = self.link.send(send2.at[index], recv2.at[index], place.across(2))
        kept = keep1[index, c] + recv1[index, c].astype(F32)
        step.wait_recv()
        return kept + recv2[index].astype(F32)


def reduce_bufs(dims, rows):
    items_dev, width, chips = dims["items_dev"], dims["model"], dims["chips"]
    bufs = [
        pltpu.VMEM((items_dev, chips, 2, rows, width), BF),
        pltpu.VMEM((items_dev, chips, rows, width), BF),
        pltpu.VMEM((items_dev, chips, rows, width), BF),
        pltpu.VMEM((items_dev, chips, rows, width), F32),
    ]
    if dims["bits"] == 3:
        bufs += [pltpu.VMEM((items_dev, rows, width), BF) for _ in range(2)]
    return bufs


def moments(value):
    mean = jnp.mean(value, axis=-1, keepdims=True)
    centered = value - mean
    inv = lax.rsqrt(jnp.mean(centered * centered, axis=-1, keepdims=True) + EPS)
    return centered * inv, inv


def norm_back(normed, inv, gain, grad):
    scaled = grad * gain
    mean = jnp.mean(scaled, axis=-1, keepdims=True)
    cross = jnp.mean(scaled * normed, axis=-1, keepdims=True)
    return inv * (scaled - mean - normed * cross)


def rows_back(link, place, src, dst):
    dims, me, h = place.dims, place.me, place.h
    count = dims["items_dev"]
    base = link.count
    link.count += count + 1
    copies = []
    for k in range(count):
        target = place.q * count + k
        copy = pltpu.make_async_remote_copy(
            src_ref=src.at[k],
            dst_ref=dst.at[h],
            send_sem=link.send_sems.at[base + k],
            recv_sem=link.recv_sems.at[base + h],
            device_id={"seq": target},
            device_id_type=MESH,
        )
        copies.append((target != me, copy))
        pl.when(target != me)(copy.start)
    own = pltpu.make_async_copy(
        src.at[lax.rem(me, count)], dst.at[h], link.send_sems.at[base + count]
    )
    mine = me // count == place.q
    pl.when(mine)(own.start)

    def done():
        pl.when(mine)(own.wait)
        for half in range(count):
            copy = pltpu.make_async_remote_copy(
                src_ref=src.at[0],
                dst_ref=dst.at[half],
                send_sem=link.send_sems.at[base],
                recv_sem=link.recv_sems.at[base + half],
                device_id={"seq": me},
                device_id_type=MESH,
            )
            pl.when(half * dims["group"] + me // count != me)(copy.wait_recv)
        for other, copy in copies:
            pl.when(other)(copy.wait_send)

    return done


def half_mask(rows, half):
    return (lax.broadcasted_iota(jnp.int32, (rows, 128), 1) // HEAD_DIM) == half


def attend(q_ref, k_ref, v_ref, valid, p_ref, mix_ref, causal, block, first, last, pump):
    keys = k_ref.shape[0]
    for pair in range(q_ref.shape[1] // 128):
        lanes = slice(pair * 128, pair * 128 + 128)
        for start in range(first, last, block):
            stop = start + block if causal else keys
            halves = []
            for half in range(2):
                query = q_ref[start : start + block, lanes]
                query = jnp.where(half_mask(block, half), query, jnp.zeros_like(query))
                scores = nt(k_ref[:stop, lanes], query) * SCALE
                scores = jnp.where(valid(start, stop), scores, NEG)
                top = jnp.max(scores, axis=0, keepdims=True)
                grown = jnp.exp(scores - top)
                probs = (grown * (1.0 / jnp.sum(grown, axis=0, keepdims=True))).astype(BF)
                p_ref[2 * pair + half, :stop, start : start + block] = probs
                mixed = tn(v_ref[:stop, lanes], probs)
                halves.append(mixed[half * HEAD_DIM : (half + 1) * HEAD_DIM])
            mix_ref[start : start + block, lanes] = jnp.concatenate(halves, axis=0).T.astype(BF)
        if pair == 0:
            pump()


def attend_back(
    q_ref, k_ref, v_ref, p_ref, grad_ref, dq_ref, dk_ref, dv_ref, causal, block, first, last,
    pump,
):
    keys = k_ref.shape[0]
    for pair in range(q_ref.shape[1] // 128):
        lanes = slice(pair * 128, pair * 128 + 128)
        for start in range(first, last, block):
            stop = start + block if causal else keys
            halves = []
            sum_k, sum_v = None, None
            for half in range(2):
                mask = half_mask(block, half)
                query = q_ref[start : start + block, lanes]
                query = jnp.where(mask, query, jnp.zeros_like(query))
                grad = grad_ref[start : start + block, lanes]
                grad = jnp.where(mask, grad, jnp.zeros_like(grad))
                low = p_ref[2 * pair + half, :stop, start : start + block]
                probs = low.astype(F32)
                grad_probs = nt(v_ref[:stop, lanes], grad)
                delta = jnp.sum(probs * grad_probs, axis=0, keepdims=True)
                grad_scores = (probs * (grad_probs - delta)).astype(BF)
                turned = tn(k_ref[:stop, lanes], grad_scores) * SCALE
                halves.append(turned[half * HEAD_DIM : (half + 1) * HEAD_DIM])
                new_k, new_v = nn(grad_scores, query), nn(low, grad)
                sum_k = new_k if sum_k is None else sum_k + new_k
                sum_v = new_v if sum_v is None else sum_v + new_v
            old = start if causal else (keys if start else 0)
            for ref, value in ((dk_ref, sum_k), (dv_ref, sum_v)):
                if old:
                    ref[:old, lanes] = ref[:old, lanes] + value[:old]
                if old < stop:
                    ref[old:stop, lanes] = value[old:]
            dq_ref[start : start + block, lanes] = jnp.concatenate(halves, axis=0).T.astype(BF)
        if pair == 0:
            pump()


class Box:
    def __init__(self, names, refs):
        for name, ref in zip(names, refs):
            setattr(self, name, ref)


class Quarters:
    def __init__(self, link, place, grad, box_names, box):
        self.link, self.place, self.grad = link, place, grad
        self.recv, self.sums, self.last, self.lines, self.total, self.moved, self.done, self.out = (
            getattr(box, name) if name else None for name in box_names
        )

    def send(self):
        place, piece, link = self.place, self.piece, self.link
        self.steps = []
        for i, near in enumerate((place.tx, place.ty)):
            copies = [
                (self.grad.at[piece(near, i)], self.recv.at[i, 0], place.line(near)),
                (self.grad.at[piece(place.txy, i)], self.recv.at[i, 1], place.line(near)),
            ]
            self.steps.append(link.batch(copies, self.recv.at[i]))
        self.flying = list(self.steps)

    def turn(self):
        place, piece, link = self.place, self.piece, self.link
        steps = []
        for i, far in enumerate((place.ty, place.tx)):
            self.steps[i].wait_recv()
            value = self.grad[piece(far, i)].astype(F32) + self.recv[i, 1].astype(F32)
            self.sums[i] = value.astype(BF)
            steps.append(link.send(self.sums.at[i], self.last.at[i], place.line(far)))
        self.steps = steps
        self.flying += steps

    def add(self):
        place = self.place
        for i in range(2):
            self.steps[i].wait_recv()
            value = self.grad[self.piece(place.t, i)].astype(F32)
            value = value + self.recv[i, 0].astype(F32) + self.last[i].astype(F32)
            self.total[self.halves(i)] = value.astype(BF)
        if self.lines is not None:
            share, items = place.dims["share"], place.dims["items"]
            copies = []
            for a in range(1, items // share):
                target = {"items": lax.rem(place.it + a * share, items)}
                copies.append((self.total, self.lines.at[a - 1], target))
            step = self.link.batch(copies, self.lines)
            step.wait()
            self.link.open.pop()
            value = self.total[...].astype(F32)
            for a in range(1, items // share):
                value = value + self.lines[a - 1].astype(F32)
            self.total[...] = value.astype(BF)
        self.along()

    def gather(self):
        self.close()
        place, out = self.place, self.out
        self.own = self.link.local(self.done, out.at[place.t])
        self.near = [
            self.link.send(self.done, out.at[place.t], place.line(near))
            for near in (place.tx, place.ty)
        ]

    def forward(self):
        place, out, link = self.place, self.out, self.link
        self.steps = []
        for i, (source, near) in enumerate(((place.ty, place.tx), (place.tx, place.ty))):
            self.near[1 - i].wait_recv()
            part = out.at[self.cut(source, i)]
            self.steps.append(link.send(part, part, place.line(near)))

    def finish(self):
        arrive(self.steps)
        self.own.wait()


class Hidden(Quarters):
    def piece(self, t, i):
        rows = self.grad.shape[2] // 2
        return slice(None), t, slice(i * rows, (i + 1) * rows)

    def halves(self, i):
        rows = self.grad.shape[2] // 2
        return slice(None), slice(i * rows, (i + 1) * rows)

    def cut(self, t, i):
        rows = self.out.shape[1] // 2
        return t, slice(i * rows, (i + 1) * rows)

    def along(self):
        self.steps = [self.link.send(self.total.at[1], self.moved, self.place.partner())]

    def close(self):
        arrive(self.steps)
        self.done[...] = (self.total[0].astype(F32) + self.moved[...].astype(F32)).astype(BF)


class Columns(Quarters):
    def piece(self, t, i):
        blocks = self.grad.shape[1] // 2
        return slice(None), slice(i * blocks, (i + 1) * blocks), t

    def halves(self, i):
        blocks = self.grad.shape[1] // 2
        return slice(None), slice(i * blocks, (i + 1) * blocks)

    def cut(self, t, i):
        cols = self.out.shape[3] // 2
        return t, slice(None), slice(None), slice(i * cols, (i + 1) * cols)

    def along(self):
        place = self.place
        copies = []
        for d in range(1, place.dims["seq"]):
            target = place.seq_shift(d)
            copies.append((self.total.at[:, target], self.moved.at[place.me], {"seq": target}))
        self.steps = [self.link.batch(copies, self.moved.at[0 : place.dims["seq"] - 1])]
        self.own = self.link.local(self.total.at[:, place.me], self.moved.at[place.me])

    def close(self):
        arrive(self.steps)
        self.own.wait()
        dims = self.place.dims
        group, width = dims["group"], dims["width"]
        for index in range(3):
            for q in range(group):
                value = self.moved[q, index].astype(F32)
                for half in range(1, dims["items_dev"]):
                    value = value + self.moved[half * group + q, index].astype(F32)
                self.done[index, :, q * width : (q + 1) * width] = value.astype(BF)


class Rows(Quarters):
    def piece(self, t, i):
        return i, t

    def halves(self, i):
        return i

    def cut(self, t, i):
        cols = self.out.shape[2] // 2
        return t, slice(None), slice(i * cols, (i + 1) * cols)

    def along(self):
        self.moved_done = rows_back(self.link, self.place, self.total, self.moved)

    def close(self):
        self.moved_done()
        value = self.moved[0].astype(F32)
        for half in range(1, self.place.dims["items_dev"]):
            value = value + self.moved[half].astype(F32)
        self.done[...] = value.astype(BF)


class Stage:
    def __init__(self, sems, place, part, bufs, mid, spread, before):
        self.link, self.place, self.mid, self.spread = Link(*sems), place, mid, spread
        self.before = before
        self.reduce = Reduce(self.link, place, part, bufs)
        self.started, self.waits = {}, {}

    def start(self, k):
        self.reduce.start(k, k)

    def middle(self, k):
        self.reduce.middle(k, k)

    def end(self, k):
        place, spread = self.place, self.spread
        spread[k, place.c, place.b1, place.b0] = self.mid(k, self.reduce.end(k))
        self.started[k] = spread_start(self.link, place, spread, k)

    def forward(self, k):
        self.waits[k] = spread_end(self.link, self.place, self.spread, k, self.started[k])

    def arrive(self, k):
        arrive(self.waits[k])

    def release(self, k):
        done = (self.reduce.zero[k], self.reduce.one[k])
        for copy in done:
            copy.wait_send()
        late = {id(copy) for copy in done}
        self.link.open = [copy for copy in self.link.open if id(copy) not in late]


def stage_steps(stage, compute, flight=None, ended=None, after=None):
    before = stage.before
    compute(0, (lambda: before.forward(1)) if before else (lambda: None))
    stage.start(0)
    compute(1, lambda: None)
    stage.start(1)
    if before:
        before.link.finish()
    stage.middle(0)
    stage.middle(1)
    if flight:
        flight()
    stage.end(0)
    stage.end(1)
    if ended:
        ended()
    stage.forward(0)
    if after:
        after()


def layer_kernel(dims, names, *refs):
    b = Box(names, refs)
    b.grad_third, b.grad_r2, b.grad_r1, b.gc1_all = b.first, b.second, b.first, b.gy_all
    place = Place(dims)
    sems = b.send_sems, b.recv_sems
    link = Link(*sems, dims["chain"])
    width, block, items_dev = dims["width"], dims["block"], dims["items_dev"]
    h, t, q_place = place.h, place.t, place.q
    c, b1, b0 = place.c, place.b1, place.b0
    partner = place.partner()
    wr = b.w_sq.shape[0] // dims["share"]
    model = dims["model"]
    total_dec, total_mem = dims["total_dec"], dims["total_mem"]
    rb = b.dec.shape[1]

    def rows_of(ref, cols=model):
        return ref[...].reshape(-1, ref.shape[-1])[:, :cols]

    def chunk(ref, k):
        return ref[k].reshape(-1, model)

    half_rows = total_dec // 2

    def span(k):
        return slice(k * half_rows, (k + 1) * half_rows)

    def put(k, value, before=None):
        if before:
            before.release(k)
        b.part[k] = value.astype(BF).reshape(b.part.shape[1:])

    def weight(ref, index):
        return ref[index].reshape(model, width)

    weights = (b.w_sq, b.w_sk, b.w_sv, b.w_so, b.w_ck, b.w_cv, b.w_cq, b.w_co)
    rows_t = pl.ds(pl.multiple_of(t * wr, wr), wr)
    staged = [link.local(w.at[rows_t], b.staged.at[i]) for i, w in enumerate(weights)]
    own_fin = link.local(b.f_in, b.own_fin)
    own_fout = link.local(b.f_out, b.own_fout)
    greet(place.seq_peers() + place.items_peers())

    swap_x = link.send(b.dec.at[1 - h], b.x_all.at[h, c, b1, b0], partner)
    b.x_all[h, c, b1, b0] = b.dec[h]
    first_x = spread_start(link, place, b.x_all, h)
    for copy in staged:
        copy.wait()
    self_steps = [columns_out(link, place, b.staged.at[i], b.o_self.at[i], width) for i in range(3)]
    waits = spread_end(link, place, b.x_all, h, first_x)
    swap_x.wait_recv()
    second_x = spread_start(link, place, b.x_all, 1 - h)
    so_arrived, so_sent = rows_out(link, place, b.staged.at[3], b.o_so)

    def share_columns(steps, dst):
        arrive(steps[0])
        steps[1].wait()
        blocks = dims["seq"] // 2
        return Share(
            link, place, lambda t: dst.at[:, t],
            lambda t, i: dst.at[i * blocks : (i + 1) * blocks, t],
        )

    def share_rows(dst):
        return Share(link, place, lambda t: dst.at[:, t], lambda t, i: dst.at[i, t])

    def share_hidden(dst):
        rows = dst.shape[1] // 2
        return Share(
            link, place, lambda t: dst.at[t], lambda t, i: dst.at[t, i * rows : (i + 1) * rows]
        )

    self_share = [share_columns(self_steps[i], b.o_self.at[i]) for i in range(3)]
    waits += spread_end(link, place, b.x_all, 1 - h, second_x)
    so_arrived()
    so_share = share_rows(b.o_so)
    cross_steps = [
        columns_out(link, place, b.staged.at[4 + i], b.o_cross.at[i], width) for i in range(3)
    ]
    co_arrived, co_sent = rows_out(link, place, b.staged.at[7], b.o_co)
    b.m_all[h, c, b1, b0] = b.mem[h]
    swap_m = link.send(b.mem.at[1 - h], b.m_all.at[h, c, b1, b0], partner)
    first_m = spread_start(link, place, b.m_all, h)
    for share in self_share:
        share.forward()

    arrive(waits)
    rows = rows_of(b.x_all)
    for index, dst in enumerate((b.sq, b.sk, b.sv)):
        self_share[index].wait()
        dst[...] = nn(rows, weight(b.o_self, index)).astype(BF)
    so_share.forward()
    cross_share = [share_columns(cross_steps[i], b.o_cross.at[i]) for i in range(3)]
    co_arrived()
    co_share = share_rows(b.o_co)
    mem_waits = spread_end(link, place, b.m_all, h, first_m)
    swap_m.wait_recv()
    second_m = spread_start(link, place, b.m_all, 1 - h)
    own_fin.wait()
    own_fout.wait()
    fr, gr = b.o_fin.shape[1], b.o_fout.shape[1]
    step_fin = link.send(b.own_fin.at[pl.ds(pl.multiple_of(t * fr, fr), fr)], b.o_fin.at[t], partner)
    step_fout = link.send(
        b.own_fout.at[pl.ds(pl.multiple_of(t * gr, gr), gr)], b.o_fout.at[t], partner
    )
    length, mem_length = b.dec_len[h], b.mem_len[h]

    def self_ok(start, stop):
        keys = lax.broadcasted_iota(jnp.int32, (stop, block), 0)
        spots = lax.broadcasted_iota(jnp.int32, (stop, block), 1) + start
        return (keys <= spots) & (keys < length)

    bufs = [b.recv0, b.send1, b.recv1, b.keep1]
    if dims["bits"] == 3:
        bufs += [b.send2, b.recv2]

    def forward(index, res, summed, out):
        def mid(k, total):
            value = res(k) + total
            summed[k] = value
            normed, _ = moments(value)
            result = normed * b.gain[index : index + 1] + b.bias[index : index + 1]
            out[k] = result
            return result.astype(BF)

        return mid

    def self_part(k, pump):
        attend(
            b.sq, b.sk, b.sv, self_ok, b.sp, b.smix, True, block,
            k * half_rows, (k + 1) * half_rows, pump,
        )
        if k == 0:
            so_share.wait()
        put(k, nn(b.smix[span(k)], rows_of(b.o_so)))

    def memory_part():
        arrive(mem_waits)
        mems = rows_of(b.m_all)
        cross_share[0].wait()
        b.ck[...] = nn(mems, weight(b.o_cross, 0)).astype(BF)
        cross_share[1].wait()
        b.cv[...] = nn(mems, weight(b.o_cross, 1)).astype(BF)
        spots = lax.broadcasted_iota(jnp.int32, (total_mem, 128), 0)
        cells = b.m_all[...].reshape(-1, b.m_all.shape[-1])[:, model:].astype(F32)
        b.keep[...] = ((spots < mem_length) & ((cells > 0.5) | (spots == 0))).astype(F32)

    stage = Stage(
        sems, place, b.part, bufs,
        forward(0, lambda k: b.x_all[k, c, b1, b0].astype(F32), b.sum_one, b.first), b.first_all, None,
    )
    def cross_weights():
        mem_waits.extend(spread_end(link, place, b.m_all, 1 - h, second_m))
        for share in cross_share + [co_share]:
            share.forward()

    stage_steps(stage, self_part, after=cross_weights)
    memory_part()
    b.c_own[h] = b.cot[h]
    swap_c = link.send(b.cot.at[1 - h], b.c_own.at[h], partner)
    ffn_share = []

    def cross_part(k, pump):
        last.arrive(k)
        if k == 0:
            cross_share[2].wait()
        b.cq[span(k)] = nn(chunk(b.first_all, k), weight(b.o_cross, 2)).astype(BF)
        attend(
            b.cq, b.ck, b.cv, lambda start, stop: b.keep[:, 0:1] > 0.5, b.cp, b.cmix, False, block,
            k * half_rows, (k + 1) * half_rows, pump,
        )
        if k == 0:
            co_share.wait()
            step_fin.wait_recv()
            ffn_share.append(share_hidden(b.o_fin))
        put(k, nn(b.cmix[span(k)], rows_of(b.o_co)), last)

    last = stage
    stage = Stage(
        sems, place, b.part, bufs, forward(1, lambda k: b.first[k], b.sum_two, b.second),
        b.second_all, last,
    )
    def ffn_weights():
        step_fout.wait_recv()
        ffn_share.append(share_hidden(b.o_fout))
        for share in ffn_share:
            share.forward()

    stage_steps(stage, cross_part, after=ffn_weights)

    w_ins = (lambda: b.own_fin[...], lambda: b.o_fin[...].reshape(model, -1))
    w_outs = (lambda: b.own_fout[...], lambda: b.o_fout[...].reshape(-1, model))
    hidden = b.own_fin.shape[1]
    last_second = stage

    def ffn_part(k, pump):
        last_second.arrive(k)
        if k == 0:
            ffn_share[0].wait()
        rows = chunk(b.second_all, k)
        for index in range(2):
            if index:
                pump()
            pre = nn(rows, w_ins[index]())
            cdf = 0.5 * (1.0 + lax.erf(pre * (0.5**0.5)))
            cols = slice(index * hidden, (index + 1) * hidden)
            b.act[span(k), cols] = (pre * cdf).astype(BF)
            b.slope[span(k), cols] = (
                cdf + pre * (jnp.exp(-0.5 * pre * pre) * 0.3989422804014327)
            ).astype(BF)
        if k == 0:
            ffn_share[1].wait()
        total = nn(b.act[span(k), :hidden], w_outs[0]())
        put(k, total + nn(b.act[span(k), hidden:], w_outs[1]()), last_second)

    swap_c.wait_recv()

    def add_sums(index, k, normed, grad):
        new = (jnp.sum(grad * normed, axis=0, keepdims=True), jnp.sum(grad, axis=0, keepdims=True))
        for row, value in zip((index, 3 + index), new):
            b.sums[row : row + 1] = value if k == 0 else b.sums[row : row + 1] + value

    def turn(k, total):
        gain = b.gain[2:3]
        normed, inv = moments(b.second[k] + total)
        spots = lax.broadcasted_iota(jnp.int32, (rb, model), 0) + (k * dims["group"] + q_place) * rb
        kept = spots < length
        b.layer[k] = jnp.where(kept, normed * gain + b.bias[2:3], 0.0).astype(BF)
        grad = jnp.where(kept, b.c_own[k].astype(F32), 0.0)
        add_sums(2, k, normed, grad)
        result = norm_back(normed, inv, gain, grad)
        b.grad_third[k] = result
        return result.astype(BF)

    stage = Stage(sems, place, b.part, bufs, turn, b.gy_all, last_second)
    stage_steps(stage, ffn_part)

    last_turn = stage

    def ffn_back(k, pump):
        last_turn.arrive(k)
        grad = chunk(b.gy_all, k)
        total = None
        for index in range(2):
            if index:
                pump()
            cols = slice(index * hidden, (index + 1) * hidden)
            grad_pre = (nt(grad, w_outs[index]()) * b.slope[span(k), cols].astype(F32)).astype(BF)
            b.slope[span(k), cols] = grad_pre
            term = nt(grad_pre, w_ins[index]())
            total = term if total is None else total + term
        put(k, total, last_turn)

    way_fout = Hidden(
        link, place, b.g_fout, ("q_fout", "t_fout", "u_fout", dims["lines"] and "l_fout", "s_fout", "z_fout", "d_fout", "r_fout"), b
    )
    way_fin = Hidden(
        link, place, b.g_fin, ("q_fin", "t_fin", "u_fin", dims["lines"] and "l_fin", "s_fin", "z_fin", "d_fin", "r_fin"), b
    )
    way_cross = Columns(
        link, place, b.g_cross, ("q_cross", "t_cross", "u_cross", dims["lines"] and "l_cross", "s_cross", "z_cross", "d_cross", "r_cross"), b
    )
    way_self = Columns(
        link, place, b.g_self, ("q_self", "t_self", "u_self", dims["lines"] and "l_self", "s_self", "z_self", "d_self", "r_self"), b
    )
    way_co = Rows(
        link, place, b.g_co, ("q_co", "t_co", "u_co", dims["lines"] and "l_co", "s_co", "z_co", "d_co", "r_co"), b
    )
    way_so = Rows(
        link, place, b.g_so, ("q_so", "t_so", "u_so", dims["lines"] and "l_so", "s_so", "z_so", "d_so", "r_so"), b
    )

    def backward(index, res, summed, out):
        def mid(k, total):
            normed, inv = moments(summed[k])
            grad = res[k] + total
            add_sums(index, k, normed, grad)
            result = norm_back(normed, inv, b.gain[index : index + 1], grad)
            out[k] = result
            return result.astype(BF)

        return mid

    def out_grads():
        grad = rows_of(b.gy_all)
        for index in range(2):
            cols = slice(index * hidden, (index + 1) * hidden)
            value = tn(b.act[:, cols], grad)
            b.g_fout[index] = value.astype(BF).reshape(b.g_fout.shape[1:])
        way_fout.send()

    def in_grads():
        rows = rows_of(b.second_all)
        for index in range(2):
            cols = slice(index * hidden, (index + 1) * hidden)
            value = tn(rows, b.slope[:, cols])
            b.g_fin[index] = value.astype(BF).reshape(b.g_fin.shape[1:])
        way_fin.send()

    stage = Stage(
        sems, place, b.part, bufs, backward(1, b.grad_third, b.sum_two, b.grad_r2), b.gc2_all,
        last_turn,
    )
    stage_steps(stage, ffn_back, out_grads, in_grads)

    last_back = stage

    def cross_back(k, pump):
        last_back.arrive(k)
        b.dmix[span(k)] = nt(chunk(b.gc2_all, k), rows_of(b.o_co)).astype(BF)
        attend_back(
            b.cq, b.ck, b.cv, b.cp, b.dmix, b.dq, b.sum_dk, b.sum_dv, False, block,
            k * half_rows, (k + 1) * half_rows, pump,
        )
        put(k, nt(b.dq[span(k)], weight(b.o_cross, 2)), last_back)

    def cross_grads():
        way_fout.turn()
        mems = rows_of(b.m_all)
        shape = b.g_cross.shape[1:]
        b.dck[...] = (b.sum_dk[:total_mem] * SCALE).astype(BF)
        b.dcv[...] = b.sum_dv[:total_mem].astype(BF)
        b.g_cross[0] = tn(rows_of(b.first_all), b.dq[...]).astype(BF).reshape(shape)
        b.g_cross[1] = tn(mems, b.dck[...]).astype(BF).reshape(shape)
        b.g_cross[2] = tn(mems, b.dcv[...]).astype(BF).reshape(shape)
        way_cross.send()
        b.g_co[...] = tn(b.cmix[...], rows_of(b.gc2_all)).astype(BF).reshape(b.g_co.shape)
        way_co.send()

    def part_mem():
        value = nt(b.dck[...], weight(b.o_cross, 0)) + nt(b.dcv[...], weight(b.o_cross, 1))
        b.part_m[...] = value.astype(BF).reshape(b.part_m.shape)

    stage = Stage(
        sems, place, b.part, bufs, backward(0, b.grad_r2, b.sum_one, b.grad_r1), b.gc1_all,
        last_back,
    )
    def cross_ended():
        part_mem()
        way_fin.turn()

    stage_steps(stage, cross_back, cross_grads, cross_ended)

    for k in range(2):
        stage.arrive(k)
        pump = (lambda: stage.forward(1)) if k == 0 else (lambda: None)
        b.dmix[span(k)] = nt(chunk(b.gc1_all, k), rows_of(b.o_so)).astype(BF)
        attend_back(
            b.sq, b.sk, b.sv, b.sp, b.dmix, b.dq, b.sum_dk, b.sum_dv, True, block,
            k * half_rows, (k + 1) * half_rows, pump,
        )
    b.dsk[...] = (b.sum_dk[...] * SCALE).astype(BF)
    b.dsv[...] = b.sum_dv[...].astype(BF)
    for k in range(2):
        total = nt(b.dq[span(k)], weight(b.o_self, 0)) + nt(b.dsk[span(k)], weight(b.o_self, 1))
        put(k, total + nt(b.dsv[span(k)], weight(b.o_self, 2)), stage)
    stage.link.finish()
    chain = Link(*sems)
    ks = (1 - h, h)
    red_x = Reduce(chain, place, b.part, bufs)
    mem_bufs = [b.recv0_m, b.send1_m, b.recv1_m, b.keep1_m]
    if dims["bits"] == 3:
        mem_bufs += [b.send2_m, b.recv2_m]
    red_m = Reduce(link, place, b.part_m, mem_bufs)
    for red in (red_x, red_m):
        for index in range(2):
            red.start(index, ks[index])
    rows = rows_of(b.x_all)
    shape = b.g_self.shape[1:]
    b.g_self[0] = tn(rows, b.dq[...]).astype(BF).reshape(shape)
    b.g_self[1] = tn(rows, b.dsk[...]).astype(BF).reshape(shape)
    b.g_self[2] = tn(rows, b.dsv[...]).astype(BF).reshape(shape)
    way_self.send()
    b.g_so[...] = tn(b.smix[...], rows_of(b.gc1_all)).astype(BF).reshape(b.g_so.shape)
    way_so.send()
    way_fout.add()
    way_cross.turn()
    way_co.turn()
    for red in (red_x, red_m):
        for index in range(2):
            red.middle(index, ks[index])
    copies = []
    for d in range(1, dims["seq"]):
        copies.append((b.sums, b.sums_seq.at[d - 1], {"seq": place.seq_shift(d)}))
    seq_sums = link.batch(copies, b.sums_seq)
    way_fin.add()
    swap_l = link.send(b.layer.at[1 - h], b.layer_out.at[h], partner)
    b.layer_out[h] = b.layer[h]
    b.send_x[...] = (red_x.end(0) + b.grad_r1[1 - h]).astype(BF)
    swap_x = link.send(b.send_x, b.recv_x, partner)
    b.grad_dec[h] = red_x.end(1) + b.grad_r1[h]
    b.send_m[...] = red_m.end(0).astype(BF)
    swap_m = link.send(b.send_m, b.recv_m, partner)
    b.grad_mem[h] = red_m.end(1)
    way_fout.gather()
    way_self.turn()
    way_so.turn()
    way_cross.add()
    way_co.add()
    way_fin.gather()
    way_fout.forward()
    seq_sums.wait_recv()
    value = b.sums[...]
    for d in range(1, dims["seq"]):
        value = value + b.sums_seq[d - 1]
    b.sums_line[...] = value
    copies = []
    for e in range(1, dims["items"]):
        target = {"items": lax.rem(place.it + e, dims["items"])}
        copies.append((b.sums_line, b.sums_items.at[e - 1], target))
    item_sums = link.batch(copies, b.sums_items)
    swap_x.wait_recv()
    b.grad_dec[1 - h] = b.recv_x[...].astype(F32)
    swap_m.wait_recv()
    b.grad_mem[1 - h] = b.recv_m[...].astype(F32)
    swap_l.wait_recv()
    way_self.add()
    way_so.add()
    way_cross.gather()
    way_co.gather()
    way_fin.forward()
    item_sums.wait_recv()
    value = b.sums_line[...]
    for e in range(1, dims["items"]):
        value = value + b.sums_items[e - 1]
    b.sums_out[...] = value
    way_cross.forward()
    way_co.forward()
    way_self.gather()
    way_so.gather()
    way_self.forward()
    way_so.forward()
    for way in (way_fout, way_fin, way_cross, way_co, way_self, way_so):
        way.finish()
    so_sent()
    co_sent()
    chain.finish()
    link.finish()


def shape(dims, dtype):
    return jax.ShapeDtypeStruct(tuple(dims), dtype)


def shards(
    mesh, dec_in, memory, dec_len, mem_len, cell_mask, self_query, self_key, self_value, self_out,
    cross_query, cross_key, cross_value, cross_out, ffn_in, ffn_out, norm_gain, norm_bias, cotangent,
):
    items_dev, rb, model = dec_in.shape
    mb = memory.shape[1]
    seq, items = mesh.shape["seq"], mesh.shape["items"]
    group = seq // items_dev
    share = 4
    bits = group.bit_length() - 1
    chips = group // 4
    width = model // group
    total_dec, total_mem = rb * seq, mb * seq
    heads = width // HEAD_DIM
    hidden = ffn_in.shape[1]
    wr = self_query.shape[0] // share
    fr, gr = model // share, hidden // share
    lines = items // share - 1
    dims = {
        "items_dev": items_dev, "items": items, "seq": seq, "group": group, "share": share,
        "bits": bits, "chips": chips, "width": width, "model": model, "block": 256,
        "total_dec": total_dec, "total_mem": total_mem, "lines": lines,
        "chain": 12 + 2 * (bits - 2),
    }
    cells = jnp.broadcast_to((cell_mask == 1).astype(BF)[:, :, None], (items_dev, mb, 128))
    mem_cells = jnp.concatenate([memory, cells], axis=2)

    ins = [
        ("dec", dec_in, VM), ("mem", mem_cells, VM), ("cot", cotangent, VM),
        ("dec_len", dec_len, SM), ("mem_len", mem_len, SM),
        ("w_sq", self_query, HBM), ("w_sk", self_key, HBM), ("w_sv", self_value, HBM),
        ("w_so", self_out, HBM), ("w_cq", cross_query, HBM), ("w_ck", cross_key, HBM),
        ("w_cv", cross_value, HBM), ("w_co", cross_out, HBM), ("f_in", ffn_in, HBM),
        ("f_out", ffn_out, HBM), ("gain", norm_gain, VM), ("bias", norm_bias, VM),
    ]
    own, own_m = (items_dev, rb, model), (items_dev, mb, model)
    grid = (items_dev, chips, 2, 2)
    outs = [
        ("layer_out", own, BF, VM), ("grad_dec", own, F32, VM), ("grad_mem", own_m, F32, VM),
        ("sums_out", (8, model), F32, VM),
        ("r_cross", (share, 3, wr, model), BF, HBM), ("r_self", (share, 3, wr, model), BF, HBM),
        ("r_co", (share, wr, model), BF, HBM), ("r_so", (share, wr, model), BF, HBM),
        ("r_fin", (share, fr, hidden), BF, HBM), ("r_fout", (share, gr, model), BF, HBM),
    ]
    cols = (3, seq, share, wr, width)
    scratch = [
        ("x_all", grid + (rb, model), BF), ("m_all", grid + (mb, model + 128), BF),
        ("c_own", own, BF), ("staged", (8, wr, model), BF),
        ("own_fin", (model, hidden), BF), ("own_fout", (hidden, model), BF),
        ("o_self", cols, BF), ("o_cross", cols, BF),
        ("o_so", (items_dev, share, wr, model), BF), ("o_co", (items_dev, share, wr, model), BF),
        ("o_fin", (share, fr, hidden), BF), ("o_fout", (share, gr, model), BF),
        ("sq", (total_dec, width), BF), ("sk", (total_dec, width), BF), ("sv", (total_dec, width), BF),
        ("cq", (total_dec, width), BF), ("ck", (total_mem, width), BF), ("cv", (total_mem, width), BF),
        ("sp", (heads, total_dec, total_dec), BF), ("cp", (heads, total_mem, total_dec), BF),
        ("smix", (total_dec, width), BF), ("cmix", (total_dec, width), BF),
        ("keep", (total_mem, 128), F32),
        ("part", grid + (rb, model), BF), ("part_m", grid + (mb, model), BF),
        ("first_all", grid + (rb, model), BF), ("second_all", grid + (rb, model), BF),
        ("gy_all", grid + (rb, model), BF), ("gc2_all", grid + (rb, model), BF),
        ("sum_one", own, F32), ("sum_two", own, F32), ("first", own, F32), ("second", own, F32),
        ("layer", own, BF), ("sum_dk", (total_dec, width), F32), ("sum_dv", (total_dec, width), F32),
        ("act", (total_dec, 2 * hidden), BF), ("slope", (total_dec, 2 * hidden), BF),
        ("dmix", (total_dec, width), BF), ("dq", (total_dec, width), BF),
        ("dsk", (total_dec, width), BF), ("dsv", (total_dec, width), BF),
        ("dck", (total_mem, width), BF), ("dcv", (total_mem, width), BF),
        ("send_x", (rb, model), BF), ("recv_x", (rb, model), BF),
        ("send_m", (mb, model), BF), ("recv_m", (mb, model), BF),
        ("sums", (8, model), F32), ("sums_line", (8, model), F32),
        ("sums_seq", (seq - 1, 8, model), F32), ("sums_items", (items - 1, 8, model), F32),
    ]
    for name, rows in (("", rb), ("_m", mb)):
        scratch += [
            ("recv0" + name, (items_dev, chips, 2, rows, model), BF),
            ("send1" + name, (items_dev, chips, rows, model), BF),
            ("recv1" + name, (items_dev, chips, rows, model), BF),
            ("keep1" + name, (items_dev, chips, rows, model), F32),
        ]
        if bits == 3:
            scratch += [
                ("send2" + name, (items_dev, rows, model), BF),
                ("recv2" + name, (items_dev, rows, model), BF),
            ]
    for name, grad, quarter, piece, moved, done in (
        ("fin", (2, share, fr, hidden), (2, fr, hidden), (2, fr // 2, hidden), (fr, hidden),
         (fr, hidden)),
        ("fout", (2, share, gr, model), (2, gr, model), (2, gr // 2, model), (gr, model), (gr, model)),
        ("cross", cols, (3, seq, wr, width), (3, seq // 2, wr, width), (seq, 3, wr, width),
         (3, wr, model)),
        ("self", cols, (3, seq, wr, width), (3, seq // 2, wr, width), (seq, 3, wr, width),
         (3, wr, model)),
        ("co", (items_dev, share, wr, model), (items_dev, wr, model), (wr, model),
         (items_dev, wr, model), (wr, model)),
        ("so", (items_dev, share, wr, model), (items_dev, wr, model), (wr, model),
         (items_dev, wr, model), (wr, model)),
    ):
        scratch += [
            ("g_" + name, grad, BF), ("q_" + name, (2, 2) + piece, BF), ("t_" + name, (2,) + piece, BF),
            ("u_" + name, (2,) + piece, BF), ("s_" + name, quarter, BF), ("z_" + name, moved, BF),
            ("d_" + name, done, BF),
        ]
        if lines:
            scratch.append(("l_" + name, (lines,) + quarter, BF))
    copies = dims["chain"] + 160 + 12 * (bits - 2)
    names = [x[0] for x in ins + outs + scratch] + ["send_sems", "recv_sems"]
    results = pl.pallas_call(
        functools.partial(layer_kernel, dims, names),
        name="layer",
        out_shape=[shape(x[1], x[2]) for x in outs],
        in_specs=[x[2] for x in ins],
        out_specs=[x[3] for x in outs],
        scratch_shapes=[pltpu.VMEM(x[1], x[2]) for x in scratch]
        + [pltpu.SemaphoreType.DMA((copies,)), pltpu.SemaphoreType.DMA((copies,))],
        compiler_params=pltpu.CompilerParams(
            collective_id=0, has_side_effects=True, vmem_limit_bytes=VMEM_BYTES
        ),
    )(*[x[1] for x in ins])
    layer_out, grad_dec, grad_memory, sums, r_cross, r_self, r_co, r_so, r_fin, r_fout = results
    f_cross = r_cross.transpose(1, 0, 2, 3).reshape(3, share * wr, model).astype(F32)
    f_self = r_self.transpose(1, 0, 2, 3).reshape(3, share * wr, model).astype(F32)
    return (
        layer_out, grad_dec, grad_memory,
        f_self[0], f_self[1], f_self[2], r_so.reshape(share * wr, model).astype(F32),
        f_cross[0], f_cross[1], f_cross[2], r_co.reshape(share * wr, model).astype(F32),
        r_fin.reshape(model, hidden).astype(F32), r_fout.reshape(hidden, model).astype(F32),
        sums[0:3], sums[3:6],
    )


def solution(mesh):
    rows = P("seq", None)
    tokens = P("items", "seq", None)
    placed = (
        (tokens, tokens, P("items"), P("items"), P("items", "seq"))
        + (rows,) * 8
        + (P(None, "seq"), rows, P(), P(), tokens)
    )
    return jax.shard_map(
        functools.partial(shards, mesh),
        mesh=mesh,
        in_specs=placed,
        out_specs=(tokens,) * 3 + (rows,) * 8 + (P(None, "seq"), rows, P(), P()),
        check_vma=False,
    )
```

```python
import functools

import jax
import jax.numpy as jnp
from jax import lax
from jax.experimental import pallas as pl
from jax.experimental.pallas import tpu as pltpu
from jax.sharding import PartitionSpec as P

HEAD_DIM = 64
EPS = 1e-05
NEG = -1e30
SCALE = HEAD_DIM ** (-0.5)
BF = jnp.bfloat16
F32 = jnp.float32
VMEM_BYTES = 63 * 1024 * 1024
MESH = pl.DeviceIdType.MESH
VM = pl.BlockSpec(memory_space=pltpu.VMEM)
HBM = pl.BlockSpec(memory_space=pl.ANY)
SM = pl.BlockSpec(memory_space=pltpu.SMEM)


def nn(left, right):
    return lax.dot_general(left, right, (((1,), (0,)), ((), ())), preferred_element_type=F32)


def nt(left, right):
    return lax.dot_general(left, right, (((1,), (1,)), ((), ())), preferred_element_type=F32)


def tn(left, right):
    return lax.dot_general(left, right, (((0,), (0,)), ((), ())), preferred_element_type=F32)


class Link:
    def __init__(self, send_sems, recv_sems, first=0):
        self.send_sems, self.recv_sems, self.count, self.open = send_sems, recv_sems, first, []

    def index(self):
        self.count += 1
        return self.count - 1

    def make(self, src, dst, device, index):
        return pltpu.make_async_remote_copy(
            src_ref=src,
            dst_ref=dst,
            send_sem=self.send_sems.at[index],
            recv_sem=self.recv_sems.at[index],
            device_id=device,
            device_id_type=MESH,
        )

    def send(self, src, dst, device):
        copy = self.make(src, dst, device, self.index())
        copy.start()
        self.open.append(copy)
        return copy

    def batch(self, copies, whole):
        index = self.index()
        for copy in copies:
            self.make(*copy, index).start()
        wait = self.make(whole, whole, copies[0][2], index)
        self.open.append(wait)
        return wait

    def settle(self, copy):
        copy.wait_send()
        self.open = [other for other in self.open if other is not copy]

    def local(self, src, dst):
        copy = pltpu.make_async_copy(src, dst, self.send_sems.at[self.index()])
        copy.start()
        return copy

    def finish(self, kept=()):
        late = {id(copy) for copy in kept}
        for copy in self.open:
            if id(copy) not in late:
                copy.wait_send()
        self.open = [copy for copy in self.open if id(copy) in late]


def greet(devices):
    barrier = pltpu.get_barrier_semaphore()
    for device in devices:
        pl.semaphore_signal(barrier, inc=1, device_id=device, device_id_type=MESH)
    pl.semaphore_wait(barrier, len(devices))


class Place:
    def __init__(self, dims):
        self.dims = dims
        group, share = dims["group"], dims["share"]
        self.me = lax.axis_index("seq")
        self.h = self.me // group
        self.q = self.me % group
        self.b0 = self.q % 2
        self.b1 = (self.q // 2) % 2
        self.c = self.q // 4
        self.it = lax.axis_index("items")
        self.base = (self.it // share) * share
        self.t = self.it % share
        x, y = self.t % 2, self.t // 2
        self.tx, self.ty, self.txy = y * 2 + 1 - x, (1 - y) * 2 + x, (1 - y) * 2 + 1 - x

    def across(self, bit):
        value = (self.q // (1 << bit)) % 2
        return {"seq": self.me + (1 - 2 * value) * (1 << bit)}

    def partner(self):
        return {"seq": (1 - self.h) * self.dims["group"] + self.q}

    def seq_shift(self, d):
        return lax.rem(self.me + d, self.dims["seq"])

    def line(self, t):
        return {"items": self.base + t}

    def seq_peers(self):
        return [{"seq": self.seq_shift(d)} for d in range(1, self.dims["seq"])]

    def items_peers(self):
        count = self.dims["items"]
        return [{"items": lax.rem(self.it + e, count)} for e in range(1, count)]


def spread_start(link, place, out, k):
    bits = place.dims["bits"]
    c, b1, b0 = place.c, place.b1, place.b0
    if bits == 3:
        step = link.send(out.at[k, c, b1, b0], out.at[k, c, b1, b0], place.across(2))
        step.wait_recv()
    waits = []
    high = link.send(out.at[k, :, b1, b0], out.at[k, :, b1, b0], place.across(1))
    waits.append(link.send(out.at[k, :, b1, b0], out.at[k, :, b1, b0], place.across(0)))
    return high, waits


def spread_end(link, place, out, k, started):
    high, waits = started
    b1, b0 = place.b1, place.b0
    high.wait_recv()
    waits.append(link.send(out.at[k, :, 1 - b1, b0], out.at[k, :, 1 - b1, b0], place.across(0)))
    return waits


def columns_out(link, place, src, dst, width):
    seq, group = place.dims["seq"], place.dims["group"]
    copies = []
    for d in range(1, seq):
        target = place.seq_shift(d)
        cols = pl.ds(pl.multiple_of(lax.rem(target, group) * width, width), width)
        copies.append((src.at[:, cols], dst.at[place.me, place.t], {"seq": target}))
    steps = [link.batch(copies, dst.at[0 : seq - 1, place.t])]
    cols = pl.ds(pl.multiple_of(place.q * width, width), width)
    return steps, link.local(src.at[:, cols], dst.at[place.me, place.t])


def rows_out(link, place, src, dst):
    dims, me = place.dims, place.me
    slot = lax.rem(me, dims["items_dev"])
    base = link.count
    link.count += dims["items_dev"] + 1
    copies = []
    for half in range(dims["items_dev"]):
        target = half * dims["group"] + me // dims["items_dev"]
        copy = pltpu.make_async_remote_copy(
            src_ref=src,
            dst_ref=dst.at[slot, place.t],
            send_sem=link.send_sems.at[base + half],
            recv_sem=link.recv_sems.at[base + slot],
            device_id={"seq": target},
            device_id_type=MESH,
        )
        copies.append((target != me, copy))
        pl.when(target != me)(copy.start)
    own = pltpu.make_async_copy(
        src, dst.at[slot, place.t], link.send_sems.at[base + dims["items_dev"]]
    )
    mine = me // dims["items_dev"] == place.q
    pl.when(mine)(own.start)

    def arrived():
        pl.when(mine)(own.wait)
        for block in range(dims["items_dev"]):
            copy = pltpu.make_async_remote_copy(
                src_ref=src,
                dst_ref=dst.at[block, place.t],
                send_sem=link.send_sems.at[base],
                recv_sem=link.recv_sems.at[base + block],
                device_id={"seq": me},
                device_id_type=MESH,
            )
            pl.when(place.q * dims["items_dev"] + block != me)(copy.wait_recv)

    def sent():
        for other, copy in copies:
            pl.when(other)(copy.wait_send)

    return arrived, sent


class Share:
    def __init__(self, link, place, slab, half):
        self.link, self.place, self.half = link, place, half
        t = place.t
        self.from_x = link.send(slab(t), slab(t), place.line(place.tx))
        self.from_y = link.send(slab(t), slab(t), place.line(place.ty))

    def forward(self):
        link, place, half = self.link, self.place, self.half
        self.from_y.wait_recv()
        part = half(place.ty, 0)
        self.steps = [link.send(part, part, place.line(place.tx))]
        self.from_x.wait_recv()
        part = half(place.tx, 1)
        self.steps.append(link.send(part, part, place.line(place.ty)))

    def wait(self):
        arrive(self.steps)


def arrive(steps):
    for step in steps:
        step.wait_recv()


class Reduce:
    def __init__(self, link, place, part, bufs):
        self.link, self.place, self.part, self.bufs = link, place, part, bufs
        self.zero, self.one = {}, {}

    def start(self, index, k):
        place = self.place
        self.zero[index] = self.link.send(
            self.part.at[k, :, :, 1 - place.b0], self.bufs[0].at[index], place.across(0)
        )

    def middle(self, index, k):
        place, part = self.place, self.part
        recv0, send1, recv1, keep1 = self.bufs[:4]
        self.zero[index].wait_recv()
        b1, b0 = place.b1, place.b0
        for c in range(part.shape[1]):
            value = part[k, c, 1 - b1, b0].astype(F32) + recv0[index, c, 1 - b1].astype(F32)
            send1[index, c] = value.astype(BF)
        self.one[index] = self.link.send(send1.at[index], recv1.at[index], place.across(1))
        for c in range(part.shape[1]):
            keep1[index, c] = part[k, c, b1, b0].astype(F32) + recv0[index, c, b1].astype(F32)

    def end(self, index):
        place = self.place
        recv1, keep1 = self.bufs[2:4]
        self.one[index].wait_recv()
        if place.dims["bits"] == 2:
            return keep1[index, 0] + recv1[index, 0].astype(F32)
        send2, recv2 = self.bufs[4:6]
        c = place.c
        send2[index] = (keep1[index, 1 - c] + recv1[index, 1 - c].astype(F32)).astype(BF)
        step = self.link.send(send2.at[index], recv2.at[index], place.across(2))
        kept = keep1[index, c] + recv1[index, c].astype(F32)
        step.wait_recv()
        return kept + recv2[index].astype(F32)


def reduce_bufs(dims, rows):
    items_dev, width, chips = dims["items_dev"], dims["model"], dims["chips"]
    bufs = [
        pltpu.VMEM((items_dev, chips, 2, rows, width), BF),
        pltpu.VMEM((items_dev, chips, rows, width), BF),
        pltpu.VMEM((items_dev, chips, rows, width), BF),
        pltpu.VMEM((items_dev, chips, rows, width), F32),
    ]
    if dims["bits"] == 3:
        bufs += [pltpu.VMEM((items_dev, rows, width), BF) for _ in range(2)]
    return bufs


def moments(value):
    mean = jnp.mean(value, axis=-1, keepdims=True)
    centered = value - mean
    inv = lax.rsqrt(jnp.mean(centered * centered, axis=-1, keepdims=True) + EPS)
    return centered * inv, inv


def norm_back(normed, inv, gain, grad):
    scaled = grad * gain
    mean = jnp.mean(scaled, axis=-1, keepdims=True)
    cross = jnp.mean(scaled * normed, axis=-1, keepdims=True)
    return inv * (scaled - mean - normed * cross)


def rows_back(link, place, src, dst):
    dims, me, h = place.dims, place.me, place.h
    count = dims["items_dev"]
    base = link.count
    link.count += count + 1
    copies = []
    for k in range(count):
        target = place.q * count + k
        copy = pltpu.make_async_remote_copy(
            src_ref=src.at[k],
            dst_ref=dst.at[h],
            send_sem=link.send_sems.at[base + k],
            recv_sem=link.recv_sems.at[base + h],
            device_id={"seq": target},
            device_id_type=MESH,
        )
        copies.append((target != me, copy))
        pl.when(target != me)(copy.start)
    own = pltpu.make_async_copy(
        src.at[lax.rem(me, count)], dst.at[h], link.send_sems.at[base + count]
    )
    mine = me // count == place.q
    pl.when(mine)(own.start)

    def done():
        pl.when(mine)(own.wait)
        for half in range(count):
            copy = pltpu.make_async_remote_copy(
                src_ref=src.at[0],
                dst_ref=dst.at[half],
                send_sem=link.send_sems.at[base],
                recv_sem=link.recv_sems.at[base + half],
                device_id={"seq": me},
                device_id_type=MESH,
            )
            pl.when(half * dims["group"] + me // count != me)(copy.wait_recv)
        for other, copy in copies:
            pl.when(other)(copy.wait_send)

    return done


def half_mask(rows, half):
    return (lax.broadcasted_iota(jnp.int32, (rows, 128), 1) // HEAD_DIM) == half


def attend(q_ref, k_ref, v_ref, valid, p_ref, mix_ref, causal, block, first, last, pump):
    keys = k_ref.shape[0]
    for pair in range(q_ref.shape[1] // 128):
        lanes = slice(pair * 128, pair * 128 + 128)
        for start in range(first, last, block):
            stop = start + block if causal else keys
            halves = []
            for half in range(2):
                query = q_ref[start : start + block, lanes]
                query = jnp.where(half_mask(block, half), query, jnp.zeros_like(query))
                scores = nt(k_ref[:stop, lanes], query) * SCALE
                scores = jnp.where(valid(start, stop), scores, NEG)
                top = jnp.max(scores, axis=0, keepdims=True)
                grown = jnp.exp(scores - top)
                probs = (grown * (1.0 / jnp.sum(grown, axis=0, keepdims=True))).astype(BF)
                p_ref[2 * pair + half, :stop, start : start + block] = probs
                mixed = tn(v_ref[:stop, lanes], probs)
                halves.append(mixed[half * HEAD_DIM : (half + 1) * HEAD_DIM])
            mix_ref[start : start + block, lanes] = jnp.concatenate(halves, axis=0).T.astype(BF)
        if pair == 0:
            pump()


def attend_back(
    q_ref, k_ref, v_ref, p_ref, grad_ref, dq_ref, dk_ref, dv_ref, causal, block, first, last,
    pump,
):
    keys = k_ref.shape[0]
    for pair in range(q_ref.shape[1] // 128):
        lanes = slice(pair * 128, pair * 128 + 128)
        for start in range(first, last, block):
            stop = start + block if causal else keys
            halves = []
            sum_k, sum_v = None, None
            for half in range(2):
                mask = half_mask(block, half)
                query = q_ref[start : start + block, lanes]
                query = jnp.where(mask, query, jnp.zeros_like(query))
                grad = grad_ref[start : start + block, lanes]
                grad = jnp.where(mask, grad, jnp.zeros_like(grad))
                low = p_ref[2 * pair + half, :stop, start : start + block]
                probs = low.astype(F32)
                grad_probs = nt(v_ref[:stop, lanes], grad)
                delta = jnp.sum(probs * grad_probs, axis=0, keepdims=True)
                grad_scores = (probs * (grad_probs - delta)).astype(BF)
                turned = tn(k_ref[:stop, lanes], grad_scores) * SCALE
                halves.append(turned[half * HEAD_DIM : (half + 1) * HEAD_DIM])
                new_k, new_v = nn(grad_scores, query), nn(low, grad)
                sum_k = new_k if sum_k is None else sum_k + new_k
                sum_v = new_v if sum_v is None else sum_v + new_v
            old = start if causal else (keys if start else 0)
            for ref, value in ((dk_ref, sum_k), (dv_ref, sum_v)):
                if old:
                    ref[:old, lanes] = ref[:old, lanes] + value[:old]
                if old < stop:
                    ref[old:stop, lanes] = value[old:]
            dq_ref[start : start + block, lanes] = jnp.concatenate(halves, axis=0).T.astype(BF)
        if pair == 0:
            pump()


class Box:
    def __init__(self, names, refs):
        for name, ref in zip(names, refs):
            setattr(self, name, ref)


class Quarters:
    def __init__(self, link, place, grad, box_names, box):
        self.link, self.place, self.grad = link, place, grad
        self.recv, self.sums, self.last, self.lines, self.total, self.moved, self.done, self.out = (
            getattr(box, name) if name else None for name in box_names
        )

    def send(self):
        place, piece, link = self.place, self.piece, self.link
        self.steps = []
        for i, near in enumerate((place.tx, place.ty)):
            copies = [
                (self.grad.at[piece(near, i)], self.recv.at[i, 0], place.line(near)),
                (self.grad.at[piece(place.txy, i)], self.recv.at[i, 1], place.line(near)),
            ]
            self.steps.append(link.batch(copies, self.recv.at[i]))
        self.flying = list(self.steps)

    def turn(self):
        place, piece, link = self.place, self.piece, self.link
        steps = []
        for i, far in enumerate((place.ty, place.tx)):
            self.steps[i].wait_recv()
            value = self.grad[piece(far, i)].astype(F32) + self.recv[i, 1].astype(F32)
            self.sums[i] = value.astype(BF)
            steps.append(link.send(self.sums.at[i], self.last.at[i], place.line(far)))
        self.steps = steps
        self.flying += steps

    def add(self):
        place = self.place
        for i in range(2):
            self.steps[i].wait_recv()
            value = self.grad[self.piece(place.t, i)].astype(F32)
            value = value + self.recv[i, 0].astype(F32) + self.last[i].astype(F32)
            self.total[self.halves(i)] = value.astype(BF)
        if self.lines is not None:
            share, items = place.dims["share"], place.dims["items"]
            copies = []
            for a in range(1, items // share):
                target = {"items": lax.rem(place.it + a * share, items)}
                copies.append((self.total, self.lines.at[a - 1], target))
            step = self.link.batch(copies, self.lines)
            step.wait()
            self.link.open.pop()
            value = self.total[...].astype(F32)
            for a in range(1, items // share):
                value = value + self.lines[a - 1].astype(F32)
            self.total[...] = value.astype(BF)
        self.along()

    def gather(self):
        self.close()
        place, out = self.place, self.out
        self.own = self.link.local(self.done, out.at[place.t])
        self.near = [
            self.link.send(self.done, out.at[place.t], place.line(near))
            for near in (place.tx, place.ty)
        ]

    def forward(self):
        place, out, link = self.place, self.out, self.link
        self.steps = []
        for i, (source, near) in enumerate(((place.ty, place.tx), (place.tx, place.ty))):
            self.near[1 - i].wait_recv()
            part = out.at[self.cut(source, i)]
            self.steps.append(link.send(part, part, place.line(near)))

    def finish(self):
        arrive(self.steps)
        self.own.wait()


class Hidden(Quarters):
    def piece(self, t, i):
        rows = self.grad.shape[2] // 2
        return slice(None), t, slice(i * rows, (i + 1) * rows)

    def halves(self, i):
        rows = self.grad.shape[2] // 2
        return slice(None), slice(i * rows, (i + 1) * rows)

    def cut(self, t, i):
        rows = self.out.shape[1] // 2
        return t, slice(i * rows, (i + 1) * rows)

    def along(self):
        self.steps = [self.link.send(self.total.at[1], self.moved, self.place.partner())]

    def close(self):
        arrive(self.steps)
        self.done[...] = (self.total[0].astype(F32) + self.moved[...].astype(F32)).astype(BF)


class Columns(Quarters):
    def piece(self, t, i):
        blocks = self.grad.shape[1] // 2
        return slice(None), slice(i * blocks, (i + 1) * blocks), t

    def halves(self, i):
        blocks = self.grad.shape[1] // 2
        return slice(None), slice(i * blocks, (i + 1) * blocks)

    def cut(self, t, i):
        cols = self.out.shape[3] // 2
        return t, slice(None), slice(None), slice(i * cols, (i + 1) * cols)

    def along(self):
        place = self.place
        copies = []
        for d in range(1, place.dims["seq"]):
            target = place.seq_shift(d)
            copies.append((self.total.at[:, target], self.moved.at[place.me], {"seq": target}))
        self.steps = [self.link.batch(copies, self.moved.at[0 : place.dims["seq"] - 1])]
        self.own = self.link.local(self.total.at[:, place.me], self.moved.at[place.me])

    def close(self):
        arrive(self.steps)
        self.own.wait()
        dims = self.place.dims
        group, width = dims["group"], dims["width"]
        for index in range(3):
            for q in range(group):
                value = self.moved[q, index].astype(F32)
                for half in range(1, dims["items_dev"]):
                    value = value + self.moved[half * group + q, index].astype(F32)
                self.done[index, :, q * width : (q + 1) * width] = value.astype(BF)


class Rows(Quarters):
    def piece(self, t, i):
        return i, t

    def halves(self, i):
        return i

    def cut(self, t, i):
        cols = self.out.shape[2] // 2
        return t, slice(None), slice(i * cols, (i + 1) * cols)

    def along(self):
        self.moved_done = rows_back(self.link, self.place, self.total, self.moved)

    def close(self):
        self.moved_done()
        value = self.moved[0].astype(F32)
        for half in range(1, self.place.dims["items_dev"]):
            value = value + self.moved[half].astype(F32)
        self.done[...] = value.astype(BF)


class Stage:
    def __init__(self, sems, place, part, bufs, mid, spread, before):
        self.link, self.place, self.mid, self.spread = Link(*sems), place, mid, spread
        self.before = before
        self.reduce = Reduce(self.link, place, part, bufs)
        self.started, self.waits = {}, {}

    def start(self, k):
        self.reduce.start(k, k)

    def middle(self, k):
        self.reduce.middle(k, k)

    def end(self, k):
        place, spread = self.place, self.spread
        spread[k, place.c, place.b1, place.b0] = self.mid(k, self.reduce.end(k))
        self.started[k] = spread_start(self.link, place, spread, k)

    def forward(self, k):
        self.waits[k] = spread_end(self.link, self.place, self.spread, k, self.started[k])

    def arrive(self, k):
        arrive(self.waits[k])

    def release(self, k):
        done = (self.reduce.zero[k], self.reduce.one[k])
        for copy in done:
            copy.wait_send()
        late = {id(copy) for copy in done}
        self.link.open = [copy for copy in self.link.open if id(copy) not in late]


def stage_steps(stage, compute, flight=None, ended=None, after=None):
    before = stage.before
    compute(0, (lambda: before.forward(1)) if before else (lambda: None))
    stage.start(0)
    compute(1, lambda: None)
    stage.start(1)
    if before:
        before.link.finish()
    stage.middle(0)
    stage.middle(1)
    if flight:
        flight()
    stage.end(0)
    stage.end(1)
    if ended:
        ended()
    stage.forward(0)
    if after:
        after()


def layer_kernel(dims, names, *refs):
    b = Box(names, refs)
    b.grad_third, b.grad_r2, b.grad_r1, b.gc1_all = b.first, b.second, b.first, b.gy_all
    place = Place(dims)
    sems = b.send_sems, b.recv_sems
    link = Link(*sems, dims["chain"])
    width, block, items_dev = dims["width"], dims["block"], dims["items_dev"]
    h, t, q_place = place.h, place.t, place.q
    c, b1, b0 = place.c, place.b1, place.b0
    partner = place.partner()
    wr = b.w_sq.shape[0] // dims["share"]
    model = dims["model"]
    total_dec, total_mem = dims["total_dec"], dims["total_mem"]
    rb = b.dec.shape[1]

    def rows_of(ref, cols=model):
        return ref[...].reshape(-1, ref.shape[-1])[:, :cols]

    def chunk(ref, k):
        return ref[k].reshape(-1, model)

    half_rows = total_dec // 2

    def span(k):
        return slice(k * half_rows, (k + 1) * half_rows)

    def put(k, value, before=None):
        if before:
            before.release(k)
        b.part[k] = value.astype(BF).reshape(b.part.shape[1:])

    def weight(ref, index):
        return ref[index].reshape(model, width)

    weights = (b.w_sq, b.w_sk, b.w_sv, b.w_so, b.w_ck, b.w_cv, b.w_cq, b.w_co)
    rows_t = pl.ds(pl.multiple_of(t * wr, wr), wr)
    index = link.index()
    for i, w in enumerate(weights):
        pltpu.make_async_copy(w.at[rows_t], b.staged.at[i], b.send_sems.at[index]).start()
    staged = pltpu.make_async_copy(b.staged, b.staged, b.send_sems.at[index])
    own_fin = link.local(b.f_in, b.own_fin)
    own_fout = link.local(b.f_out, b.own_fout)
    greet(place.seq_peers() + place.items_peers())

    swap_x = link.send(b.dec.at[1 - h], b.x_all.at[h, c, b1, b0], partner)
    def share_columns(steps, dst):
        arrive(steps[0])
        steps[1].wait()
        blocks = dims["seq"] // 2
        return Share(
            link, place, lambda t: dst.at[:, t],
            lambda t, i: dst.at[i * blocks : (i + 1) * blocks, t],
        )

    def share_rows(dst):
        return Share(link, place, lambda t: dst.at[:, t], lambda t, i: dst.at[i, t])

    def share_hidden(dst):
        rows = dst.shape[1] // 2
        return Share(
            link, place, lambda t: dst.at[t], lambda t, i: dst.at[t, i * rows : (i + 1) * rows]
        )

    def join_cells():
        mb = b.cells.shape[1]
        same = lax.broadcasted_iota(jnp.int32, (mb, mb), 0) == lax.broadcasted_iota(
            jnp.int32, (mb, mb), 1
        )
        for k in range(items_dev):
            flags = (b.cells[k : k + 1] == 1).astype(F32)
            column = jnp.sum(jnp.where(same, flags, 0.0), axis=1, keepdims=True)
            b.mem_cells[k, :, :model] = b.mem[k]
            b.mem_cells[k, :, model:] = jnp.broadcast_to(column, (mb, 128)).astype(BF)

    def self_columns(i):
        return columns_out(link, place, b.staged.at[i], b.o_self.at[i], width)

    b.x_all[h, c, b1, b0] = b.dec[h]
    staged.wait()
    steps_q = self_columns(0)
    first_x = spread_start(link, place, b.x_all, h)
    link.settle(steps_q[0][0])
    steps_k = self_columns(1)
    waits = spread_end(link, place, b.x_all, h, first_x)
    swap_x.wait_recv()
    second_x = spread_start(link, place, b.x_all, 1 - h)
    self_share = [share_columns(steps_q, b.o_self.at[0])]
    link.settle(steps_k[0][0])
    steps_v = self_columns(2)
    so_arrived, so_sent = rows_out(link, place, b.staged.at[3], b.o_so)
    waits += spread_end(link, place, b.x_all, 1 - h, second_x)
    self_share.append(share_columns(steps_k, b.o_self.at[1]))
    self_share[0].forward()
    self_share.append(share_columns(steps_v, b.o_self.at[2]))
    so_arrived()
    so_share = share_rows(b.o_so)
    cross_steps = [
        columns_out(link, place, b.staged.at[4 + i], b.o_cross.at[i], width) for i in range(3)
    ]
    co_arrived, co_sent = rows_out(link, place, b.staged.at[7], b.o_co)
    join_cells()
    b.m_all[h, c, b1, b0] = b.mem_cells[h]
    swap_m = link.send(b.mem_cells.at[1 - h], b.m_all.at[h, c, b1, b0], partner)
    first_m = spread_start(link, place, b.m_all, h)

    arrive(waits)
    rows = rows_of(b.x_all)
    for index, dst in enumerate((b.sq, b.sk, b.sv)):
        if index:
            self_share[index].forward()
        self_share[index].wait()
        dst[...] = nn(rows, weight(b.o_self, index)).astype(BF)
    so_share.forward()
    cross_share = [share_columns(cross_steps[i], b.o_cross.at[i]) for i in range(3)]
    co_arrived()
    co_share = share_rows(b.o_co)
    mem_waits = spread_end(link, place, b.m_all, h, first_m)
    swap_m.wait_recv()
    second_m = spread_start(link, place, b.m_all, 1 - h)
    own_fin.wait()
    own_fout.wait()
    fr, gr = b.o_fin.shape[1], b.o_fout.shape[1]
    step_fin = link.send(b.own_fin.at[pl.ds(pl.multiple_of(t * fr, fr), fr)], b.o_fin.at[t], partner)
    step_fout = link.send(
        b.own_fout.at[pl.ds(pl.multiple_of(t * gr, gr), gr)], b.o_fout.at[t], partner
    )
    length, mem_length = b.dec_len[h], b.mem_len[h]

    def self_ok(start, stop):
        keys = lax.broadcasted_iota(jnp.int32, (stop, block), 0)
        spots = lax.broadcasted_iota(jnp.int32, (stop, block), 1) + start
        return (keys <= spots) & (keys < length)

    bufs = [b.recv0, b.send1, b.recv1, b.keep1]
    if dims["bits"] == 3:
        bufs += [b.send2, b.recv2]

    def forward(index, res, summed, out):
        def mid(k, total):
            value = res(k) + total
            summed[k] = value
            normed, _ = moments(value)
            result = normed * b.gain[index : index + 1] + b.bias[index : index + 1]
            out[k] = result
            return result.astype(BF)

        return mid

    def self_part(k, pump):
        attend(
            b.sq, b.sk, b.sv, self_ok, b.sp, b.smix, True, block,
            k * half_rows, (k + 1) * half_rows, pump,
        )
        if k == 0:
            so_share.wait()
        put(k, nn(b.smix[span(k)], rows_of(b.o_so)))

    def memory_part():
        arrive(mem_waits)
        mems = rows_of(b.m_all)
        cross_share[0].wait()
        b.ck[...] = nn(mems, weight(b.o_cross, 0)).astype(BF)
        cross_share[1].wait()
        b.cv[...] = nn(mems, weight(b.o_cross, 1)).astype(BF)
        spots = lax.broadcasted_iota(jnp.int32, (total_mem, 128), 0)
        cells = b.m_all[...].reshape(-1, b.m_all.shape[-1])[:, model:].astype(F32)
        b.keep[...] = ((spots < mem_length) & ((cells > 0.5) | (spots == 0))).astype(F32)

    stage = Stage(
        sems, place, b.part, bufs,
        forward(0, lambda k: b.x_all[k, c, b1, b0].astype(F32), b.sum_one, b.first), b.first_all, None,
    )
    def cross_weights():
        mem_waits.extend(spread_end(link, place, b.m_all, 1 - h, second_m))
        for share in cross_share + [co_share]:
            share.forward()

    stage_steps(stage, self_part, after=cross_weights)
    memory_part()
    b.c_own[h] = b.cot[h]
    swap_c = link.send(b.cot.at[1 - h], b.c_own.at[h], partner)
    ffn_share = []

    def cross_part(k, pump):
        last.arrive(k)
        if k == 0:
            cross_share[2].wait()
        b.cq[span(k)] = nn(chunk(b.first_all, k), weight(b.o_cross, 2)).astype(BF)
        attend(
            b.cq, b.ck, b.cv, lambda start, stop: b.keep[:, 0:1] > 0.5, b.cp, b.cmix, False, block,
            k * half_rows, (k + 1) * half_rows, pump,
        )
        if k == 0:
            co_share.wait()
            step_fin.wait_recv()
            ffn_share.append(share_hidden(b.o_fin))
        put(k, nn(b.cmix[span(k)], rows_of(b.o_co)), last)

    last = stage
    stage = Stage(
        sems, place, b.part, bufs, forward(1, lambda k: b.first[k], b.sum_two, b.second),
        b.second_all, last,
    )
    def ffn_weights():
        step_fout.wait_recv()
        ffn_share.append(share_hidden(b.o_fout))
        for share in ffn_share:
            share.forward()

    stage_steps(stage, cross_part, after=ffn_weights)

    w_ins = (lambda: b.own_fin[...], lambda: b.o_fin[...].reshape(model, -1))
    w_outs = (lambda: b.own_fout[...], lambda: b.o_fout[...].reshape(-1, model))
    hidden = b.own_fin.shape[1]
    last_second = stage

    def ffn_part(k, pump):
        last_second.arrive(k)
        if k == 0:
            ffn_share[0].wait()
        rows = chunk(b.second_all, k)
        for index in range(2):
            if index:
                pump()
            pre = nn(rows, w_ins[index]())
            cdf = 0.5 * (1.0 + lax.erf(pre * (0.5**0.5)))
            cols = slice(index * hidden, (index + 1) * hidden)
            b.act[span(k), cols] = (pre * cdf).astype(BF)
            b.slope[span(k), cols] = (
                cdf + pre * (jnp.exp(-0.5 * pre * pre) * 0.3989422804014327)
            ).astype(BF)
        if k == 0:
            ffn_share[1].wait()
        total = nn(b.act[span(k), :hidden], w_outs[0]())
        put(k, total + nn(b.act[span(k), hidden:], w_outs[1]()), last_second)

    swap_c.wait_recv()

    def add_sums(index, k, normed, grad):
        new = (jnp.sum(grad * normed, axis=0, keepdims=True), jnp.sum(grad, axis=0, keepdims=True))
        for row, value in zip((index, 3 + index), new):
            b.sums[row : row + 1] = value if k == 0 else b.sums[row : row + 1] + value

    def turn(k, total):
        gain = b.gain[2:3]
        normed, inv = moments(b.second[k] + total)
        spots = lax.broadcasted_iota(jnp.int32, (rb, model), 0) + (k * dims["group"] + q_place) * rb
        kept = spots < length
        b.layer[k] = jnp.where(kept, normed * gain + b.bias[2:3], 0.0).astype(BF)
        grad = jnp.where(kept, b.c_own[k].astype(F32), 0.0)
        add_sums(2, k, normed, grad)
        result = norm_back(normed, inv, gain, grad)
        b.grad_third[k] = result
        return result.astype(BF)

    stage = Stage(sems, place, b.part, bufs, turn, b.gy_all, last_second)
    stage_steps(stage, ffn_part)

    last_turn = stage

    def ffn_back(k, pump):
        last_turn.arrive(k)
        grad = chunk(b.gy_all, k)
        total = None
        for index in range(2):
            if index:
                pump()
            cols = slice(index * hidden, (index + 1) * hidden)
            grad_pre = (nt(grad, w_outs[index]()) * b.slope[span(k), cols].astype(F32)).astype(BF)
            b.slope[span(k), cols] = grad_pre
            term = nt(grad_pre, w_ins[index]())
            total = term if total is None else total + term
        put(k, total, last_turn)

    way_fout = Hidden(
        link, place, b.g_fout, ("q_fout", "t_fout", "u_fout", dims["lines"] and "l_fout", "s_fout", "z_fout", "d_fout", "r_fout"), b
    )
    way_fin = Hidden(
        link, place, b.g_fin, ("q_fin", "t_fin", "u_fin", dims["lines"] and "l_fin", "s_fin", "z_fin", "d_fin", "r_fin"), b
    )
    way_cross = Columns(
        link, place, b.g_cross, ("q_cross", "t_cross", "u_cross", dims["lines"] and "l_cross", "s_cross", "z_cross", "d_cross", "r_cross"), b
    )
    way_self = Columns(
        link, place, b.g_self, ("q_self", "t_self", "u_self", dims["lines"] and "l_self", "s_self", "z_self", "d_self", "r_self"), b
    )
    way_co = Rows(
        link, place, b.g_co, ("q_co", "t_co", "u_co", dims["lines"] and "l_co", "s_co", "z_co", "d_co", "r_co"), b
    )
    way_so = Rows(
        link, place, b.g_so, ("q_so", "t_so", "u_so", dims["lines"] and "l_so", "s_so", "z_so", "d_so", "r_so"), b
    )

    def backward(index, res, summed, out):
        def mid(k, total):
            normed, inv = moments(summed[k])
            grad = res[k] + total
            add_sums(index, k, normed, grad)
            result = norm_back(normed, inv, b.gain[index : index + 1], grad)
            out[k] = result
            return result.astype(BF)

        return mid

    def out_grads():
        grad = rows_of(b.gy_all)
        for index in range(2):
            cols = slice(index * hidden, (index + 1) * hidden)
            value = tn(b.act[:, cols], grad)
            b.g_fout[index] = value.astype(BF).reshape(b.g_fout.shape[1:])
        way_fout.send()

    def in_grads():
        rows = rows_of(b.second_all)
        for index in range(2):
            cols = slice(index * hidden, (index + 1) * hidden)
            value = tn(rows, b.slope[:, cols])
            b.g_fin[index] = value.astype(BF).reshape(b.g_fin.shape[1:])
        way_fin.send()

    stage = Stage(
        sems, place, b.part, bufs, backward(1, b.grad_third, b.sum_two, b.grad_r2), b.gc2_all,
        last_turn,
    )
    stage_steps(stage, ffn_back, out_grads, in_grads)

    last_back = stage

    def cross_back(k, pump):
        last_back.arrive(k)
        b.dmix[span(k)] = nt(chunk(b.gc2_all, k), rows_of(b.o_co)).astype(BF)
        attend_back(
            b.cq, b.ck, b.cv, b.cp, b.dmix, b.dq, b.sum_dk, b.sum_dv, False, block,
            k * half_rows, (k + 1) * half_rows, pump,
        )
        put(k, nt(b.dq[span(k)], weight(b.o_cross, 2)), last_back)

    def cross_grads():
        way_fout.turn()
        mems = rows_of(b.m_all)
        shape = b.g_cross.shape[1:]
        b.dck[...] = (b.sum_dk[:total_mem] * SCALE).astype(BF)
        b.dcv[...] = b.sum_dv[:total_mem].astype(BF)
        b.g_cross[0] = tn(rows_of(b.first_all), b.dq[...]).astype(BF).reshape(shape)
        b.g_cross[1] = tn(mems, b.dck[...]).astype(BF).reshape(shape)
        b.g_cross[2] = tn(mems, b.dcv[...]).astype(BF).reshape(shape)
        way_cross.send()
        b.g_co[...] = tn(b.cmix[...], rows_of(b.gc2_all)).astype(BF).reshape(b.g_co.shape)
        way_co.send()

    def part_mem():
        value = nt(b.dck[...], weight(b.o_cross, 0)) + nt(b.dcv[...], weight(b.o_cross, 1))
        b.part_m[...] = value.astype(BF).reshape(b.part_m.shape)

    stage = Stage(
        sems, place, b.part, bufs, backward(0, b.grad_r2, b.sum_one, b.grad_r1), b.gc1_all,
        last_back,
    )
    def cross_ended():
        part_mem()
        way_fin.turn()

    stage_steps(stage, cross_back, cross_grads, cross_ended)

    for k in range(2):
        stage.arrive(k)
        pump = (lambda: stage.forward(1)) if k == 0 else (lambda: None)
        b.dmix[span(k)] = nt(chunk(b.gc1_all, k), rows_of(b.o_so)).astype(BF)
        attend_back(
            b.sq, b.sk, b.sv, b.sp, b.dmix, b.dq, b.sum_dk, b.sum_dv, True, block,
            k * half_rows, (k + 1) * half_rows, pump,
        )
    b.dsk[...] = (b.sum_dk[...] * SCALE).astype(BF)
    b.dsv[...] = b.sum_dv[...].astype(BF)
    for k in range(2):
        total = nt(b.dq[span(k)], weight(b.o_self, 0)) + nt(b.dsk[span(k)], weight(b.o_self, 1))
        put(k, total + nt(b.dsv[span(k)], weight(b.o_self, 2)), stage)
    stage.link.finish()
    chain = Link(*sems)
    ks = (1 - h, h)
    red_x = Reduce(chain, place, b.part, bufs)
    mem_bufs = [b.recv0_m, b.send1_m, b.recv1_m, b.keep1_m]
    if dims["bits"] == 3:
        mem_bufs += [b.send2_m, b.recv2_m]
    red_m = Reduce(link, place, b.part_m, mem_bufs)
    for red in (red_x, red_m):
        for index in range(2):
            red.start(index, ks[index])
    rows = rows_of(b.x_all)
    shape = b.g_self.shape[1:]
    b.g_self[0] = tn(rows, b.dq[...]).astype(BF).reshape(shape)
    b.g_self[1] = tn(rows, b.dsk[...]).astype(BF).reshape(shape)
    b.g_self[2] = tn(rows, b.dsv[...]).astype(BF).reshape(shape)
    way_self.send()
    b.g_so[...] = tn(b.smix[...], rows_of(b.gc1_all)).astype(BF).reshape(b.g_so.shape)
    way_so.send()
    way_fout.add()
    way_cross.turn()
    way_co.turn()
    for red in (red_x, red_m):
        for index in range(2):
            red.middle(index, ks[index])
    copies = []
    for d in range(1, dims["seq"]):
        copies.append((b.sums, b.sums_seq.at[d - 1], {"seq": place.seq_shift(d)}))
    seq_sums = link.batch(copies, b.sums_seq)
    way_fin.add()
    swap_l = link.send(b.layer.at[1 - h], b.layer_out.at[h], partner)
    b.layer_out[h] = b.layer[h]
    b.send_x[...] = (red_x.end(0) + b.grad_r1[1 - h]).astype(BF)
    swap_x = link.send(b.send_x, b.recv_x, partner)
    b.grad_dec[h] = red_x.end(1) + b.grad_r1[h]
    b.send_m[...] = red_m.end(0).astype(BF)
    swap_m = link.send(b.send_m, b.recv_m, partner)
    b.grad_mem[h] = red_m.end(1)
    way_fout.gather()
    way_self.turn()
    way_so.turn()
    way_cross.add()
    way_co.add()
    way_fin.gather()
    way_fout.forward()
    seq_sums.wait_recv()
    value = b.sums[...]
    for d in range(1, dims["seq"]):
        value = value + b.sums_seq[d - 1]
    b.sums_line[...] = value
    copies = []
    for e in range(1, dims["items"]):
        target = {"items": lax.rem(place.it + e, dims["items"])}
        copies.append((b.sums_line, b.sums_items.at[e - 1], target))
    item_sums = link.batch(copies, b.sums_items)
    swap_x.wait_recv()
    b.grad_dec[1 - h] = b.recv_x[...].astype(F32)
    swap_m.wait_recv()
    b.grad_mem[1 - h] = b.recv_m[...].astype(F32)
    swap_l.wait_recv()
    way_self.add()
    way_so.add()
    way_cross.gather()
    way_co.gather()
    way_fin.forward()
    item_sums.wait_recv()
    value = b.sums_line[...]
    for e in range(1, dims["items"]):
        value = value + b.sums_items[e - 1]
    b.sums_out[...] = value
    way_cross.forward()
    way_co.forward()
    way_self.gather()
    way_so.gather()
    way_self.forward()
    way_so.forward()
    for way in (way_fout, way_fin, way_cross, way_co, way_self, way_so):
        way.finish()
    so_sent()
    co_sent()
    chain.finish()
    link.finish()


def shape(dims, dtype):
    return jax.ShapeDtypeStruct(tuple(dims), dtype)


def outputs_kernel(layer, dec, mem, cross, own, co, so, fin, fout, sums, *outs):
    o_layer, o_dec, o_mem = outs[:3]
    o_layer[...] = layer[...]
    o_dec[...] = dec[...]
    o_mem[...] = mem[...]
    for index in range(3):
        outs[3 + index][...] = own[0, index].astype(F32)
        outs[7 + index][...] = cross[0, index].astype(F32)
    outs[6][...] = so[0].astype(F32)
    outs[10][...] = co[0].astype(F32)
    outs[11][...] = fin[0].astype(F32)
    outs[12][...] = fout[0].astype(F32)
    outs[13][...] = sums[0:3]
    outs[14][...] = sums[3:6]


def shards(
    mesh, dec_in, memory, dec_len, mem_len, cell_mask, self_query, self_key, self_value, self_out,
    cross_query, cross_key, cross_value, cross_out, ffn_in, ffn_out, norm_gain, norm_bias, cotangent,
):
    items_dev, rb, model = dec_in.shape
    mb = memory.shape[1]
    seq, items = mesh.shape["seq"], mesh.shape["items"]
    group = seq // items_dev
    share = 4
    bits = group.bit_length() - 1
    chips = group // 4
    width = model // group
    total_dec, total_mem = rb * seq, mb * seq
    heads = width // HEAD_DIM
    hidden = ffn_in.shape[1]
    wr = self_query.shape[0] // share
    fr, gr = model // share, hidden // share
    lines = items // share - 1
    dims = {
        "items_dev": items_dev, "items": items, "seq": seq, "group": group, "share": share,
        "bits": bits, "chips": chips, "width": width, "model": model, "block": 256,
        "total_dec": total_dec, "total_mem": total_mem, "lines": lines,
        "chain": 12 + 2 * (bits - 2),
    }
    ins = [
        ("dec", dec_in, VM), ("mem", memory, VM), ("cells", cell_mask, VM), ("cot", cotangent, VM),
        ("dec_len", dec_len, SM), ("mem_len", mem_len, SM),
        ("w_sq", self_query, HBM), ("w_sk", self_key, HBM), ("w_sv", self_value, HBM),
        ("w_so", self_out, HBM), ("w_cq", cross_query, HBM), ("w_ck", cross_key, HBM),
        ("w_cv", cross_value, HBM), ("w_co", cross_out, HBM), ("f_in", ffn_in, HBM),
        ("f_out", ffn_out, HBM), ("gain", norm_gain, VM), ("bias", norm_bias, VM),
    ]
    own, own_m = (items_dev, rb, model), (items_dev, mb, model)
    grid = (items_dev, chips, 2, 2)
    outs = [
        ("layer_out", own, BF, VM), ("grad_dec", own, F32, VM), ("grad_mem", own_m, F32, VM),
        ("sums_out", (8, model), F32, VM),
        ("r_cross", (share, 3, wr, model), BF, HBM), ("r_self", (share, 3, wr, model), BF, HBM),
        ("r_co", (share, wr, model), BF, HBM), ("r_so", (share, wr, model), BF, HBM),
        ("r_fin", (share, fr, hidden), BF, HBM), ("r_fout", (share, gr, model), BF, HBM),
    ]
    cols = (3, seq, share, wr, width)
    scratch = [
        ("x_all", grid + (rb, model), BF), ("m_all", grid + (mb, model + 128), BF),
        ("mem_cells", (items_dev, mb, model + 128), BF), ("c_own", own, BF), ("staged", (8, wr, model), BF),
        ("own_fin", (model, hidden), BF), ("own_fout", (hidden, model), BF),
        ("o_self", cols, BF), ("o_cross", cols, BF),
        ("o_so", (items_dev, share, wr, model), BF), ("o_co", (items_dev, share, wr, model), BF),
        ("o_fin", (share, fr, hidden), BF), ("o_fout", (share, gr, model), BF),
        ("sq", (total_dec, width), BF), ("sk", (total_dec, width), BF), ("sv", (total_dec, width), BF),
        ("cq", (total_dec, width), BF), ("ck", (total_mem, width), BF), ("cv", (total_mem, width), BF),
        ("sp", (heads, total_dec, total_dec), BF), ("cp", (heads, total_mem, total_dec), BF),
        ("smix", (total_dec, width), BF), ("cmix", (total_dec, width), BF),
        ("keep", (total_mem, 128), F32),
        ("part", grid + (rb, model), BF), ("part_m", grid + (mb, model), BF),
        ("first_all", grid + (rb, model), BF), ("second_all", grid + (rb, model), BF),
        ("gy_all", grid + (rb, model), BF), ("gc2_all", grid + (rb, model), BF),
        ("sum_one", own, F32), ("sum_two", own, F32), ("first", own, F32), ("second", own, F32),
        ("layer", own, BF), ("sum_dk", (total_dec, width), F32), ("sum_dv", (total_dec, width), F32),
        ("act", (total_dec, 2 * hidden), BF), ("slope", (total_dec, 2 * hidden), BF),
        ("dmix", (total_dec, width), BF), ("dq", (total_dec, width), BF),
        ("dsk", (total_dec, width), BF), ("dsv", (total_dec, width), BF),
        ("dck", (total_mem, width), BF), ("dcv", (total_mem, width), BF),
        ("send_x", (rb, model), BF), ("recv_x", (rb, model), BF),
        ("send_m", (mb, model), BF), ("recv_m", (mb, model), BF),
        ("sums", (8, model), F32), ("sums_line", (8, model), F32),
        ("sums_seq", (seq - 1, 8, model), F32), ("sums_items", (items - 1, 8, model), F32),
    ]
    for name, rows in (("", rb), ("_m", mb)):
        scratch += [
            ("recv0" + name, (items_dev, chips, 2, rows, model), BF),
            ("send1" + name, (items_dev, chips, rows, model), BF),
            ("recv1" + name, (items_dev, chips, rows, model), BF),
            ("keep1" + name, (items_dev, chips, rows, model), F32),
        ]
        if bits == 3:
            scratch += [
                ("send2" + name, (items_dev, rows, model), BF),
                ("recv2" + name, (items_dev, rows, model), BF),
            ]
    for name, grad, quarter, piece, moved, done in (
        ("fin", (2, share, fr, hidden), (2, fr, hidden), (2, fr // 2, hidden), (fr, hidden),
         (fr, hidden)),
        ("fout", (2, share, gr, model), (2, gr, model), (2, gr // 2, model), (gr, model), (gr, model)),
        ("cross", cols, (3, seq, wr, width), (3, seq // 2, wr, width), (seq, 3, wr, width),
         (3, wr, model)),
        ("self", cols, (3, seq, wr, width), (3, seq // 2, wr, width), (seq, 3, wr, width),
         (3, wr, model)),
        ("co", (items_dev, share, wr, model), (items_dev, wr, model), (wr, model),
         (items_dev, wr, model), (wr, model)),
        ("so", (items_dev, share, wr, model), (items_dev, wr, model), (wr, model),
         (items_dev, wr, model), (wr, model)),
    ):
        scratch += [
            ("g_" + name, grad, BF), ("q_" + name, (2, 2) + piece, BF), ("t_" + name, (2,) + piece, BF),
            ("u_" + name, (2,) + piece, BF), ("s_" + name, quarter, BF), ("z_" + name, moved, BF),
            ("d_" + name, done, BF),
        ]
        if lines:
            scratch.append(("l_" + name, (lines,) + quarter, BF))
    copies = dims["chain"] + 153 + 12 * (bits - 2)
    names = [x[0] for x in ins + outs + scratch] + ["send_sems", "recv_sems"]
    results = pl.pallas_call(
        functools.partial(layer_kernel, dims, names),
        name="layer",
        out_shape=[shape(x[1], x[2]) for x in outs],
        in_specs=[x[2] for x in ins],
        out_specs=[x[3] for x in outs],
        scratch_shapes=[pltpu.VMEM(x[1], x[2]) for x in scratch]
        + [pltpu.SemaphoreType.DMA((copies,)), pltpu.SemaphoreType.DMA((copies,))],
        compiler_params=pltpu.CompilerParams(
            collective_id=0, has_side_effects=True, vmem_limit_bytes=VMEM_BYTES
        ),
    )(*[x[1] for x in ins])
    layer_out, grad_dec, grad_memory, sums, r_cross, r_self, r_co, r_so, r_fin, r_fout = results
    tok, mem_rows = items_dev * rb, items_dev * mb
    pieces = (
        ((tok, model), (tok // share, model), BF), ((tok, model), (tok // share, model), F32),
        ((mem_rows, model), (mem_rows // share, model), F32),
    )
    heads_in = [
        pl.BlockSpec((1, 3, wr, model), lambda i: (i, 0, 0, 0)),
        pl.BlockSpec((1, 3, wr, model), lambda i: (i, 0, 0, 0)),
        pl.BlockSpec((1, wr, model), lambda i: (i, 0, 0)),
        pl.BlockSpec((1, wr, model), lambda i: (i, 0, 0)),
        pl.BlockSpec((1, fr, hidden), lambda i: (i, 0, 0)),
        pl.BlockSpec((1, gr, model), lambda i: (i, 0, 0)),
        pl.BlockSpec((8, model), lambda i: (0, 0)),
    ]
    row_specs = [pl.BlockSpec(x[1], lambda i: (i, 0)) for x in pieces]
    square = (share * wr, model)
    outs = pl.pallas_call(
        outputs_kernel,
        name="outputs",
        grid=(share,),
        in_specs=row_specs + heads_in,
        out_specs=row_specs
        + [pl.BlockSpec((wr, model), lambda i: (i, 0))] * 8
        + [pl.BlockSpec((fr, hidden), lambda i: (i, 0)), pl.BlockSpec((gr, model), lambda i: (i, 0))]
        + [pl.BlockSpec((3, model), lambda i: (0, 0))] * 2,
        out_shape=[shape(x[0], x[2]) for x in pieces]
        + [shape(square, F32)] * 8
        + [shape((model, hidden), F32), shape((hidden, model), F32)]
        + [shape((3, model), F32)] * 2,
        compiler_params=pltpu.CompilerParams(vmem_limit_bytes=VMEM_BYTES // 2),
    )(
        layer_out.reshape(tok, model), grad_dec.reshape(tok, model),
        grad_memory.reshape(mem_rows, model), r_cross, r_self, r_co, r_so, r_fin, r_fout, sums,
    )
    return (
        outs[0].reshape(own), outs[1].reshape(own), outs[2].reshape(own_m), *outs[3:],
    )


def solution(mesh):
    rows = P("seq", None)
    tokens = P("items", "seq", None)
    placed = (
        (tokens, tokens, P("items"), P("items"), P("items", "seq"))
        + (rows,) * 8
        + (P(None, "seq"), rows, P(), P(), tokens)
    )
    return jax.shard_map(
        functools.partial(shards, mesh),
        mesh=mesh,
        in_specs=placed,
        out_specs=(tokens,) * 3 + (rows,) * 8 + (P(None, "seq"), rows, P(), P()),
        check_vma=False,
    )
```

```python
import functools

import jax
import jax.numpy as jnp
from jax import lax
from jax.experimental import pallas as pl
from jax.experimental.pallas import tpu as pltpu
from jax.sharding import PartitionSpec as P

HEAD_DIM = 64
EPS = 1e-05
NEG = -1e30
SCALE = HEAD_DIM ** (-0.5)
BF = jnp.bfloat16
F32 = jnp.float32
VMEM_BYTES = 63 * 1024 * 1024
MESH = pl.DeviceIdType.MESH
VM = pl.BlockSpec(memory_space=pltpu.VMEM)
HBM = pl.BlockSpec(memory_space=pl.ANY)
SM = pl.BlockSpec(memory_space=pltpu.SMEM)


def nn(left, right):
    return lax.dot_general(left, right, (((1,), (0,)), ((), ())), preferred_element_type=F32)


def nt(left, right):
    return lax.dot_general(left, right, (((1,), (1,)), ((), ())), preferred_element_type=F32)


def tn(left, right):
    return lax.dot_general(left, right, (((0,), (0,)), ((), ())), preferred_element_type=F32)


class Link:
    def __init__(self, send_sems, recv_sems, first=0):
        self.send_sems, self.recv_sems, self.count, self.open = send_sems, recv_sems, first, []

    def index(self):
        self.count += 1
        return self.count - 1

    def make(self, src, dst, device, index):
        return pltpu.make_async_remote_copy(
            src_ref=src,
            dst_ref=dst,
            send_sem=self.send_sems.at[index],
            recv_sem=self.recv_sems.at[index],
            device_id=device,
            device_id_type=MESH,
        )

    def send(self, src, dst, device):
        copy = self.make(src, dst, device, self.index())
        copy.start()
        self.open.append(copy)
        return copy

    def batch(self, copies, whole):
        index = self.index()
        for copy in copies:
            self.make(*copy, index).start()
        wait = self.make(whole, whole, copies[0][2], index)
        self.open.append(wait)
        return wait

    def settle(self, copy):
        copy.wait_send()
        self.open = [other for other in self.open if other is not copy]

    def local(self, src, dst):
        copy = pltpu.make_async_copy(src, dst, self.send_sems.at[self.index()])
        copy.start()
        return copy

    def finish(self, kept=()):
        late = {id(copy) for copy in kept}
        for copy in self.open:
            if id(copy) not in late:
                copy.wait_send()
        self.open = [copy for copy in self.open if id(copy) in late]


def greet(devices):
    barrier = pltpu.get_barrier_semaphore()
    for device in devices:
        pl.semaphore_signal(barrier, inc=1, device_id=device, device_id_type=MESH)
    pl.semaphore_wait(barrier, len(devices))


class Place:
    def __init__(self, dims):
        self.dims = dims
        group, share = dims["group"], dims["share"]
        self.me = lax.axis_index("seq")
        self.h = self.me // group
        self.q = self.me % group
        self.b0 = self.q % 2
        self.b1 = (self.q // 2) % 2
        self.c = self.q // 4
        self.it = lax.axis_index("items")
        self.base = (self.it // share) * share
        self.t = self.it % share
        x, y = self.t % 2, self.t // 2
        self.tx, self.ty, self.txy = y * 2 + 1 - x, (1 - y) * 2 + x, (1 - y) * 2 + 1 - x

    def across(self, bit):
        value = (self.q // (1 << bit)) % 2
        return {"seq": self.me + (1 - 2 * value) * (1 << bit)}

    def partner(self):
        return {"seq": (1 - self.h) * self.dims["group"] + self.q}

    def seq_shift(self, d):
        return lax.rem(self.me + d, self.dims["seq"])

    def line(self, t):
        return {"items": self.base + t}

    def seq_peers(self):
        return [{"seq": self.seq_shift(d)} for d in range(1, self.dims["seq"])]

    def items_peers(self):
        count = self.dims["items"]
        return [{"items": lax.rem(self.it + e, count)} for e in range(1, count)]


def spread_start(link, place, out, k):
    bits = place.dims["bits"]
    c, b1, b0 = place.c, place.b1, place.b0
    if bits == 3:
        step = link.send(out.at[k, c, b1, b0], out.at[k, c, b1, b0], place.across(2))
        step.wait_recv()
    waits = []
    high = link.send(out.at[k, :, b1, b0], out.at[k, :, b1, b0], place.across(1))
    waits.append(link.send(out.at[k, :, b1, b0], out.at[k, :, b1, b0], place.across(0)))
    return high, waits


def spread_end(link, place, out, k, started):
    high, waits = started
    b1, b0 = place.b1, place.b0
    high.wait_recv()
    waits.append(link.send(out.at[k, :, 1 - b1, b0], out.at[k, :, 1 - b1, b0], place.across(0)))
    return waits


def columns_out(link, place, src, dst, width):
    seq, group = place.dims["seq"], place.dims["group"]
    copies = []
    for d in range(1, seq):
        target = place.seq_shift(d)
        cols = pl.ds(pl.multiple_of(lax.rem(target, group) * width, width), width)
        copies.append((src.at[:, :, cols], dst.at[:, place.me, place.t], {"seq": target}))
    steps = link.batch(copies, dst.at[:, 0 : seq - 1, place.t])
    cols = pl.ds(pl.multiple_of(place.q * width, width), width)
    return steps, link.local(src.at[:, :, cols], dst.at[:, place.me, place.t])


def rows_out(link, place, src, dst):
    dims, me = place.dims, place.me
    slot = lax.rem(me, dims["items_dev"])
    base = link.count
    link.count += dims["items_dev"] + 1
    copies = []
    for half in range(dims["items_dev"]):
        target = half * dims["group"] + me // dims["items_dev"]
        copy = pltpu.make_async_remote_copy(
            src_ref=src,
            dst_ref=dst.at[slot, place.t],
            send_sem=link.send_sems.at[base + half],
            recv_sem=link.recv_sems.at[base + slot],
            device_id={"seq": target},
            device_id_type=MESH,
        )
        copies.append((target != me, copy))
        pl.when(target != me)(copy.start)
    own = pltpu.make_async_copy(
        src, dst.at[slot, place.t], link.send_sems.at[base + dims["items_dev"]]
    )
    mine = me // dims["items_dev"] == place.q
    pl.when(mine)(own.start)

    def arrived():
        pl.when(mine)(own.wait)
        for block in range(dims["items_dev"]):
            copy = pltpu.make_async_remote_copy(
                src_ref=src,
                dst_ref=dst.at[block, place.t],
                send_sem=link.send_sems.at[base],
                recv_sem=link.recv_sems.at[base + block],
                device_id={"seq": me},
                device_id_type=MESH,
            )
            pl.when(place.q * dims["items_dev"] + block != me)(copy.wait_recv)

    def sent():
        for other, copy in copies:
            pl.when(other)(copy.wait_send)

    return arrived, sent


class Share:
    def __init__(self, link, place, slab, half):
        self.link, self.place, self.half = link, place, half
        t = place.t
        self.from_x = link.send(slab(t), slab(t), place.line(place.tx))
        self.from_y = link.send(slab(t), slab(t), place.line(place.ty))

    def forward(self):
        link, place, half = self.link, self.place, self.half
        self.from_y.wait_recv()
        part = half(place.ty, 0)
        self.steps = [link.send(part, part, place.line(place.tx))]
        self.from_x.wait_recv()
        part = half(place.tx, 1)
        self.steps.append(link.send(part, part, place.line(place.ty)))

    def wait(self):
        arrive(self.steps)


def arrive(steps):
    for step in steps:
        step.wait_recv()


class Reduce:
    def __init__(self, link, place, part, bufs):
        self.link, self.place, self.part, self.bufs = link, place, part, bufs
        self.zero, self.one = {}, {}

    def start(self, index, k):
        place = self.place
        self.zero[index] = self.link.send(
            self.part.at[k, :, :, 1 - place.b0], self.bufs[0].at[index], place.across(0)
        )

    def middle(self, index, k):
        place, part = self.place, self.part
        recv0, send1, recv1, keep1 = self.bufs[:4]
        self.zero[index].wait_recv()
        b1, b0 = place.b1, place.b0
        for c in range(part.shape[1]):
            value = part[k, c, 1 - b1, b0].astype(F32) + recv0[index, c, 1 - b1].astype(F32)
            send1[index, c] = value.astype(BF)
        self.one[index] = self.link.send(send1.at[index], recv1.at[index], place.across(1))
        for c in range(part.shape[1]):
            keep1[index, c] = part[k, c, b1, b0].astype(F32) + recv0[index, c, b1].astype(F32)

    def end(self, index):
        place = self.place
        recv1, keep1 = self.bufs[2:4]
        self.one[index].wait_recv()
        if place.dims["bits"] == 2:
            return keep1[index, 0] + recv1[index, 0].astype(F32)
        send2, recv2 = self.bufs[4:6]
        c = place.c
        send2[index] = (keep1[index, 1 - c] + recv1[index, 1 - c].astype(F32)).astype(BF)
        step = self.link.send(send2.at[index], recv2.at[index], place.across(2))
        kept = keep1[index, c] + recv1[index, c].astype(F32)
        step.wait_recv()
        return kept + recv2[index].astype(F32)


def reduce_bufs(dims, rows):
    items_dev, width, chips = dims["items_dev"], dims["model"], dims["chips"]
    bufs = [
        pltpu.VMEM((items_dev, chips, 2, rows, width), BF),
        pltpu.VMEM((items_dev, chips, rows, width), BF),
        pltpu.VMEM((items_dev, chips, rows, width), BF),
        pltpu.VMEM((items_dev, chips, rows, width), F32),
    ]
    if dims["bits"] == 3:
        bufs += [pltpu.VMEM((items_dev, rows, width), BF) for _ in range(2)]
    return bufs


def moments(value):
    mean = jnp.mean(value, axis=-1, keepdims=True)
    centered = value - mean
    inv = lax.rsqrt(jnp.mean(centered * centered, axis=-1, keepdims=True) + EPS)
    return centered * inv, inv


def norm_back(normed, inv, gain, grad):
    scaled = grad * gain
    mean = jnp.mean(scaled, axis=-1, keepdims=True)
    cross = jnp.mean(scaled * normed, axis=-1, keepdims=True)
    return inv * (scaled - mean - normed * cross)


def rows_back(link, place, src, dst):
    dims, me, h = place.dims, place.me, place.h
    count = dims["items_dev"]
    base = link.count
    link.count += count + 1
    copies = []
    for k in range(count):
        target = place.q * count + k
        copy = pltpu.make_async_remote_copy(
            src_ref=src.at[k],
            dst_ref=dst.at[h],
            send_sem=link.send_sems.at[base + k],
            recv_sem=link.recv_sems.at[base + h],
            device_id={"seq": target},
            device_id_type=MESH,
        )
        copies.append((target != me, copy))
        pl.when(target != me)(copy.start)
    own = pltpu.make_async_copy(
        src.at[lax.rem(me, count)], dst.at[h], link.send_sems.at[base + count]
    )
    mine = me // count == place.q
    pl.when(mine)(own.start)

    def done():
        pl.when(mine)(own.wait)
        for half in range(count):
            copy = pltpu.make_async_remote_copy(
                src_ref=src.at[0],
                dst_ref=dst.at[half],
                send_sem=link.send_sems.at[base],
                recv_sem=link.recv_sems.at[base + half],
                device_id={"seq": me},
                device_id_type=MESH,
            )
            pl.when(half * dims["group"] + me // count != me)(copy.wait_recv)
        for other, copy in copies:
            pl.when(other)(copy.wait_send)

    return done


def half_mask(rows, half):
    return (lax.broadcasted_iota(jnp.int32, (rows, 128), 1) // HEAD_DIM) == half


def attend(q_ref, k_ref, v_ref, valid, p_ref, mix_ref, causal, block, first, last, pump):
    keys = k_ref.shape[0]
    for pair in range(q_ref.shape[1] // 128):
        lanes = slice(pair * 128, pair * 128 + 128)
        for start in range(first, last, block):
            stop = start + block if causal else keys
            halves = []
            for half in range(2):
                query = q_ref[start : start + block, lanes]
                query = jnp.where(half_mask(block, half), query, jnp.zeros_like(query))
                scores = nt(k_ref[:stop, lanes], query) * SCALE
                scores = jnp.where(valid(start, stop), scores, NEG)
                top = jnp.max(scores, axis=0, keepdims=True)
                grown = jnp.exp(scores - top)
                probs = (grown * (1.0 / jnp.sum(grown, axis=0, keepdims=True))).astype(BF)
                p_ref[2 * pair + half, :stop, start : start + block] = probs
                mixed = tn(v_ref[:stop, lanes], probs)
                halves.append(mixed[half * HEAD_DIM : (half + 1) * HEAD_DIM])
            mix_ref[start : start + block, lanes] = jnp.concatenate(halves, axis=0).T.astype(BF)
        if pair == 0:
            pump()


def attend_back(
    q_ref, k_ref, v_ref, p_ref, grad_ref, dq_ref, dk_ref, dv_ref, causal, block, first, last,
    pump,
):
    keys = k_ref.shape[0]
    for pair in range(q_ref.shape[1] // 128):
        lanes = slice(pair * 128, pair * 128 + 128)
        for start in range(first, last, block):
            stop = start + block if causal else keys
            halves = []
            sum_k, sum_v = None, None
            for half in range(2):
                mask = half_mask(block, half)
                query = q_ref[start : start + block, lanes]
                query = jnp.where(mask, query, jnp.zeros_like(query))
                grad = grad_ref[start : start + block, lanes]
                grad = jnp.where(mask, grad, jnp.zeros_like(grad))
                low = p_ref[2 * pair + half, :stop, start : start + block]
                probs = low.astype(F32)
                grad_probs = nt(v_ref[:stop, lanes], grad)
                delta = jnp.sum(probs * grad_probs, axis=0, keepdims=True)
                grad_scores = (probs * (grad_probs - delta)).astype(BF)
                turned = tn(k_ref[:stop, lanes], grad_scores) * SCALE
                halves.append(turned[half * HEAD_DIM : (half + 1) * HEAD_DIM])
                new_k, new_v = nn(grad_scores, query), nn(low, grad)
                sum_k = new_k if sum_k is None else sum_k + new_k
                sum_v = new_v if sum_v is None else sum_v + new_v
            old = start if causal else (keys if start else 0)
            for ref, value in ((dk_ref, sum_k), (dv_ref, sum_v)):
                if old:
                    ref[:old, lanes] = ref[:old, lanes] + value[:old]
                if old < stop:
                    ref[old:stop, lanes] = value[old:]
            dq_ref[start : start + block, lanes] = jnp.concatenate(halves, axis=0).T.astype(BF)
        if pair == 0:
            pump()


class Box:
    def __init__(self, names, refs):
        for name, ref in zip(names, refs):
            setattr(self, name, ref)


class Quarters:
    def __init__(self, link, place, grad, box_names, box):
        self.link, self.place, self.grad = link, place, grad
        self.recv, self.sums, self.last, self.lines, self.total, self.moved, self.done, self.out = (
            getattr(box, name) if name else None for name in box_names
        )

    def send(self):
        place, piece, link = self.place, self.piece, self.link
        self.steps = []
        for i, near in enumerate((place.tx, place.ty)):
            copies = [
                (self.grad.at[piece(near, i)], self.recv.at[i, 0], place.line(near)),
                (self.grad.at[piece(place.txy, i)], self.recv.at[i, 1], place.line(near)),
            ]
            self.steps.append(link.batch(copies, self.recv.at[i]))
        self.flying = list(self.steps)

    def turn(self):
        place, piece, link = self.place, self.piece, self.link
        steps = []
        for i, far in enumerate((place.ty, place.tx)):
            self.steps[i].wait_recv()
            value = self.grad[piece(far, i)].astype(F32) + self.recv[i, 1].astype(F32)
            self.sums[i] = value.astype(BF)
            steps.append(link.send(self.sums.at[i], self.last.at[i], place.line(far)))
        self.steps = steps
        self.flying += steps

    def add(self):
        place = self.place
        for i in range(2):
            self.steps[i].wait_recv()
            value = self.grad[self.piece(place.t, i)].astype(F32)
            value = value + self.recv[i, 0].astype(F32) + self.last[i].astype(F32)
            self.total[self.halves(i)] = value.astype(BF)
        if self.lines is not None:
            share, items = place.dims["share"], place.dims["items"]
            copies = []
            for a in range(1, items // share):
                target = {"items": lax.rem(place.it + a * share, items)}
                copies.append((self.total, self.lines.at[a - 1], target))
            step = self.link.batch(copies, self.lines)
            step.wait()
            self.link.open.pop()
            value = self.total[...].astype(F32)
            for a in range(1, items // share):
                value = value + self.lines[a - 1].astype(F32)
            self.total[...] = value.astype(BF)
        self.along()

    def gather(self):
        self.close()
        place, out = self.place, self.out
        self.own = self.link.local(self.done, out.at[place.t])
        self.near = [
            self.link.send(self.done, out.at[place.t], place.line(near))
            for near in (place.tx, place.ty)
        ]

    def forward(self):
        place, out, link = self.place, self.out, self.link
        self.steps = []
        for i, (source, near) in enumerate(((place.ty, place.tx), (place.tx, place.ty))):
            self.near[1 - i].wait_recv()
            part = out.at[self.cut(source, i)]
            self.steps.append(link.send(part, part, place.line(near)))

    def finish(self):
        arrive(self.steps)
        self.own.wait()


class Hidden(Quarters):
    def piece(self, t, i):
        rows = self.grad.shape[2] // 2
        return slice(None), t, slice(i * rows, (i + 1) * rows)

    def halves(self, i):
        rows = self.grad.shape[2] // 2
        return slice(None), slice(i * rows, (i + 1) * rows)

    def cut(self, t, i):
        rows = self.out.shape[1] // 2
        return t, slice(i * rows, (i + 1) * rows)

    def along(self):
        self.steps = [self.link.send(self.total.at[1], self.moved, self.place.partner())]

    def close(self):
        arrive(self.steps)
        self.done[...] = (self.total[0].astype(F32) + self.moved[...].astype(F32)).astype(BF)


class Columns(Quarters):
    def piece(self, t, i):
        blocks = self.grad.shape[1] // 2
        return slice(None), slice(i * blocks, (i + 1) * blocks), t

    def halves(self, i):
        blocks = self.grad.shape[1] // 2
        return slice(None), slice(i * blocks, (i + 1) * blocks)

    def cut(self, t, i):
        cols = self.out.shape[3] // 2
        return t, slice(None), slice(None), slice(i * cols, (i + 1) * cols)

    def along(self):
        place = self.place
        copies = []
        for d in range(1, place.dims["seq"]):
            target = place.seq_shift(d)
            copies.append((self.total.at[:, target], self.moved.at[place.me], {"seq": target}))
        self.steps = [self.link.batch(copies, self.moved.at[0 : place.dims["seq"] - 1])]
        self.own = self.link.local(self.total.at[:, place.me], self.moved.at[place.me])

    def close(self):
        arrive(self.steps)
        self.own.wait()
        dims = self.place.dims
        group, width = dims["group"], dims["width"]
        for index in range(3):
            for q in range(group):
                value = self.moved[q, index].astype(F32)
                for half in range(1, dims["items_dev"]):
                    value = value + self.moved[half * group + q, index].astype(F32)
                self.done[index, :, q * width : (q + 1) * width] = value.astype(BF)


class Rows(Quarters):
    def piece(self, t, i):
        return i, t

    def halves(self, i):
        return i

    def cut(self, t, i):
        cols = self.out.shape[2] // 2
        return t, slice(None), slice(i * cols, (i + 1) * cols)

    def along(self):
        self.moved_done = rows_back(self.link, self.place, self.total, self.moved)

    def close(self):
        self.moved_done()
        value = self.moved[0].astype(F32)
        for half in range(1, self.place.dims["items_dev"]):
            value = value + self.moved[half].astype(F32)
        self.done[...] = value.astype(BF)


class Stage:
    def __init__(self, sems, place, part, bufs, mid, spread, before):
        self.link, self.place, self.mid, self.spread = Link(*sems), place, mid, spread
        self.before = before
        self.reduce = Reduce(self.link, place, part, bufs)
        self.started, self.waits = {}, {}

    def start(self, k):
        self.reduce.start(k, k)

    def middle(self, k):
        self.reduce.middle(k, k)

    def end(self, k):
        place, spread = self.place, self.spread
        spread[k, place.c, place.b1, place.b0] = self.mid(k, self.reduce.end(k))
        self.started[k] = spread_start(self.link, place, spread, k)

    def forward(self, k):
        self.waits[k] = spread_end(self.link, self.place, self.spread, k, self.started[k])

    def arrive(self, k):
        arrive(self.waits[k])

    def release(self, k):
        done = (self.reduce.zero[k], self.reduce.one[k])
        for copy in done:
            copy.wait_send()
        late = {id(copy) for copy in done}
        self.link.open = [copy for copy in self.link.open if id(copy) not in late]


def stage_steps(stage, compute, flight=None, ended=None, after=None):
    before = stage.before
    compute(0, (lambda: before.forward(1)) if before else (lambda: None))
    stage.start(0)
    compute(1, lambda: None)
    stage.start(1)
    if before:
        before.link.finish()
    stage.middle(0)
    stage.middle(1)
    if flight:
        flight()
    stage.end(0)
    stage.end(1)
    if ended:
        ended()
    stage.forward(0)
    if after:
        after()


def layer_kernel(dims, names, *refs):
    b = Box(names, refs)
    b.grad_third, b.grad_r2, b.grad_r1, b.gc1_all = b.first, b.second, b.first, b.gy_all
    place = Place(dims)
    sems = b.send_sems, b.recv_sems
    link = Link(*sems, dims["chain"])
    width, block, items_dev = dims["width"], dims["block"], dims["items_dev"]
    h, t, q_place = place.h, place.t, place.q
    c, b1, b0 = place.c, place.b1, place.b0
    partner = place.partner()
    wr = b.w_sq.shape[0] // dims["share"]
    model = dims["model"]
    total_dec, total_mem = dims["total_dec"], dims["total_mem"]
    rb = b.dec.shape[1]

    def rows_of(ref, cols=model):
        return ref[...].reshape(-1, ref.shape[-1])[:, :cols]

    def chunk(ref, k):
        return ref[k].reshape(-1, model)

    half_rows = total_dec // 2

    def span(k):
        return slice(k * half_rows, (k + 1) * half_rows)

    def put(k, value, before=None):
        if before:
            before.release(k)
        b.part[k] = value.astype(BF).reshape(b.part.shape[1:])

    def weight(ref, index):
        return ref[index].reshape(model, width)

    weights = (b.w_sq, b.w_sk, b.w_sv, b.w_so, b.w_ck, b.w_cv, b.w_cq, b.w_co)
    rows_t = pl.ds(pl.multiple_of(t * wr, wr), wr)
    index = link.index()
    for i, w in enumerate(weights):
        pltpu.make_async_copy(w.at[rows_t], b.staged.at[i], b.send_sems.at[index]).start()
    staged = pltpu.make_async_copy(b.staged, b.staged, b.send_sems.at[index])
    own_fin = link.local(b.f_in, b.own_fin)
    own_fout = link.local(b.f_out, b.own_fout)
    greet(place.seq_peers() + place.items_peers())

    swap_x = link.send(b.dec.at[1 - h], b.x_all.at[h, c, b1, b0], partner)
    def share_columns(dst):
        blocks = dims["seq"] // 2
        return Share(
            link, place, lambda t: dst.at[:, t],
            lambda t, i: dst.at[i * blocks : (i + 1) * blocks, t],
        )

    def share_rows(dst):
        return Share(link, place, lambda t: dst.at[:, t], lambda t, i: dst.at[i, t])

    def share_hidden(dst):
        rows = dst.shape[1] // 2
        return Share(
            link, place, lambda t: dst.at[t], lambda t, i: dst.at[t, i * rows : (i + 1) * rows]
        )

    def join_cells():
        mb = b.cells.shape[1]
        same = lax.broadcasted_iota(jnp.int32, (mb, mb), 0) == lax.broadcasted_iota(
            jnp.int32, (mb, mb), 1
        )
        for k in range(items_dev):
            flags = (b.cells[k : k + 1] == 1).astype(F32)
            column = jnp.sum(jnp.where(same, flags, 0.0), axis=1, keepdims=True)
            b.mem_cells[k, :, :model] = b.mem[k]
            b.mem_cells[k, :, model:] = jnp.broadcast_to(column, (mb, 128)).astype(BF)

    b.x_all[h, c, b1, b0] = b.dec[h]
    first_x = spread_start(link, place, b.x_all, h)
    staged.wait()
    steps, own_self = columns_out(link, place, b.staged.at[0:3], b.o_self, width)
    waits = spread_end(link, place, b.x_all, h, first_x)
    swap_x.wait_recv()
    second_x = spread_start(link, place, b.x_all, 1 - h)
    so_arrived, so_sent = rows_out(link, place, b.staged.at[3], b.o_so)
    steps.wait_recv()
    own_self.wait()
    self_share = [share_columns(b.o_self.at[i]) for i in range(3)]
    waits += spread_end(link, place, b.x_all, 1 - h, second_x)
    so_arrived()
    so_share = share_rows(b.o_so)
    cross_steps, own_cross = columns_out(link, place, b.staged.at[4:7], b.o_cross, width)
    co_arrived, co_sent = rows_out(link, place, b.staged.at[7], b.o_co)
    join_cells()
    b.m_all[h, c, b1, b0] = b.mem_cells[h]
    swap_m = link.send(b.mem_cells.at[1 - h], b.m_all.at[h, c, b1, b0], partner)
    first_m = spread_start(link, place, b.m_all, h)
    own_fin.wait()
    own_fout.wait()
    fr, gr = b.o_fin.shape[1], b.o_fout.shape[1]
    step_fin = link.send(b.own_fin.at[pl.ds(pl.multiple_of(t * fr, fr), fr)], b.o_fin.at[t], partner)
    step_fout = link.send(
        b.own_fout.at[pl.ds(pl.multiple_of(t * gr, gr), gr)], b.o_fout.at[t], partner
    )
    for share in self_share:
        share.forward()

    arrive(waits)
    rows = rows_of(b.x_all)
    for index, dst in enumerate((b.sq, b.sk, b.sv)):
        self_share[index].wait()
        dst[...] = nn(rows, weight(b.o_self, index)).astype(BF)
    so_share.forward()
    cross_steps.wait_recv()
    own_cross.wait()
    cross_share = [share_columns(b.o_cross.at[i]) for i in range(3)]
    co_arrived()
    co_share = share_rows(b.o_co)
    mem_waits = spread_end(link, place, b.m_all, h, first_m)
    swap_m.wait_recv()
    second_m = spread_start(link, place, b.m_all, 1 - h)
    length, mem_length = b.dec_len[h], b.mem_len[h]

    def self_ok(start, stop):
        keys = lax.broadcasted_iota(jnp.int32, (stop, block), 0)
        spots = lax.broadcasted_iota(jnp.int32, (stop, block), 1) + start
        return (keys <= spots) & (keys < length)

    bufs = [b.recv0, b.send1, b.recv1, b.keep1]
    if dims["bits"] == 3:
        bufs += [b.send2, b.recv2]

    def forward(index, res, summed, out):
        def mid(k, total):
            value = res(k) + total
            summed[k] = value
            normed, _ = moments(value)
            result = normed * b.gain[index : index + 1] + b.bias[index : index + 1]
            out[k] = result
            return result.astype(BF)

        return mid

    def self_part(k, pump):
        attend(
            b.sq, b.sk, b.sv, self_ok, b.sp, b.smix, True, block,
            k * half_rows, (k + 1) * half_rows, pump,
        )
        if k == 0:
            so_share.wait()
        put(k, nn(b.smix[span(k)], rows_of(b.o_so)))

    def memory_part():
        arrive(mem_waits)
        mems = rows_of(b.m_all)
        cross_share[0].wait()
        b.ck[...] = nn(mems, weight(b.o_cross, 0)).astype(BF)
        cross_share[1].wait()
        b.cv[...] = nn(mems, weight(b.o_cross, 1)).astype(BF)
        spots = lax.broadcasted_iota(jnp.int32, (total_mem, 128), 0)
        cells = b.m_all[...].reshape(-1, b.m_all.shape[-1])[:, model:].astype(F32)
        b.keep[...] = ((spots < mem_length) & ((cells > 0.5) | (spots == 0))).astype(F32)

    stage = Stage(
        sems, place, b.part, bufs,
        forward(0, lambda k: b.x_all[k, c, b1, b0].astype(F32), b.sum_one, b.first), b.first_all, None,
    )
    def cross_weights():
        mem_waits.extend(spread_end(link, place, b.m_all, 1 - h, second_m))
        for share in cross_share + [co_share]:
            share.forward()
        step_fin.wait_recv()
        ffn_share.append(share_hidden(b.o_fin))
        step_fout.wait_recv()
        ffn_share.append(share_hidden(b.o_fout))

    ffn_share = []
    stage_steps(stage, self_part, after=cross_weights)
    memory_part()
    b.c_own[h] = b.cot[h]
    swap_c = link.send(b.cot.at[1 - h], b.c_own.at[h], partner)

    def cross_part(k, pump):
        last.arrive(k)
        if k == 0:
            cross_share[2].wait()
        b.cq[span(k)] = nn(chunk(b.first_all, k), weight(b.o_cross, 2)).astype(BF)
        attend(
            b.cq, b.ck, b.cv, lambda start, stop: b.keep[:, 0:1] > 0.5, b.cp, b.cmix, False, block,
            k * half_rows, (k + 1) * half_rows, pump,
        )
        if k == 0:
            co_share.wait()
        put(k, nn(b.cmix[span(k)], rows_of(b.o_co)), last)

    last = stage
    stage = Stage(
        sems, place, b.part, bufs, forward(1, lambda k: b.first[k], b.sum_two, b.second),
        b.second_all, last,
    )
    def ffn_weights():
        for share in ffn_share:
            share.forward()

    stage_steps(stage, cross_part, ffn_weights)

    w_ins = (lambda: b.own_fin[...], lambda: b.o_fin[...].reshape(model, -1))
    w_outs = (lambda: b.own_fout[...], lambda: b.o_fout[...].reshape(-1, model))
    hidden = b.own_fin.shape[1]
    last_second = stage

    def ffn_part(k, pump):
        last_second.arrive(k)
        if k == 0:
            ffn_share[0].wait()
        rows = chunk(b.second_all, k)
        for index in range(2):
            if index:
                pump()
            pre = nn(rows, w_ins[index]())
            cdf = 0.5 * (1.0 + lax.erf(pre * (0.5**0.5)))
            cols = slice(index * hidden, (index + 1) * hidden)
            b.act[span(k), cols] = (pre * cdf).astype(BF)
            b.slope[span(k), cols] = (
                cdf + pre * (jnp.exp(-0.5 * pre * pre) * 0.3989422804014327)
            ).astype(BF)
        if k == 0:
            ffn_share[1].wait()
        total = nn(b.act[span(k), :hidden], w_outs[0]())
        put(k, total + nn(b.act[span(k), hidden:], w_outs[1]()), last_second)

    swap_c.wait_recv()

    def add_sums(index, k, normed, grad):
        new = (jnp.sum(grad * normed, axis=0, keepdims=True), jnp.sum(grad, axis=0, keepdims=True))
        for row, value in zip((index, 3 + index), new):
            b.sums[row : row + 1] = value if k == 0 else b.sums[row : row + 1] + value

    def turn(k, total):
        gain = b.gain[2:3]
        normed, inv = moments(b.second[k] + total)
        spots = lax.broadcasted_iota(jnp.int32, (rb, model), 0) + (k * dims["group"] + q_place) * rb
        kept = spots < length
        b.layer[k] = jnp.where(kept, normed * gain + b.bias[2:3], 0.0).astype(BF)
        grad = jnp.where(kept, b.c_own[k].astype(F32), 0.0)
        add_sums(2, k, normed, grad)
        result = norm_back(normed, inv, gain, grad)
        b.grad_third[k] = result
        return result.astype(BF)

    stage = Stage(sems, place, b.part, bufs, turn, b.gy_all, last_second)
    stage_steps(stage, ffn_part)

    last_turn = stage

    def ffn_back(k, pump):
        last_turn.arrive(k)
        grad = chunk(b.gy_all, k)
        total = None
        for index in range(2):
            if index:
                pump()
            cols = slice(index * hidden, (index + 1) * hidden)
            grad_pre = (nt(grad, w_outs[index]()) * b.slope[span(k), cols].astype(F32)).astype(BF)
            b.slope[span(k), cols] = grad_pre
            term = nt(grad_pre, w_ins[index]())
            total = term if total is None else total + term
        put(k, total, last_turn)

    way_fout = Hidden(
        link, place, b.g_fout, ("q_fout", "t_fout", "u_fout", dims["lines"] and "l_fout", "s_fout", "z_fout", "d_fout", "r_fout"), b
    )
    way_fin = Hidden(
        link, place, b.g_fin, ("q_fin", "t_fin", "u_fin", dims["lines"] and "l_fin", "s_fin", "z_fin", "d_fin", "r_fin"), b
    )
    way_cross = Columns(
        link, place, b.g_cross, ("q_cross", "t_cross", "u_cross", dims["lines"] and "l_cross", "s_cross", "z_cross", "d_cross", "r_cross"), b
    )
    way_self = Columns(
        link, place, b.g_self, ("q_self", "t_self", "u_self", dims["lines"] and "l_self", "s_self", "z_self", "d_self", "r_self"), b
    )
    way_co = Rows(
        link, place, b.g_co, ("q_co", "t_co", "u_co", dims["lines"] and "l_co", "s_co", "z_co", "d_co", "r_co"), b
    )
    way_so = Rows(
        link, place, b.g_so, ("q_so", "t_so", "u_so", dims["lines"] and "l_so", "s_so", "z_so", "d_so", "r_so"), b
    )

    def backward(index, res, summed, out):
        def mid(k, total):
            normed, inv = moments(summed[k])
            grad = res[k] + total
            add_sums(index, k, normed, grad)
            result = norm_back(normed, inv, b.gain[index : index + 1], grad)
            out[k] = result
            return result.astype(BF)

        return mid

    def out_grads():
        grad = rows_of(b.gy_all)
        for index in range(2):
            cols = slice(index * hidden, (index + 1) * hidden)
            value = tn(b.act[:, cols], grad)
            b.g_fout[index] = value.astype(BF).reshape(b.g_fout.shape[1:])
        way_fout.send()

    def in_grads():
        rows = rows_of(b.second_all)
        for index in range(2):
            cols = slice(index * hidden, (index + 1) * hidden)
            value = tn(rows, b.slope[:, cols])
            b.g_fin[index] = value.astype(BF).reshape(b.g_fin.shape[1:])
        way_fin.send()

    stage = Stage(
        sems, place, b.part, bufs, backward(1, b.grad_third, b.sum_two, b.grad_r2), b.gc2_all,
        last_turn,
    )
    stage_steps(stage, ffn_back, out_grads, in_grads)

    last_back = stage

    def cross_back(k, pump):
        last_back.arrive(k)
        b.dmix[span(k)] = nt(chunk(b.gc2_all, k), rows_of(b.o_co)).astype(BF)
        attend_back(
            b.cq, b.ck, b.cv, b.cp, b.dmix, b.dq, b.sum_dk, b.sum_dv, False, block,
            k * half_rows, (k + 1) * half_rows, pump,
        )
        put(k, nt(b.dq[span(k)], weight(b.o_cross, 2)), last_back)

    def cross_grads():
        way_fout.turn()
        mems = rows_of(b.m_all)
        shape = b.g_cross.shape[1:]
        b.dck[...] = (b.sum_dk[:total_mem] * SCALE).astype(BF)
        b.dcv[...] = b.sum_dv[:total_mem].astype(BF)
        b.g_cross[0] = tn(rows_of(b.first_all), b.dq[...]).astype(BF).reshape(shape)
        b.g_cross[1] = tn(mems, b.dck[...]).astype(BF).reshape(shape)
        b.g_cross[2] = tn(mems, b.dcv[...]).astype(BF).reshape(shape)
        way_cross.send()
        b.g_co[...] = tn(b.cmix[...], rows_of(b.gc2_all)).astype(BF).reshape(b.g_co.shape)
        way_co.send()

    def part_mem():
        value = nt(b.dck[...], weight(b.o_cross, 0)) + nt(b.dcv[...], weight(b.o_cross, 1))
        b.part_m[...] = value.astype(BF).reshape(b.part_m.shape)

    stage = Stage(
        sems, place, b.part, bufs, backward(0, b.grad_r2, b.sum_one, b.grad_r1), b.gc1_all,
        last_back,
    )
    def cross_ended():
        part_mem()
        way_fin.turn()

    stage_steps(stage, cross_back, cross_grads, cross_ended)

    for k in range(2):
        stage.arrive(k)
        pump = (lambda: stage.forward(1)) if k == 0 else (lambda: None)
        b.dmix[span(k)] = nt(chunk(b.gc1_all, k), rows_of(b.o_so)).astype(BF)
        attend_back(
            b.sq, b.sk, b.sv, b.sp, b.dmix, b.dq, b.sum_dk, b.sum_dv, True, block,
            k * half_rows, (k + 1) * half_rows, pump,
        )
    b.dsk[...] = (b.sum_dk[...] * SCALE).astype(BF)
    b.dsv[...] = b.sum_dv[...].astype(BF)
    for k in range(2):
        total = nt(b.dq[span(k)], weight(b.o_self, 0)) + nt(b.dsk[span(k)], weight(b.o_self, 1))
        put(k, total + nt(b.dsv[span(k)], weight(b.o_self, 2)), stage)
    stage.link.finish()
    chain = Link(*sems)
    ks = (1 - h, h)
    red_x = Reduce(chain, place, b.part, bufs)
    mem_bufs = [b.recv0_m, b.send1_m, b.recv1_m, b.keep1_m]
    if dims["bits"] == 3:
        mem_bufs += [b.send2_m, b.recv2_m]
    red_m = Reduce(link, place, b.part_m, mem_bufs)
    for red in (red_x, red_m):
        for index in range(2):
            red.start(index, ks[index])
    rows = rows_of(b.x_all)
    shape = b.g_self.shape[1:]
    b.g_self[0] = tn(rows, b.dq[...]).astype(BF).reshape(shape)
    b.g_self[1] = tn(rows, b.dsk[...]).astype(BF).reshape(shape)
    b.g_self[2] = tn(rows, b.dsv[...]).astype(BF).reshape(shape)
    way_self.send()
    b.g_so[...] = tn(b.smix[...], rows_of(b.gc1_all)).astype(BF).reshape(b.g_so.shape)
    way_so.send()
    way_fout.add()
    way_cross.turn()
    way_co.turn()
    for red in (red_x, red_m):
        for index in range(2):
            red.middle(index, ks[index])
    copies = []
    for d in range(1, dims["seq"]):
        copies.append((b.sums, b.sums_seq.at[d - 1], {"seq": place.seq_shift(d)}))
    seq_sums = link.batch(copies, b.sums_seq)
    way_fin.add()
    swap_l = link.send(b.layer.at[1 - h], b.layer_out.at[h], partner)
    b.layer_out[h] = b.layer[h]
    b.send_x[...] = (red_x.end(0) + b.grad_r1[1 - h]).astype(BF)
    swap_x = link.send(b.send_x, b.recv_x, partner)
    b.grad_dec[h] = red_x.end(1) + b.grad_r1[h]
    b.send_m[...] = red_m.end(0).astype(BF)
    swap_m = link.send(b.send_m, b.recv_m, partner)
    b.grad_mem[h] = red_m.end(1)
    way_fout.gather()
    way_self.turn()
    way_so.turn()
    way_cross.add()
    way_co.add()
    way_fin.gather()
    way_fout.forward()
    seq_sums.wait_recv()
    value = b.sums[...]
    for d in range(1, dims["seq"]):
        value = value + b.sums_seq[d - 1]
    b.sums_line[...] = value
    copies = []
    for e in range(1, dims["items"]):
        target = {"items": lax.rem(place.it + e, dims["items"])}
        copies.append((b.sums_line, b.sums_items.at[e - 1], target))
    item_sums = link.batch(copies, b.sums_items)
    swap_x.wait_recv()
    b.grad_dec[1 - h] = b.recv_x[...].astype(F32)
    swap_m.wait_recv()
    b.grad_mem[1 - h] = b.recv_m[...].astype(F32)
    swap_l.wait_recv()
    way_self.add()
    way_so.add()
    way_cross.gather()
    way_co.gather()
    way_fin.forward()
    item_sums.wait_recv()
    value = b.sums_line[...]
    for e in range(1, dims["items"]):
        value = value + b.sums_items[e - 1]
    b.sums_out[...] = value
    way_cross.forward()
    way_co.forward()
    way_self.gather()
    way_so.gather()
    way_self.forward()
    way_so.forward()
    for way in (way_fout, way_fin, way_cross, way_co, way_self, way_so):
        way.finish()
    so_sent()
    co_sent()
    chain.finish()
    link.finish()


def shape(dims, dtype):
    return jax.ShapeDtypeStruct(tuple(dims), dtype)


def outputs_kernel(layer, dec, mem, cross, own, co, so, fin, fout, sums, *outs):
    o_layer, o_dec, o_mem = outs[:3]
    o_layer[...] = layer[...]
    o_dec[...] = dec[...]
    o_mem[...] = mem[...]
    for index in range(3):
        outs[3 + index][...] = own[0, index].astype(F32)
        outs[7 + index][...] = cross[0, index].astype(F32)
    outs[6][...] = so[0].astype(F32)
    outs[10][...] = co[0].astype(F32)
    outs[11][...] = fin[0].astype(F32)
    outs[12][...] = fout[0].astype(F32)
    outs[13][...] = sums[0:3]
    outs[14][...] = sums[3:6]


def shards(
    mesh, dec_in, memory, dec_len, mem_len, cell_mask, self_query, self_key, self_value, self_out,
    cross_query, cross_key, cross_value, cross_out, ffn_in, ffn_out, norm_gain, norm_bias, cotangent,
):
    items_dev, rb, model = dec_in.shape
    mb = memory.shape[1]
    seq, items = mesh.shape["seq"], mesh.shape["items"]
    group = seq // items_dev
    share = 4
    bits = group.bit_length() - 1
    chips = group // 4
    width = model // group
    total_dec, total_mem = rb * seq, mb * seq
    heads = width // HEAD_DIM
    hidden = ffn_in.shape[1]
    wr = self_query.shape[0] // share
    fr, gr = model // share, hidden // share
    lines = items // share - 1
    dims = {
        "items_dev": items_dev, "items": items, "seq": seq, "group": group, "share": share,
        "bits": bits, "chips": chips, "width": width, "model": model, "block": 256,
        "total_dec": total_dec, "total_mem": total_mem, "lines": lines,
        "chain": 12 + 2 * (bits - 2),
    }
    ins = [
        ("dec", dec_in, VM), ("mem", memory, VM), ("cells", cell_mask, VM), ("cot", cotangent, VM),
        ("dec_len", dec_len, SM), ("mem_len", mem_len, SM),
        ("w_sq", self_query, HBM), ("w_sk", self_key, HBM), ("w_sv", self_value, HBM),
        ("w_so", self_out, HBM), ("w_cq", cross_query, HBM), ("w_ck", cross_key, HBM),
        ("w_cv", cross_value, HBM), ("w_co", cross_out, HBM), ("f_in", ffn_in, HBM),
        ("f_out", ffn_out, HBM), ("gain", norm_gain, VM), ("bias", norm_bias, VM),
    ]
    own, own_m = (items_dev, rb, model), (items_dev, mb, model)
    grid = (items_dev, chips, 2, 2)
    outs = [
        ("layer_out", own, BF, VM), ("grad_dec", own, F32, VM), ("grad_mem", own_m, F32, VM),
        ("sums_out", (8, model), F32, VM),
        ("r_cross", (share, 3, wr, model), BF, HBM), ("r_self", (share, 3, wr, model), BF, HBM),
        ("r_co", (share, wr, model), BF, HBM), ("r_so", (share, wr, model), BF, HBM),
        ("r_fin", (share, fr, hidden), BF, HBM), ("r_fout", (share, gr, model), BF, HBM),
    ]
    cols = (3, seq, share, wr, width)
    scratch = [
        ("x_all", grid + (rb, model), BF), ("m_all", grid + (mb, model + 128), BF),
        ("mem_cells", (items_dev, mb, model + 128), BF), ("c_own", own, BF), ("staged", (8, wr, model), BF),
        ("own_fin", (model, hidden), BF), ("own_fout", (hidden, model), BF),
        ("o_self", cols, BF), ("o_cross", cols, BF),
        ("o_so", (items_dev, share, wr, model), BF), ("o_co", (items_dev, share, wr, model), BF),
        ("o_fin", (share, fr, hidden), BF), ("o_fout", (share, gr, model), BF),
        ("sq", (total_dec, width), BF), ("sk", (total_dec, width), BF), ("sv", (total_dec, width), BF),
        ("cq", (total_dec, width), BF), ("ck", (total_mem, width), BF), ("cv", (total_mem, width), BF),
        ("sp", (heads, total_dec, total_dec), BF), ("cp", (heads, total_mem, total_dec), BF),
        ("smix", (total_dec, width), BF), ("cmix", (total_dec, width), BF),
        ("keep", (total_mem, 128), F32),
        ("part", grid + (rb, model), BF), ("part_m", grid + (mb, model), BF),
        ("first_all", grid + (rb, model), BF), ("second_all", grid + (rb, model), BF),
        ("gy_all", grid + (rb, model), BF), ("gc2_all", grid + (rb, model), BF),
        ("sum_one", own, F32), ("sum_two", own, F32), ("first", own, F32), ("second", own, F32),
        ("layer", own, BF), ("sum_dk", (total_dec, width), F32), ("sum_dv", (total_dec, width), F32),
        ("act", (total_dec, 2 * hidden), BF), ("slope", (total_dec, 2 * hidden), BF),
        ("dmix", (total_dec, width), BF), ("dq", (total_dec, width), BF),
        ("dsk", (total_dec, width), BF), ("dsv", (total_dec, width), BF),
        ("dck", (total_mem, width), BF), ("dcv", (total_mem, width), BF),
        ("send_x", (rb, model), BF), ("recv_x", (rb, model), BF),
        ("send_m", (mb, model), BF), ("recv_m", (mb, model), BF),
        ("sums", (8, model), F32), ("sums_line", (8, model), F32),
        ("sums_seq", (seq - 1, 8, model), F32), ("sums_items", (items - 1, 8, model), F32),
    ]
    for name, rows in (("", rb), ("_m", mb)):
        scratch += [
            ("recv0" + name, (items_dev, chips, 2, rows, model), BF),
            ("send1" + name, (items_dev, chips, rows, model), BF),
            ("recv1" + name, (items_dev, chips, rows, model), BF),
            ("keep1" + name, (items_dev, chips, rows, model), F32),
        ]
        if bits == 3:
            scratch += [
                ("send2" + name, (items_dev, rows, model), BF),
                ("recv2" + name, (items_dev, rows, model), BF),
            ]
    for name, grad, quarter, piece, moved, done in (
        ("fin", (2, share, fr, hidden), (2, fr, hidden), (2, fr // 2, hidden), (fr, hidden),
         (fr, hidden)),
        ("fout", (2, share, gr, model), (2, gr, model), (2, gr // 2, model), (gr, model), (gr, model)),
        ("cross", cols, (3, seq, wr, width), (3, seq // 2, wr, width), (seq, 3, wr, width),
         (3, wr, model)),
        ("self", cols, (3, seq, wr, width), (3, seq // 2, wr, width), (seq, 3, wr, width),
         (3, wr, model)),
        ("co", (items_dev, share, wr, model), (items_dev, wr, model), (wr, model),
         (items_dev, wr, model), (wr, model)),
        ("so", (items_dev, share, wr, model), (items_dev, wr, model), (wr, model),
         (items_dev, wr, model), (wr, model)),
    ):
        scratch += [
            ("g_" + name, grad, BF), ("q_" + name, (2, 2) + piece, BF), ("t_" + name, (2,) + piece, BF),
            ("u_" + name, (2,) + piece, BF), ("s_" + name, quarter, BF), ("z_" + name, moved, BF),
            ("d_" + name, done, BF),
        ]
        if lines:
            scratch.append(("l_" + name, (lines,) + quarter, BF))
    copies = dims["chain"] + 145 + 12 * (bits - 2)
    names = [x[0] for x in ins + outs + scratch] + ["send_sems", "recv_sems"]
    results = pl.pallas_call(
        functools.partial(layer_kernel, dims, names),
        name="layer",
        out_shape=[shape(x[1], x[2]) for x in outs],
        in_specs=[x[2] for x in ins],
        out_specs=[x[3] for x in outs],
        scratch_shapes=[pltpu.VMEM(x[1], x[2]) for x in scratch]
        + [pltpu.SemaphoreType.DMA((copies,)), pltpu.SemaphoreType.DMA((copies,))],
        compiler_params=pltpu.CompilerParams(
            collective_id=0, has_side_effects=True, vmem_limit_bytes=VMEM_BYTES
        ),
    )(*[x[1] for x in ins])
    layer_out, grad_dec, grad_memory, sums, r_cross, r_self, r_co, r_so, r_fin, r_fout = results
    tok, mem_rows = items_dev * rb, items_dev * mb
    pieces = (
        ((tok, model), (tok // share, model), BF), ((tok, model), (tok // share, model), F32),
        ((mem_rows, model), (mem_rows // share, model), F32),
    )
    heads_in = [
        pl.BlockSpec((1, 3, wr, model), lambda i: (i, 0, 0, 0)),
        pl.BlockSpec((1, 3, wr, model), lambda i: (i, 0, 0, 0)),
        pl.BlockSpec((1, wr, model), lambda i: (i, 0, 0)),
        pl.BlockSpec((1, wr, model), lambda i: (i, 0, 0)),
        pl.BlockSpec((1, fr, hidden), lambda i: (i, 0, 0)),
        pl.BlockSpec((1, gr, model), lambda i: (i, 0, 0)),
        pl.BlockSpec((8, model), lambda i: (0, 0)),
    ]
    row_specs = [pl.BlockSpec(x[1], lambda i: (i, 0)) for x in pieces]
    square = (share * wr, model)
    outs = pl.pallas_call(
        outputs_kernel,
        name="outputs",
        grid=(share,),
        in_specs=row_specs + heads_in,
        out_specs=row_specs
        + [pl.BlockSpec((wr, model), lambda i: (i, 0))] * 8
        + [pl.BlockSpec((fr, hidden), lambda i: (i, 0)), pl.BlockSpec((gr, model), lambda i: (i, 0))]
        + [pl.BlockSpec((3, model), lambda i: (0, 0))] * 2,
        out_shape=[shape(x[0], x[2]) for x in pieces]
        + [shape(square, F32)] * 8
        + [shape((model, hidden), F32), shape((hidden, model), F32)]
        + [shape((3, model), F32)] * 2,
        compiler_params=pltpu.CompilerParams(vmem_limit_bytes=VMEM_BYTES),
    )(
        layer_out.reshape(tok, model), grad_dec.reshape(tok, model),
        grad_memory.reshape(mem_rows, model), r_cross, r_self, r_co, r_so, r_fin, r_fout, sums,
    )
    return (
        outs[0].reshape(own), outs[1].reshape(own), outs[2].reshape(own_m), *outs[3:],
    )


def solution(mesh):
    rows = P("seq", None)
    tokens = P("items", "seq", None)
    placed = (
        (tokens, tokens, P("items"), P("items"), P("items", "seq"))
        + (rows,) * 8
        + (P(None, "seq"), rows, P(), P(), tokens)
    )
    return jax.shard_map(
        functools.partial(shards, mesh),
        mesh=mesh,
        in_specs=placed,
        out_specs=(tokens,) * 3 + (rows,) * 8 + (P(None, "seq"), rows, P(), P()),
        check_vma=False,
    )
```

```python
import functools

import jax
import jax.numpy as jnp
from jax import lax
from jax.experimental import pallas as pl
from jax.experimental.pallas import tpu as pltpu
from jax.sharding import PartitionSpec as P

HEAD_DIM = 64
EPS = 1e-05
NEG = -1e30
SCALE = HEAD_DIM ** (-0.5)
BF = jnp.bfloat16
F32 = jnp.float32
VMEM_BYTES = 63 * 1024 * 1024
MESH = pl.DeviceIdType.MESH
VM = pl.BlockSpec(memory_space=pltpu.VMEM)
HBM = pl.BlockSpec(memory_space=pl.ANY)
SM = pl.BlockSpec(memory_space=pltpu.SMEM)


def nn(left, right):
    return lax.dot_general(left, right, (((1,), (0,)), ((), ())), preferred_element_type=F32)


def nt(left, right):
    return lax.dot_general(left, right, (((1,), (1,)), ((), ())), preferred_element_type=F32)


def tn(left, right):
    return lax.dot_general(left, right, (((0,), (0,)), ((), ())), preferred_element_type=F32)


class Link:
    def __init__(self, send_sems, recv_sems, first=0):
        self.send_sems, self.recv_sems, self.count, self.open = send_sems, recv_sems, first, []

    def index(self):
        self.count += 1
        return self.count - 1

    def make(self, src, dst, device, index):
        return pltpu.make_async_remote_copy(
            src_ref=src,
            dst_ref=dst,
            send_sem=self.send_sems.at[index],
            recv_sem=self.recv_sems.at[index],
            device_id=device,
            device_id_type=MESH,
        )

    def send(self, src, dst, device):
        copy = self.make(src, dst, device, self.index())
        copy.start()
        self.open.append(copy)
        return copy

    def batch(self, copies, whole):
        index = self.index()
        for copy in copies:
            self.make(*copy, index).start()
        wait = self.make(whole, whole, copies[0][2], index)
        self.open.append(wait)
        return wait

    def settle(self, copy):
        copy.wait_send()
        self.open = [other for other in self.open if other is not copy]

    def local(self, src, dst):
        copy = pltpu.make_async_copy(src, dst, self.send_sems.at[self.index()])
        copy.start()
        return copy

    def finish(self, kept=()):
        late = {id(copy) for copy in kept}
        for copy in self.open:
            if id(copy) not in late:
                copy.wait_send()
        self.open = [copy for copy in self.open if id(copy) in late]


def greet(devices):
    barrier = pltpu.get_barrier_semaphore()
    for device in devices:
        pl.semaphore_signal(barrier, inc=1, device_id=device, device_id_type=MESH)
    pl.semaphore_wait(barrier, len(devices))


class Place:
    def __init__(self, dims):
        self.dims = dims
        group, share = dims["group"], dims["share"]
        self.me = lax.axis_index("seq")
        self.h = self.me // group
        self.q = self.me % group
        self.b0 = self.q % 2
        self.b1 = (self.q // 2) % 2
        self.c = self.q // 4
        self.it = lax.axis_index("items")
        self.base = (self.it // share) * share
        self.t = self.it % share
        x, y = self.t % 2, self.t // 2
        self.tx, self.ty, self.txy = y * 2 + 1 - x, (1 - y) * 2 + x, (1 - y) * 2 + 1 - x

    def across(self, bit):
        value = (self.q // (1 << bit)) % 2
        return {"seq": self.me + (1 - 2 * value) * (1 << bit)}

    def partner(self):
        return {"seq": (1 - self.h) * self.dims["group"] + self.q}

    def seq_shift(self, d):
        return lax.rem(self.me + d, self.dims["seq"])

    def line(self, t):
        return {"items": self.base + t}

    def seq_peers(self):
        return [{"seq": self.seq_shift(d)} for d in range(1, self.dims["seq"])]

    def items_peers(self):
        count = self.dims["items"]
        return [{"items": lax.rem(self.it + e, count)} for e in range(1, count)]


def spread_start(link, place, out, k):
    bits = place.dims["bits"]
    c, b1, b0 = place.c, place.b1, place.b0
    if bits == 3:
        step = link.send(out.at[k, c, b1, b0], out.at[k, c, b1, b0], place.across(2))
        step.wait_recv()
    waits = []
    high = link.send(out.at[k, :, b1, b0], out.at[k, :, b1, b0], place.across(1))
    waits.append(link.send(out.at[k, :, b1, b0], out.at[k, :, b1, b0], place.across(0)))
    return high, waits


def spread_end(link, place, out, k, started):
    high, waits = started
    b1, b0 = place.b1, place.b0
    high.wait_recv()
    waits.append(link.send(out.at[k, :, 1 - b1, b0], out.at[k, :, 1 - b1, b0], place.across(0)))
    return waits


def columns_out(link, place, src, dst, width):
    seq, group = place.dims["seq"], place.dims["group"]
    copies = []
    for d in range(1, seq):
        target = place.seq_shift(d)
        cols = pl.ds(pl.multiple_of(lax.rem(target, group) * width, width), width)
        copies.append((src.at[:, :, cols], dst.at[:, place.me, place.t], {"seq": target}))
    steps = link.batch(copies, dst.at[:, 0 : seq - 1, place.t])
    cols = pl.ds(pl.multiple_of(place.q * width, width), width)
    return steps, link.local(src.at[:, :, cols], dst.at[:, place.me, place.t])


def rows_out(link, place, src, dst):
    dims, me = place.dims, place.me
    slot = lax.rem(me, dims["items_dev"])
    base = link.count
    link.count += dims["items_dev"] + 1
    copies = []
    for half in range(dims["items_dev"]):
        target = half * dims["group"] + me // dims["items_dev"]
        copy = pltpu.make_async_remote_copy(
            src_ref=src,
            dst_ref=dst.at[slot, place.t],
            send_sem=link.send_sems.at[base + half],
            recv_sem=link.recv_sems.at[base + slot],
            device_id={"seq": target},
            device_id_type=MESH,
        )
        copies.append((target != me, copy))
        pl.when(target != me)(copy.start)
    own = pltpu.make_async_copy(
        src, dst.at[slot, place.t], link.send_sems.at[base + dims["items_dev"]]
    )
    mine = me // dims["items_dev"] == place.q
    pl.when(mine)(own.start)

    def arrived():
        pl.when(mine)(own.wait)
        for block in range(dims["items_dev"]):
            copy = pltpu.make_async_remote_copy(
                src_ref=src,
                dst_ref=dst.at[block, place.t],
                send_sem=link.send_sems.at[base],
                recv_sem=link.recv_sems.at[base + block],
                device_id={"seq": me},
                device_id_type=MESH,
            )
            pl.when(place.q * dims["items_dev"] + block != me)(copy.wait_recv)

    def sent():
        for other, copy in copies:
            pl.when(other)(copy.wait_send)

    return arrived, sent


class Share:
    def __init__(self, link, place, slab, half):
        self.link, self.place, self.half = link, place, half
        t = place.t
        self.from_x = link.send(slab(t), slab(t), place.line(place.tx))
        self.from_y = link.send(slab(t), slab(t), place.line(place.ty))

    def forward(self):
        link, place, half = self.link, self.place, self.half
        self.from_y.wait_recv()
        part = half(place.ty, 0)
        self.steps = [link.send(part, part, place.line(place.tx))]
        self.from_x.wait_recv()
        part = half(place.tx, 1)
        self.steps.append(link.send(part, part, place.line(place.ty)))

    def wait(self):
        arrive(self.steps)


def arrive(steps):
    for step in steps:
        step.wait_recv()


class Reduce:
    def __init__(self, link, place, part, bufs):
        self.link, self.place, self.part, self.bufs = link, place, part, bufs
        self.zero, self.one = {}, {}

    def start(self, index, k):
        place = self.place
        self.zero[index] = self.link.send(
            self.part.at[k, :, :, 1 - place.b0], self.bufs[0].at[index], place.across(0)
        )

    def middle(self, index, k):
        place, part = self.place, self.part
        recv0, send1, recv1, keep1 = self.bufs[:4]
        self.zero[index].wait_recv()
        b1, b0 = place.b1, place.b0
        for c in range(part.shape[1]):
            value = part[k, c, 1 - b1, b0].astype(F32) + recv0[index, c, 1 - b1].astype(F32)
            send1[index, c] = value.astype(BF)
        self.one[index] = self.link.send(send1.at[index], recv1.at[index], place.across(1))
        for c in range(part.shape[1]):
            keep1[index, c] = part[k, c, b1, b0].astype(F32) + recv0[index, c, b1].astype(F32)

    def end(self, index):
        place = self.place
        recv1, keep1 = self.bufs[2:4]
        self.one[index].wait_recv()
        if place.dims["bits"] == 2:
            return keep1[index, 0] + recv1[index, 0].astype(F32)
        send2, recv2 = self.bufs[4:6]
        c = place.c
        send2[index] = (keep1[index, 1 - c] + recv1[index, 1 - c].astype(F32)).astype(BF)
        step = self.link.send(send2.at[index], recv2.at[index], place.across(2))
        kept = keep1[index, c] + recv1[index, c].astype(F32)
        step.wait_recv()
        return kept + recv2[index].astype(F32)


def reduce_bufs(dims, rows):
    items_dev, width, chips = dims["items_dev"], dims["model"], dims["chips"]
    bufs = [
        pltpu.VMEM((items_dev, chips, 2, rows, width), BF),
        pltpu.VMEM((items_dev, chips, rows, width), BF),
        pltpu.VMEM((items_dev, chips, rows, width), BF),
        pltpu.VMEM((items_dev, chips, rows, width), F32),
    ]
    if dims["bits"] == 3:
        bufs += [pltpu.VMEM((items_dev, rows, width), BF) for _ in range(2)]
    return bufs


def moments(value):
    mean = jnp.mean(value, axis=-1, keepdims=True)
    centered = value - mean
    inv = lax.rsqrt(jnp.mean(centered * centered, axis=-1, keepdims=True) + EPS)
    return centered * inv, inv


def norm_back(normed, inv, gain, grad):
    scaled = grad * gain
    mean = jnp.mean(scaled, axis=-1, keepdims=True)
    cross = jnp.mean(scaled * normed, axis=-1, keepdims=True)
    return inv * (scaled - mean - normed * cross)


def rows_back(link, place, src, dst):
    dims, me, h = place.dims, place.me, place.h
    count = dims["items_dev"]
    base = link.count
    link.count += count + 1
    copies = []
    for k in range(count):
        target = place.q * count + k
        copy = pltpu.make_async_remote_copy(
            src_ref=src.at[k],
            dst_ref=dst.at[h],
            send_sem=link.send_sems.at[base + k],
            recv_sem=link.recv_sems.at[base + h],
            device_id={"seq": target},
            device_id_type=MESH,
        )
        copies.append((target != me, copy))
        pl.when(target != me)(copy.start)
    own = pltpu.make_async_copy(
        src.at[lax.rem(me, count)], dst.at[h], link.send_sems.at[base + count]
    )
    mine = me // count == place.q
    pl.when(mine)(own.start)

    def done():
        pl.when(mine)(own.wait)
        for half in range(count):
            copy = pltpu.make_async_remote_copy(
                src_ref=src.at[0],
                dst_ref=dst.at[half],
                send_sem=link.send_sems.at[base],
                recv_sem=link.recv_sems.at[base + half],
                device_id={"seq": me},
                device_id_type=MESH,
            )
            pl.when(half * dims["group"] + me // count != me)(copy.wait_recv)
        for other, copy in copies:
            pl.when(other)(copy.wait_send)

    return done


def half_mask(rows, half):
    return (lax.broadcasted_iota(jnp.int32, (rows, 128), 1) // HEAD_DIM) == half


def attend(q_ref, k_ref, v_ref, valid, p_ref, mix_ref, causal, block, first, last, pump):
    keys = k_ref.shape[0]
    for pair in range(q_ref.shape[1] // 128):
        lanes = slice(pair * 128, pair * 128 + 128)
        for start in range(first, last, block):
            stop = start + block if causal else keys
            halves = []
            for half in range(2):
                query = q_ref[start : start + block, lanes]
                query = jnp.where(half_mask(block, half), query, jnp.zeros_like(query))
                scores = nt(k_ref[:stop, lanes], query) * SCALE
                scores = jnp.where(valid(start, stop), scores, NEG)
                top = jnp.max(scores, axis=0, keepdims=True)
                grown = jnp.exp(scores - top)
                probs = (grown * (1.0 / jnp.sum(grown, axis=0, keepdims=True))).astype(BF)
                p_ref[2 * pair + half, :stop, start : start + block] = probs
                mixed = tn(v_ref[:stop, lanes], probs)
                halves.append(mixed[half * HEAD_DIM : (half + 1) * HEAD_DIM])
            mix_ref[start : start + block, lanes] = jnp.concatenate(halves, axis=0).T.astype(BF)
        if pair == 0:
            pump()


def attend_back(
    q_ref, k_ref, v_ref, p_ref, grad_ref, dq_ref, dk_ref, dv_ref, causal, block, first, last,
    pump,
):
    keys = k_ref.shape[0]
    for pair in range(q_ref.shape[1] // 128):
        lanes = slice(pair * 128, pair * 128 + 128)
        for start in range(first, last, block):
            stop = start + block if causal else keys
            halves = []
            sum_k, sum_v = None, None
            for half in range(2):
                mask = half_mask(block, half)
                query = q_ref[start : start + block, lanes]
                query = jnp.where(mask, query, jnp.zeros_like(query))
                grad = grad_ref[start : start + block, lanes]
                grad = jnp.where(mask, grad, jnp.zeros_like(grad))
                low = p_ref[2 * pair + half, :stop, start : start + block]
                probs = low.astype(F32)
                grad_probs = nt(v_ref[:stop, lanes], grad)
                delta = jnp.sum(probs * grad_probs, axis=0, keepdims=True)
                grad_scores = (probs * (grad_probs - delta)).astype(BF)
                turned = tn(k_ref[:stop, lanes], grad_scores) * SCALE
                halves.append(turned[half * HEAD_DIM : (half + 1) * HEAD_DIM])
                new_k, new_v = nn(grad_scores, query), nn(low, grad)
                sum_k = new_k if sum_k is None else sum_k + new_k
                sum_v = new_v if sum_v is None else sum_v + new_v
            old = start if causal else (keys if start else 0)
            for ref, value in ((dk_ref, sum_k), (dv_ref, sum_v)):
                if old:
                    ref[:old, lanes] = ref[:old, lanes] + value[:old]
                if old < stop:
                    ref[old:stop, lanes] = value[old:]
            dq_ref[start : start + block, lanes] = jnp.concatenate(halves, axis=0).T.astype(BF)
        if pair == 0:
            pump()


class Box:
    def __init__(self, names, refs):
        for name, ref in zip(names, refs):
            setattr(self, name, ref)


class Quarters:
    def __init__(self, link, place, grad, box_names, box):
        self.link, self.place, self.grad = link, place, grad
        self.recv, self.sums, self.last, self.lines, self.total, self.moved, self.done, self.out = (
            getattr(box, name) if name else None for name in box_names
        )

    def send(self):
        place, piece, link = self.place, self.piece, self.link
        self.steps = []
        for i, near in enumerate((place.tx, place.ty)):
            copies = [
                (self.grad.at[piece(near, i)], self.recv.at[i, 0], place.line(near)),
                (self.grad.at[piece(place.txy, i)], self.recv.at[i, 1], place.line(near)),
            ]
            self.steps.append(link.batch(copies, self.recv.at[i]))
        self.flying = list(self.steps)

    def turn(self):
        place, piece, link = self.place, self.piece, self.link
        steps = []
        for i, far in enumerate((place.ty, place.tx)):
            self.steps[i].wait_recv()
            value = self.grad[piece(far, i)].astype(F32) + self.recv[i, 1].astype(F32)
            self.sums[i] = value.astype(BF)
            steps.append(link.send(self.sums.at[i], self.last.at[i], place.line(far)))
        self.steps = steps
        self.flying += steps

    def add(self):
        place = self.place
        for i in range(2):
            self.steps[i].wait_recv()
            value = self.grad[self.piece(place.t, i)].astype(F32)
            value = value + self.recv[i, 0].astype(F32) + self.last[i].astype(F32)
            self.total[self.halves(i)] = value.astype(BF)
        if self.lines is not None:
            share, items = place.dims["share"], place.dims["items"]
            copies = []
            for a in range(1, items // share):
                target = {"items": lax.rem(place.it + a * share, items)}
                copies.append((self.total, self.lines.at[a - 1], target))
            step = self.link.batch(copies, self.lines)
            step.wait()
            self.link.open.pop()
            value = self.total[...].astype(F32)
            for a in range(1, items // share):
                value = value + self.lines[a - 1].astype(F32)
            self.total[...] = value.astype(BF)
        self.along()

    def gather(self):
        self.close()
        place, out = self.place, self.out
        self.own = self.link.local(self.done, out.at[place.t])
        self.near = [
            self.link.send(self.done, out.at[place.t], place.line(near))
            for near in (place.tx, place.ty)
        ]

    def forward(self):
        place, out, link = self.place, self.out, self.link
        self.steps = []
        for i, (source, near) in enumerate(((place.ty, place.tx), (place.tx, place.ty))):
            self.near[1 - i].wait_recv()
            part = out.at[self.cut(source, i)]
            self.steps.append(link.send(part, part, place.line(near)))

    def finish(self):
        arrive(self.steps)
        self.own.wait()


class Hidden(Quarters):
    def piece(self, t, i):
        rows = self.grad.shape[2] // 2
        return slice(None), t, slice(i * rows, (i + 1) * rows)

    def halves(self, i):
        rows = self.grad.shape[2] // 2
        return slice(None), slice(i * rows, (i + 1) * rows)

    def cut(self, t, i):
        rows = self.out.shape[1] // 2
        return t, slice(i * rows, (i + 1) * rows)

    def along(self):
        self.steps = [self.link.send(self.total.at[1], self.moved, self.place.partner())]

    def close(self):
        arrive(self.steps)
        self.done[...] = (self.total[0].astype(F32) + self.moved[...].astype(F32)).astype(BF)


class HiddenFirst(Quarters):
    def cross(self):
        self.step = self.link.send(self.grad.at[1], self.moved, self.place.partner())

    def send(self):
        self.step.wait_recv()
        for t in range(self.place.dims["share"]):
            value = self.grad[0, t].astype(F32) + self.moved[t].astype(F32)
            self.grad[0, t] = value.astype(BF)
        self.total = self.done
        super().send()

    def piece(self, t, i):
        rows = self.grad.shape[2] // 2
        return 0, t, slice(i * rows, (i + 1) * rows)

    def halves(self, i):
        rows = self.grad.shape[2] // 2
        return slice(i * rows, (i + 1) * rows)

    cut = Hidden.cut

    def along(self):
        pass

    def close(self):
        pass


class Columns(Quarters):
    def piece(self, t, i):
        blocks = self.grad.shape[1] // 2
        return slice(None), slice(i * blocks, (i + 1) * blocks), t

    def halves(self, i):
        blocks = self.grad.shape[1] // 2
        return slice(None), slice(i * blocks, (i + 1) * blocks)

    def cut(self, t, i):
        cols = self.out.shape[3] // 2
        return t, slice(None), slice(None), slice(i * cols, (i + 1) * cols)

    def along(self):
        place = self.place
        copies = []
        for d in range(1, place.dims["seq"]):
            target = place.seq_shift(d)
            copies.append((self.total.at[:, target], self.moved.at[place.me], {"seq": target}))
        self.steps = [self.link.batch(copies, self.moved.at[0 : place.dims["seq"] - 1])]
        self.own = self.link.local(self.total.at[:, place.me], self.moved.at[place.me])

    def close(self):
        arrive(self.steps)
        self.own.wait()
        dims = self.place.dims
        group, width = dims["group"], dims["width"]
        for index in range(3):
            for q in range(group):
                value = self.moved[q, index].astype(F32)
                for half in range(1, dims["items_dev"]):
                    value = value + self.moved[half * group + q, index].astype(F32)
                self.done[index, :, q * width : (q + 1) * width] = value.astype(BF)


class Rows(Quarters):
    def piece(self, t, i):
        return i, t

    def halves(self, i):
        return i

    def cut(self, t, i):
        cols = self.out.shape[2] // 2
        return t, slice(None), slice(i * cols, (i + 1) * cols)

    def along(self):
        self.moved_done = rows_back(self.link, self.place, self.total, self.moved)

    def close(self):
        self.moved_done()
        value = self.moved[0].astype(F32)
        for half in range(1, self.place.dims["items_dev"]):
            value = value + self.moved[half].astype(F32)
        self.done[...] = value.astype(BF)


class Stage:
    def __init__(self, sems, place, part, bufs, mid, spread, before):
        self.link, self.place, self.mid, self.spread = Link(*sems), place, mid, spread
        self.before = before
        self.reduce = Reduce(self.link, place, part, bufs)
        self.started, self.waits = {}, {}

    def start(self, k):
        self.reduce.start(k, k)

    def middle(self, k):
        self.reduce.middle(k, k)

    def end(self, k):
        place, spread = self.place, self.spread
        spread[k, place.c, place.b1, place.b0] = self.mid(k, self.reduce.end(k))
        self.started[k] = spread_start(self.link, place, spread, k)

    def forward(self, k):
        self.waits[k] = spread_end(self.link, self.place, self.spread, k, self.started[k])

    def arrive(self, k):
        arrive(self.waits[k])

    def release(self, k):
        done = (self.reduce.zero[k], self.reduce.one[k])
        for copy in done:
            copy.wait_send()
        late = {id(copy) for copy in done}
        self.link.open = [copy for copy in self.link.open if id(copy) not in late]


def stage_steps(stage, compute, flight=None, ended=None, after=None):
    before = stage.before
    compute(0, (lambda: before.forward(1)) if before else (lambda: None))
    stage.start(0)
    compute(1, lambda: None)
    stage.start(1)
    if before:
        before.link.finish()
    stage.middle(0)
    stage.middle(1)
    if flight:
        flight()
    stage.end(0)
    stage.end(1)
    if ended:
        ended()
    stage.forward(0)
    if after:
        after()


def layer_kernel(dims, names, *refs):
    b = Box(names, refs)
    b.grad_third, b.grad_r2, b.grad_r1, b.gc1_all = b.first, b.second, b.first, b.gy_all
    place = Place(dims)
    sems = b.send_sems, b.recv_sems
    link = Link(*sems, dims["chain"])
    width, block, items_dev = dims["width"], dims["block"], dims["items_dev"]
    h, t, q_place = place.h, place.t, place.q
    c, b1, b0 = place.c, place.b1, place.b0
    partner = place.partner()
    wr = b.w_sq.shape[0] // dims["share"]
    model = dims["model"]
    total_dec, total_mem = dims["total_dec"], dims["total_mem"]
    rb = b.dec.shape[1]

    def rows_of(ref, cols=model):
        return ref[...].reshape(-1, ref.shape[-1])[:, :cols]

    def chunk(ref, k):
        return ref[k].reshape(-1, model)

    half_rows = total_dec // 2

    def span(k):
        return slice(k * half_rows, (k + 1) * half_rows)

    def put(k, value, before=None):
        if before:
            before.release(k)
        b.part[k] = value.astype(BF).reshape(b.part.shape[1:])

    def weight(ref, index):
        return ref[index].reshape(model, width)

    weights = (b.w_sq, b.w_sk, b.w_sv, b.w_so, b.w_ck, b.w_cv, b.w_cq, b.w_co)
    rows_t = pl.ds(pl.multiple_of(t * wr, wr), wr)
    index = link.index()
    for i, w in enumerate(weights):
        pltpu.make_async_copy(w.at[rows_t], b.staged.at[i], b.send_sems.at[index]).start()
    staged = pltpu.make_async_copy(b.staged, b.staged, b.send_sems.at[index])
    own_fin = link.local(b.f_in, b.own_fin)
    own_fout = link.local(b.f_out, b.own_fout)
    greet(place.seq_peers() + place.items_peers())

    swap_x = link.send(b.dec.at[1 - h], b.x_all.at[h, c, b1, b0], partner)
    def share_columns(dst):
        blocks = dims["seq"] // 2
        return Share(
            link, place, lambda t: dst.at[:, t],
            lambda t, i: dst.at[i * blocks : (i + 1) * blocks, t],
        )

    def share_rows(dst):
        return Share(link, place, lambda t: dst.at[:, t], lambda t, i: dst.at[i, t])

    def share_hidden(dst):
        rows = dst.shape[1] // 2
        return Share(
            link, place, lambda t: dst.at[t], lambda t, i: dst.at[t, i * rows : (i + 1) * rows]
        )

    def join_cells():
        mb = b.cells.shape[1]
        same = lax.broadcasted_iota(jnp.int32, (mb, mb), 0) == lax.broadcasted_iota(
            jnp.int32, (mb, mb), 1
        )
        for k in range(items_dev):
            flags = (b.cells[k : k + 1] == 1).astype(F32)
            column = jnp.sum(jnp.where(same, flags, 0.0), axis=1, keepdims=True)
            b.mem_cells[k, :, :model] = b.mem[k]
            b.mem_cells[k, :, model:] = jnp.broadcast_to(column, (mb, 128)).astype(BF)

    b.x_all[h, c, b1, b0] = b.dec[h]
    first_x = spread_start(link, place, b.x_all, h)
    staged.wait()
    steps, own_self = columns_out(link, place, b.staged.at[0:3], b.o_self, width)
    waits = spread_end(link, place, b.x_all, h, first_x)
    swap_x.wait_recv()
    second_x = spread_start(link, place, b.x_all, 1 - h)
    so_arrived, so_sent = rows_out(link, place, b.staged.at[3], b.o_so)
    steps.wait_recv()
    own_self.wait()
    self_share = [share_columns(b.o_self.at[i]) for i in range(3)]
    waits += spread_end(link, place, b.x_all, 1 - h, second_x)
    so_arrived()
    so_share = share_rows(b.o_so)
    cross_steps, own_cross = columns_out(link, place, b.staged.at[4:7], b.o_cross, width)
    co_arrived, co_sent = rows_out(link, place, b.staged.at[7], b.o_co)
    join_cells()
    b.m_all[h, c, b1, b0] = b.mem_cells[h]
    swap_m = link.send(b.mem_cells.at[1 - h], b.m_all.at[h, c, b1, b0], partner)
    first_m = spread_start(link, place, b.m_all, h)
    own_fin.wait()
    own_fout.wait()
    fr, gr = b.o_fin.shape[1], b.o_fout.shape[1]
    step_fin = link.send(b.own_fin.at[pl.ds(pl.multiple_of(t * fr, fr), fr)], b.o_fin.at[t], partner)
    step_fout = link.send(
        b.own_fout.at[pl.ds(pl.multiple_of(t * gr, gr), gr)], b.o_fout.at[t], partner
    )
    for share in self_share:
        share.forward()

    arrive(waits)
    rows = rows_of(b.x_all)
    for index, dst in enumerate((b.sq, b.sk, b.sv)):
        self_share[index].wait()
        dst[...] = nn(rows, weight(b.o_self, index)).astype(BF)
    so_share.forward()
    cross_steps.wait_recv()
    own_cross.wait()
    cross_share = [share_columns(b.o_cross.at[i]) for i in range(3)]
    co_arrived()
    co_share = share_rows(b.o_co)
    mem_waits = spread_end(link, place, b.m_all, h, first_m)
    swap_m.wait_recv()
    second_m = spread_start(link, place, b.m_all, 1 - h)
    length, mem_length = b.dec_len[h], b.mem_len[h]

    def self_ok(start, stop):
        keys = lax.broadcasted_iota(jnp.int32, (stop, block), 0)
        spots = lax.broadcasted_iota(jnp.int32, (stop, block), 1) + start
        return (keys <= spots) & (keys < length)

    bufs = [b.recv0, b.send1, b.recv1, b.keep1]
    if dims["bits"] == 3:
        bufs += [b.send2, b.recv2]

    def forward(index, res, summed, out):
        def mid(k, total):
            value = res(k) + total
            summed[k] = value
            normed, _ = moments(value)
            result = normed * b.gain[index : index + 1] + b.bias[index : index + 1]
            out[k] = result
            return result.astype(BF)

        return mid

    def self_part(k, pump):
        attend(
            b.sq, b.sk, b.sv, self_ok, b.sp, b.smix, True, block,
            k * half_rows, (k + 1) * half_rows, pump,
        )
        if k == 0:
            so_share.wait()
        put(k, nn(b.smix[span(k)], rows_of(b.o_so)))

    def memory_part():
        arrive(mem_waits)
        mems = rows_of(b.m_all)
        cross_share[0].wait()
        b.ck[...] = nn(mems, weight(b.o_cross, 0)).astype(BF)
        cross_share[1].wait()
        b.cv[...] = nn(mems, weight(b.o_cross, 1)).astype(BF)
        spots = lax.broadcasted_iota(jnp.int32, (total_mem, 128), 0)
        cells = b.m_all[...].reshape(-1, b.m_all.shape[-1])[:, model:].astype(F32)
        b.keep[...] = ((spots < mem_length) & ((cells > 0.5) | (spots == 0))).astype(F32)

    stage = Stage(
        sems, place, b.part, bufs,
        forward(0, lambda k: b.x_all[k, c, b1, b0].astype(F32), b.sum_one, b.first), b.first_all, None,
    )
    def cross_weights():
        mem_waits.extend(spread_end(link, place, b.m_all, 1 - h, second_m))
        for share in cross_share + [co_share]:
            share.forward()
        step_fin.wait_recv()
        ffn_share.append(share_hidden(b.o_fin))
        step_fout.wait_recv()
        ffn_share.append(share_hidden(b.o_fout))

    ffn_share = []
    stage_steps(stage, self_part, after=cross_weights)
    memory_part()
    b.c_own[h] = b.cot[h]
    swap_c = link.send(b.cot.at[1 - h], b.c_own.at[h], partner)

    def cross_part(k, pump):
        last.arrive(k)
        if k == 0:
            cross_share[2].wait()
        b.cq[span(k)] = nn(chunk(b.first_all, k), weight(b.o_cross, 2)).astype(BF)
        attend(
            b.cq, b.ck, b.cv, lambda start, stop: b.keep[:, 0:1] > 0.5, b.cp, b.cmix, False, block,
            k * half_rows, (k + 1) * half_rows, pump,
        )
        if k == 0:
            co_share.wait()
        put(k, nn(b.cmix[span(k)], rows_of(b.o_co)), last)

    last = stage
    stage = Stage(
        sems, place, b.part, bufs, forward(1, lambda k: b.first[k], b.sum_two, b.second),
        b.second_all, last,
    )
    def ffn_weights():
        for share in ffn_share:
            share.forward()

    stage_steps(stage, cross_part, ffn_weights)

    w_ins = (lambda: b.own_fin[...], lambda: b.o_fin[...].reshape(model, -1))
    w_outs = (lambda: b.own_fout[...], lambda: b.o_fout[...].reshape(-1, model))
    hidden = b.own_fin.shape[1]
    last_second = stage

    def ffn_part(k, pump):
        last_second.arrive(k)
        if k == 0:
            ffn_share[0].wait()
        rows = chunk(b.second_all, k)
        for index in range(2):
            if index:
                pump()
            pre = nn(rows, w_ins[index]())
            cdf = 0.5 * (1.0 + lax.erf(pre * (0.5**0.5)))
            cols = slice(index * hidden, (index + 1) * hidden)
            b.act[span(k), cols] = (pre * cdf).astype(BF)
            b.slope[span(k), cols] = (
                cdf + pre * (jnp.exp(-0.5 * pre * pre) * 0.3989422804014327)
            ).astype(BF)
        if k == 0:
            ffn_share[1].wait()
        total = nn(b.act[span(k), :hidden], w_outs[0]())
        put(k, total + nn(b.act[span(k), hidden:], w_outs[1]()), last_second)

    swap_c.wait_recv()

    def add_sums(index, k, normed, grad):
        new = (jnp.sum(grad * normed, axis=0, keepdims=True), jnp.sum(grad, axis=0, keepdims=True))
        for row, value in zip((index, 3 + index), new):
            b.sums[row : row + 1] = value if k == 0 else b.sums[row : row + 1] + value

    def turn(k, total):
        gain = b.gain[2:3]
        normed, inv = moments(b.second[k] + total)
        spots = lax.broadcasted_iota(jnp.int32, (rb, model), 0) + (k * dims["group"] + q_place) * rb
        kept = spots < length
        b.layer[k] = jnp.where(kept, normed * gain + b.bias[2:3], 0.0).astype(BF)
        grad = jnp.where(kept, b.c_own[k].astype(F32), 0.0)
        add_sums(2, k, normed, grad)
        result = norm_back(normed, inv, gain, grad)
        b.grad_third[k] = result
        return result.astype(BF)

    stage = Stage(sems, place, b.part, bufs, turn, b.gy_all, last_second)
    stage_steps(stage, ffn_part)

    last_turn = stage

    way_fout = HiddenFirst(
        link, place, b.g_fout,
        ("q_fout", "t_fout", "u_fout", dims["lines"] and "l_fout", "", "z_fout", "d_fout", "r_fout"), b
    )
    def out_grads():
        grad = rows_of(b.gy_all)
        for index in range(2):
            cols = slice(index * hidden, (index + 1) * hidden)
            value = tn(b.act[:, cols], grad)
            b.g_fout[index] = value.astype(BF).reshape(b.g_fout.shape[1:])
        way_fout.cross()

    def ffn_back(k, pump):
        last_turn.arrive(k)
        if k == 1:
            out_grads()
        grad = chunk(b.gy_all, k)
        total = None
        for index in range(2):
            if index:
                pump()
            cols = slice(index * hidden, (index + 1) * hidden)
            grad_pre = (nt(grad, w_outs[index]()) * b.slope[span(k), cols].astype(F32)).astype(BF)
            b.slope[span(k), cols] = grad_pre
            term = nt(grad_pre, w_ins[index]())
            total = term if total is None else total + term
        put(k, total, last_turn)

    way_fin = Hidden(
        link, place, b.g_fin, ("q_fin", "t_fin", "u_fin", dims["lines"] and "l_fin", "s_fin", "z_fin", "d_fin", "r_fin"), b
    )
    way_cross = Columns(
        link, place, b.g_cross, ("q_cross", "t_cross", "u_cross", dims["lines"] and "l_cross", "s_cross", "z_cross", "d_cross", "r_cross"), b
    )
    way_self = Columns(
        link, place, b.g_self, ("q_self", "t_self", "u_self", dims["lines"] and "l_self", "s_self", "z_self", "d_self", "r_self"), b
    )
    way_co = Rows(
        link, place, b.g_co, ("q_co", "t_co", "u_co", dims["lines"] and "l_co", "s_co", "z_co", "d_co", "r_co"), b
    )
    way_so = Rows(
        link, place, b.g_so, ("q_so", "t_so", "u_so", dims["lines"] and "l_so", "s_so", "z_so", "d_so", "r_so"), b
    )

    def backward(index, res, summed, out):
        def mid(k, total):
            normed, inv = moments(summed[k])
            grad = res[k] + total
            add_sums(index, k, normed, grad)
            result = norm_back(normed, inv, b.gain[index : index + 1], grad)
            out[k] = result
            return result.astype(BF)

        return mid

    def in_grads():
        rows = rows_of(b.second_all)
        for index in range(2):
            cols = slice(index * hidden, (index + 1) * hidden)
            value = tn(rows, b.slope[:, cols])
            b.g_fin[index] = value.astype(BF).reshape(b.g_fin.shape[1:])
        way_fin.send()

    stage = Stage(
        sems, place, b.part, bufs, backward(1, b.grad_third, b.sum_two, b.grad_r2), b.gc2_all,
        last_turn,
    )
    stage_steps(stage, ffn_back, in_grads)

    last_back = stage

    def cross_back(k, pump):
        last_back.arrive(k)
        b.dmix[span(k)] = nt(chunk(b.gc2_all, k), rows_of(b.o_co)).astype(BF)
        attend_back(
            b.cq, b.ck, b.cv, b.cp, b.dmix, b.dq, b.sum_dk, b.sum_dv, False, block,
            k * half_rows, (k + 1) * half_rows, pump,
        )
        put(k, nt(b.dq[span(k)], weight(b.o_cross, 2)), last_back)
        if k == 1:
            way_fin.turn()

    def cross_grads():
        mems = rows_of(b.m_all)
        shape = b.g_cross.shape[1:]
        b.dck[...] = (b.sum_dk[:total_mem] * SCALE).astype(BF)
        b.dcv[...] = b.sum_dv[:total_mem].astype(BF)
        b.g_cross[0] = tn(rows_of(b.first_all), b.dq[...]).astype(BF).reshape(shape)
        b.g_cross[1] = tn(mems, b.dck[...]).astype(BF).reshape(shape)
        b.g_cross[2] = tn(mems, b.dcv[...]).astype(BF).reshape(shape)
        way_cross.send()
        b.g_co[...] = tn(b.cmix[...], rows_of(b.gc2_all)).astype(BF).reshape(b.g_co.shape)
        way_co.send()

    def part_mem():
        value = nt(b.dck[...], weight(b.o_cross, 0)) + nt(b.dcv[...], weight(b.o_cross, 1))
        b.part_m[...] = value.astype(BF).reshape(b.part_m.shape)

    stage = Stage(
        sems, place, b.part, bufs, backward(0, b.grad_r2, b.sum_one, b.grad_r1), b.gc1_all,
        last_back,
    )
    stage_steps(stage, cross_back, cross_grads, part_mem)

    for k in range(2):
        stage.arrive(k)
        pump = (lambda: stage.forward(1)) if k == 0 else (lambda: None)
        b.dmix[span(k)] = nt(chunk(b.gc1_all, k), rows_of(b.o_so)).astype(BF)
        attend_back(
            b.sq, b.sk, b.sv, b.sp, b.dmix, b.dq, b.sum_dk, b.sum_dv, True, block,
            k * half_rows, (k + 1) * half_rows, pump,
        )
    b.dsk[...] = (b.sum_dk[...] * SCALE).astype(BF)
    b.dsv[...] = b.sum_dv[...].astype(BF)
    for k in range(2):
        total = nt(b.dq[span(k)], weight(b.o_self, 0)) + nt(b.dsk[span(k)], weight(b.o_self, 1))
        put(k, total + nt(b.dsv[span(k)], weight(b.o_self, 2)), stage)
    stage.link.finish()
    chain = Link(*sems)
    ks = (1 - h, h)
    red_x = Reduce(chain, place, b.part, bufs)
    mem_bufs = [b.recv0_m, b.send1_m, b.recv1_m, b.keep1_m]
    if dims["bits"] == 3:
        mem_bufs += [b.send2_m, b.recv2_m]
    red_m = Reduce(link, place, b.part_m, mem_bufs)
    for red in (red_x, red_m):
        for index in range(2):
            red.start(index, ks[index])
    rows = rows_of(b.x_all)
    shape = b.g_self.shape[1:]
    b.g_self[0] = tn(rows, b.dq[...]).astype(BF).reshape(shape)
    b.g_self[1] = tn(rows, b.dsk[...]).astype(BF).reshape(shape)
    b.g_self[2] = tn(rows, b.dsv[...]).astype(BF).reshape(shape)
    way_self.send()
    b.g_so[...] = tn(b.smix[...], rows_of(b.gc1_all)).astype(BF).reshape(b.g_so.shape)
    way_so.send()
    way_cross.turn()
    way_co.turn()
    way_fin.add()
    for red in (red_x, red_m):
        for index in range(2):
            red.middle(index, ks[index])
    copies = []
    for d in range(1, dims["seq"]):
        copies.append((b.sums, b.sums_seq.at[d - 1], {"seq": place.seq_shift(d)}))
    seq_sums = link.batch(copies, b.sums_seq)
    way_fout.send()
    swap_l = link.send(b.layer.at[1 - h], b.layer_out.at[h], partner)
    b.layer_out[h] = b.layer[h]
    b.send_x[...] = (red_x.end(0) + b.grad_r1[1 - h]).astype(BF)
    swap_x = link.send(b.send_x, b.recv_x, partner)
    b.grad_dec[h] = red_x.end(1) + b.grad_r1[h]
    b.send_m[...] = red_m.end(0).astype(BF)
    swap_m = link.send(b.send_m, b.recv_m, partner)
    b.grad_mem[h] = red_m.end(1)
    way_self.turn()
    way_so.turn()
    way_fout.turn()
    way_cross.add()
    way_co.add()
    way_fin.gather()
    seq_sums.wait_recv()
    value = b.sums[...]
    for d in range(1, dims["seq"]):
        value = value + b.sums_seq[d - 1]
    b.sums_line[...] = value
    copies = []
    for e in range(1, dims["items"]):
        target = {"items": lax.rem(place.it + e, dims["items"])}
        copies.append((b.sums_line, b.sums_items.at[e - 1], target))
    item_sums = link.batch(copies, b.sums_items)
    swap_x.wait_recv()
    b.grad_dec[1 - h] = b.recv_x[...].astype(F32)
    swap_m.wait_recv()
    b.grad_mem[1 - h] = b.recv_m[...].astype(F32)
    swap_l.wait_recv()
    way_self.add()
    way_so.add()
    way_fout.add()
    way_fout.gather()
    way_cross.gather()
    way_co.gather()
    way_fin.forward()
    way_fout.forward()
    item_sums.wait_recv()
    value = b.sums_line[...]
    for e in range(1, dims["items"]):
        value = value + b.sums_items[e - 1]
    b.sums_out[...] = value
    way_cross.forward()
    way_co.forward()
    way_self.gather()
    way_so.gather()
    way_self.forward()
    way_so.forward()
    for way in (way_fout, way_fin, way_cross, way_co, way_self, way_so):
        way.finish()
    so_sent()
    co_sent()
    chain.finish()
    link.finish()


def shape(dims, dtype):
    return jax.ShapeDtypeStruct(tuple(dims), dtype)


def outputs_kernel(layer, dec, mem, cross, own, co, so, fin, fout, sums, *outs):
    o_layer, o_dec, o_mem = outs[:3]
    o_layer[...] = layer[...]
    o_dec[...] = dec[...]
    o_mem[...] = mem[...]
    for index in range(3):
        outs[3 + index][...] = own[0, index].astype(F32)
        outs[7 + index][...] = cross[0, index].astype(F32)
    outs[6][...] = so[0].astype(F32)
    outs[10][...] = co[0].astype(F32)
    outs[11][...] = fin[0].astype(F32)
    outs[12][...] = fout[0].astype(F32)
    outs[13][...] = sums[0:3]
    outs[14][...] = sums[3:6]


def shards(
    mesh, dec_in, memory, dec_len, mem_len, cell_mask, self_query, self_key, self_value, self_out,
    cross_query, cross_key, cross_value, cross_out, ffn_in, ffn_out, norm_gain, norm_bias, cotangent,
):
    items_dev, rb, model = dec_in.shape
    mb = memory.shape[1]
    seq, items = mesh.shape["seq"], mesh.shape["items"]
    group = seq // items_dev
    share = 4
    bits = group.bit_length() - 1
    chips = group // 4
    width = model // group
    total_dec, total_mem = rb * seq, mb * seq
    heads = width // HEAD_DIM
    hidden = ffn_in.shape[1]
    wr = self_query.shape[0] // share
    fr, gr = model // share, hidden // share
    lines = items // share - 1
    dims = {
        "items_dev": items_dev, "items": items, "seq": seq, "group": group, "share": share,
        "bits": bits, "chips": chips, "width": width, "model": model, "block": 256,
        "total_dec": total_dec, "total_mem": total_mem, "lines": lines,
        "chain": 12 + 2 * (bits - 2),
    }
    ins = [
        ("dec", dec_in, VM), ("mem", memory, VM), ("cells", cell_mask, VM), ("cot", cotangent, VM),
        ("dec_len", dec_len, SM), ("mem_len", mem_len, SM),
        ("w_sq", self_query, HBM), ("w_sk", self_key, HBM), ("w_sv", self_value, HBM),
        ("w_so", self_out, HBM), ("w_cq", cross_query, HBM), ("w_ck", cross_key, HBM),
        ("w_cv", cross_value, HBM), ("w_co", cross_out, HBM), ("f_in", ffn_in, HBM),
        ("f_out", ffn_out, HBM), ("gain", norm_gain, VM), ("bias", norm_bias, VM),
    ]
    own, own_m = (items_dev, rb, model), (items_dev, mb, model)
    grid = (items_dev, chips, 2, 2)
    outs = [
        ("layer_out", own, BF, VM), ("grad_dec", own, F32, VM), ("grad_mem", own_m, F32, VM),
        ("sums_out", (8, model), F32, VM),
        ("r_cross", (share, 3, wr, model), BF, HBM), ("r_self", (share, 3, wr, model), BF, HBM),
        ("r_co", (share, wr, model), BF, HBM), ("r_so", (share, wr, model), BF, HBM),
        ("r_fin", (share, fr, hidden), BF, HBM), ("r_fout", (share, gr, model), BF, HBM),
    ]
    cols = (3, seq, share, wr, width)
    scratch = [
        ("x_all", grid + (rb, model), BF), ("m_all", grid + (mb, model + 128), BF),
        ("mem_cells", (items_dev, mb, model + 128), BF), ("c_own", own, BF), ("staged", (8, wr, model), BF),
        ("own_fin", (model, hidden), BF), ("own_fout", (hidden, model), BF),
        ("o_self", cols, BF), ("o_cross", cols, BF),
        ("o_so", (items_dev, share, wr, model), BF), ("o_co", (items_dev, share, wr, model), BF),
        ("o_fin", (share, fr, hidden), BF), ("o_fout", (share, gr, model), BF),
        ("sq", (total_dec, width), BF), ("sk", (total_dec, width), BF), ("sv", (total_dec, width), BF),
        ("cq", (total_dec, width), BF), ("ck", (total_mem, width), BF), ("cv", (total_mem, width), BF),
        ("sp", (heads, total_dec, total_dec), BF), ("cp", (heads, total_mem, total_dec), BF),
        ("smix", (total_dec, width), BF), ("cmix", (total_dec, width), BF),
        ("keep", (total_mem, 128), F32),
        ("part", grid + (rb, model), BF), ("part_m", grid + (mb, model), BF),
        ("first_all", grid + (rb, model), BF), ("second_all", grid + (rb, model), BF),
        ("gy_all", grid + (rb, model), BF), ("gc2_all", grid + (rb, model), BF),
        ("sum_one", own, F32), ("sum_two", own, F32), ("first", own, F32), ("second", own, F32),
        ("layer", own, BF), ("sum_dk", (total_dec, width), F32), ("sum_dv", (total_dec, width), F32),
        ("act", (total_dec, 2 * hidden), BF), ("slope", (total_dec, 2 * hidden), BF),
        ("dmix", (total_dec, width), BF), ("dq", (total_dec, width), BF),
        ("dsk", (total_dec, width), BF), ("dsv", (total_dec, width), BF),
        ("dck", (total_mem, width), BF), ("dcv", (total_mem, width), BF),
        ("send_x", (rb, model), BF), ("recv_x", (rb, model), BF),
        ("send_m", (mb, model), BF), ("recv_m", (mb, model), BF),
        ("sums", (8, model), F32), ("sums_line", (8, model), F32),
        ("sums_seq", (seq - 1, 8, model), F32), ("sums_items", (items - 1, 8, model), F32),
    ]
    for name, rows in (("", rb), ("_m", mb)):
        scratch += [
            ("recv0" + name, (items_dev, chips, 2, rows, model), BF),
            ("send1" + name, (items_dev, chips, rows, model), BF),
            ("recv1" + name, (items_dev, chips, rows, model), BF),
            ("keep1" + name, (items_dev, chips, rows, model), F32),
        ]
        if bits == 3:
            scratch += [
                ("send2" + name, (items_dev, rows, model), BF),
                ("recv2" + name, (items_dev, rows, model), BF),
            ]
    for name, grad, quarter, piece, moved, done in (
        ("fin", (2, share, fr, hidden), (2, fr, hidden), (2, fr // 2, hidden), (fr, hidden),
         (fr, hidden)),
        ("fout", (2, share, gr, model), (gr, model), (gr // 2, model), (share, gr, model), (gr, model)),
        ("cross", cols, (3, seq, wr, width), (3, seq // 2, wr, width), (seq, 3, wr, width),
         (3, wr, model)),
        ("self", cols, (3, seq, wr, width), (3, seq // 2, wr, width), (seq, 3, wr, width),
         (3, wr, model)),
        ("co", (items_dev, share, wr, model), (items_dev, wr, model), (wr, model),
         (items_dev, wr, model), (wr, model)),
        ("so", (items_dev, share, wr, model), (items_dev, wr, model), (wr, model),
         (items_dev, wr, model), (wr, model)),
    ):
        scratch += [
            ("g_" + name, grad, BF), ("q_" + name, (2, 2) + piece, BF), ("t_" + name, (2,) + piece, BF),
            ("u_" + name, (2,) + piece, BF), ("z_" + name, moved, BF), ("d_" + name, done, BF),
        ]
        if name != "fout":
            scratch.append(("s_" + name, quarter, BF))
        if lines:
            scratch.append(("l_" + name, (lines,) + quarter, BF))
    copies = dims["chain"] + 145 + 12 * (bits - 2)
    names = [x[0] for x in ins + outs + scratch] + ["send_sems", "recv_sems"]
    results = pl.pallas_call(
        functools.partial(layer_kernel, dims, names),
        name="layer",
        out_shape=[shape(x[1], x[2]) for x in outs],
        in_specs=[x[2] for x in ins],
        out_specs=[x[3] for x in outs],
        scratch_shapes=[pltpu.VMEM(x[1], x[2]) for x in scratch]
        + [pltpu.SemaphoreType.DMA((copies,)), pltpu.SemaphoreType.DMA((copies,))],
        compiler_params=pltpu.CompilerParams(
            collective_id=0, has_side_effects=True, vmem_limit_bytes=VMEM_BYTES
        ),
    )(*[x[1] for x in ins])
    layer_out, grad_dec, grad_memory, sums, r_cross, r_self, r_co, r_so, r_fin, r_fout = results
    tok, mem_rows = items_dev * rb, items_dev * mb
    pieces = (
        ((tok, model), (tok // share, model), BF), ((tok, model), (tok // share, model), F32),
        ((mem_rows, model), (mem_rows // share, model), F32),
    )
    heads_in = [
        pl.BlockSpec((1, 3, wr, model), lambda i: (i, 0, 0, 0)),
        pl.BlockSpec((1, 3, wr, model), lambda i: (i, 0, 0, 0)),
        pl.BlockSpec((1, wr, model), lambda i: (i, 0, 0)),
        pl.BlockSpec((1, wr, model), lambda i: (i, 0, 0)),
        pl.BlockSpec((1, fr, hidden), lambda i: (i, 0, 0)),
        pl.BlockSpec((1, gr, model), lambda i: (i, 0, 0)),
        pl.BlockSpec((8, model), lambda i: (0, 0)),
    ]
    row_specs = [pl.BlockSpec(x[1], lambda i: (i, 0)) for x in pieces]
    square = (share * wr, model)
    outs = pl.pallas_call(
        outputs_kernel,
        name="outputs",
        grid=(share,),
        in_specs=row_specs + heads_in,
        out_specs=row_specs
        + [pl.BlockSpec((wr, model), lambda i: (i, 0))] * 8
        + [pl.BlockSpec((fr, hidden), lambda i: (i, 0)), pl.BlockSpec((gr, model), lambda i: (i, 0))]
        + [pl.BlockSpec((3, model), lambda i: (0, 0))] * 2,
        out_shape=[shape(x[0], x[2]) for x in pieces]
        + [shape(square, F32)] * 8
        + [shape((model, hidden), F32), shape((hidden, model), F32)]
        + [shape((3, model), F32)] * 2,
        compiler_params=pltpu.CompilerParams(vmem_limit_bytes=VMEM_BYTES),
    )(
        layer_out.reshape(tok, model), grad_dec.reshape(tok, model),
        grad_memory.reshape(mem_rows, model), r_cross, r_self, r_co, r_so, r_fin, r_fout, sums,
    )
    return (
        outs[0].reshape(own), outs[1].reshape(own), outs[2].reshape(own_m), *outs[3:],
    )


def solution(mesh):
    rows = P("seq", None)
    tokens = P("items", "seq", None)
    placed = (
        (tokens, tokens, P("items"), P("items"), P("items", "seq"))
        + (rows,) * 8
        + (P(None, "seq"), rows, P(), P(), tokens)
    )
    return jax.shard_map(
        functools.partial(shards, mesh),
        mesh=mesh,
        in_specs=placed,
        out_specs=(tokens,) * 3 + (rows,) * 8 + (P(None, "seq"), rows, P(), P()),
        check_vma=False,
    )
```

```python
import functools

import jax
import jax.numpy as jnp
from jax import lax
from jax.experimental import pallas as pl
from jax.experimental.pallas import tpu as pltpu
from jax.sharding import PartitionSpec as P

HEAD_DIM = 64
EPS = 1e-05
NEG = -1e30
SCALE = HEAD_DIM ** (-0.5)
BF = jnp.bfloat16
F32 = jnp.float32
VMEM_BYTES = 63 * 1024 * 1024
MESH = pl.DeviceIdType.MESH
VM = pl.BlockSpec(memory_space=pltpu.VMEM)
HBM = pl.BlockSpec(memory_space=pl.ANY)
SM = pl.BlockSpec(memory_space=pltpu.SMEM)


def nn(left, right):
    return lax.dot_general(left, right, (((1,), (0,)), ((), ())), preferred_element_type=F32)


def nt(left, right):
    return lax.dot_general(left, right, (((1,), (1,)), ((), ())), preferred_element_type=F32)


def tn(left, right):
    return lax.dot_general(left, right, (((0,), (0,)), ((), ())), preferred_element_type=F32)


class Link:
    def __init__(self, send_sems, recv_sems, first=0):
        self.send_sems, self.recv_sems, self.count, self.open = send_sems, recv_sems, first, []

    def index(self):
        self.count += 1
        return self.count - 1

    def make(self, src, dst, device, index):
        return pltpu.make_async_remote_copy(
            src_ref=src,
            dst_ref=dst,
            send_sem=self.send_sems.at[index],
            recv_sem=self.recv_sems.at[index],
            device_id=device,
            device_id_type=MESH,
        )

    def send(self, src, dst, device):
        copy = self.make(src, dst, device, self.index())
        copy.start()
        self.open.append(copy)
        return copy

    def batch(self, copies, whole):
        index = self.index()
        for copy in copies:
            self.make(*copy, index).start()
        wait = self.make(whole, whole, copies[0][2], index)
        self.open.append(wait)
        return wait

    def settle(self, copy):
        copy.wait_send()
        self.open = [other for other in self.open if other is not copy]

    def local(self, src, dst):
        copy = pltpu.make_async_copy(src, dst, self.send_sems.at[self.index()])
        copy.start()
        return copy

    def finish(self, kept=()):
        late = {id(copy) for copy in kept}
        for copy in self.open:
            if id(copy) not in late:
                copy.wait_send()
        self.open = [copy for copy in self.open if id(copy) in late]


def greet(devices):
    barrier = pltpu.get_barrier_semaphore()
    for device in devices:
        pl.semaphore_signal(barrier, inc=1, device_id=device, device_id_type=MESH)
    pl.semaphore_wait(barrier, len(devices))


class Place:
    def __init__(self, dims):
        self.dims = dims
        group, share = dims["group"], dims["share"]
        self.me = lax.axis_index("seq")
        self.h = self.me // group
        self.q = self.me % group
        self.b0 = self.q % 2
        self.b1 = (self.q // 2) % 2
        self.c = self.q // 4
        self.it = lax.axis_index("items")
        self.base = (self.it // share) * share
        self.t = self.it % share
        x, y = self.t % 2, self.t // 2
        self.tx, self.ty, self.txy = y * 2 + 1 - x, (1 - y) * 2 + x, (1 - y) * 2 + 1 - x

    def across(self, bit):
        value = (self.q // (1 << bit)) % 2
        return {"seq": self.me + (1 - 2 * value) * (1 << bit)}

    def partner(self):
        return {"seq": (1 - self.h) * self.dims["group"] + self.q}

    def seq_shift(self, d):
        return lax.rem(self.me + d, self.dims["seq"])

    def line(self, t):
        return {"items": self.base + t}

    def seq_peers(self):
        return [{"seq": self.seq_shift(d)} for d in range(1, self.dims["seq"])]

    def items_peers(self):
        count = self.dims["items"]
        return [{"items": lax.rem(self.it + e, count)} for e in range(1, count)]


def spread_start(link, place, out, k):
    bits = place.dims["bits"]
    c, b1, b0 = place.c, place.b1, place.b0
    if bits == 3:
        step = link.send(out.at[k, c, b1, b0], out.at[k, c, b1, b0], place.across(2))
        step.wait_recv()
    waits = []
    high = link.send(out.at[k, :, b1, b0], out.at[k, :, b1, b0], place.across(1))
    waits.append(link.send(out.at[k, :, b1, b0], out.at[k, :, b1, b0], place.across(0)))
    return high, waits


def spread_end(link, place, out, k, started):
    high, waits = started
    b1, b0 = place.b1, place.b0
    high.wait_recv()
    waits.append(link.send(out.at[k, :, 1 - b1, b0], out.at[k, :, 1 - b1, b0], place.across(0)))
    return waits


def columns_out(link, place, src, dst, width):
    seq, group = place.dims["seq"], place.dims["group"]
    copies = []
    for d in range(1, seq):
        target = place.seq_shift(d)
        cols = pl.ds(pl.multiple_of(lax.rem(target, group) * width, width), width)
        copies.append((src.at[:, :, cols], dst.at[:, place.me, place.t], {"seq": target}))
    steps = link.batch(copies, dst.at[:, 0 : seq - 1, place.t])
    cols = pl.ds(pl.multiple_of(place.q * width, width), width)
    return steps, link.local(src.at[:, :, cols], dst.at[:, place.me, place.t])


def rows_out(link, place, src, dst):
    dims, me = place.dims, place.me
    slot = lax.rem(me, dims["items_dev"])
    base = link.count
    link.count += dims["items_dev"] + 1
    copies = []
    for half in range(dims["items_dev"]):
        target = half * dims["group"] + me // dims["items_dev"]
        copy = pltpu.make_async_remote_copy(
            src_ref=src,
            dst_ref=dst.at[slot, place.t],
            send_sem=link.send_sems.at[base + half],
            recv_sem=link.recv_sems.at[base + slot],
            device_id={"seq": target},
            device_id_type=MESH,
        )
        copies.append((target != me, copy))
        pl.when(target != me)(copy.start)
    own = pltpu.make_async_copy(
        src, dst.at[slot, place.t], link.send_sems.at[base + dims["items_dev"]]
    )
    mine = me // dims["items_dev"] == place.q
    pl.when(mine)(own.start)

    def arrived():
        pl.when(mine)(own.wait)
        for block in range(dims["items_dev"]):
            copy = pltpu.make_async_remote_copy(
                src_ref=src,
                dst_ref=dst.at[block, place.t],
                send_sem=link.send_sems.at[base],
                recv_sem=link.recv_sems.at[base + block],
                device_id={"seq": me},
                device_id_type=MESH,
            )
            pl.when(place.q * dims["items_dev"] + block != me)(copy.wait_recv)

    def sent():
        for other, copy in copies:
            pl.when(other)(copy.wait_send)

    return arrived, sent


class Share:
    def __init__(self, link, place, slab, half):
        self.link, self.place, self.half = link, place, half
        t = place.t
        self.from_x = link.send(slab(t), slab(t), place.line(place.tx))
        self.from_y = link.send(slab(t), slab(t), place.line(place.ty))

    def forward(self):
        link, place, half = self.link, self.place, self.half
        self.from_y.wait_recv()
        part = half(place.ty, 0)
        self.steps = [link.send(part, part, place.line(place.tx))]
        self.from_x.wait_recv()
        part = half(place.tx, 1)
        self.steps.append(link.send(part, part, place.line(place.ty)))

    def wait(self):
        arrive(self.steps)


def arrive(steps):
    for step in steps:
        step.wait_recv()


class Reduce:
    def __init__(self, link, place, part, bufs):
        self.link, self.place, self.part, self.bufs = link, place, part, bufs
        self.zero, self.one = {}, {}

    def start(self, index, k):
        place = self.place
        self.zero[index] = self.link.send(
            self.part.at[k, :, :, 1 - place.b0], self.bufs[0].at[index], place.across(0)
        )

    def middle(self, index, k):
        place, part = self.place, self.part
        recv0, send1, recv1, keep1 = self.bufs[:4]
        self.zero[index].wait_recv()
        b1, b0 = place.b1, place.b0
        for c in range(part.shape[1]):
            value = part[k, c, 1 - b1, b0].astype(F32) + recv0[index, c, 1 - b1].astype(F32)
            send1[index, c] = value.astype(BF)
        self.one[index] = self.link.send(send1.at[index], recv1.at[index], place.across(1))
        for c in range(part.shape[1]):
            keep1[index, c] = part[k, c, b1, b0].astype(F32) + recv0[index, c, b1].astype(F32)

    def end(self, index):
        place = self.place
        recv1, keep1 = self.bufs[2:4]
        self.one[index].wait_recv()
        if place.dims["bits"] == 2:
            return keep1[index, 0] + recv1[index, 0].astype(F32)
        send2, recv2 = self.bufs[4:6]
        c = place.c
        send2[index] = (keep1[index, 1 - c] + recv1[index, 1 - c].astype(F32)).astype(BF)
        step = self.link.send(send2.at[index], recv2.at[index], place.across(2))
        kept = keep1[index, c] + recv1[index, c].astype(F32)
        step.wait_recv()
        return kept + recv2[index].astype(F32)


def reduce_bufs(dims, rows):
    items_dev, width, chips = dims["items_dev"], dims["model"], dims["chips"]
    bufs = [
        pltpu.VMEM((items_dev, chips, 2, rows, width), BF),
        pltpu.VMEM((items_dev, chips, rows, width), BF),
        pltpu.VMEM((items_dev, chips, rows, width), BF),
        pltpu.VMEM((items_dev, chips, rows, width), F32),
    ]
    if dims["bits"] == 3:
        bufs += [pltpu.VMEM((items_dev, rows, width), BF) for _ in range(2)]
    return bufs


def moments(value):
    mean = jnp.mean(value, axis=-1, keepdims=True)
    centered = value - mean
    inv = lax.rsqrt(jnp.mean(centered * centered, axis=-1, keepdims=True) + EPS)
    return centered * inv, inv


def norm_back(normed, inv, gain, grad):
    scaled = grad * gain
    mean = jnp.mean(scaled, axis=-1, keepdims=True)
    cross = jnp.mean(scaled * normed, axis=-1, keepdims=True)
    return inv * (scaled - mean - normed * cross)


def rows_back(link, place, src, dst):
    dims, me, h = place.dims, place.me, place.h
    count = dims["items_dev"]
    base = link.count
    link.count += count + 1
    copies = []
    for k in range(count):
        target = place.q * count + k
        copy = pltpu.make_async_remote_copy(
            src_ref=src.at[k],
            dst_ref=dst.at[h],
            send_sem=link.send_sems.at[base + k],
            recv_sem=link.recv_sems.at[base + h],
            device_id={"seq": target},
            device_id_type=MESH,
        )
        copies.append((target != me, copy))
        pl.when(target != me)(copy.start)
    own = pltpu.make_async_copy(
        src.at[lax.rem(me, count)], dst.at[h], link.send_sems.at[base + count]
    )
    mine = me // count == place.q
    pl.when(mine)(own.start)

    def done():
        pl.when(mine)(own.wait)
        for half in range(count):
            copy = pltpu.make_async_remote_copy(
                src_ref=src.at[0],
                dst_ref=dst.at[half],
                send_sem=link.send_sems.at[base],
                recv_sem=link.recv_sems.at[base + half],
                device_id={"seq": me},
                device_id_type=MESH,
            )
            pl.when(half * dims["group"] + me // count != me)(copy.wait_recv)
        for other, copy in copies:
            pl.when(other)(copy.wait_send)

    return done


def half_mask(rows, half):
    return (lax.broadcasted_iota(jnp.int32, (rows, 128), 1) // HEAD_DIM) == half


def attend(q_ref, k_ref, v_ref, valid, p_ref, mix_ref, causal, block, first, last, pump):
    keys = k_ref.shape[0]
    for pair in range(q_ref.shape[1] // 128):
        lanes = slice(pair * 128, pair * 128 + 128)
        for start in range(first, last, block):
            stop = start + block if causal else keys
            halves = []
            for half in range(2):
                query = q_ref[start : start + block, lanes]
                query = jnp.where(half_mask(block, half), query, jnp.zeros_like(query))
                scores = nt(k_ref[:stop, lanes], query) * SCALE
                scores = jnp.where(valid(start, stop), scores, NEG)
                top = jnp.max(scores, axis=0, keepdims=True)
                grown = jnp.exp(scores - top)
                probs = (grown * (1.0 / jnp.sum(grown, axis=0, keepdims=True))).astype(BF)
                p_ref[2 * pair + half, :stop, start : start + block] = probs
                mixed = tn(v_ref[:stop, lanes], probs)
                halves.append(mixed[half * HEAD_DIM : (half + 1) * HEAD_DIM])
            mix_ref[start : start + block, lanes] = jnp.concatenate(halves, axis=0).T.astype(BF)
        if pair == 0:
            pump()


def attend_back(
    q_ref, k_ref, v_ref, p_ref, grad_ref, dq_ref, dk_ref, dv_ref, causal, block, first, last,
    pump,
):
    keys = k_ref.shape[0]
    for pair in range(q_ref.shape[1] // 128):
        lanes = slice(pair * 128, pair * 128 + 128)
        for start in range(first, last, block):
            stop = start + block if causal else keys
            halves = []
            sum_k, sum_v = None, None
            for half in range(2):
                mask = half_mask(block, half)
                query = q_ref[start : start + block, lanes]
                query = jnp.where(mask, query, jnp.zeros_like(query))
                grad = grad_ref[start : start + block, lanes]
                grad = jnp.where(mask, grad, jnp.zeros_like(grad))
                low = p_ref[2 * pair + half, :stop, start : start + block]
                probs = low.astype(F32)
                grad_probs = nt(v_ref[:stop, lanes], grad)
                delta = jnp.sum(probs * grad_probs, axis=0, keepdims=True)
                grad_scores = (probs * (grad_probs - delta)).astype(BF)
                turned = tn(k_ref[:stop, lanes], grad_scores) * SCALE
                halves.append(turned[half * HEAD_DIM : (half + 1) * HEAD_DIM])
                new_k, new_v = nn(grad_scores, query), nn(low, grad)
                sum_k = new_k if sum_k is None else sum_k + new_k
                sum_v = new_v if sum_v is None else sum_v + new_v
            old = start if causal else (keys if start else 0)
            for ref, value in ((dk_ref, sum_k), (dv_ref, sum_v)):
                if old:
                    ref[:old, lanes] = ref[:old, lanes] + value[:old]
                if old < stop:
                    ref[old:stop, lanes] = value[old:]
            dq_ref[start : start + block, lanes] = jnp.concatenate(halves, axis=0).T.astype(BF)
        if pair == 0:
            pump()


class Box:
    def __init__(self, names, refs):
        for name, ref in zip(names, refs):
            setattr(self, name, ref)


class Quarters:
    def __init__(self, link, place, grad, box_names, box):
        self.link, self.place, self.grad = link, place, grad
        self.recv, self.sums, self.last, self.lines, self.total, self.moved, self.done, self.out = (
            getattr(box, name) if name else None for name in box_names
        )

    def send(self):
        place, piece, link = self.place, self.piece, self.link
        self.steps = []
        for i, near in enumerate((place.tx, place.ty)):
            copies = [
                (self.grad.at[piece(near, i)], self.recv.at[i, 0], place.line(near)),
                (self.grad.at[piece(place.txy, i)], self.recv.at[i, 1], place.line(near)),
            ]
            self.steps.append(link.batch(copies, self.recv.at[i]))
        self.flying = list(self.steps)

    def turn(self):
        place, piece, link = self.place, self.piece, self.link
        steps = []
        for i, far in enumerate((place.ty, place.tx)):
            self.steps[i].wait_recv()
            value = self.grad[piece(far, i)].astype(F32) + self.recv[i, 1].astype(F32)
            self.sums[i] = value.astype(BF)
            steps.append(link.send(self.sums.at[i], self.last.at[i], place.line(far)))
        self.steps = steps
        self.flying += steps

    def add(self):
        place = self.place
        for i in range(2):
            self.steps[i].wait_recv()
            value = self.grad[self.piece(place.t, i)].astype(F32)
            value = value + self.recv[i, 0].astype(F32) + self.last[i].astype(F32)
            self.total[self.halves(i)] = value.astype(BF)
        if self.lines is not None:
            share, items = place.dims["share"], place.dims["items"]
            copies = []
            for a in range(1, items // share):
                target = {"items": lax.rem(place.it + a * share, items)}
                copies.append((self.total, self.lines.at[a - 1], target))
            step = self.link.batch(copies, self.lines)
            step.wait()
            self.link.open.pop()
            value = self.total[...].astype(F32)
            for a in range(1, items // share):
                value = value + self.lines[a - 1].astype(F32)
            self.total[...] = value.astype(BF)
        self.along()

    def gather(self):
        self.close()
        place, out = self.place, self.out
        self.own = self.link.local(self.done, out.at[place.t])
        self.near = [
            self.link.send(self.done, out.at[place.t], place.line(near))
            for near in (place.tx, place.ty)
        ]

    def forward(self):
        place, out, link = self.place, self.out, self.link
        self.steps = []
        for i, (source, near) in enumerate(((place.ty, place.tx), (place.tx, place.ty))):
            self.near[1 - i].wait_recv()
            part = out.at[self.cut(source, i)]
            self.steps.append(link.send(part, part, place.line(near)))

    def finish(self):
        arrive(self.steps)
        self.own.wait()


class Hidden(Quarters):
    def piece(self, t, i):
        rows = self.grad.shape[2] // 2
        return slice(None), t, slice(i * rows, (i + 1) * rows)

    def halves(self, i):
        rows = self.grad.shape[2] // 2
        return slice(None), slice(i * rows, (i + 1) * rows)

    def cut(self, t, i):
        rows = self.out.shape[1] // 2
        return t, slice(i * rows, (i + 1) * rows)

    def along(self):
        self.steps = [self.link.send(self.total.at[1], self.moved, self.place.partner())]

    def close(self):
        arrive(self.steps)
        self.done[...] = (self.total[0].astype(F32) + self.moved[...].astype(F32)).astype(BF)


class Columns(Quarters):
    def piece(self, t, i):
        blocks = self.grad.shape[1] // 2
        return slice(None), slice(i * blocks, (i + 1) * blocks), t

    def halves(self, i):
        blocks = self.grad.shape[1] // 2
        return slice(None), slice(i * blocks, (i + 1) * blocks)

    def cut(self, t, i):
        cols = self.out.shape[3] // 2
        return t, slice(None), slice(None), slice(i * cols, (i + 1) * cols)

    def along(self):
        place = self.place
        copies = []
        for d in range(1, place.dims["seq"]):
            target = place.seq_shift(d)
            copies.append((self.total.at[:, target], self.moved.at[place.me], {"seq": target}))
        self.steps = [self.link.batch(copies, self.moved.at[0 : place.dims["seq"] - 1])]
        self.own = self.link.local(self.total.at[:, place.me], self.moved.at[place.me])

    def close(self):
        arrive(self.steps)
        self.own.wait()
        dims = self.place.dims
        group, width = dims["group"], dims["width"]
        for index in range(3):
            for q in range(group):
                value = self.moved[q, index].astype(F32)
                for half in range(1, dims["items_dev"]):
                    value = value + self.moved[half * group + q, index].astype(F32)
                self.done[index, :, q * width : (q + 1) * width] = value.astype(BF)


class Rows(Quarters):
    def piece(self, t, i):
        return i, t

    def halves(self, i):
        return i

    def cut(self, t, i):
        cols = self.out.shape[2] // 2
        return t, slice(None), slice(i * cols, (i + 1) * cols)

    def along(self):
        self.moved_done = rows_back(self.link, self.place, self.total, self.moved)

    def close(self):
        self.moved_done()
        value = self.moved[0].astype(F32)
        for half in range(1, self.place.dims["items_dev"]):
            value = value + self.moved[half].astype(F32)
        self.done[...] = value.astype(BF)


class Stage:
    def __init__(self, sems, place, part, bufs, mid, spread, before):
        self.link, self.place, self.mid, self.spread = Link(*sems), place, mid, spread
        self.before = before
        self.reduce = Reduce(self.link, place, part, bufs)
        self.started, self.waits = {}, {}

    def start(self, k):
        self.reduce.start(k, k)

    def middle(self, k):
        self.reduce.middle(k, k)

    def end(self, k):
        place, spread = self.place, self.spread
        spread[k, place.c, place.b1, place.b0] = self.mid(k, self.reduce.end(k))
        self.started[k] = spread_start(self.link, place, spread, k)

    def forward(self, k):
        self.waits[k] = spread_end(self.link, self.place, self.spread, k, self.started[k])

    def arrive(self, k):
        arrive(self.waits[k])

    def release(self, k):
        done = (self.reduce.zero[k], self.reduce.one[k])
        for copy in done:
            copy.wait_send()
        late = {id(copy) for copy in done}
        self.link.open = [copy for copy in self.link.open if id(copy) not in late]


def stage_steps(stage, compute, flight=None, ended=None, after=None):
    before = stage.before
    compute(0, (lambda: before.forward(1)) if before else (lambda: None))
    stage.start(0)
    compute(1, lambda: None)
    stage.start(1)
    if before:
        before.link.finish()
    stage.middle(0)
    stage.middle(1)
    if flight:
        flight()
    stage.end(0)
    stage.end(1)
    if ended:
        ended()
    stage.forward(0)
    if after:
        after()


def layer_kernel(dims, names, *refs):
    b = Box(names, refs)
    b.grad_third, b.grad_r2, b.grad_r1, b.gc1_all = b.first, b.second, b.first, b.gy_all
    place = Place(dims)
    sems = b.send_sems, b.recv_sems
    link = Link(*sems, dims["chain"])
    width, block, items_dev = dims["width"], dims["block"], dims["items_dev"]
    h, t, q_place = place.h, place.t, place.q
    c, b1, b0 = place.c, place.b1, place.b0
    partner = place.partner()
    wr = b.w_sq.shape[0] // dims["share"]
    model = dims["model"]
    total_dec, total_mem = dims["total_dec"], dims["total_mem"]
    rb = b.dec.shape[1]

    def rows_of(ref, cols=model):
        return ref[...].reshape(-1, ref.shape[-1])[:, :cols]

    def chunk(ref, k):
        return ref[k].reshape(-1, model)

    half_rows = total_dec // 2

    def span(k):
        return slice(k * half_rows, (k + 1) * half_rows)

    def put(k, value, before=None):
        if before:
            before.release(k)
        b.part[k] = value.astype(BF).reshape(b.part.shape[1:])

    def weight(ref, index):
        return ref[index].reshape(model, width)

    weights = (b.w_sq, b.w_sk, b.w_sv, b.w_so, b.w_ck, b.w_cv, b.w_cq, b.w_co)
    rows_t = pl.ds(pl.multiple_of(t * wr, wr), wr)
    index = link.index()
    for i, w in enumerate(weights):
        pltpu.make_async_copy(w.at[rows_t], b.staged.at[i], b.send_sems.at[index]).start()
    staged = pltpu.make_async_copy(b.staged, b.staged, b.send_sems.at[index])
    own_fin = link.local(b.f_in, b.own_fin)
    own_fout = link.local(b.f_out, b.own_fout)
    greet(place.seq_peers() + place.items_peers())

    swap_x = link.send(b.dec.at[1 - h], b.x_all.at[h, c, b1, b0], partner)
    def share_columns(dst):
        blocks = dims["seq"] // 2
        return Share(
            link, place, lambda t: dst.at[:, t],
            lambda t, i: dst.at[i * blocks : (i + 1) * blocks, t],
        )

    def share_rows(dst):
        return Share(link, place, lambda t: dst.at[:, t], lambda t, i: dst.at[i, t])

    def share_hidden(dst):
        rows = dst.shape[1] // 2
        return Share(
            link, place, lambda t: dst.at[t], lambda t, i: dst.at[t, i * rows : (i + 1) * rows]
        )

    def join_cells():
        mb = b.cells.shape[1]
        same = lax.broadcasted_iota(jnp.int32, (mb, mb), 0) == lax.broadcasted_iota(
            jnp.int32, (mb, mb), 1
        )
        for k in range(items_dev):
            flags = (b.cells[k : k + 1] == 1).astype(F32)
            column = jnp.sum(jnp.where(same, flags, 0.0), axis=1, keepdims=True)
            b.mem_cells[k, :, :model] = b.mem[k]
            b.mem_cells[k, :, model:] = jnp.broadcast_to(column, (mb, 128)).astype(BF)

    b.x_all[h, c, b1, b0] = b.dec[h]
    first_x = spread_start(link, place, b.x_all, h)
    staged.wait()
    steps, own_self = columns_out(link, place, b.staged.at[0:3], b.o_self, width)
    waits = spread_end(link, place, b.x_all, h, first_x)
    swap_x.wait_recv()
    second_x = spread_start(link, place, b.x_all, 1 - h)
    so_arrived, so_sent = rows_out(link, place, b.staged.at[3], b.o_so)
    steps.wait_recv()
    own_self.wait()
    self_share = [share_columns(b.o_self.at[i]) for i in range(3)]
    waits += spread_end(link, place, b.x_all, 1 - h, second_x)
    so_arrived()
    so_share = share_rows(b.o_so)
    cross_steps, own_cross = columns_out(link, place, b.staged.at[4:7], b.o_cross, width)
    co_arrived, co_sent = rows_out(link, place, b.staged.at[7], b.o_co)
    join_cells()
    b.m_all[h, c, b1, b0] = b.mem_cells[h]
    swap_m = link.send(b.mem_cells.at[1 - h], b.m_all.at[h, c, b1, b0], partner)
    first_m = spread_start(link, place, b.m_all, h)
    own_fin.wait()
    own_fout.wait()
    fr, gr = b.o_fin.shape[1], b.o_fout.shape[1]
    step_fin = link.send(b.own_fin.at[pl.ds(pl.multiple_of(t * fr, fr), fr)], b.o_fin.at[t], partner)
    for share in self_share:
        share.forward()

    arrive(waits)
    rows = rows_of(b.x_all)
    for index, dst in enumerate((b.sq, b.sk, b.sv)):
        self_share[index].wait()
        dst[...] = nn(rows, weight(b.o_self, index)).astype(BF)
    so_share.forward()
    cross_steps.wait_recv()
    own_cross.wait()
    cross_share = [share_columns(b.o_cross.at[i]) for i in range(3)]
    co_arrived()
    co_share = share_rows(b.o_co)
    mem_waits = spread_end(link, place, b.m_all, h, first_m)
    swap_m.wait_recv()
    second_m = spread_start(link, place, b.m_all, 1 - h)
    length, mem_length = b.dec_len[h], b.mem_len[h]

    def self_ok(start, stop):
        keys = lax.broadcasted_iota(jnp.int32, (stop, block), 0)
        spots = lax.broadcasted_iota(jnp.int32, (stop, block), 1) + start
        return (keys <= spots) & (keys < length)

    bufs = [b.recv0, b.send1, b.recv1, b.keep1]
    if dims["bits"] == 3:
        bufs += [b.send2, b.recv2]

    def forward(index, res, summed, out):
        def mid(k, total):
            value = res(k) + total
            summed[k] = value
            normed, _ = moments(value)
            result = normed * b.gain[index : index + 1] + b.bias[index : index + 1]
            out[k] = result
            return result.astype(BF)

        return mid

    def self_part(k, pump):
        attend(
            b.sq, b.sk, b.sv, self_ok, b.sp, b.smix, True, block,
            k * half_rows, (k + 1) * half_rows, pump,
        )
        if k == 0:
            so_share.wait()
        put(k, nn(b.smix[span(k)], rows_of(b.o_so)))

    def memory_part():
        arrive(mem_waits)
        mems = rows_of(b.m_all)
        cross_share[0].wait()
        b.ck[...] = nn(mems, weight(b.o_cross, 0)).astype(BF)
        cross_share[1].wait()
        b.cv[...] = nn(mems, weight(b.o_cross, 1)).astype(BF)
        spots = lax.broadcasted_iota(jnp.int32, (total_mem, 128), 0)
        cells = b.m_all[...].reshape(-1, b.m_all.shape[-1])[:, model:].astype(F32)
        b.keep[...] = ((spots < mem_length) & ((cells > 0.5) | (spots == 0))).astype(F32)

    stage = Stage(
        sems, place, b.part, bufs,
        forward(0, lambda k: b.x_all[k, c, b1, b0].astype(F32), b.sum_one, b.first), b.first_all, None,
    )
    def cross_weights():
        mem_waits.extend(spread_end(link, place, b.m_all, 1 - h, second_m))
        for share in cross_share + [co_share]:
            share.forward()
        step_fin.wait_recv()
        ffn_share.append(share_hidden(b.o_fin))

    ffn_share = []
    stage_steps(stage, self_part, after=cross_weights)
    step_fout = link.send(
        b.own_fout.at[pl.ds(pl.multiple_of(t * gr, gr), gr)], b.o_fout.at[t], partner
    )
    memory_part()
    b.c_own[h] = b.cot[h]

    def cross_part(k, pump):
        last.arrive(k)
        if k == 0:
            cross_share[2].wait()
        b.cq[span(k)] = nn(chunk(b.first_all, k), weight(b.o_cross, 2)).astype(BF)
        attend(
            b.cq, b.ck, b.cv, lambda start, stop: b.keep[:, 0:1] > 0.5, b.cp, b.cmix, False, block,
            k * half_rows, (k + 1) * half_rows, pump,
        )
        if k == 0:
            co_share.wait()
        put(k, nn(b.cmix[span(k)], rows_of(b.o_co)), last)

    last = stage
    stage = Stage(
        sems, place, b.part, bufs, forward(1, lambda k: b.first[k], b.sum_two, b.second),
        b.second_all, last,
    )
    def ffn_weights():
        ffn_share[0].forward()
        step_fout.wait_recv()
        ffn_share.append(share_hidden(b.o_fout))

    stage_steps(stage, cross_part, ffn_weights)
    swap_c = link.send(b.cot.at[1 - h], b.c_own.at[h], partner)

    w_ins = (lambda: b.own_fin[...], lambda: b.o_fin[...].reshape(model, -1))
    w_outs = (lambda: b.own_fout[...], lambda: b.o_fout[...].reshape(-1, model))
    hidden = b.own_fin.shape[1]
    last_second = stage

    def ffn_part(k, pump):
        last_second.arrive(k)
        if k == 0:
            ffn_share[0].wait()
        rows = chunk(b.second_all, k)
        for index in range(2):
            if index:
                pump()
            pre = nn(rows, w_ins[index]())
            cdf = 0.5 * (1.0 + lax.erf(pre * (0.5**0.5)))
            cols = slice(index * hidden, (index + 1) * hidden)
            b.act[span(k), cols] = (pre * cdf).astype(BF)
            b.slope[span(k), cols] = (
                cdf + pre * (jnp.exp(-0.5 * pre * pre) * 0.3989422804014327)
            ).astype(BF)
        if k == 0:
            ffn_share[1].forward()
            ffn_share[1].wait()
        total = nn(b.act[span(k), :hidden], w_outs[0]())
        put(k, total + nn(b.act[span(k), hidden:], w_outs[1]()), last_second)

    swap_c.wait_recv()

    def add_sums(index, k, normed, grad):
        new = (jnp.sum(grad * normed, axis=0, keepdims=True), jnp.sum(grad, axis=0, keepdims=True))
        for row, value in zip((index, 3 + index), new):
            b.sums[row : row + 1] = value if k == 0 else b.sums[row : row + 1] + value

    def turn(k, total):
        gain = b.gain[2:3]
        normed, inv = moments(b.second[k] + total)
        spots = lax.broadcasted_iota(jnp.int32, (rb, model), 0) + (k * dims["group"] + q_place) * rb
        kept = spots < length
        b.layer[k] = jnp.where(kept, normed * gain + b.bias[2:3], 0.0).astype(BF)
        grad = jnp.where(kept, b.c_own[k].astype(F32), 0.0)
        add_sums(2, k, normed, grad)
        result = norm_back(normed, inv, gain, grad)
        b.grad_third[k] = result
        return result.astype(BF)

    stage = Stage(sems, place, b.part, bufs, turn, b.gy_all, last_second)
    stage_steps(stage, ffn_part)

    last_turn = stage

    way_fout = Hidden(
        link, place, b.g_fout, ("q_fout", "t_fout", "u_fout", dims["lines"] and "l_fout", "s_fout", "z_fout", "d_fout", "r_fout"), b
    )
    def out_grads():
        grad = rows_of(b.gy_all)
        for index in range(2):
            cols = slice(index * hidden, (index + 1) * hidden)
            value = tn(b.act[:, cols], grad)
            b.g_fout[index] = value.astype(BF).reshape(b.g_fout.shape[1:])
        way_fout.send()

    def ffn_back(k, pump):
        last_turn.arrive(k)
        if k == 1:
            out_grads()
        grad = chunk(b.gy_all, k)
        total = None
        for index in range(2):
            if index:
                pump()
            cols = slice(index * hidden, (index + 1) * hidden)
            grad_pre = (nt(grad, w_outs[index]()) * b.slope[span(k), cols].astype(F32)).astype(BF)
            b.slope[span(k), cols] = grad_pre
            term = nt(grad_pre, w_ins[index]())
            total = term if total is None else total + term
        put(k, total, last_turn)

    way_fin = Hidden(
        link, place, b.g_fin, ("q_fin", "t_fin", "u_fin", dims["lines"] and "l_fin", "s_fin", "z_fin", "d_fin", "r_fin"), b
    )
    way_cross = Columns(
        link, place, b.g_cross, ("q_cross", "t_cross", "u_cross", dims["lines"] and "l_cross", "s_cross", "z_cross", "d_cross", "r_cross"), b
    )
    way_self = Columns(
        link, place, b.g_self, ("q_self", "t_self", "u_self", dims["lines"] and "l_self", "s_self", "z_self", "d_self", "r_self"), b
    )
    way_co = Rows(
        link, place, b.g_co, ("q_co", "t_co", "u_co", dims["lines"] and "l_co", "s_co", "z_co", "d_co", "r_co"), b
    )
    way_so = Rows(
        link, place, b.g_so, ("q_so", "t_so", "u_so", dims["lines"] and "l_so", "s_so", "z_so", "d_so", "r_so"), b
    )

    def backward(index, res, summed, out):
        def mid(k, total):
            normed, inv = moments(summed[k])
            grad = res[k] + total
            add_sums(index, k, normed, grad)
            result = norm_back(normed, inv, b.gain[index : index + 1], grad)
            out[k] = result
            return result.astype(BF)

        return mid

    def in_grads():
        rows = rows_of(b.second_all)
        for index in range(2):
            cols = slice(index * hidden, (index + 1) * hidden)
            value = tn(rows, b.slope[:, cols])
            b.g_fin[index] = value.astype(BF).reshape(b.g_fin.shape[1:])
        way_fin.send()

    stage = Stage(
        sems, place, b.part, bufs, backward(1, b.grad_third, b.sum_two, b.grad_r2), b.gc2_all,
        last_turn,
    )
    stage_steps(stage, ffn_back, in_grads)

    last_back = stage

    def cross_back(k, pump):
        last_back.arrive(k)
        b.dmix[span(k)] = nt(chunk(b.gc2_all, k), rows_of(b.o_co)).astype(BF)
        attend_back(
            b.cq, b.ck, b.cv, b.cp, b.dmix, b.dq, b.sum_dk, b.sum_dv, False, block,
            k * half_rows, (k + 1) * half_rows, pump,
        )
        put(k, nt(b.dq[span(k)], weight(b.o_cross, 2)), last_back)
        if k == 1:
            way_fout.turn()

    def cross_grads():
        mems = rows_of(b.m_all)
        shape = b.g_cross.shape[1:]
        b.dck[...] = (b.sum_dk[:total_mem] * SCALE).astype(BF)
        b.dcv[...] = b.sum_dv[:total_mem].astype(BF)
        b.g_cross[0] = tn(rows_of(b.first_all), b.dq[...]).astype(BF).reshape(shape)
        b.g_cross[1] = tn(mems, b.dck[...]).astype(BF).reshape(shape)
        b.g_cross[2] = tn(mems, b.dcv[...]).astype(BF).reshape(shape)
        way_cross.send()
        b.g_co[...] = tn(b.cmix[...], rows_of(b.gc2_all)).astype(BF).reshape(b.g_co.shape)
        way_co.send()
        way_fin.turn()

    def part_mem():
        value = nt(b.dck[...], weight(b.o_cross, 0)) + nt(b.dcv[...], weight(b.o_cross, 1))
        b.part_m[...] = value.astype(BF).reshape(b.part_m.shape)
        for index in range(2):
            red_m.start(index, ks[index])

    stage = Stage(
        sems, place, b.part, bufs, backward(0, b.grad_r2, b.sum_one, b.grad_r1), b.gc1_all,
        last_back,
    )
    ks = (1 - h, h)
    mem_bufs = [b.recv0_m, b.send1_m, b.recv1_m, b.keep1_m]
    if dims["bits"] == 3:
        mem_bufs += [b.send2_m, b.recv2_m]
    red_m = Reduce(link, place, b.part_m, mem_bufs)
    stage_steps(stage, cross_back, cross_grads, part_mem)

    swap_l = link.send(b.layer.at[1 - h], b.layer_out.at[h], partner)
    b.layer_out[h] = b.layer[h]
    for k in range(2):
        stage.arrive(k)
        pump = (lambda: stage.forward(1)) if k == 0 else (lambda: None)
        b.dmix[span(k)] = nt(chunk(b.gc1_all, k), rows_of(b.o_so)).astype(BF)
        attend_back(
            b.sq, b.sk, b.sv, b.sp, b.dmix, b.dq, b.sum_dk, b.sum_dv, True, block,
            k * half_rows, (k + 1) * half_rows, pump,
        )
        red_m.middle(k, ks[k])
    b.dsk[...] = (b.sum_dk[...] * SCALE).astype(BF)
    b.dsv[...] = b.sum_dv[...].astype(BF)
    for k in range(2):
        total = nt(b.dq[span(k)], weight(b.o_self, 0)) + nt(b.dsk[span(k)], weight(b.o_self, 1))
        put(k, total + nt(b.dsv[span(k)], weight(b.o_self, 2)), stage)
    stage.link.finish()
    chain = Link(*sems)
    red_x = Reduce(chain, place, b.part, bufs)
    for index in range(2):
        red_x.start(index, ks[index])
    rows = rows_of(b.x_all)
    shape = b.g_self.shape[1:]
    b.g_self[0] = tn(rows, b.dq[...]).astype(BF).reshape(shape)
    b.g_self[1] = tn(rows, b.dsk[...]).astype(BF).reshape(shape)
    b.g_self[2] = tn(rows, b.dsv[...]).astype(BF).reshape(shape)
    way_self.send()
    b.g_so[...] = tn(b.smix[...], rows_of(b.gc1_all)).astype(BF).reshape(b.g_so.shape)
    way_so.send()
    for index in range(2):
        red_x.middle(index, ks[index])
    way_fout.add()
    way_cross.turn()
    way_co.turn()
    copies = []
    for d in range(1, dims["seq"]):
        copies.append((b.sums, b.sums_seq.at[d - 1], {"seq": place.seq_shift(d)}))
    seq_sums = link.batch(copies, b.sums_seq)
    way_fin.add()
    b.send_x[...] = (red_x.end(0) + b.grad_r1[1 - h]).astype(BF)
    swap_x = link.send(b.send_x, b.recv_x, partner)
    b.grad_dec[h] = red_x.end(1) + b.grad_r1[h]
    b.send_m[...] = red_m.end(0).astype(BF)
    swap_m = link.send(b.send_m, b.recv_m, partner)
    b.grad_mem[h] = red_m.end(1)
    way_self.turn()
    way_so.turn()
    way_cross.add()
    way_co.add()
    way_fout.gather()
    seq_sums.wait_recv()
    value = b.sums[...]
    for d in range(1, dims["seq"]):
        value = value + b.sums_seq[d - 1]
    b.sums_line[...] = value
    copies = []
    for e in range(1, dims["items"]):
        target = {"items": lax.rem(place.it + e, dims["items"])}
        copies.append((b.sums_line, b.sums_items.at[e - 1], target))
    item_sums = link.batch(copies, b.sums_items)
    way_self.add()
    way_so.add()
    way_fin.gather()
    way_fout.forward()
    swap_x.wait_recv()
    b.grad_dec[1 - h] = b.recv_x[...].astype(F32)
    swap_m.wait_recv()
    b.grad_mem[1 - h] = b.recv_m[...].astype(F32)
    swap_l.wait_recv()
    way_cross.gather()
    way_co.gather()
    way_fin.forward()
    item_sums.wait_recv()
    value = b.sums_line[...]
    for e in range(1, dims["items"]):
        value = value + b.sums_items[e - 1]
    b.sums_out[...] = value
    way_self.gather()
    way_so.gather()
    way_cross.forward()
    way_co.forward()
    way_self.forward()
    way_so.forward()
    for way in (way_fout, way_fin, way_cross, way_co, way_self, way_so):
        way.finish()
    so_sent()
    co_sent()
    chain.finish()
    link.finish()


def shape(dims, dtype):
    return jax.ShapeDtypeStruct(tuple(dims), dtype)


def outputs_kernel(layer, dec, mem, cross, own, co, so, fin, fout, sums, *outs):
    o_layer, o_dec, o_mem = outs[:3]
    o_layer[...] = layer[...]
    o_dec[...] = dec[...]
    o_mem[...] = mem[...]
    for index in range(3):
        outs[3 + index][...] = own[0, index].astype(F32)
        outs[7 + index][...] = cross[0, index].astype(F32)
    outs[6][...] = so[0].astype(F32)
    outs[10][...] = co[0].astype(F32)
    outs[11][...] = fin[0].astype(F32)
    outs[12][...] = fout[0].astype(F32)
    outs[13][...] = sums[0:3]
    outs[14][...] = sums[3:6]


def shards(
    mesh, dec_in, memory, dec_len, mem_len, cell_mask, self_query, self_key, self_value, self_out,
    cross_query, cross_key, cross_value, cross_out, ffn_in, ffn_out, norm_gain, norm_bias, cotangent,
):
    items_dev, rb, model = dec_in.shape
    mb = memory.shape[1]
    seq, items = mesh.shape["seq"], mesh.shape["items"]
    group = seq // items_dev
    share = 4
    bits = group.bit_length() - 1
    chips = group // 4
    width = model // group
    total_dec, total_mem = rb * seq, mb * seq
    heads = width // HEAD_DIM
    hidden = ffn_in.shape[1]
    wr = self_query.shape[0] // share
    fr, gr = model // share, hidden // share
    lines = items // share - 1
    dims = {
        "items_dev": items_dev, "items": items, "seq": seq, "group": group, "share": share,
        "bits": bits, "chips": chips, "width": width, "model": model, "block": 256,
        "total_dec": total_dec, "total_mem": total_mem, "lines": lines,
        "chain": 12 + 2 * (bits - 2),
    }
    ins = [
        ("dec", dec_in, VM), ("mem", memory, VM), ("cells", cell_mask, VM), ("cot", cotangent, VM),
        ("dec_len", dec_len, SM), ("mem_len", mem_len, SM),
        ("w_sq", self_query, HBM), ("w_sk", self_key, HBM), ("w_sv", self_value, HBM),
        ("w_so", self_out, HBM), ("w_cq", cross_query, HBM), ("w_ck", cross_key, HBM),
        ("w_cv", cross_value, HBM), ("w_co", cross_out, HBM), ("f_in", ffn_in, HBM),
        ("f_out", ffn_out, HBM), ("gain", norm_gain, VM), ("bias", norm_bias, VM),
    ]
    own, own_m = (items_dev, rb, model), (items_dev, mb, model)
    grid = (items_dev, chips, 2, 2)
    outs = [
        ("layer_out", own, BF, VM), ("grad_dec", own, F32, VM), ("grad_mem", own_m, F32, VM),
        ("sums_out", (8, model), F32, VM),
        ("r_cross", (share, 3, wr, model), BF, HBM), ("r_self", (share, 3, wr, model), BF, HBM),
        ("r_co", (share, wr, model), BF, HBM), ("r_so", (share, wr, model), BF, HBM),
        ("r_fin", (share, fr, hidden), BF, HBM), ("r_fout", (share, gr, model), BF, HBM),
    ]
    cols = (3, seq, share, wr, width)
    scratch = [
        ("x_all", grid + (rb, model), BF), ("m_all", grid + (mb, model + 128), BF),
        ("mem_cells", (items_dev, mb, model + 128), BF), ("c_own", own, BF), ("staged", (8, wr, model), BF),
        ("own_fin", (model, hidden), BF), ("own_fout", (hidden, model), BF),
        ("o_self", cols, BF), ("o_cross", cols, BF),
        ("o_so", (items_dev, share, wr, model), BF), ("o_co", (items_dev, share, wr, model), BF),
        ("o_fin", (share, fr, hidden), BF), ("o_fout", (share, gr, model), BF),
        ("sq", (total_dec, width), BF), ("sk", (total_dec, width), BF), ("sv", (total_dec, width), BF),
        ("cq", (total_dec, width), BF), ("ck", (total_mem, width), BF), ("cv", (total_mem, width), BF),
        ("sp", (heads, total_dec, total_dec), BF), ("cp", (heads, total_mem, total_dec), BF),
        ("smix", (total_dec, width), BF), ("cmix", (total_dec, width), BF),
        ("keep", (total_mem, 128), F32),
        ("part", grid + (rb, model), BF), ("part_m", grid + (mb, model), BF),
        ("first_all", grid + (rb, model), BF), ("second_all", grid + (rb, model), BF),
        ("gy_all", grid + (rb, model), BF), ("gc2_all", grid + (rb, model), BF),
        ("sum_one", own, F32), ("sum_two", own, F32), ("first", own, F32), ("second", own, F32),
        ("layer", own, BF), ("sum_dk", (total_dec, width), F32), ("sum_dv", (total_dec, width), F32),
        ("act", (total_dec, 2 * hidden), BF), ("slope", (total_dec, 2 * hidden), BF),
        ("dmix", (total_dec, width), BF), ("dq", (total_dec, width), BF),
        ("dsk", (total_dec, width), BF), ("dsv", (total_dec, width), BF),
        ("dck", (total_mem, width), BF), ("dcv", (total_mem, width), BF),
        ("send_x", (rb, model), BF), ("recv_x", (rb, model), BF),
        ("send_m", (mb, model), BF), ("recv_m", (mb, model), BF),
        ("sums", (8, model), F32), ("sums_line", (8, model), F32),
        ("sums_seq", (seq - 1, 8, model), F32), ("sums_items", (items - 1, 8, model), F32),
    ]
    for name, rows in (("", rb), ("_m", mb)):
        scratch += [
            ("recv0" + name, (items_dev, chips, 2, rows, model), BF),
            ("send1" + name, (items_dev, chips, rows, model), BF),
            ("recv1" + name, (items_dev, chips, rows, model), BF),
            ("keep1" + name, (items_dev, chips, rows, model), F32),
        ]
        if bits == 3:
            scratch += [
                ("send2" + name, (items_dev, rows, model), BF),
                ("recv2" + name, (items_dev, rows, model), BF),
            ]
    for name, grad, quarter, piece, moved, done in (
        ("fin", (2, share, fr, hidden), (2, fr, hidden), (2, fr // 2, hidden), (fr, hidden),
         (fr, hidden)),
        ("fout", (2, share, gr, model), (2, gr, model), (2, gr // 2, model), (gr, model), (gr, model)),
        ("cross", cols, (3, seq, wr, width), (3, seq // 2, wr, width), (seq, 3, wr, width),
         (3, wr, model)),
        ("self", cols, (3, seq, wr, width), (3, seq // 2, wr, width), (seq, 3, wr, width),
         (3, wr, model)),
        ("co", (items_dev, share, wr, model), (items_dev, wr, model), (wr, model),
         (items_dev, wr, model), (wr, model)),
        ("so", (items_dev, share, wr, model), (items_dev, wr, model), (wr, model),
         (items_dev, wr, model), (wr, model)),
    ):
        scratch += [
            ("g_" + name, grad, BF), ("q_" + name, (2, 2) + piece, BF), ("t_" + name, (2,) + piece, BF),
            ("u_" + name, (2,) + piece, BF), ("s_" + name, quarter, BF), ("z_" + name, moved, BF),
            ("d_" + name, done, BF),
        ]
        if lines:
            scratch.append(("l_" + name, (lines,) + quarter, BF))
    copies = dims["chain"] + 145 + 12 * (bits - 2)
    names = [x[0] for x in ins + outs + scratch] + ["send_sems", "recv_sems"]
    results = pl.pallas_call(
        functools.partial(layer_kernel, dims, names),
        name="layer",
        out_shape=[shape(x[1], x[2]) for x in outs],
        in_specs=[x[2] for x in ins],
        out_specs=[x[3] for x in outs],
        scratch_shapes=[pltpu.VMEM(x[1], x[2]) for x in scratch]
        + [pltpu.SemaphoreType.DMA((copies,)), pltpu.SemaphoreType.DMA((copies,))],
        compiler_params=pltpu.CompilerParams(
            collective_id=0, has_side_effects=True, vmem_limit_bytes=VMEM_BYTES
        ),
    )(*[x[1] for x in ins])
    layer_out, grad_dec, grad_memory, sums, r_cross, r_self, r_co, r_so, r_fin, r_fout = results
    tok, mem_rows = items_dev * rb, items_dev * mb
    pieces = (
        ((tok, model), (tok // share, model), BF), ((tok, model), (tok // share, model), F32),
        ((mem_rows, model), (mem_rows // share, model), F32),
    )
    heads_in = [
        pl.BlockSpec((1, 3, wr, model), lambda i: (i, 0, 0, 0)),
        pl.BlockSpec((1, 3, wr, model), lambda i: (i, 0, 0, 0)),
        pl.BlockSpec((1, wr, model), lambda i: (i, 0, 0)),
        pl.BlockSpec((1, wr, model), lambda i: (i, 0, 0)),
        pl.BlockSpec((1, fr, hidden), lambda i: (i, 0, 0)),
        pl.BlockSpec((1, gr, model), lambda i: (i, 0, 0)),
        pl.BlockSpec((8, model), lambda i: (0, 0)),
    ]
    row_specs = [pl.BlockSpec(x[1], lambda i: (i, 0)) for x in pieces]
    square = (share * wr, model)
    outs = pl.pallas_call(
        outputs_kernel,
        name="outputs",
        grid=(share,),
        in_specs=row_specs + heads_in,
        out_specs=row_specs
        + [pl.BlockSpec((wr, model), lambda i: (i, 0))] * 8
        + [pl.BlockSpec((fr, hidden), lambda i: (i, 0)), pl.BlockSpec((gr, model), lambda i: (i, 0))]
        + [pl.BlockSpec((3, model), lambda i: (0, 0))] * 2,
        out_shape=[shape(x[0], x[2]) for x in pieces]
        + [shape(square, F32)] * 8
        + [shape((model, hidden), F32), shape((hidden, model), F32)]
        + [shape((3, model), F32)] * 2,
        compiler_params=pltpu.CompilerParams(vmem_limit_bytes=VMEM_BYTES),
    )(
        layer_out.reshape(tok, model), grad_dec.reshape(tok, model),
        grad_memory.reshape(mem_rows, model), r_cross, r_self, r_co, r_so, r_fin, r_fout, sums,
    )
    return (
        outs[0].reshape(own), outs[1].reshape(own), outs[2].reshape(own_m), *outs[3:],
    )


def solution(mesh):
    rows = P("seq", None)
    tokens = P("items", "seq", None)
    placed = (
        (tokens, tokens, P("items"), P("items"), P("items", "seq"))
        + (rows,) * 8
        + (P(None, "seq"), rows, P(), P(), tokens)
    )
    return jax.shard_map(
        functools.partial(shards, mesh),
        mesh=mesh,
        in_specs=placed,
        out_specs=(tokens,) * 3 + (rows,) * 8 + (P(None, "seq"), rows, P(), P()),
        check_vma=False,
    )
```

```python
import functools

import jax
import jax.numpy as jnp
from jax import lax
from jax.experimental import pallas as pl
from jax.experimental.pallas import tpu as pltpu
from jax.sharding import PartitionSpec as P

HEAD_DIM = 64
EPS = 1e-05
NEG = -1e30
SCALE = HEAD_DIM ** (-0.5)
BF = jnp.bfloat16
F32 = jnp.float32
VMEM_BYTES = 63 * 1024 * 1024
MESH = pl.DeviceIdType.MESH
VM = pl.BlockSpec(memory_space=pltpu.VMEM)
HBM = pl.BlockSpec(memory_space=pl.ANY)
SM = pl.BlockSpec(memory_space=pltpu.SMEM)


def nn(left, right):
    return lax.dot_general(left, right, (((1,), (0,)), ((), ())), preferred_element_type=F32)


def nt(left, right):
    return lax.dot_general(left, right, (((1,), (1,)), ((), ())), preferred_element_type=F32)


def tn(left, right):
    return lax.dot_general(left, right, (((0,), (0,)), ((), ())), preferred_element_type=F32)


class Link:
    def __init__(self, send_sems, recv_sems, first=0):
        self.send_sems, self.recv_sems, self.count, self.open = send_sems, recv_sems, first, []

    def index(self):
        self.count += 1
        return self.count - 1

    def make(self, src, dst, device, index):
        return pltpu.make_async_remote_copy(
            src_ref=src,
            dst_ref=dst,
            send_sem=self.send_sems.at[index],
            recv_sem=self.recv_sems.at[index],
            device_id=device,
            device_id_type=MESH,
        )

    def send(self, src, dst, device):
        copy = self.make(src, dst, device, self.index())
        copy.start()
        self.open.append(copy)
        return copy

    def batch(self, copies, whole):
        index = self.index()
        for copy in copies:
            self.make(*copy, index).start()
        wait = self.make(whole, whole, copies[0][2], index)
        self.open.append(wait)
        return wait

    def settle(self, copy):
        copy.wait_send()
        self.open = [other for other in self.open if other is not copy]

    def local(self, src, dst):
        copy = pltpu.make_async_copy(src, dst, self.send_sems.at[self.index()])
        copy.start()
        return copy

    def finish(self, kept=()):
        late = {id(copy) for copy in kept}
        for copy in self.open:
            if id(copy) not in late:
                copy.wait_send()
        self.open = [copy for copy in self.open if id(copy) in late]


def greet(devices):
    barrier = pltpu.get_barrier_semaphore()
    for device in devices:
        pl.semaphore_signal(barrier, inc=1, device_id=device, device_id_type=MESH)
    pl.semaphore_wait(barrier, len(devices))


class Place:
    def __init__(self, dims):
        self.dims = dims
        group, share = dims["group"], dims["share"]
        self.me = lax.axis_index("seq")
        self.h = self.me // group
        self.q = self.me % group
        self.b0 = self.q % 2
        self.b1 = (self.q // 2) % 2
        self.c = self.q // 4
        self.it = lax.axis_index("items")
        self.base = (self.it // share) * share
        self.t = self.it % share
        x, y = self.t % 2, self.t // 2
        self.tx, self.ty, self.txy = y * 2 + 1 - x, (1 - y) * 2 + x, (1 - y) * 2 + 1 - x

    def across(self, bit):
        value = (self.q // (1 << bit)) % 2
        return {"seq": self.me + (1 - 2 * value) * (1 << bit)}

    def partner(self):
        return {"seq": (1 - self.h) * self.dims["group"] + self.q}

    def seq_shift(self, d):
        return lax.rem(self.me + d, self.dims["seq"])

    def line(self, t):
        return {"items": self.base + t}

    def seq_peers(self):
        return [{"seq": self.seq_shift(d)} for d in range(1, self.dims["seq"])]

    def items_peers(self):
        count = self.dims["items"]
        return [{"items": lax.rem(self.it + e, count)} for e in range(1, count)]


def spread_start(link, place, out, k):
    bits = place.dims["bits"]
    c, b1, b0 = place.c, place.b1, place.b0
    if bits == 3:
        step = link.send(out.at[k, c, b1, b0], out.at[k, c, b1, b0], place.across(2))
        step.wait_recv()
    waits = []
    high = link.send(out.at[k, :, b1, b0], out.at[k, :, b1, b0], place.across(1))
    waits.append(link.send(out.at[k, :, b1, b0], out.at[k, :, b1, b0], place.across(0)))
    return high, waits


def spread_end(link, place, out, k, started):
    high, waits = started
    b1, b0 = place.b1, place.b0
    high.wait_recv()
    waits.append(link.send(out.at[k, :, 1 - b1, b0], out.at[k, :, 1 - b1, b0], place.across(0)))
    return waits


def columns_out(link, place, src, dst, width):
    seq, group = place.dims["seq"], place.dims["group"]
    copies = []
    for d in range(1, seq):
        target = place.seq_shift(d)
        cols = pl.ds(pl.multiple_of(lax.rem(target, group) * width, width), width)
        copies.append((src.at[:, :, cols], dst.at[:, place.me, place.t], {"seq": target}))
    steps = link.batch(copies, dst.at[:, 0 : seq - 1, place.t])
    cols = pl.ds(pl.multiple_of(place.q * width, width), width)
    return steps, link.local(src.at[:, :, cols], dst.at[:, place.me, place.t])


def rows_out(link, place, src, dst):
    dims, me = place.dims, place.me
    slot = lax.rem(me, dims["items_dev"])
    base = link.count
    link.count += dims["items_dev"] + 1
    copies = []
    for half in range(dims["items_dev"]):
        target = half * dims["group"] + me // dims["items_dev"]
        copy = pltpu.make_async_remote_copy(
            src_ref=src,
            dst_ref=dst.at[slot, place.t],
            send_sem=link.send_sems.at[base + half],
            recv_sem=link.recv_sems.at[base + slot],
            device_id={"seq": target},
            device_id_type=MESH,
        )
        copies.append((target != me, copy))
        pl.when(target != me)(copy.start)
    own = pltpu.make_async_copy(
        src, dst.at[slot, place.t], link.send_sems.at[base + dims["items_dev"]]
    )
    mine = me // dims["items_dev"] == place.q
    pl.when(mine)(own.start)

    def arrived():
        pl.when(mine)(own.wait)
        for block in range(dims["items_dev"]):
            copy = pltpu.make_async_remote_copy(
                src_ref=src,
                dst_ref=dst.at[block, place.t],
                send_sem=link.send_sems.at[base],
                recv_sem=link.recv_sems.at[base + block],
                device_id={"seq": me},
                device_id_type=MESH,
            )
            pl.when(place.q * dims["items_dev"] + block != me)(copy.wait_recv)

    def sent():
        for other, copy in copies:
            pl.when(other)(copy.wait_send)

    return arrived, sent


class Share:
    def __init__(self, link, place, slab, half):
        self.link, self.place, self.half = link, place, half
        t = place.t
        self.from_x = link.send(slab(t), slab(t), place.line(place.tx))
        self.from_y = link.send(slab(t), slab(t), place.line(place.ty))

    def forward(self):
        link, place, half = self.link, self.place, self.half
        self.from_y.wait_recv()
        part = half(place.ty, 0)
        self.steps = [link.send(part, part, place.line(place.tx))]
        self.from_x.wait_recv()
        part = half(place.tx, 1)
        self.steps.append(link.send(part, part, place.line(place.ty)))

    def wait(self):
        arrive(self.steps)


def arrive(steps):
    for step in steps:
        step.wait_recv()


class Reduce:
    def __init__(self, link, place, part, bufs):
        self.link, self.place, self.part, self.bufs = link, place, part, bufs
        self.zero, self.one = {}, {}

    def start(self, index, k):
        place = self.place
        self.zero[index] = self.link.send(
            self.part.at[k, :, :, 1 - place.b0], self.bufs[0].at[index], place.across(0)
        )

    def middle(self, index, k):
        place, part = self.place, self.part
        recv0, send1, recv1, keep1 = self.bufs[:4]
        self.zero[index].wait_recv()
        b1, b0 = place.b1, place.b0
        for c in range(part.shape[1]):
            value = part[k, c, 1 - b1, b0].astype(F32) + recv0[index, c, 1 - b1].astype(F32)
            send1[index, c] = value.astype(BF)
        self.one[index] = self.link.send(send1.at[index], recv1.at[index], place.across(1))
        for c in range(part.shape[1]):
            keep1[index, c] = part[k, c, b1, b0].astype(F32) + recv0[index, c, b1].astype(F32)

    def end(self, index):
        place = self.place
        recv1, keep1 = self.bufs[2:4]
        self.one[index].wait_recv()
        if place.dims["bits"] == 2:
            return keep1[index, 0] + recv1[index, 0].astype(F32)
        send2, recv2 = self.bufs[4:6]
        c = place.c
        send2[index] = (keep1[index, 1 - c] + recv1[index, 1 - c].astype(F32)).astype(BF)
        step = self.link.send(send2.at[index], recv2.at[index], place.across(2))
        kept = keep1[index, c] + recv1[index, c].astype(F32)
        step.wait_recv()
        return kept + recv2[index].astype(F32)


def reduce_bufs(dims, rows):
    items_dev, width, chips = dims["items_dev"], dims["model"], dims["chips"]
    bufs = [
        pltpu.VMEM((items_dev, chips, 2, rows, width), BF),
        pltpu.VMEM((items_dev, chips, rows, width), BF),
        pltpu.VMEM((items_dev, chips, rows, width), BF),
        pltpu.VMEM((items_dev, chips, rows, width), F32),
    ]
    if dims["bits"] == 3:
        bufs += [pltpu.VMEM((items_dev, rows, width), BF) for _ in range(2)]
    return bufs


def moments(value):
    mean = jnp.mean(value, axis=-1, keepdims=True)
    centered = value - mean
    inv = lax.rsqrt(jnp.mean(centered * centered, axis=-1, keepdims=True) + EPS)
    return centered * inv, inv


def norm_back(normed, inv, gain, grad):
    scaled = grad * gain
    mean = jnp.mean(scaled, axis=-1, keepdims=True)
    cross = jnp.mean(scaled * normed, axis=-1, keepdims=True)
    return inv * (scaled - mean - normed * cross)


def rows_back(link, place, src, dst):
    dims, me, h = place.dims, place.me, place.h
    count = dims["items_dev"]
    base = link.count
    link.count += count + 1
    copies = []
    for k in range(count):
        target = place.q * count + k
        copy = pltpu.make_async_remote_copy(
            src_ref=src.at[k],
            dst_ref=dst.at[h],
            send_sem=link.send_sems.at[base + k],
            recv_sem=link.recv_sems.at[base + h],
            device_id={"seq": target},
            device_id_type=MESH,
        )
        copies.append((target != me, copy))
        pl.when(target != me)(copy.start)
    own = pltpu.make_async_copy(
        src.at[lax.rem(me, count)], dst.at[h], link.send_sems.at[base + count]
    )
    mine = me // count == place.q
    pl.when(mine)(own.start)

    def done():
        pl.when(mine)(own.wait)
        for half in range(count):
            copy = pltpu.make_async_remote_copy(
                src_ref=src.at[0],
                dst_ref=dst.at[half],
                send_sem=link.send_sems.at[base],
                recv_sem=link.recv_sems.at[base + half],
                device_id={"seq": me},
                device_id_type=MESH,
            )
            pl.when(half * dims["group"] + me // count != me)(copy.wait_recv)
        for other, copy in copies:
            pl.when(other)(copy.wait_send)

    return done


def half_mask(rows, half):
    return (lax.broadcasted_iota(jnp.int32, (rows, 128), 1) // HEAD_DIM) == half


def attend(q_ref, k_ref, v_ref, valid, p_ref, mix_ref, causal, block, first, last, pump):
    keys = k_ref.shape[0]
    for pair in range(q_ref.shape[1] // 128):
        lanes = slice(pair * 128, pair * 128 + 128)
        for start in range(first, last, block):
            stop = start + block if causal else keys
            halves = []
            for half in range(2):
                query = q_ref[start : start + block, lanes]
                query = jnp.where(half_mask(block, half), query, jnp.zeros_like(query))
                scores = nt(k_ref[:stop, lanes], query) * SCALE
                scores = jnp.where(valid(start, stop), scores, NEG)
                top = jnp.max(scores, axis=0, keepdims=True)
                grown = jnp.exp(scores - top)
                probs = (grown * (1.0 / jnp.sum(grown, axis=0, keepdims=True))).astype(BF)
                p_ref[2 * pair + half, :stop, start : start + block] = probs
                mixed = tn(v_ref[:stop, lanes], probs)
                halves.append(mixed[half * HEAD_DIM : (half + 1) * HEAD_DIM])
            mix_ref[start : start + block, lanes] = jnp.concatenate(halves, axis=0).T.astype(BF)
        if pair == 0:
            pump()


def attend_back(
    q_ref, k_ref, v_ref, p_ref, grad_ref, dq_ref, dk_ref, dv_ref, causal, block, first, last,
    pump,
):
    keys = k_ref.shape[0]
    for pair in range(q_ref.shape[1] // 128):
        lanes = slice(pair * 128, pair * 128 + 128)
        for start in range(first, last, block):
            stop = start + block if causal else keys
            halves = []
            sum_k, sum_v = None, None
            for half in range(2):
                mask = half_mask(block, half)
                query = q_ref[start : start + block, lanes]
                query = jnp.where(mask, query, jnp.zeros_like(query))
                grad = grad_ref[start : start + block, lanes]
                grad = jnp.where(mask, grad, jnp.zeros_like(grad))
                low = p_ref[2 * pair + half, :stop, start : start + block]
                probs = low.astype(F32)
                grad_probs = nt(v_ref[:stop, lanes], grad)
                delta = jnp.sum(probs * grad_probs, axis=0, keepdims=True)
                grad_scores = (probs * (grad_probs - delta)).astype(BF)
                turned = tn(k_ref[:stop, lanes], grad_scores) * SCALE
                halves.append(turned[half * HEAD_DIM : (half + 1) * HEAD_DIM])
                new_k, new_v = nn(grad_scores, query), nn(low, grad)
                sum_k = new_k if sum_k is None else sum_k + new_k
                sum_v = new_v if sum_v is None else sum_v + new_v
            old = start if causal else (keys if start else 0)
            for ref, value in ((dk_ref, sum_k), (dv_ref, sum_v)):
                if old:
                    ref[:old, lanes] = ref[:old, lanes] + value[:old]
                if old < stop:
                    ref[old:stop, lanes] = value[old:]
            dq_ref[start : start + block, lanes] = jnp.concatenate(halves, axis=0).T.astype(BF)
        if pair == 0:
            pump()


class Box:
    def __init__(self, names, refs):
        for name, ref in zip(names, refs):
            setattr(self, name, ref)


class Quarters:
    def __init__(self, link, place, grad, box_names, box):
        self.link, self.place, self.grad = link, place, grad
        self.recv, self.sums, self.last, self.lines, self.total, self.moved, self.done, self.out = (
            getattr(box, name) if name else None for name in box_names
        )

    def send(self):
        place, piece, link = self.place, self.piece, self.link
        self.steps = []
        for i, near in enumerate((place.tx, place.ty)):
            copies = [
                (self.grad.at[piece(near, i)], self.recv.at[i, 0], place.line(near)),
                (self.grad.at[piece(place.txy, i)], self.recv.at[i, 1], place.line(near)),
            ]
            self.steps.append(link.batch(copies, self.recv.at[i]))
        self.flying = list(self.steps)

    def turn(self):
        place, piece, link = self.place, self.piece, self.link
        steps = []
        for i, far in enumerate((place.ty, place.tx)):
            self.steps[i].wait_recv()
            value = self.grad[piece(far, i)].astype(F32) + self.recv[i, 1].astype(F32)
            self.sums[i] = value.astype(BF)
            steps.append(link.send(self.sums.at[i], self.last.at[i], place.line(far)))
        self.steps = steps
        self.flying += steps

    def add(self):
        place = self.place
        for i in range(2):
            self.steps[i].wait_recv()
            value = self.grad[self.piece(place.t, i)].astype(F32)
            value = value + self.recv[i, 0].astype(F32) + self.last[i].astype(F32)
            self.total[self.halves(i)] = value.astype(BF)
        if self.lines is not None:
            share, items = place.dims["share"], place.dims["items"]
            copies = []
            for a in range(1, items // share):
                target = {"items": lax.rem(place.it + a * share, items)}
                copies.append((self.total, self.lines.at[a - 1], target))
            step = self.link.batch(copies, self.lines)
            step.wait()
            self.link.open.pop()
            value = self.total[...].astype(F32)
            for a in range(1, items // share):
                value = value + self.lines[a - 1].astype(F32)
            self.total[...] = value.astype(BF)
        self.along()

    def gather(self):
        self.close()
        place, out = self.place, self.out
        self.own = self.link.local(self.done, out.at[place.t])
        self.near = [
            self.link.send(self.done, out.at[place.t], place.line(near))
            for near in (place.tx, place.ty)
        ]

    def forward(self):
        place, out, link = self.place, self.out, self.link
        self.steps = []
        for i, (source, near) in enumerate(((place.ty, place.tx), (place.tx, place.ty))):
            self.near[1 - i].wait_recv()
            part = out.at[self.cut(source, i)]
            self.steps.append(link.send(part, part, place.line(near)))

    def finish(self):
        arrive(self.steps)
        self.own.wait()


class Hidden(Quarters):
    def piece(self, t, i):
        rows = self.grad.shape[2] // 2
        return slice(None), t, slice(i * rows, (i + 1) * rows)

    def halves(self, i):
        rows = self.grad.shape[2] // 2
        return slice(None), slice(i * rows, (i + 1) * rows)

    def cut(self, t, i):
        rows = self.out.shape[1] // 2
        return t, slice(i * rows, (i + 1) * rows)

    def along(self):
        self.steps = [self.link.send(self.total.at[1], self.moved, self.place.partner())]

    def close(self):
        arrive(self.steps)
        self.done[...] = (self.total[0].astype(F32) + self.moved[...].astype(F32)).astype(BF)


class Columns(Quarters):
    def piece(self, t, i):
        blocks = self.grad.shape[1] // 2
        return slice(None), slice(i * blocks, (i + 1) * blocks), t

    def halves(self, i):
        blocks = self.grad.shape[1] // 2
        return slice(None), slice(i * blocks, (i + 1) * blocks)

    def cut(self, t, i):
        cols = self.out.shape[3] // 2
        return t, slice(None), slice(None), slice(i * cols, (i + 1) * cols)

    def along(self):
        place = self.place
        copies = []
        for d in range(1, place.dims["seq"]):
            target = place.seq_shift(d)
            copies.append((self.total.at[:, target], self.moved.at[place.me], {"seq": target}))
        self.steps = [self.link.batch(copies, self.moved.at[0 : place.dims["seq"] - 1])]
        self.own = self.link.local(self.total.at[:, place.me], self.moved.at[place.me])

    def close(self):
        arrive(self.steps)
        self.own.wait()
        dims = self.place.dims
        group, width = dims["group"], dims["width"]
        for index in range(3):
            for q in range(group):
                value = self.moved[q, index].astype(F32)
                for half in range(1, dims["items_dev"]):
                    value = value + self.moved[half * group + q, index].astype(F32)
                self.done[index, :, q * width : (q + 1) * width] = value.astype(BF)


class Rows(Quarters):
    def piece(self, t, i):
        return i, t

    def halves(self, i):
        return i

    def cut(self, t, i):
        cols = self.out.shape[2] // 2
        return t, slice(None), slice(i * cols, (i + 1) * cols)

    def along(self):
        self.moved_done = rows_back(self.link, self.place, self.total, self.moved)

    def close(self):
        self.moved_done()
        value = self.moved[0].astype(F32)
        for half in range(1, self.place.dims["items_dev"]):
            value = value + self.moved[half].astype(F32)
        self.done[...] = value.astype(BF)


class Stage:
    def __init__(self, sems, place, part, bufs, mid, spread, before):
        self.link, self.place, self.mid, self.spread = Link(*sems), place, mid, spread
        self.before = before
        self.reduce = Reduce(self.link, place, part, bufs)
        self.started, self.waits = {}, {}

    def start(self, k):
        self.reduce.start(k, k)

    def middle(self, k):
        self.reduce.middle(k, k)

    def end(self, k):
        place, spread = self.place, self.spread
        spread[k, place.c, place.b1, place.b0] = self.mid(k, self.reduce.end(k))
        self.started[k] = spread_start(self.link, place, spread, k)

    def forward(self, k):
        self.waits[k] = spread_end(self.link, self.place, self.spread, k, self.started[k])

    def arrive(self, k):
        arrive(self.waits[k])

    def release(self, k):
        done = (self.reduce.zero[k], self.reduce.one[k])
        for copy in done:
            copy.wait_send()
        late = {id(copy) for copy in done}
        self.link.open = [copy for copy in self.link.open if id(copy) not in late]


def stage_steps(stage, compute, flight=None, ended=None, after=None):
    before = stage.before
    compute(0, (lambda: before.forward(1)) if before else (lambda: None))
    stage.start(0)
    compute(1, lambda: None)
    stage.start(1)
    if before:
        before.link.finish()
    stage.middle(0)
    stage.middle(1)
    if flight:
        flight()
    stage.end(0)
    stage.end(1)
    if ended:
        ended()
    stage.forward(0)
    if after:
        after()


def layer_kernel(dims, names, *refs):
    b = Box(names, refs)
    b.grad_third, b.grad_r2, b.grad_r1, b.gc1_all = b.first, b.second, b.first, b.gy_all
    place = Place(dims)
    sems = b.send_sems, b.recv_sems
    link = Link(*sems, dims["chain"])
    width, block, items_dev = dims["width"], dims["block"], dims["items_dev"]
    h, t, q_place = place.h, place.t, place.q
    c, b1, b0 = place.c, place.b1, place.b0
    partner = place.partner()
    wr = b.w_sq.shape[0] // dims["share"]
    model = dims["model"]
    total_dec, total_mem = dims["total_dec"], dims["total_mem"]
    rb = b.dec.shape[1]

    def rows_of(ref, cols=model):
        return ref[...].reshape(-1, ref.shape[-1])[:, :cols]

    def chunk(ref, k):
        return ref[k].reshape(-1, model)

    half_rows = total_dec // 2

    def span(k):
        return slice(k * half_rows, (k + 1) * half_rows)

    def put(k, value, before=None):
        if before:
            before.release(k)
        b.part[k] = value.astype(BF).reshape(b.part.shape[1:])

    def weight(ref, index):
        return ref[index].reshape(model, width)

    weights = (b.w_sq, b.w_sk, b.w_sv, b.w_so, b.w_ck, b.w_cv, b.w_cq, b.w_co)
    rows_t = pl.ds(pl.multiple_of(t * wr, wr), wr)
    index = link.index()
    for i, w in enumerate(weights):
        pltpu.make_async_copy(w.at[rows_t], b.staged.at[i], b.send_sems.at[index]).start()
    staged = pltpu.make_async_copy(b.staged, b.staged, b.send_sems.at[index])
    own_fin = link.local(b.f_in, b.own_fin)
    own_fout = link.local(b.f_out, b.own_fout)
    greet(place.seq_peers() + place.items_peers())

    swap_x = link.send(b.dec.at[1 - h], b.x_all.at[h, c, b1, b0], partner)
    def share_columns(dst):
        blocks = dims["seq"] // 2
        return Share(
            link, place, lambda t: dst.at[:, t],
            lambda t, i: dst.at[i * blocks : (i + 1) * blocks, t],
        )

    def share_rows(dst):
        return Share(link, place, lambda t: dst.at[:, t], lambda t, i: dst.at[i, t])

    def share_hidden(dst):
        rows = dst.shape[1] // 2
        return Share(
            link, place, lambda t: dst.at[t], lambda t, i: dst.at[t, i * rows : (i + 1) * rows]
        )

    def join_cells():
        mb = b.cells.shape[1]
        same = lax.broadcasted_iota(jnp.int32, (mb, mb), 0) == lax.broadcasted_iota(
            jnp.int32, (mb, mb), 1
        )
        for k in range(items_dev):
            flags = (b.cells[k : k + 1] == 1).astype(F32)
            column = jnp.sum(jnp.where(same, flags, 0.0), axis=1, keepdims=True)
            b.mem_cells[k, :, :model] = b.mem[k]
            b.mem_cells[k, :, model:] = jnp.broadcast_to(column, (mb, 128)).astype(BF)

    b.x_all[h, c, b1, b0] = b.dec[h]
    first_x = spread_start(link, place, b.x_all, h)
    staged.wait()
    steps, own_self = columns_out(link, place, b.staged.at[0:3], b.o_self, width)
    waits = spread_end(link, place, b.x_all, h, first_x)
    swap_x.wait_recv()
    second_x = spread_start(link, place, b.x_all, 1 - h)
    so_arrived, so_sent = rows_out(link, place, b.staged.at[3], b.o_so)
    steps.wait_recv()
    own_self.wait()
    self_share = [share_columns(b.o_self.at[i]) for i in range(3)]
    waits += spread_end(link, place, b.x_all, 1 - h, second_x)
    so_arrived()
    so_share = share_rows(b.o_so)
    cross_steps, own_cross = columns_out(link, place, b.staged.at[4:7], b.o_cross, width)
    co_arrived, co_sent = rows_out(link, place, b.staged.at[7], b.o_co)
    join_cells()
    b.m_all[h, c, b1, b0] = b.mem_cells[h]
    swap_m = link.send(b.mem_cells.at[1 - h], b.m_all.at[h, c, b1, b0], partner)
    first_m = spread_start(link, place, b.m_all, h)
    own_fin.wait()
    own_fout.wait()
    fr, gr = b.o_fin.shape[1], b.o_fout.shape[1]
    step_fin = link.send(b.own_fin.at[pl.ds(pl.multiple_of(t * fr, fr), fr)], b.o_fin.at[t], partner)
    for share in self_share:
        share.forward()

    arrive(waits)
    rows = rows_of(b.x_all)
    for index, dst in enumerate((b.sq, b.sk, b.sv)):
        self_share[index].wait()
        dst[...] = nn(rows, weight(b.o_self, index)).astype(BF)
    so_share.forward()
    cross_steps.wait_recv()
    own_cross.wait()
    cross_share = [share_columns(b.o_cross.at[i]) for i in range(3)]
    co_arrived()
    co_share = share_rows(b.o_co)
    mem_waits = spread_end(link, place, b.m_all, h, first_m)
    swap_m.wait_recv()
    second_m = spread_start(link, place, b.m_all, 1 - h)
    length, mem_length = b.dec_len[h], b.mem_len[h]

    def self_ok(start, stop):
        keys = lax.broadcasted_iota(jnp.int32, (stop, block), 0)
        spots = lax.broadcasted_iota(jnp.int32, (stop, block), 1) + start
        return (keys <= spots) & (keys < length)

    bufs = [b.recv0, b.send1, b.recv1, b.keep1]
    if dims["bits"] == 3:
        bufs += [b.send2, b.recv2]

    def forward(index, res, summed, out):
        def mid(k, total):
            value = res(k) + total
            summed[k] = value
            normed, _ = moments(value)
            result = normed * b.gain[index : index + 1] + b.bias[index : index + 1]
            out[k] = result
            return result.astype(BF)

        return mid

    def self_part(k, pump):
        attend(
            b.sq, b.sk, b.sv, self_ok, b.sp, b.smix, True, block,
            k * half_rows, (k + 1) * half_rows, pump,
        )
        if k == 0:
            so_share.wait()
        put(k, nn(b.smix[span(k)], rows_of(b.o_so)))

    def memory_part():
        arrive(mem_waits)
        mems = rows_of(b.m_all)
        cross_share[0].wait()
        b.ck[...] = nn(mems, weight(b.o_cross, 0)).astype(BF)
        cross_share[1].wait()
        b.cv[...] = nn(mems, weight(b.o_cross, 1)).astype(BF)
        spots = lax.broadcasted_iota(jnp.int32, (total_mem, 128), 0)
        cells = b.m_all[...].reshape(-1, b.m_all.shape[-1])[:, model:].astype(F32)
        b.keep[...] = ((spots < mem_length) & ((cells > 0.5) | (spots == 0))).astype(F32)

    stage = Stage(
        sems, place, b.part, bufs,
        forward(0, lambda k: b.x_all[k, c, b1, b0].astype(F32), b.sum_one, b.first), b.first_all, None,
    )
    def cross_weights():
        rows = pl.ds(pl.multiple_of(t * gr, gr), gr)
        steps_fout.append(link.send(b.own_fout.at[rows], b.o_fout.at[t], partner))
        mem_waits.extend(spread_end(link, place, b.m_all, 1 - h, second_m))
        for share in cross_share + [co_share]:
            share.forward()
        step_fin.wait_recv()
        ffn_share.append(share_hidden(b.o_fin))

    ffn_share, steps_fout = [], []
    stage_steps(stage, self_part, after=cross_weights)
    memory_part()
    b.c_own[h] = b.cot[h]

    def cross_part(k, pump):
        last.arrive(k)
        if k == 0:
            cross_share[2].wait()
        b.cq[span(k)] = nn(chunk(b.first_all, k), weight(b.o_cross, 2)).astype(BF)
        attend(
            b.cq, b.ck, b.cv, lambda start, stop: b.keep[:, 0:1] > 0.5, b.cp, b.cmix, False, block,
            k * half_rows, (k + 1) * half_rows, pump,
        )
        if k == 0:
            co_share.wait()
        put(k, nn(b.cmix[span(k)], rows_of(b.o_co)), last)

    last = stage
    stage = Stage(
        sems, place, b.part, bufs, forward(1, lambda k: b.first[k], b.sum_two, b.second),
        b.second_all, last,
    )
    def ffn_weights():
        ffn_share[0].forward()
        arrive(steps_fout)
        ffn_share.append(share_hidden(b.o_fout))

    stage_steps(stage, cross_part, ffn_weights)
    swap_c = link.send(b.cot.at[1 - h], b.c_own.at[h], partner)

    w_ins = (lambda: b.own_fin[...], lambda: b.o_fin[...].reshape(model, -1))
    w_outs = (lambda: b.own_fout[...], lambda: b.o_fout[...].reshape(-1, model))
    hidden = b.own_fin.shape[1]
    last_second = stage

    def ffn_part(k, pump):
        last_second.arrive(k)
        if k == 0:
            ffn_share[0].wait()
        rows = chunk(b.second_all, k)
        for index in range(2):
            if index:
                pump()
            pre = nn(rows, w_ins[index]())
            cdf = 0.5 * (1.0 + lax.erf(pre * (0.5**0.5)))
            cols = slice(index * hidden, (index + 1) * hidden)
            b.act[span(k), cols] = (pre * cdf).astype(BF)
            b.slope[span(k), cols] = (
                cdf + pre * (jnp.exp(-0.5 * pre * pre) * 0.3989422804014327)
            ).astype(BF)
        if k == 0:
            ffn_share[1].forward()
            ffn_share[1].wait()
        total = nn(b.act[span(k), :hidden], w_outs[0]())
        put(k, total + nn(b.act[span(k), hidden:], w_outs[1]()), last_second)

    swap_c.wait_recv()

    def add_sums(index, k, normed, grad):
        new = (jnp.sum(grad * normed, axis=0, keepdims=True), jnp.sum(grad, axis=0, keepdims=True))
        for row, value in zip((index, 3 + index), new):
            b.sums[row : row + 1] = value if k == 0 else b.sums[row : row + 1] + value

    def turn(k, total):
        gain = b.gain[2:3]
        normed, inv = moments(b.second[k] + total)
        spots = lax.broadcasted_iota(jnp.int32, (rb, model), 0) + (k * dims["group"] + q_place) * rb
        kept = spots < length
        b.layer[k] = jnp.where(kept, normed * gain + b.bias[2:3], 0.0).astype(BF)
        grad = jnp.where(kept, b.c_own[k].astype(F32), 0.0)
        add_sums(2, k, normed, grad)
        result = norm_back(normed, inv, gain, grad)
        b.grad_third[k] = result
        return result.astype(BF)

    stage = Stage(sems, place, b.part, bufs, turn, b.gy_all, last_second)
    stage_steps(stage, ffn_part)

    last_turn = stage

    way_fout = Hidden(
        link, place, b.g_fout, ("q_fout", "t_fout", "u_fout", dims["lines"] and "l_fout", "s_fout", "z_fout", "d_fout", "r_fout"), b
    )
    def out_grads():
        grad = rows_of(b.gy_all)
        for index in range(2):
            cols = slice(index * hidden, (index + 1) * hidden)
            value = tn(b.act[:, cols], grad)
            b.g_fout[index] = value.astype(BF).reshape(b.g_fout.shape[1:])
        way_fout.send()

    def ffn_back(k, pump):
        last_turn.arrive(k)
        if k == 1:
            out_grads()
        grad = chunk(b.gy_all, k)
        total = None
        for index in range(2):
            if index:
                pump()
            cols = slice(index * hidden, (index + 1) * hidden)
            grad_pre = (nt(grad, w_outs[index]()) * b.slope[span(k), cols].astype(F32)).astype(BF)
            b.slope[span(k), cols] = grad_pre
            term = nt(grad_pre, w_ins[index]())
            total = term if total is None else total + term
        put(k, total, last_turn)

    way_fin = Hidden(
        link, place, b.g_fin, ("q_fin", "t_fin", "u_fin", dims["lines"] and "l_fin", "s_fin", "z_fin", "d_fin", "r_fin"), b
    )
    way_cross = Columns(
        link, place, b.g_cross, ("q_cross", "t_cross", "u_cross", dims["lines"] and "l_cross", "s_cross", "z_cross", "d_cross", "r_cross"), b
    )
    way_self = Columns(
        link, place, b.g_self, ("q_self", "t_self", "u_self", dims["lines"] and "l_self", "s_self", "z_self", "d_self", "r_self"), b
    )
    way_co = Rows(
        link, place, b.g_co, ("q_co", "t_co", "u_co", dims["lines"] and "l_co", "s_co", "z_co", "d_co", "r_co"), b
    )
    way_so = Rows(
        link, place, b.g_so, ("q_so", "t_so", "u_so", dims["lines"] and "l_so", "s_so", "z_so", "d_so", "r_so"), b
    )

    def backward(index, res, summed, out):
        def mid(k, total):
            normed, inv = moments(summed[k])
            grad = res[k] + total
            add_sums(index, k, normed, grad)
            result = norm_back(normed, inv, b.gain[index : index + 1], grad)
            out[k] = result
            return result.astype(BF)

        return mid

    def in_grads():
        rows = rows_of(b.second_all)
        for index in range(2):
            cols = slice(index * hidden, (index + 1) * hidden)
            value = tn(rows, b.slope[:, cols])
            b.g_fin[index] = value.astype(BF).reshape(b.g_fin.shape[1:])
        way_fin.send()

    stage = Stage(
        sems, place, b.part, bufs, backward(1, b.grad_third, b.sum_two, b.grad_r2), b.gc2_all,
        last_turn,
    )
    stage_steps(stage, ffn_back, in_grads)

    last_back = stage

    def cross_back(k, pump):
        last_back.arrive(k)
        b.dmix[span(k)] = nt(chunk(b.gc2_all, k), rows_of(b.o_co)).astype(BF)
        attend_back(
            b.cq, b.ck, b.cv, b.cp, b.dmix, b.dq, b.sum_dk, b.sum_dv, False, block,
            k * half_rows, (k + 1) * half_rows, pump,
        )
        put(k, nt(b.dq[span(k)], weight(b.o_cross, 2)), last_back)
        if k == 1:
            way_fout.turn()

    def cross_grads():
        mems = rows_of(b.m_all)
        shape = b.g_cross.shape[1:]
        b.dck[...] = (b.sum_dk[:total_mem] * SCALE).astype(BF)
        b.dcv[...] = b.sum_dv[:total_mem].astype(BF)
        b.g_cross[0] = tn(rows_of(b.first_all), b.dq[...]).astype(BF).reshape(shape)
        b.g_cross[1] = tn(mems, b.dck[...]).astype(BF).reshape(shape)
        b.g_cross[2] = tn(mems, b.dcv[...]).astype(BF).reshape(shape)
        way_cross.send()
        b.g_co[...] = tn(b.cmix[...], rows_of(b.gc2_all)).astype(BF).reshape(b.g_co.shape)
        way_co.send()
        way_fin.turn()

    def part_mem():
        value = nt(b.dck[...], weight(b.o_cross, 0)) + nt(b.dcv[...], weight(b.o_cross, 1))
        b.part_m[...] = value.astype(BF).reshape(b.part_m.shape)
        for index in range(2):
            red_m.start(index, ks[index])

    stage = Stage(
        sems, place, b.part, bufs, backward(0, b.grad_r2, b.sum_one, b.grad_r1), b.gc1_all,
        last_back,
    )
    ks = (1 - h, h)
    mem_bufs = [b.recv0_m, b.send1_m, b.recv1_m, b.keep1_m]
    if dims["bits"] == 3:
        mem_bufs += [b.send2_m, b.recv2_m]
    red_m = Reduce(link, place, b.part_m, mem_bufs)
    stage_steps(stage, cross_back, cross_grads, part_mem)

    swap_l = link.send(b.layer.at[1 - h], b.layer_out.at[h], partner)
    b.layer_out[h] = b.layer[h]
    way_fout.add()
    for k in range(2):
        stage.arrive(k)
        pump = (lambda: stage.forward(1)) if k == 0 else (lambda: None)
        b.dmix[span(k)] = nt(chunk(b.gc1_all, k), rows_of(b.o_so)).astype(BF)
        attend_back(
            b.sq, b.sk, b.sv, b.sp, b.dmix, b.dq, b.sum_dk, b.sum_dv, True, block,
            k * half_rows, (k + 1) * half_rows, pump,
        )
        red_m.middle(k, ks[k])
    b.dsk[...] = (b.sum_dk[...] * SCALE).astype(BF)
    b.dsv[...] = b.sum_dv[...].astype(BF)
    for k in range(2):
        total = nt(b.dq[span(k)], weight(b.o_self, 0)) + nt(b.dsk[span(k)], weight(b.o_self, 1))
        put(k, total + nt(b.dsv[span(k)], weight(b.o_self, 2)), stage)
    stage.link.finish()
    chain = Link(*sems)
    red_x = Reduce(chain, place, b.part, bufs)
    for index in range(2):
        red_x.start(index, ks[index])
    way_cross.turn()
    way_co.turn()
    way_fin.add()
    rows = rows_of(b.x_all)
    shape = b.g_self.shape[1:]
    b.g_self[0] = tn(rows, b.dq[...]).astype(BF).reshape(shape)
    b.g_self[1] = tn(rows, b.dsk[...]).astype(BF).reshape(shape)
    b.g_self[2] = tn(rows, b.dsv[...]).astype(BF).reshape(shape)
    way_self.send()
    b.g_so[...] = tn(b.smix[...], rows_of(b.gc1_all)).astype(BF).reshape(b.g_so.shape)
    way_so.send()
    for index in range(2):
        red_x.middle(index, ks[index])
    b.send_m[...] = red_m.end(0).astype(BF)
    swap_m = link.send(b.send_m, b.recv_m, partner)
    b.grad_mem[h] = red_m.end(1)
    copies = []
    for d in range(1, dims["seq"]):
        copies.append((b.sums, b.sums_seq.at[d - 1], {"seq": place.seq_shift(d)}))
    seq_sums = link.batch(copies, b.sums_seq)
    way_cross.add()
    way_co.add()
    b.send_x[...] = (red_x.end(0) + b.grad_r1[1 - h]).astype(BF)
    swap_x = link.send(b.send_x, b.recv_x, partner)
    b.grad_dec[h] = red_x.end(1) + b.grad_r1[h]
    way_fout.gather()
    way_self.turn()
    way_so.turn()
    way_fin.gather()
    way_fout.forward()
    way_self.add()
    way_so.add()
    way_cross.gather()
    way_co.gather()
    way_fin.forward()
    seq_sums.wait_recv()
    value = b.sums[...]
    for d in range(1, dims["seq"]):
        value = value + b.sums_seq[d - 1]
    b.sums_line[...] = value
    copies = []
    for e in range(1, dims["items"]):
        target = {"items": lax.rem(place.it + e, dims["items"])}
        copies.append((b.sums_line, b.sums_items.at[e - 1], target))
    item_sums = link.batch(copies, b.sums_items)
    swap_x.wait_recv()
    b.grad_dec[1 - h] = b.recv_x[...].astype(F32)
    swap_m.wait_recv()
    b.grad_mem[1 - h] = b.recv_m[...].astype(F32)
    swap_l.wait_recv()
    way_self.gather()
    way_so.gather()
    way_cross.forward()
    way_co.forward()
    item_sums.wait_recv()
    value = b.sums_line[...]
    for e in range(1, dims["items"]):
        value = value + b.sums_items[e - 1]
    b.sums_out[...] = value
    way_self.forward()
    way_so.forward()
    for way in (way_fout, way_fin, way_cross, way_co, way_self, way_so):
        way.finish()
    so_sent()
    co_sent()
    chain.finish()
    link.finish()


def shape(dims, dtype):
    return jax.ShapeDtypeStruct(tuple(dims), dtype)


def outputs_kernel(layer, dec, mem, cross, own, co, so, fin, fout, sums, *outs):
    o_layer, o_dec, o_mem = outs[:3]
    o_layer[...] = layer[...]
    o_dec[...] = dec[...]
    o_mem[...] = mem[...]
    for index in range(3):
        outs[3 + index][...] = own[0, index].astype(F32)
        outs[7 + index][...] = cross[0, index].astype(F32)
    outs[6][...] = so[0].astype(F32)
    outs[10][...] = co[0].astype(F32)
    outs[11][...] = fin[0].astype(F32)
    outs[12][...] = fout[0].astype(F32)
    outs[13][...] = sums[0:3]
    outs[14][...] = sums[3:6]


def shards(
    mesh, dec_in, memory, dec_len, mem_len, cell_mask, self_query, self_key, self_value, self_out,
    cross_query, cross_key, cross_value, cross_out, ffn_in, ffn_out, norm_gain, norm_bias, cotangent,
):
    items_dev, rb, model = dec_in.shape
    mb = memory.shape[1]
    seq, items = mesh.shape["seq"], mesh.shape["items"]
    group = seq // items_dev
    share = 4
    bits = group.bit_length() - 1
    chips = group // 4
    width = model // group
    total_dec, total_mem = rb * seq, mb * seq
    heads = width // HEAD_DIM
    hidden = ffn_in.shape[1]
    wr = self_query.shape[0] // share
    fr, gr = model // share, hidden // share
    lines = items // share - 1
    dims = {
        "items_dev": items_dev, "items": items, "seq": seq, "group": group, "share": share,
        "bits": bits, "chips": chips, "width": width, "model": model, "block": 256,
        "total_dec": total_dec, "total_mem": total_mem, "lines": lines,
        "chain": 12 + 2 * (bits - 2),
    }
    ins = [
        ("dec", dec_in, VM), ("mem", memory, VM), ("cells", cell_mask, VM), ("cot", cotangent, VM),
        ("dec_len", dec_len, SM), ("mem_len", mem_len, SM),
        ("w_sq", self_query, HBM), ("w_sk", self_key, HBM), ("w_sv", self_value, HBM),
        ("w_so", self_out, HBM), ("w_cq", cross_query, HBM), ("w_ck", cross_key, HBM),
        ("w_cv", cross_value, HBM), ("w_co", cross_out, HBM), ("f_in", ffn_in, HBM),
        ("f_out", ffn_out, HBM), ("gain", norm_gain, VM), ("bias", norm_bias, VM),
    ]
    own, own_m = (items_dev, rb, model), (items_dev, mb, model)
    grid = (items_dev, chips, 2, 2)
    outs = [
        ("layer_out", own, BF, VM), ("grad_dec", own, F32, VM), ("grad_mem", own_m, F32, VM),
        ("sums_out", (8, model), F32, VM),
        ("r_cross", (share, 3, wr, model), BF, HBM), ("r_self", (share, 3, wr, model), BF, HBM),
        ("r_co", (share, wr, model), BF, HBM), ("r_so", (share, wr, model), BF, HBM),
        ("r_fin", (share, fr, hidden), BF, HBM), ("r_fout", (share, gr, model), BF, HBM),
    ]
    cols = (3, seq, share, wr, width)
    scratch = [
        ("x_all", grid + (rb, model), BF), ("m_all", grid + (mb, model + 128), BF),
        ("mem_cells", (items_dev, mb, model + 128), BF), ("c_own", own, BF), ("staged", (8, wr, model), BF),
        ("own_fin", (model, hidden), BF), ("own_fout", (hidden, model), BF),
        ("o_self", cols, BF), ("o_cross", cols, BF),
        ("o_so", (items_dev, share, wr, model), BF), ("o_co", (items_dev, share, wr, model), BF),
        ("o_fin", (share, fr, hidden), BF), ("o_fout", (share, gr, model), BF),
        ("sq", (total_dec, width), BF), ("sk", (total_dec, width), BF), ("sv", (total_dec, width), BF),
        ("cq", (total_dec, width), BF), ("ck", (total_mem, width), BF), ("cv", (total_mem, width), BF),
        ("sp", (heads, total_dec, total_dec), BF), ("cp", (heads, total_mem, total_dec), BF),
        ("smix", (total_dec, width), BF), ("cmix", (total_dec, width), BF),
        ("keep", (total_mem, 128), F32),
        ("part", grid + (rb, model), BF), ("part_m", grid + (mb, model), BF),
        ("first_all", grid + (rb, model), BF), ("second_all", grid + (rb, model), BF),
        ("gy_all", grid + (rb, model), BF), ("gc2_all", grid + (rb, model), BF),
        ("sum_one", own, F32), ("sum_two", own, F32), ("first", own, F32), ("second", own, F32),
        ("layer", own, BF), ("sum_dk", (total_dec, width), F32), ("sum_dv", (total_dec, width), F32),
        ("act", (total_dec, 2 * hidden), BF), ("slope", (total_dec, 2 * hidden), BF),
        ("dmix", (total_dec, width), BF), ("dq", (total_dec, width), BF),
        ("dsk", (total_dec, width), BF), ("dsv", (total_dec, width), BF),
        ("dck", (total_mem, width), BF), ("dcv", (total_mem, width), BF),
        ("send_x", (rb, model), BF), ("recv_x", (rb, model), BF),
        ("send_m", (mb, model), BF), ("recv_m", (mb, model), BF),
        ("sums", (8, model), F32), ("sums_line", (8, model), F32),
        ("sums_seq", (seq - 1, 8, model), F32), ("sums_items", (items - 1, 8, model), F32),
    ]
    for name, rows in (("", rb), ("_m", mb)):
        scratch += [
            ("recv0" + name, (items_dev, chips, 2, rows, model), BF),
            ("send1" + name, (items_dev, chips, rows, model), BF),
            ("recv1" + name, (items_dev, chips, rows, model), BF),
            ("keep1" + name, (items_dev, chips, rows, model), F32),
        ]
        if bits == 3:
            scratch += [
                ("send2" + name, (items_dev, rows, model), BF),
                ("recv2" + name, (items_dev, rows, model), BF),
            ]
    for name, grad, quarter, piece, moved, done in (
        ("fin", (2, share, fr, hidden), (2, fr, hidden), (2, fr // 2, hidden), (fr, hidden),
         (fr, hidden)),
        ("fout", (2, share, gr, model), (2, gr, model), (2, gr // 2, model), (gr, model), (gr, model)),
        ("cross", cols, (3, seq, wr, width), (3, seq // 2, wr, width), (seq, 3, wr, width),
         (3, wr, model)),
        ("self", cols, (3, seq, wr, width), (3, seq // 2, wr, width), (seq, 3, wr, width),
         (3, wr, model)),
        ("co", (items_dev, share, wr, model), (items_dev, wr, model), (wr, model),
         (items_dev, wr, model), (wr, model)),
        ("so", (items_dev, share, wr, model), (items_dev, wr, model), (wr, model),
         (items_dev, wr, model), (wr, model)),
    ):
        scratch += [
            ("g_" + name, grad, BF), ("q_" + name, (2, 2) + piece, BF), ("t_" + name, (2,) + piece, BF),
            ("u_" + name, (2,) + piece, BF), ("s_" + name, quarter, BF), ("z_" + name, moved, BF),
            ("d_" + name, done, BF),
        ]
        if lines:
            scratch.append(("l_" + name, (lines,) + quarter, BF))
    copies = dims["chain"] + 145 + 12 * (bits - 2)
    names = [x[0] for x in ins + outs + scratch] + ["send_sems", "recv_sems"]
    results = pl.pallas_call(
        functools.partial(layer_kernel, dims, names),
        name="layer",
        out_shape=[shape(x[1], x[2]) for x in outs],
        in_specs=[x[2] for x in ins],
        out_specs=[x[3] for x in outs],
        scratch_shapes=[pltpu.VMEM(x[1], x[2]) for x in scratch]
        + [pltpu.SemaphoreType.DMA((copies,)), pltpu.SemaphoreType.DMA((copies,))],
        compiler_params=pltpu.CompilerParams(
            collective_id=0, has_side_effects=True, vmem_limit_bytes=VMEM_BYTES
        ),
    )(*[x[1] for x in ins])
    layer_out, grad_dec, grad_memory, sums, r_cross, r_self, r_co, r_so, r_fin, r_fout = results
    tok, mem_rows = items_dev * rb, items_dev * mb
    pieces = (
        ((tok, model), (tok // share, model), BF), ((tok, model), (tok // share, model), F32),
        ((mem_rows, model), (mem_rows // share, model), F32),
    )
    heads_in = [
        pl.BlockSpec((1, 3, wr, model), lambda i: (i, 0, 0, 0)),
        pl.BlockSpec((1, 3, wr, model), lambda i: (i, 0, 0, 0)),
        pl.BlockSpec((1, wr, model), lambda i: (i, 0, 0)),
        pl.BlockSpec((1, wr, model), lambda i: (i, 0, 0)),
        pl.BlockSpec((1, fr, hidden), lambda i: (i, 0, 0)),
        pl.BlockSpec((1, gr, model), lambda i: (i, 0, 0)),
        pl.BlockSpec((8, model), lambda i: (0, 0)),
    ]
    row_specs = [pl.BlockSpec(x[1], lambda i: (i, 0)) for x in pieces]
    square = (share * wr, model)
    outs = pl.pallas_call(
        outputs_kernel,
        name="outputs",
        grid=(share,),
        in_specs=row_specs + heads_in,
        out_specs=row_specs
        + [pl.BlockSpec((wr, model), lambda i: (i, 0))] * 8
        + [pl.BlockSpec((fr, hidden), lambda i: (i, 0)), pl.BlockSpec((gr, model), lambda i: (i, 0))]
        + [pl.BlockSpec((3, model), lambda i: (0, 0))] * 2,
        out_shape=[shape(x[0], x[2]) for x in pieces]
        + [shape(square, F32)] * 8
        + [shape((model, hidden), F32), shape((hidden, model), F32)]
        + [shape((3, model), F32)] * 2,
        compiler_params=pltpu.CompilerParams(vmem_limit_bytes=VMEM_BYTES),
    )(
        layer_out.reshape(tok, model), grad_dec.reshape(tok, model),
        grad_memory.reshape(mem_rows, model), r_cross, r_self, r_co, r_so, r_fin, r_fout, sums,
    )
    return (
        outs[0].reshape(own), outs[1].reshape(own), outs[2].reshape(own_m), *outs[3:],
    )


def solution(mesh):
    rows = P("seq", None)
    tokens = P("items", "seq", None)
    placed = (
        (tokens, tokens, P("items"), P("items"), P("items", "seq"))
        + (rows,) * 8
        + (P(None, "seq"), rows, P(), P(), tokens)
    )
    return jax.shard_map(
        functools.partial(shards, mesh),
        mesh=mesh,
        in_specs=placed,
        out_specs=(tokens,) * 3 + (rows,) * 8 + (P(None, "seq"), rows, P(), P()),
        check_vma=False,
    )
```

```python
import functools

import jax
import jax.numpy as jnp
from jax import lax
from jax.experimental import pallas as pl
from jax.experimental.pallas import tpu as pltpu
from jax.sharding import PartitionSpec as P

HEAD_DIM = 64
EPS = 1e-05
NEG = -1e30
SCALE = HEAD_DIM ** (-0.5)
BF = jnp.bfloat16
F32 = jnp.float32
VMEM_BYTES = 63 * 1024 * 1024
MESH = pl.DeviceIdType.MESH
VM = pl.BlockSpec(memory_space=pltpu.VMEM)
HBM = pl.BlockSpec(memory_space=pl.ANY)
SM = pl.BlockSpec(memory_space=pltpu.SMEM)


def nn(left, right):
    return lax.dot_general(left, right, (((1,), (0,)), ((), ())), preferred_element_type=F32)


def nt(left, right):
    return lax.dot_general(left, right, (((1,), (1,)), ((), ())), preferred_element_type=F32)


def tn(left, right):
    return lax.dot_general(left, right, (((0,), (0,)), ((), ())), preferred_element_type=F32)


class Link:
    def __init__(self, send_sems, recv_sems, first=0):
        self.send_sems, self.recv_sems, self.count, self.open = send_sems, recv_sems, first, []

    def index(self):
        self.count += 1
        return self.count - 1

    def make(self, src, dst, device, index):
        return pltpu.make_async_remote_copy(
            src_ref=src,
            dst_ref=dst,
            send_sem=self.send_sems.at[index],
            recv_sem=self.recv_sems.at[index],
            device_id=device,
            device_id_type=MESH,
        )

    def send(self, src, dst, device):
        copy = self.make(src, dst, device, self.index())
        copy.start()
        self.open.append(copy)
        return copy

    def batch(self, copies, whole):
        index = self.index()
        for copy in copies:
            self.make(*copy, index).start()
        wait = self.make(whole, whole, copies[0][2], index)
        self.open.append(wait)
        return wait

    def settle(self, copy):
        copy.wait_send()
        self.open = [other for other in self.open if other is not copy]

    def local(self, src, dst):
        copy = pltpu.make_async_copy(src, dst, self.send_sems.at[self.index()])
        copy.start()
        return copy

    def finish(self, kept=()):
        late = {id(copy) for copy in kept}
        for copy in self.open:
            if id(copy) not in late:
                copy.wait_send()
        self.open = [copy for copy in self.open if id(copy) in late]


def greet(devices):
    barrier = pltpu.get_barrier_semaphore()
    for device in devices:
        pl.semaphore_signal(barrier, inc=1, device_id=device, device_id_type=MESH)
    pl.semaphore_wait(barrier, len(devices))


class Place:
    def __init__(self, dims):
        self.dims = dims
        group, share = dims["group"], dims["share"]
        self.me = lax.axis_index("seq")
        self.h = self.me // group
        self.q = self.me % group
        self.b0 = self.q % 2
        self.b1 = (self.q // 2) % 2
        self.c = self.q // 4
        self.it = lax.axis_index("items")
        self.base = (self.it // share) * share
        self.t = self.it % share
        x, y = self.t % 2, self.t // 2
        self.tx, self.ty, self.txy = y * 2 + 1 - x, (1 - y) * 2 + x, (1 - y) * 2 + 1 - x

    def across(self, bit):
        value = (self.q // (1 << bit)) % 2
        return {"seq": self.me + (1 - 2 * value) * (1 << bit)}

    def partner(self):
        return {"seq": (1 - self.h) * self.dims["group"] + self.q}

    def seq_shift(self, d):
        return lax.rem(self.me + d, self.dims["seq"])

    def line(self, t):
        return {"items": self.base + t}

    def seq_peers(self):
        return [{"seq": self.seq_shift(d)} for d in range(1, self.dims["seq"])]

    def items_peers(self):
        count = self.dims["items"]
        return [{"items": lax.rem(self.it + e, count)} for e in range(1, count)]


def spread_start(link, place, out, k):
    bits = place.dims["bits"]
    c, b1, b0 = place.c, place.b1, place.b0
    if bits == 3:
        step = link.send(out.at[k, c, b1, b0], out.at[k, c, b1, b0], place.across(2))
        step.wait_recv()
    waits = []
    high = link.send(out.at[k, :, b1, b0], out.at[k, :, b1, b0], place.across(1))
    waits.append(link.send(out.at[k, :, b1, b0], out.at[k, :, b1, b0], place.across(0)))
    return high, waits


def spread_end(link, place, out, k, started):
    high, waits = started
    b1, b0 = place.b1, place.b0
    high.wait_recv()
    waits.append(link.send(out.at[k, :, 1 - b1, b0], out.at[k, :, 1 - b1, b0], place.across(0)))
    return waits


def columns_out(link, place, src, dst, width):
    seq, group = place.dims["seq"], place.dims["group"]
    copies = []
    for d in range(1, seq):
        target = place.seq_shift(d)
        cols = pl.ds(pl.multiple_of(lax.rem(target, group) * width, width), width)
        copies.append((src.at[:, :, cols], dst.at[:, place.me, place.t], {"seq": target}))
    steps = link.batch(copies, dst.at[:, 0 : seq - 1, place.t])
    cols = pl.ds(pl.multiple_of(place.q * width, width), width)
    return steps, link.local(src.at[:, :, cols], dst.at[:, place.me, place.t])


def rows_out(link, place, src, dst):
    dims, me = place.dims, place.me
    slot = lax.rem(me, dims["items_dev"])
    base = link.count
    link.count += dims["items_dev"] + 1
    copies = []
    for half in range(dims["items_dev"]):
        target = half * dims["group"] + me // dims["items_dev"]
        copy = pltpu.make_async_remote_copy(
            src_ref=src,
            dst_ref=dst.at[slot, place.t],
            send_sem=link.send_sems.at[base + half],
            recv_sem=link.recv_sems.at[base + slot],
            device_id={"seq": target},
            device_id_type=MESH,
        )
        copies.append((target != me, copy))
        pl.when(target != me)(copy.start)
    own = pltpu.make_async_copy(
        src, dst.at[slot, place.t], link.send_sems.at[base + dims["items_dev"]]
    )
    mine = me // dims["items_dev"] == place.q
    pl.when(mine)(own.start)

    def arrived():
        pl.when(mine)(own.wait)
        for block in range(dims["items_dev"]):
            copy = pltpu.make_async_remote_copy(
                src_ref=src,
                dst_ref=dst.at[block, place.t],
                send_sem=link.send_sems.at[base],
                recv_sem=link.recv_sems.at[base + block],
                device_id={"seq": me},
                device_id_type=MESH,
            )
            pl.when(place.q * dims["items_dev"] + block != me)(copy.wait_recv)

    def sent():
        for other, copy in copies:
            pl.when(other)(copy.wait_send)

    return arrived, sent


class Share:
    def __init__(self, link, place, slab, half):
        self.link, self.place, self.half = link, place, half
        t = place.t
        self.from_x = link.send(slab(t), slab(t), place.line(place.tx))
        self.from_y = link.send(slab(t), slab(t), place.line(place.ty))

    def forward(self):
        link, place, half = self.link, self.place, self.half
        self.from_y.wait_recv()
        part = half(place.ty, 0)
        self.steps = [link.send(part, part, place.line(place.tx))]
        self.from_x.wait_recv()
        part = half(place.tx, 1)
        self.steps.append(link.send(part, part, place.line(place.ty)))

    def wait(self):
        arrive(self.steps)


def arrive(steps):
    for step in steps:
        step.wait_recv()


class Reduce:
    def __init__(self, link, place, part, bufs):
        self.link, self.place, self.part, self.bufs = link, place, part, bufs
        self.zero, self.one = {}, {}

    def start(self, index, k):
        place = self.place
        self.zero[index] = self.link.send(
            self.part.at[k, :, :, 1 - place.b0], self.bufs[0].at[index], place.across(0)
        )

    def middle(self, index, k):
        place, part = self.place, self.part
        recv0, send1, recv1, keep1 = self.bufs[:4]
        self.zero[index].wait_recv()
        b1, b0 = place.b1, place.b0
        for c in range(part.shape[1]):
            value = part[k, c, 1 - b1, b0].astype(F32) + recv0[index, c, 1 - b1].astype(F32)
            send1[index, c] = value.astype(BF)
        self.one[index] = self.link.send(send1.at[index], recv1.at[index], place.across(1))
        for c in range(part.shape[1]):
            keep1[index, c] = part[k, c, b1, b0].astype(F32) + recv0[index, c, b1].astype(F32)

    def end(self, index):
        place = self.place
        recv1, keep1 = self.bufs[2:4]
        self.one[index].wait_recv()
        if place.dims["bits"] == 2:
            return keep1[index, 0] + recv1[index, 0].astype(F32)
        send2, recv2 = self.bufs[4:6]
        c = place.c
        send2[index] = (keep1[index, 1 - c] + recv1[index, 1 - c].astype(F32)).astype(BF)
        step = self.link.send(send2.at[index], recv2.at[index], place.across(2))
        kept = keep1[index, c] + recv1[index, c].astype(F32)
        step.wait_recv()
        return kept + recv2[index].astype(F32)


def reduce_bufs(dims, rows):
    items_dev, width, chips = dims["items_dev"], dims["model"], dims["chips"]
    bufs = [
        pltpu.VMEM((items_dev, chips, 2, rows, width), BF),
        pltpu.VMEM((items_dev, chips, rows, width), BF),
        pltpu.VMEM((items_dev, chips, rows, width), BF),
        pltpu.VMEM((items_dev, chips, rows, width), F32),
    ]
    if dims["bits"] == 3:
        bufs += [pltpu.VMEM((items_dev, rows, width), BF) for _ in range(2)]
    return bufs


def moments(value):
    mean = jnp.mean(value, axis=-1, keepdims=True)
    centered = value - mean
    inv = lax.rsqrt(jnp.mean(centered * centered, axis=-1, keepdims=True) + EPS)
    return centered * inv, inv


def norm_back(normed, inv, gain, grad):
    scaled = grad * gain
    mean = jnp.mean(scaled, axis=-1, keepdims=True)
    cross = jnp.mean(scaled * normed, axis=-1, keepdims=True)
    return inv * (scaled - mean - normed * cross)


def rows_back(link, place, src, dst):
    dims, me, h = place.dims, place.me, place.h
    count = dims["items_dev"]
    base = link.count
    link.count += count + 1
    copies = []
    for k in range(count):
        target = place.q * count + k
        copy = pltpu.make_async_remote_copy(
            src_ref=src.at[k],
            dst_ref=dst.at[h],
            send_sem=link.send_sems.at[base + k],
            recv_sem=link.recv_sems.at[base + h],
            device_id={"seq": target},
            device_id_type=MESH,
        )
        copies.append((target != me, copy))
        pl.when(target != me)(copy.start)
    own = pltpu.make_async_copy(
        src.at[lax.rem(me, count)], dst.at[h], link.send_sems.at[base + count]
    )
    mine = me // count == place.q
    pl.when(mine)(own.start)

    def done():
        pl.when(mine)(own.wait)
        for half in range(count):
            copy = pltpu.make_async_remote_copy(
                src_ref=src.at[0],
                dst_ref=dst.at[half],
                send_sem=link.send_sems.at[base],
                recv_sem=link.recv_sems.at[base + half],
                device_id={"seq": me},
                device_id_type=MESH,
            )
            pl.when(half * dims["group"] + me // count != me)(copy.wait_recv)
        for other, copy in copies:
            pl.when(other)(copy.wait_send)

    return done


def half_mask(rows, half):
    return (lax.broadcasted_iota(jnp.int32, (rows, 128), 1) // HEAD_DIM) == half


def attend(q_ref, k_ref, v_ref, valid, p_ref, mix_ref, causal, block, first, last, pump):
    keys = k_ref.shape[0]
    for pair in range(q_ref.shape[1] // 128):
        lanes = slice(pair * 128, pair * 128 + 128)
        for start in range(first, last, block):
            stop = start + block if causal else keys
            halves = []
            for half in range(2):
                query = q_ref[start : start + block, lanes]
                query = jnp.where(half_mask(block, half), query, jnp.zeros_like(query))
                scores = nt(k_ref[:stop, lanes], query) * SCALE
                scores = jnp.where(valid(start, stop), scores, NEG)
                top = jnp.max(scores, axis=0, keepdims=True)
                grown = jnp.exp(scores - top)
                probs = (grown * (1.0 / jnp.sum(grown, axis=0, keepdims=True))).astype(BF)
                p_ref[2 * pair + half, :stop, start : start + block] = probs
                mixed = tn(v_ref[:stop, lanes], probs)
                halves.append(mixed[half * HEAD_DIM : (half + 1) * HEAD_DIM])
            mix_ref[start : start + block, lanes] = jnp.concatenate(halves, axis=0).T.astype(BF)
        if pair == 0:
            pump()


def attend_back(
    q_ref, k_ref, v_ref, p_ref, grad_ref, dq_ref, dk_ref, dv_ref, causal, block, first, last,
    pump,
):
    keys = k_ref.shape[0]
    for pair in range(q_ref.shape[1] // 128):
        lanes = slice(pair * 128, pair * 128 + 128)
        for start in range(first, last, block):
            stop = start + block if causal else keys
            halves = []
            sum_k, sum_v = None, None
            for half in range(2):
                mask = half_mask(block, half)
                query = q_ref[start : start + block, lanes]
                query = jnp.where(mask, query, jnp.zeros_like(query))
                grad = grad_ref[start : start + block, lanes]
                grad = jnp.where(mask, grad, jnp.zeros_like(grad))
                low = p_ref[2 * pair + half, :stop, start : start + block]
                probs = low.astype(F32)
                grad_probs = nt(v_ref[:stop, lanes], grad)
                delta = jnp.sum(probs * grad_probs, axis=0, keepdims=True)
                grad_scores = (probs * (grad_probs - delta)).astype(BF)
                turned = tn(k_ref[:stop, lanes], grad_scores) * SCALE
                halves.append(turned[half * HEAD_DIM : (half + 1) * HEAD_DIM])
                new_k, new_v = nn(grad_scores, query), nn(low, grad)
                sum_k = new_k if sum_k is None else sum_k + new_k
                sum_v = new_v if sum_v is None else sum_v + new_v
            old = start if causal else (keys if start else 0)
            for ref, value in ((dk_ref, sum_k), (dv_ref, sum_v)):
                if old:
                    ref[:old, lanes] = ref[:old, lanes] + value[:old]
                if old < stop:
                    ref[old:stop, lanes] = value[old:]
            dq_ref[start : start + block, lanes] = jnp.concatenate(halves, axis=0).T.astype(BF)
        if pair == 0:
            pump()


class Box:
    def __init__(self, names, refs):
        for name, ref in zip(names, refs):
            setattr(self, name, ref)


class Quarters:
    def __init__(self, link, place, grad, box_names, box):
        self.link, self.place, self.grad = link, place, grad
        self.recv, self.sums, self.last, self.lines, self.total, self.moved, self.done, self.out = (
            getattr(box, name) if name else None for name in box_names
        )

    def send(self):
        place, piece, link = self.place, self.piece, self.link
        self.steps = []
        for i, near in enumerate((place.tx, place.ty)):
            copies = [
                (self.grad.at[piece(near, i)], self.recv.at[i, 0], place.line(near)),
                (self.grad.at[piece(place.txy, i)], self.recv.at[i, 1], place.line(near)),
            ]
            self.steps.append(link.batch(copies, self.recv.at[i]))
        self.flying = list(self.steps)

    def turn(self):
        place, piece, link = self.place, self.piece, self.link
        steps = []
        for i, far in enumerate((place.ty, place.tx)):
            self.steps[i].wait_recv()
            value = self.grad[piece(far, i)].astype(F32) + self.recv[i, 1].astype(F32)
            self.sums[i] = value.astype(BF)
            steps.append(link.send(self.sums.at[i], self.last.at[i], place.line(far)))
        self.steps = steps
        self.flying += steps

    def add(self):
        place = self.place
        for i in range(2):
            self.steps[i].wait_recv()
            value = self.grad[self.piece(place.t, i)].astype(F32)
            value = value + self.recv[i, 0].astype(F32) + self.last[i].astype(F32)
            self.total[self.halves(i)] = value.astype(BF)
        if self.lines is not None:
            share, items = place.dims["share"], place.dims["items"]
            copies = []
            for a in range(1, items // share):
                target = {"items": lax.rem(place.it + a * share, items)}
                copies.append((self.total, self.lines.at[a - 1], target))
            step = self.link.batch(copies, self.lines)
            step.wait()
            self.link.open.pop()
            value = self.total[...].astype(F32)
            for a in range(1, items // share):
                value = value + self.lines[a - 1].astype(F32)
            self.total[...] = value.astype(BF)
        self.along()

    def gather(self):
        self.close()
        place, out = self.place, self.out
        self.own = self.link.local(self.done, out.at[place.t])
        self.near = [
            self.link.send(self.done, out.at[place.t], place.line(near))
            for near in (place.tx, place.ty)
        ]

    def forward(self):
        place, out, link = self.place, self.out, self.link
        self.steps = []
        for i, (source, near) in enumerate(((place.ty, place.tx), (place.tx, place.ty))):
            self.near[1 - i].wait_recv()
            part = out.at[self.cut(source, i)]
            self.steps.append(link.send(part, part, place.line(near)))

    def finish(self):
        arrive(self.steps)
        self.own.wait()


class Hidden(Quarters):
    def piece(self, t, i):
        rows = self.grad.shape[2] // 2
        return slice(None), t, slice(i * rows, (i + 1) * rows)

    def halves(self, i):
        rows = self.grad.shape[2] // 2
        return slice(None), slice(i * rows, (i + 1) * rows)

    def cut(self, t, i):
        rows = self.out.shape[1] // 2
        return t, slice(i * rows, (i + 1) * rows)

    def along(self):
        self.steps = [self.link.send(self.total.at[1], self.moved, self.place.partner())]

    def close(self):
        arrive(self.steps)
        self.done[...] = (self.total[0].astype(F32) + self.moved[...].astype(F32)).astype(BF)


class Columns(Quarters):
    def piece(self, t, i):
        blocks = self.grad.shape[1] // 2
        return slice(None), slice(i * blocks, (i + 1) * blocks), t

    def halves(self, i):
        blocks = self.grad.shape[1] // 2
        return slice(None), slice(i * blocks, (i + 1) * blocks)

    def cut(self, t, i):
        cols = self.out.shape[3] // 2
        return t, slice(None), slice(None), slice(i * cols, (i + 1) * cols)

    def along(self):
        place = self.place
        copies = []
        for d in range(1, place.dims["seq"]):
            target = place.seq_shift(d)
            copies.append((self.total.at[:, target], self.moved.at[place.me], {"seq": target}))
        self.steps = [self.link.batch(copies, self.moved.at[0 : place.dims["seq"] - 1])]
        self.own = self.link.local(self.total.at[:, place.me], self.moved.at[place.me])

    def close(self):
        arrive(self.steps)
        self.own.wait()
        dims = self.place.dims
        group, width = dims["group"], dims["width"]
        for index in range(3):
            for q in range(group):
                value = self.moved[q, index].astype(F32)
                for half in range(1, dims["items_dev"]):
                    value = value + self.moved[half * group + q, index].astype(F32)
                self.done[index, :, q * width : (q + 1) * width] = value.astype(BF)


class Rows(Quarters):
    def piece(self, t, i):
        return i, t

    def halves(self, i):
        return i

    def cut(self, t, i):
        cols = self.out.shape[2] // 2
        return t, slice(None), slice(i * cols, (i + 1) * cols)

    def along(self):
        self.moved_done = rows_back(self.link, self.place, self.total, self.moved)

    def close(self):
        self.moved_done()
        value = self.moved[0].astype(F32)
        for half in range(1, self.place.dims["items_dev"]):
            value = value + self.moved[half].astype(F32)
        self.done[...] = value.astype(BF)


class Stage:
    def __init__(self, sems, place, part, bufs, mid, spread, before):
        self.link, self.place, self.mid, self.spread = Link(*sems), place, mid, spread
        self.before = before
        self.reduce = Reduce(self.link, place, part, bufs)
        self.started, self.waits = {}, {}

    def start(self, k):
        self.reduce.start(k, k)

    def middle(self, k):
        self.reduce.middle(k, k)

    def end(self, k):
        place, spread = self.place, self.spread
        spread[k, place.c, place.b1, place.b0] = self.mid(k, self.reduce.end(k))
        self.started[k] = spread_start(self.link, place, spread, k)

    def forward(self, k):
        self.waits[k] = spread_end(self.link, self.place, self.spread, k, self.started[k])

    def arrive(self, k):
        arrive(self.waits[k])

    def release(self, k):
        done = (self.reduce.zero[k], self.reduce.one[k])
        for copy in done:
            copy.wait_send()
        late = {id(copy) for copy in done}
        self.link.open = [copy for copy in self.link.open if id(copy) not in late]


def stage_steps(stage, compute, flight=None, ended=None, after=None):
    before = stage.before
    compute(0, (lambda: before.forward(1)) if before else (lambda: None))
    stage.start(0)
    compute(1, lambda: None)
    stage.start(1)
    if before:
        before.link.finish()
    stage.middle(0)
    stage.middle(1)
    if flight:
        flight()
    stage.end(0)
    stage.end(1)
    if ended:
        ended()
    stage.forward(0)
    if after:
        after()


def layer_kernel(dims, names, *refs):
    b = Box(names, refs)
    b.grad_third, b.grad_r2, b.grad_r1, b.gc1_all = b.first, b.second, b.first, b.gy_all
    place = Place(dims)
    sems = b.send_sems, b.recv_sems
    link = Link(*sems, dims["chain"])
    width, block, items_dev = dims["width"], dims["block"], dims["items_dev"]
    h, t, q_place = place.h, place.t, place.q
    c, b1, b0 = place.c, place.b1, place.b0
    partner = place.partner()
    wr = b.w_sq.shape[0] // dims["share"]
    model = dims["model"]
    total_dec, total_mem = dims["total_dec"], dims["total_mem"]
    rb = b.dec.shape[1]

    def rows_of(ref, cols=model):
        return ref[...].reshape(-1, ref.shape[-1])[:, :cols]

    def chunk(ref, k):
        return ref[k].reshape(-1, model)

    half_rows = total_dec // 2

    def span(k):
        return slice(k * half_rows, (k + 1) * half_rows)

    def put(k, value, before=None):
        if before:
            before.release(k)
        b.part[k] = value.astype(BF).reshape(b.part.shape[1:])

    def weight(ref, index):
        return ref[index].reshape(model, width)

    weights = (b.w_sq, b.w_sk, b.w_sv, b.w_so, b.w_ck, b.w_cv, b.w_cq, b.w_co)
    rows_t = pl.ds(pl.multiple_of(t * wr, wr), wr)
    index = link.index()
    for i, w in enumerate(weights):
        pltpu.make_async_copy(w.at[rows_t], b.staged.at[i], b.send_sems.at[index]).start()
    staged = pltpu.make_async_copy(b.staged, b.staged, b.send_sems.at[index])
    own_fin = link.local(b.f_in, b.own_fin)
    own_fout = link.local(b.f_out, b.own_fout)
    greet(place.seq_peers() + place.items_peers())

    def share_columns(dst):
        blocks = dims["seq"] // 2
        return Share(
            link, place, lambda t: dst.at[:, t],
            lambda t, i: dst.at[i * blocks : (i + 1) * blocks, t],
        )

    def share_rows(dst):
        return Share(link, place, lambda t: dst.at[:, t], lambda t, i: dst.at[i, t])

    def share_hidden(dst):
        rows = dst.shape[1] // 2
        return Share(
            link, place, lambda t: dst.at[t], lambda t, i: dst.at[t, i * rows : (i + 1) * rows]
        )

    def join_cells():
        mb = b.cells.shape[1]
        same = lax.broadcasted_iota(jnp.int32, (mb, mb), 0) == lax.broadcasted_iota(
            jnp.int32, (mb, mb), 1
        )
        for k in range(items_dev):
            flags = (b.cells[k : k + 1] == 1).astype(F32)
            column = jnp.sum(jnp.where(same, flags, 0.0), axis=1, keepdims=True)
            b.mem_cells[k, :, :model] = b.mem[k]
            b.mem_cells[k, :, model:] = jnp.broadcast_to(column, (mb, 128)).astype(BF)

    staged.wait()
    steps, own_self = columns_out(link, place, b.staged.at[0:3], b.o_self, width)
    b.x_all[h, c, b1, b0] = b.dec[h]
    join_cells()
    b.m_all[h, c, b1, b0] = b.mem_cells[h]
    link.settle(steps)
    swap_x = link.send(b.dec.at[1 - h], b.x_all.at[h, c, b1, b0], partner)
    first_x = spread_start(link, place, b.x_all, h)
    so_arrived, so_sent = rows_out(link, place, b.staged.at[3], b.o_so)
    steps.wait_recv()
    own_self.wait()
    self_share = [share_columns(b.o_self.at[i]) for i in range(3)]
    waits = spread_end(link, place, b.x_all, h, first_x)
    swap_x.wait_recv()
    second_x = spread_start(link, place, b.x_all, 1 - h)
    waits += spread_end(link, place, b.x_all, 1 - h, second_x)
    cross_steps, own_cross = columns_out(link, place, b.staged.at[4:7], b.o_cross, width)
    co_arrived, co_sent = rows_out(link, place, b.staged.at[7], b.o_co)
    swap_m = link.send(b.mem_cells.at[1 - h], b.m_all.at[h, c, b1, b0], partner)
    first_m = spread_start(link, place, b.m_all, h)
    own_fin.wait()
    own_fout.wait()
    fr, gr = b.o_fin.shape[1], b.o_fout.shape[1]
    step_fin = link.send(b.own_fin.at[pl.ds(pl.multiple_of(t * fr, fr), fr)], b.o_fin.at[t], partner)
    for share in self_share:
        share.forward()
    so_arrived()
    so_share = share_rows(b.o_so)

    arrive(waits)
    rows = rows_of(b.x_all)
    for index, dst in enumerate((b.sq, b.sk, b.sv)):
        self_share[index].wait()
        dst[...] = nn(rows, weight(b.o_self, index)).astype(BF)
    so_share.forward()
    cross_steps.wait_recv()
    own_cross.wait()
    cross_share = [share_columns(b.o_cross.at[i]) for i in range(3)]
    co_arrived()
    co_share = share_rows(b.o_co)
    mem_waits = spread_end(link, place, b.m_all, h, first_m)
    swap_m.wait_recv()
    second_m = spread_start(link, place, b.m_all, 1 - h)
    length, mem_length = b.dec_len[h], b.mem_len[h]

    def self_ok(start, stop):
        keys = lax.broadcasted_iota(jnp.int32, (stop, block), 0)
        spots = lax.broadcasted_iota(jnp.int32, (stop, block), 1) + start
        return (keys <= spots) & (keys < length)

    bufs = [b.recv0, b.send1, b.recv1, b.keep1]
    if dims["bits"] == 3:
        bufs += [b.send2, b.recv2]

    def forward(index, res, summed, out):
        def mid(k, total):
            value = res(k) + total
            summed[k] = value
            normed, _ = moments(value)
            result = normed * b.gain[index : index + 1] + b.bias[index : index + 1]
            out[k] = result
            return result.astype(BF)

        return mid

    def self_part(k, pump):
        attend(
            b.sq, b.sk, b.sv, self_ok, b.sp, b.smix, True, block,
            k * half_rows, (k + 1) * half_rows, pump,
        )
        if k == 0:
            so_share.wait()
        put(k, nn(b.smix[span(k)], rows_of(b.o_so)))

    def memory_part():
        arrive(mem_waits)
        mems = rows_of(b.m_all)
        cross_share[0].wait()
        b.ck[...] = nn(mems, weight(b.o_cross, 0)).astype(BF)
        cross_share[1].wait()
        b.cv[...] = nn(mems, weight(b.o_cross, 1)).astype(BF)
        spots = lax.broadcasted_iota(jnp.int32, (total_mem, 128), 0)
        cells = b.m_all[...].reshape(-1, b.m_all.shape[-1])[:, model:].astype(F32)
        b.keep[...] = ((spots < mem_length) & ((cells > 0.5) | (spots == 0))).astype(F32)

    stage = Stage(
        sems, place, b.part, bufs,
        forward(0, lambda k: b.x_all[k, c, b1, b0].astype(F32), b.sum_one, b.first), b.first_all, None,
    )
    def cross_weights():
        rows = pl.ds(pl.multiple_of(t * gr, gr), gr)
        steps_fout.append(link.send(b.own_fout.at[rows], b.o_fout.at[t], partner))
        mem_waits.extend(spread_end(link, place, b.m_all, 1 - h, second_m))
        for share in cross_share + [co_share]:
            share.forward()
        step_fin.wait_recv()
        ffn_share.append(share_hidden(b.o_fin))

    ffn_share, steps_fout = [], []
    stage_steps(stage, self_part, after=cross_weights)
    memory_part()
    b.c_own[h] = b.cot[h]

    def cross_part(k, pump):
        last.arrive(k)
        if k == 0:
            cross_share[2].wait()
        b.cq[span(k)] = nn(chunk(b.first_all, k), weight(b.o_cross, 2)).astype(BF)
        attend(
            b.cq, b.ck, b.cv, lambda start, stop: b.keep[:, 0:1] > 0.5, b.cp, b.cmix, False, block,
            k * half_rows, (k + 1) * half_rows, pump,
        )
        if k == 0:
            co_share.wait()
        put(k, nn(b.cmix[span(k)], rows_of(b.o_co)), last)

    last = stage
    stage = Stage(
        sems, place, b.part, bufs, forward(1, lambda k: b.first[k], b.sum_two, b.second),
        b.second_all, last,
    )
    def ffn_weights():
        ffn_share[0].forward()
        arrive(steps_fout)
        ffn_share.append(share_hidden(b.o_fout))

    stage_steps(stage, cross_part, ffn_weights)
    swap_c = link.send(b.cot.at[1 - h], b.c_own.at[h], partner)

    w_ins = (lambda: b.own_fin[...], lambda: b.o_fin[...].reshape(model, -1))
    w_outs = (lambda: b.own_fout[...], lambda: b.o_fout[...].reshape(-1, model))
    hidden = b.own_fin.shape[1]
    last_second = stage

    def ffn_part(k, pump):
        last_second.arrive(k)
        if k == 0:
            ffn_share[0].wait()
        rows = chunk(b.second_all, k)
        for index in range(2):
            if index:
                pump()
                if k == 0:
                    ffn_share[1].forward()
            pre = nn(rows, w_ins[index]())
            cdf = 0.5 * (1.0 + lax.erf(pre * (0.5**0.5)))
            cols = slice(index * hidden, (index + 1) * hidden)
            b.act[span(k), cols] = (pre * cdf).astype(BF)
            b.slope[span(k), cols] = (
                cdf + pre * (jnp.exp(-0.5 * pre * pre) * 0.3989422804014327)
            ).astype(BF)
        if k == 0:
            ffn_share[1].wait()
        total = nn(b.act[span(k), :hidden], w_outs[0]())
        put(k, total + nn(b.act[span(k), hidden:], w_outs[1]()), last_second)

    swap_c.wait_recv()

    def add_sums(index, k, normed, grad):
        new = (jnp.sum(grad * normed, axis=0, keepdims=True), jnp.sum(grad, axis=0, keepdims=True))
        for row, value in zip((index, 3 + index), new):
            b.sums[row : row + 1] = value if k == 0 else b.sums[row : row + 1] + value

    def turn(k, total):
        gain = b.gain[2:3]
        normed, inv = moments(b.second[k] + total)
        spots = lax.broadcasted_iota(jnp.int32, (rb, model), 0) + (k * dims["group"] + q_place) * rb
        kept = spots < length
        b.layer[k] = jnp.where(kept, normed * gain + b.bias[2:3], 0.0).astype(BF)
        grad = jnp.where(kept, b.c_own[k].astype(F32), 0.0)
        add_sums(2, k, normed, grad)
        result = norm_back(normed, inv, gain, grad)
        b.grad_third[k] = result
        return result.astype(BF)

    stage = Stage(sems, place, b.part, bufs, turn, b.gy_all, last_second)
    stage_steps(stage, ffn_part)

    last_turn = stage

    way_fout = Hidden(
        link, place, b.g_fout, ("q_fout", "t_fout", "u_fout", dims["lines"] and "l_fout", "s_fout", "z_fout", "d_fout", "r_fout"), b
    )
    def out_grads():
        grad = rows_of(b.gy_all)
        for index in range(2):
            cols = slice(index * hidden, (index + 1) * hidden)
            value = tn(b.act[:, cols], grad)
            b.g_fout[index] = value.astype(BF).reshape(b.g_fout.shape[1:])
        way_fout.send()

    def ffn_back(k, pump):
        last_turn.arrive(k)
        if k == 1:
            out_grads()
        grad = chunk(b.gy_all, k)
        total = None
        for index in range(2):
            if index:
                pump()
            cols = slice(index * hidden, (index + 1) * hidden)
            grad_pre = (nt(grad, w_outs[index]()) * b.slope[span(k), cols].astype(F32)).astype(BF)
            b.slope[span(k), cols] = grad_pre
            term = nt(grad_pre, w_ins[index]())
            total = term if total is None else total + term
        put(k, total, last_turn)

    way_fin = Hidden(
        link, place, b.g_fin, ("q_fin", "t_fin", "u_fin", dims["lines"] and "l_fin", "s_fin", "z_fin", "d_fin", "r_fin"), b
    )
    way_cross = Columns(
        link, place, b.g_cross, ("q_cross", "t_cross", "u_cross", dims["lines"] and "l_cross", "s_cross", "z_cross", "d_cross", "r_cross"), b
    )
    way_self = Columns(
        link, place, b.g_self, ("q_self", "t_self", "u_self", dims["lines"] and "l_self", "s_self", "z_self", "d_self", "r_self"), b
    )
    way_co = Rows(
        link, place, b.g_co, ("q_co", "t_co", "u_co", dims["lines"] and "l_co", "s_co", "z_co", "d_co", "r_co"), b
    )
    way_so = Rows(
        link, place, b.g_so, ("q_so", "t_so", "u_so", dims["lines"] and "l_so", "s_so", "z_so", "d_so", "r_so"), b
    )

    def backward(index, res, summed, out):
        def mid(k, total):
            normed, inv = moments(summed[k])
            grad = res[k] + total
            add_sums(index, k, normed, grad)
            result = norm_back(normed, inv, b.gain[index : index + 1], grad)
            out[k] = result
            return result.astype(BF)

        return mid

    def in_grads():
        rows = rows_of(b.second_all)
        for index in range(2):
            cols = slice(index * hidden, (index + 1) * hidden)
            value = tn(rows, b.slope[:, cols])
            b.g_fin[index] = value.astype(BF).reshape(b.g_fin.shape[1:])
        way_fin.send()

    stage = Stage(
        sems, place, b.part, bufs, backward(1, b.grad_third, b.sum_two, b.grad_r2), b.gc2_all,
        last_turn,
    )
    stage_steps(stage, ffn_back, in_grads)

    last_back = stage

    def cross_back(k, pump):
        last_back.arrive(k)
        b.dmix[span(k)] = nt(chunk(b.gc2_all, k), rows_of(b.o_co)).astype(BF)
        attend_back(
            b.cq, b.ck, b.cv, b.cp, b.dmix, b.dq, b.sum_dk, b.sum_dv, False, block,
            k * half_rows, (k + 1) * half_rows, pump,
        )
        put(k, nt(b.dq[span(k)], weight(b.o_cross, 2)), last_back)
        if k == 1:
            way_fout.turn()

    def cross_grads():
        mems = rows_of(b.m_all)
        shape = b.g_cross.shape[1:]
        b.dck[...] = (b.sum_dk[:total_mem] * SCALE).astype(BF)
        b.dcv[...] = b.sum_dv[:total_mem].astype(BF)
        b.g_cross[0] = tn(rows_of(b.first_all), b.dq[...]).astype(BF).reshape(shape)
        b.g_cross[1] = tn(mems, b.dck[...]).astype(BF).reshape(shape)
        b.g_cross[2] = tn(mems, b.dcv[...]).astype(BF).reshape(shape)
        way_cross.send()
        b.g_co[...] = tn(b.cmix[...], rows_of(b.gc2_all)).astype(BF).reshape(b.g_co.shape)
        way_co.send()
        way_fin.turn()

    def part_mem():
        value = nt(b.dck[...], weight(b.o_cross, 0)) + nt(b.dcv[...], weight(b.o_cross, 1))
        b.part_m[...] = value.astype(BF).reshape(b.part_m.shape)
        for index in range(2):
            red_m.start(index, ks[index])

    stage = Stage(
        sems, place, b.part, bufs, backward(0, b.grad_r2, b.sum_one, b.grad_r1), b.gc1_all,
        last_back,
    )
    ks = (1 - h, h)
    mem_bufs = [b.recv0_m, b.send1_m, b.recv1_m, b.keep1_m]
    if dims["bits"] == 3:
        mem_bufs += [b.send2_m, b.recv2_m]
    red_m = Reduce(link, place, b.part_m, mem_bufs)
    stage_steps(stage, cross_back, cross_grads, part_mem)

    swap_l = link.send(b.layer.at[1 - h], b.layer_out.at[h], partner)
    b.layer_out[h] = b.layer[h]
    way_fout.add()
    for k in range(2):
        stage.arrive(k)
        pump = (lambda: stage.forward(1)) if k == 0 else (lambda: None)
        b.dmix[span(k)] = nt(chunk(b.gc1_all, k), rows_of(b.o_so)).astype(BF)
        attend_back(
            b.sq, b.sk, b.sv, b.sp, b.dmix, b.dq, b.sum_dk, b.sum_dv, True, block,
            k * half_rows, (k + 1) * half_rows, pump,
        )
        red_m.middle(k, ks[k])
    b.dsk[...] = (b.sum_dk[...] * SCALE).astype(BF)
    b.dsv[...] = b.sum_dv[...].astype(BF)
    for k in range(2):
        total = nt(b.dq[span(k)], weight(b.o_self, 0)) + nt(b.dsk[span(k)], weight(b.o_self, 1))
        put(k, total + nt(b.dsv[span(k)], weight(b.o_self, 2)), stage)
    stage.link.finish()
    chain = Link(*sems)
    red_x = Reduce(chain, place, b.part, bufs)
    for index in range(2):
        red_x.start(index, ks[index])
    way_cross.turn()
    way_co.turn()
    way_fin.add()
    rows = rows_of(b.x_all)
    shape = b.g_self.shape[1:]
    b.g_self[0] = tn(rows, b.dq[...]).astype(BF).reshape(shape)
    b.g_self[1] = tn(rows, b.dsk[...]).astype(BF).reshape(shape)
    b.g_self[2] = tn(rows, b.dsv[...]).astype(BF).reshape(shape)
    way_self.send()
    b.g_so[...] = tn(b.smix[...], rows_of(b.gc1_all)).astype(BF).reshape(b.g_so.shape)
    way_so.send()
    for index in range(2):
        red_x.middle(index, ks[index])
    b.send_m[...] = red_m.end(0).astype(BF)
    swap_m = link.send(b.send_m, b.recv_m, partner)
    b.grad_mem[h] = red_m.end(1)
    copies = []
    for d in range(1, dims["seq"]):
        copies.append((b.sums, b.sums_seq.at[d - 1], {"seq": place.seq_shift(d)}))
    seq_sums = link.batch(copies, b.sums_seq)
    way_cross.add()
    way_co.add()
    b.send_x[...] = (red_x.end(0) + b.grad_r1[1 - h]).astype(BF)
    swap_x = link.send(b.send_x, b.recv_x, partner)
    b.grad_dec[h] = red_x.end(1) + b.grad_r1[h]
    way_fout.gather()
    way_self.turn()
    way_so.turn()
    way_fin.gather()
    way_fout.forward()
    way_self.add()
    way_so.add()
    way_cross.gather()
    way_co.gather()
    way_fin.forward()
    seq_sums.wait_recv()
    value = b.sums[...]
    for d in range(1, dims["seq"]):
        value = value + b.sums_seq[d - 1]
    b.sums_line[...] = value
    copies = []
    for e in range(1, dims["items"]):
        target = {"items": lax.rem(place.it + e, dims["items"])}
        copies.append((b.sums_line, b.sums_items.at[e - 1], target))
    item_sums = link.batch(copies, b.sums_items)
    swap_x.wait_recv()
    b.grad_dec[1 - h] = b.recv_x[...].astype(F32)
    swap_m.wait_recv()
    b.grad_mem[1 - h] = b.recv_m[...].astype(F32)
    swap_l.wait_recv()
    way_self.gather()
    way_so.gather()
    way_cross.forward()
    way_co.forward()
    item_sums.wait_recv()
    value = b.sums_line[...]
    for e in range(1, dims["items"]):
        value = value + b.sums_items[e - 1]
    b.sums_out[...] = value
    way_self.forward()
    way_so.forward()
    for way in (way_fout, way_fin, way_cross, way_co, way_self, way_so):
        way.finish()
    so_sent()
    co_sent()
    chain.finish()
    link.finish()


def shape(dims, dtype):
    return jax.ShapeDtypeStruct(tuple(dims), dtype)


def outputs_kernel(layer, dec, mem, cross, own, co, so, fin, fout, sums, *outs):
    o_layer, o_dec, o_mem = outs[:3]
    o_layer[...] = layer[...]
    o_dec[...] = dec[...]
    o_mem[...] = mem[...]
    for index in range(3):
        outs[3 + index][...] = own[0, index].astype(F32)
        outs[7 + index][...] = cross[0, index].astype(F32)
    outs[6][...] = so[0].astype(F32)
    outs[10][...] = co[0].astype(F32)
    outs[11][...] = fin[0].astype(F32)
    outs[12][...] = fout[0].astype(F32)
    outs[13][...] = sums[0:3]
    outs[14][...] = sums[3:6]


def shards(
    mesh, dec_in, memory, dec_len, mem_len, cell_mask, self_query, self_key, self_value, self_out,
    cross_query, cross_key, cross_value, cross_out, ffn_in, ffn_out, norm_gain, norm_bias, cotangent,
):
    items_dev, rb, model = dec_in.shape
    mb = memory.shape[1]
    seq, items = mesh.shape["seq"], mesh.shape["items"]
    group = seq // items_dev
    share = 4
    bits = group.bit_length() - 1
    chips = group // 4
    width = model // group
    total_dec, total_mem = rb * seq, mb * seq
    heads = width // HEAD_DIM
    hidden = ffn_in.shape[1]
    wr = self_query.shape[0] // share
    fr, gr = model // share, hidden // share
    lines = items // share - 1
    dims = {
        "items_dev": items_dev, "items": items, "seq": seq, "group": group, "share": share,
        "bits": bits, "chips": chips, "width": width, "model": model, "block": 256,
        "total_dec": total_dec, "total_mem": total_mem, "lines": lines,
        "chain": 12 + 2 * (bits - 2),
    }
    ins = [
        ("dec", dec_in, VM), ("mem", memory, VM), ("cells", cell_mask, VM), ("cot", cotangent, VM),
        ("dec_len", dec_len, SM), ("mem_len", mem_len, SM),
        ("w_sq", self_query, HBM), ("w_sk", self_key, HBM), ("w_sv", self_value, HBM),
        ("w_so", self_out, HBM), ("w_cq", cross_query, HBM), ("w_ck", cross_key, HBM),
        ("w_cv", cross_value, HBM), ("w_co", cross_out, HBM), ("f_in", ffn_in, HBM),
        ("f_out", ffn_out, HBM), ("gain", norm_gain, VM), ("bias", norm_bias, VM),
    ]
    own, own_m = (items_dev, rb, model), (items_dev, mb, model)
    grid = (items_dev, chips, 2, 2)
    outs = [
        ("layer_out", own, BF, VM), ("grad_dec", own, F32, VM), ("grad_mem", own_m, F32, VM),
        ("sums_out", (8, model), F32, VM),
        ("r_cross", (share, 3, wr, model), BF, HBM), ("r_self", (share, 3, wr, model), BF, HBM),
        ("r_co", (share, wr, model), BF, HBM), ("r_so", (share, wr, model), BF, HBM),
        ("r_fin", (share, fr, hidden), BF, HBM), ("r_fout", (share, gr, model), BF, HBM),
    ]
    cols = (3, seq, share, wr, width)
    scratch = [
        ("x_all", grid + (rb, model), BF), ("m_all", grid + (mb, model + 128), BF),
        ("mem_cells", (items_dev, mb, model + 128), BF), ("c_own", own, BF), ("staged", (8, wr, model), BF),
        ("own_fin", (model, hidden), BF), ("own_fout", (hidden, model), BF),
        ("o_self", cols, BF), ("o_cross", cols, BF),
        ("o_so", (items_dev, share, wr, model), BF), ("o_co", (items_dev, share, wr, model), BF),
        ("o_fin", (share, fr, hidden), BF), ("o_fout", (share, gr, model), BF),
        ("sq", (total_dec, width), BF), ("sk", (total_dec, width), BF), ("sv", (total_dec, width), BF),
        ("cq", (total_dec, width), BF), ("ck", (total_mem, width), BF), ("cv", (total_mem, width), BF),
        ("sp", (heads, total_dec, total_dec), BF), ("cp", (heads, total_mem, total_dec), BF),
        ("smix", (total_dec, width), BF), ("cmix", (total_dec, width), BF),
        ("keep", (total_mem, 128), F32),
        ("part", grid + (rb, model), BF), ("part_m", grid + (mb, model), BF),
        ("first_all", grid + (rb, model), BF), ("second_all", grid + (rb, model), BF),
        ("gy_all", grid + (rb, model), BF), ("gc2_all", grid + (rb, model), BF),
        ("sum_one", own, F32), ("sum_two", own, F32), ("first", own, F32), ("second", own, F32),
        ("layer", own, BF), ("sum_dk", (total_dec, width), F32), ("sum_dv", (total_dec, width), F32),
        ("act", (total_dec, 2 * hidden), BF), ("slope", (total_dec, 2 * hidden), BF),
        ("dmix", (total_dec, width), BF), ("dq", (total_dec, width), BF),
        ("dsk", (total_dec, width), BF), ("dsv", (total_dec, width), BF),
        ("dck", (total_mem, width), BF), ("dcv", (total_mem, width), BF),
        ("send_x", (rb, model), BF), ("recv_x", (rb, model), BF),
        ("send_m", (mb, model), BF), ("recv_m", (mb, model), BF),
        ("sums", (8, model), F32), ("sums_line", (8, model), F32),
        ("sums_seq", (seq - 1, 8, model), F32), ("sums_items", (items - 1, 8, model), F32),
    ]
    for name, rows in (("", rb), ("_m", mb)):
        scratch += [
            ("recv0" + name, (items_dev, chips, 2, rows, model), BF),
            ("send1" + name, (items_dev, chips, rows, model), BF),
            ("recv1" + name, (items_dev, chips, rows, model), BF),
            ("keep1" + name, (items_dev, chips, rows, model), F32),
        ]
        if bits == 3:
            scratch += [
                ("send2" + name, (items_dev, rows, model), BF),
                ("recv2" + name, (items_dev, rows, model), BF),
            ]
    for name, grad, quarter, piece, moved, done in (
        ("fin", (2, share, fr, hidden), (2, fr, hidden), (2, fr // 2, hidden), (fr, hidden),
         (fr, hidden)),
        ("fout", (2, share, gr, model), (2, gr, model), (2, gr // 2, model), (gr, model), (gr, model)),
        ("cross", cols, (3, seq, wr, width), (3, seq // 2, wr, width), (seq, 3, wr, width),
         (3, wr, model)),
        ("self", cols, (3, seq, wr, width), (3, seq // 2, wr, width), (seq, 3, wr, width),
         (3, wr, model)),
        ("co", (items_dev, share, wr, model), (items_dev, wr, model), (wr, model),
         (items_dev, wr, model), (wr, model)),
        ("so", (items_dev, share, wr, model), (items_dev, wr, model), (wr, model),
         (items_dev, wr, model), (wr, model)),
    ):
        scratch += [
            ("g_" + name, grad, BF), ("q_" + name, (2, 2) + piece, BF), ("t_" + name, (2,) + piece, BF),
            ("u_" + name, (2,) + piece, BF), ("s_" + name, quarter, BF), ("z_" + name, moved, BF),
            ("d_" + name, done, BF),
        ]
        if lines:
            scratch.append(("l_" + name, (lines,) + quarter, BF))
    copies = dims["chain"] + 145 + 12 * (bits - 2)
    names = [x[0] for x in ins + outs + scratch] + ["send_sems", "recv_sems"]
    results = pl.pallas_call(
        functools.partial(layer_kernel, dims, names),
        name="layer",
        out_shape=[shape(x[1], x[2]) for x in outs],
        in_specs=[x[2] for x in ins],
        out_specs=[x[3] for x in outs],
        scratch_shapes=[pltpu.VMEM(x[1], x[2]) for x in scratch]
        + [pltpu.SemaphoreType.DMA((copies,)), pltpu.SemaphoreType.DMA((copies,))],
        compiler_params=pltpu.CompilerParams(
            collective_id=0, has_side_effects=True, vmem_limit_bytes=VMEM_BYTES
        ),
    )(*[x[1] for x in ins])
    layer_out, grad_dec, grad_memory, sums, r_cross, r_self, r_co, r_so, r_fin, r_fout = results
    tok, mem_rows = items_dev * rb, items_dev * mb
    pieces = (
        ((tok, model), (tok // share, model), BF), ((tok, model), (tok // share, model), F32),
        ((mem_rows, model), (mem_rows // share, model), F32),
    )
    heads_in = [
        pl.BlockSpec((1, 3, wr, model), lambda i: (i, 0, 0, 0)),
        pl.BlockSpec((1, 3, wr, model), lambda i: (i, 0, 0, 0)),
        pl.BlockSpec((1, wr, model), lambda i: (i, 0, 0)),
        pl.BlockSpec((1, wr, model), lambda i: (i, 0, 0)),
        pl.BlockSpec((1, fr, hidden), lambda i: (i, 0, 0)),
        pl.BlockSpec((1, gr, model), lambda i: (i, 0, 0)),
        pl.BlockSpec((8, model), lambda i: (0, 0)),
    ]
    row_specs = [pl.BlockSpec(x[1], lambda i: (i, 0)) for x in pieces]
    square = (share * wr, model)
    outs = pl.pallas_call(
        outputs_kernel,
        name="outputs",
        grid=(share,),
        in_specs=row_specs + heads_in,
        out_specs=row_specs
        + [pl.BlockSpec((wr, model), lambda i: (i, 0))] * 8
        + [pl.BlockSpec((fr, hidden), lambda i: (i, 0)), pl.BlockSpec((gr, model), lambda i: (i, 0))]
        + [pl.BlockSpec((3, model), lambda i: (0, 0))] * 2,
        out_shape=[shape(x[0], x[2]) for x in pieces]
        + [shape(square, F32)] * 8
        + [shape((model, hidden), F32), shape((hidden, model), F32)]
        + [shape((3, model), F32)] * 2,
        compiler_params=pltpu.CompilerParams(vmem_limit_bytes=VMEM_BYTES),
    )(
        layer_out.reshape(tok, model), grad_dec.reshape(tok, model),
        grad_memory.reshape(mem_rows, model), r_cross, r_self, r_co, r_so, r_fin, r_fout, sums,
    )
    return (
        outs[0].reshape(own), outs[1].reshape(own), outs[2].reshape(own_m), *outs[3:],
    )


def solution(mesh):
    rows = P("seq", None)
    tokens = P("items", "seq", None)
    placed = (
        (tokens, tokens, P("items"), P("items"), P("items", "seq"))
        + (rows,) * 8
        + (P(None, "seq"), rows, P(), P(), tokens)
    )
    return jax.shard_map(
        functools.partial(shards, mesh),
        mesh=mesh,
        in_specs=placed,
        out_specs=(tokens,) * 3 + (rows,) * 8 + (P(None, "seq"), rows, P(), P()),
        check_vma=False,
    )
```

```python
import functools

import jax
import jax.numpy as jnp
from jax import lax
from jax.experimental import pallas as pl
from jax.experimental.pallas import tpu as pltpu
from jax.sharding import PartitionSpec as P

HEAD_DIM = 64
EPS = 1e-05
NEG = -1e30
SCALE = HEAD_DIM ** (-0.5)
BF = jnp.bfloat16
F32 = jnp.float32
VMEM_BYTES = 63 * 1024 * 1024
MESH = pl.DeviceIdType.MESH
VM = pl.BlockSpec(memory_space=pltpu.VMEM)
HBM = pl.BlockSpec(memory_space=pl.ANY)
SM = pl.BlockSpec(memory_space=pltpu.SMEM)


def nn(left, right):
    return lax.dot_general(left, right, (((1,), (0,)), ((), ())), preferred_element_type=F32)


def nt(left, right):
    return lax.dot_general(left, right, (((1,), (1,)), ((), ())), preferred_element_type=F32)


def tn(left, right):
    return lax.dot_general(left, right, (((0,), (0,)), ((), ())), preferred_element_type=F32)


class Link:
    def __init__(self, send_sems, recv_sems, first=0):
        self.send_sems, self.recv_sems, self.count, self.open = send_sems, recv_sems, first, []

    def index(self):
        self.count += 1
        return self.count - 1

    def make(self, src, dst, device, index):
        return pltpu.make_async_remote_copy(
            src_ref=src,
            dst_ref=dst,
            send_sem=self.send_sems.at[index],
            recv_sem=self.recv_sems.at[index],
            device_id=device,
            device_id_type=MESH,
        )

    def send(self, src, dst, device):
        copy = self.make(src, dst, device, self.index())
        copy.start()
        self.open.append(copy)
        return copy

    def batch(self, copies, whole):
        index = self.index()
        for copy in copies:
            self.make(*copy, index).start()
        wait = self.make(whole, whole, copies[0][2], index)
        self.open.append(wait)
        return wait

    def settle(self, copy):
        copy.wait_send()
        self.open = [other for other in self.open if other is not copy]

    def local(self, src, dst):
        copy = pltpu.make_async_copy(src, dst, self.send_sems.at[self.index()])
        copy.start()
        return copy

    def finish(self, kept=()):
        late = {id(copy) for copy in kept}
        for copy in self.open:
            if id(copy) not in late:
                copy.wait_send()
        self.open = [copy for copy in self.open if id(copy) in late]


def greet(devices):
    barrier = pltpu.get_barrier_semaphore()
    for device in devices:
        pl.semaphore_signal(barrier, inc=1, device_id=device, device_id_type=MESH)
    pl.semaphore_wait(barrier, len(devices))


class Place:
    def __init__(self, dims):
        self.dims = dims
        group, share = dims["group"], dims["share"]
        self.me = lax.axis_index("seq")
        self.h = self.me // group
        self.q = self.me % group
        self.b0 = self.q % 2
        self.b1 = (self.q // 2) % 2
        self.c = self.q // 4
        self.it = lax.axis_index("items")
        self.base = (self.it // share) * share
        self.t = self.it % share
        x, y = self.t % 2, self.t // 2
        self.tx, self.ty, self.txy = y * 2 + 1 - x, (1 - y) * 2 + x, (1 - y) * 2 + 1 - x

    def across(self, bit):
        value = (self.q // (1 << bit)) % 2
        return {"seq": self.me + (1 - 2 * value) * (1 << bit)}

    def partner(self):
        return {"seq": (1 - self.h) * self.dims["group"] + self.q}

    def seq_shift(self, d):
        return lax.rem(self.me + d, self.dims["seq"])

    def line(self, t):
        return {"items": self.base + t}

    def seq_peers(self):
        return [{"seq": self.seq_shift(d)} for d in range(1, self.dims["seq"])]

    def items_peers(self):
        count = self.dims["items"]
        return [{"items": lax.rem(self.it + e, count)} for e in range(1, count)]


def spread_start(link, place, out, k):
    bits = place.dims["bits"]
    c, b1, b0 = place.c, place.b1, place.b0
    if bits == 3:
        step = link.send(out.at[k, c, b1, b0], out.at[k, c, b1, b0], place.across(2))
        step.wait_recv()
    waits = []
    high = link.send(out.at[k, :, b1, b0], out.at[k, :, b1, b0], place.across(1))
    waits.append(link.send(out.at[k, :, b1, b0], out.at[k, :, b1, b0], place.across(0)))
    return high, waits


def spread_end(link, place, out, k, started):
    high, waits = started
    b1, b0 = place.b1, place.b0
    high.wait_recv()
    waits.append(link.send(out.at[k, :, 1 - b1, b0], out.at[k, :, 1 - b1, b0], place.across(0)))
    return waits


def columns_out(link, place, src, dst, width):
    seq, group = place.dims["seq"], place.dims["group"]
    copies = []
    for d in range(1, seq):
        target = place.seq_shift(d)
        cols = pl.ds(pl.multiple_of(lax.rem(target, group) * width, width), width)
        copies.append((src.at[:, :, cols], dst.at[:, place.me, place.t], {"seq": target}))
    steps = link.batch(copies, dst.at[:, 0 : seq - 1, place.t])
    cols = pl.ds(pl.multiple_of(place.q * width, width), width)
    return steps, link.local(src.at[:, :, cols], dst.at[:, place.me, place.t])


def rows_out(link, place, src, dst):
    dims, me = place.dims, place.me
    slot = lax.rem(me, dims["items_dev"])
    base = link.count
    link.count += dims["items_dev"] + 1
    copies = []
    for half in range(dims["items_dev"]):
        target = half * dims["group"] + me // dims["items_dev"]
        copy = pltpu.make_async_remote_copy(
            src_ref=src,
            dst_ref=dst.at[slot, place.t],
            send_sem=link.send_sems.at[base + half],
            recv_sem=link.recv_sems.at[base + slot],
            device_id={"seq": target},
            device_id_type=MESH,
        )
        copies.append((target != me, copy))
        pl.when(target != me)(copy.start)
    own = pltpu.make_async_copy(
        src, dst.at[slot, place.t], link.send_sems.at[base + dims["items_dev"]]
    )
    mine = me // dims["items_dev"] == place.q
    pl.when(mine)(own.start)

    def arrived():
        pl.when(mine)(own.wait)
        for block in range(dims["items_dev"]):
            copy = pltpu.make_async_remote_copy(
                src_ref=src,
                dst_ref=dst.at[block, place.t],
                send_sem=link.send_sems.at[base],
                recv_sem=link.recv_sems.at[base + block],
                device_id={"seq": me},
                device_id_type=MESH,
            )
            pl.when(place.q * dims["items_dev"] + block != me)(copy.wait_recv)

    def sent():
        for other, copy in copies:
            pl.when(other)(copy.wait_send)

    return arrived, sent


class Share:
    def __init__(self, link, place, slab, half):
        self.link, self.place, self.half = link, place, half
        t = place.t
        self.from_x = link.send(slab(t), slab(t), place.line(place.tx))
        self.from_y = link.send(slab(t), slab(t), place.line(place.ty))

    def forward(self):
        link, place, half = self.link, self.place, self.half
        self.from_y.wait_recv()
        part = half(place.ty, 0)
        self.steps = [link.send(part, part, place.line(place.tx))]
        self.from_x.wait_recv()
        part = half(place.tx, 1)
        self.steps.append(link.send(part, part, place.line(place.ty)))

    def wait(self):
        arrive(self.steps)


def arrive(steps):
    for step in steps:
        step.wait_recv()


class Reduce:
    def __init__(self, link, place, part, bufs):
        self.link, self.place, self.part, self.bufs = link, place, part, bufs
        self.zero, self.one = {}, {}

    def start(self, index, k):
        place = self.place
        self.zero[index] = self.link.send(
            self.part.at[k, :, :, 1 - place.b0], self.bufs[0].at[index], place.across(0)
        )

    def middle(self, index, k):
        place, part = self.place, self.part
        recv0, send1, recv1, keep1 = self.bufs[:4]
        self.zero[index].wait_recv()
        b1, b0 = place.b1, place.b0
        for c in range(part.shape[1]):
            value = part[k, c, 1 - b1, b0].astype(F32) + recv0[index, c, 1 - b1].astype(F32)
            send1[index, c] = value.astype(BF)
        self.one[index] = self.link.send(send1.at[index], recv1.at[index], place.across(1))
        for c in range(part.shape[1]):
            keep1[index, c] = part[k, c, b1, b0].astype(F32) + recv0[index, c, b1].astype(F32)

    def end(self, index):
        place = self.place
        recv1, keep1 = self.bufs[2:4]
        self.one[index].wait_recv()
        if place.dims["bits"] == 2:
            return keep1[index, 0] + recv1[index, 0].astype(F32)
        send2, recv2 = self.bufs[4:6]
        c = place.c
        send2[index] = (keep1[index, 1 - c] + recv1[index, 1 - c].astype(F32)).astype(BF)
        step = self.link.send(send2.at[index], recv2.at[index], place.across(2))
        kept = keep1[index, c] + recv1[index, c].astype(F32)
        step.wait_recv()
        return kept + recv2[index].astype(F32)


def reduce_bufs(dims, rows):
    items_dev, width, chips = dims["items_dev"], dims["model"], dims["chips"]
    bufs = [
        pltpu.VMEM((items_dev, chips, 2, rows, width), BF),
        pltpu.VMEM((items_dev, chips, rows, width), BF),
        pltpu.VMEM((items_dev, chips, rows, width), BF),
        pltpu.VMEM((items_dev, chips, rows, width), F32),
    ]
    if dims["bits"] == 3:
        bufs += [pltpu.VMEM((items_dev, rows, width), BF) for _ in range(2)]
    return bufs


def moments(value):
    mean = jnp.mean(value, axis=-1, keepdims=True)
    centered = value - mean
    inv = lax.rsqrt(jnp.mean(centered * centered, axis=-1, keepdims=True) + EPS)
    return centered * inv, inv


def norm_back(normed, inv, gain, grad):
    scaled = grad * gain
    mean = jnp.mean(scaled, axis=-1, keepdims=True)
    cross = jnp.mean(scaled * normed, axis=-1, keepdims=True)
    return inv * (scaled - mean - normed * cross)


def rows_back(link, place, src, dst):
    dims, me, h = place.dims, place.me, place.h
    count = dims["items_dev"]
    base = link.count
    link.count += count + 1
    copies = []
    for k in range(count):
        target = place.q * count + k
        copy = pltpu.make_async_remote_copy(
            src_ref=src.at[k],
            dst_ref=dst.at[h],
            send_sem=link.send_sems.at[base + k],
            recv_sem=link.recv_sems.at[base + h],
            device_id={"seq": target},
            device_id_type=MESH,
        )
        copies.append((target != me, copy))
        pl.when(target != me)(copy.start)
    own = pltpu.make_async_copy(
        src.at[lax.rem(me, count)], dst.at[h], link.send_sems.at[base + count]
    )
    mine = me // count == place.q
    pl.when(mine)(own.start)

    def done():
        pl.when(mine)(own.wait)
        for half in range(count):
            copy = pltpu.make_async_remote_copy(
                src_ref=src.at[0],
                dst_ref=dst.at[half],
                send_sem=link.send_sems.at[base],
                recv_sem=link.recv_sems.at[base + half],
                device_id={"seq": me},
                device_id_type=MESH,
            )
            pl.when(half * dims["group"] + me // count != me)(copy.wait_recv)
        for other, copy in copies:
            pl.when(other)(copy.wait_send)

    return done


def half_mask(rows, half):
    return (lax.broadcasted_iota(jnp.int32, (rows, 128), 1) // HEAD_DIM) == half


def attend(q_ref, k_ref, v_ref, valid, p_ref, mix_ref, causal, block, first, last, pump):
    keys = k_ref.shape[0]
    for pair in range(q_ref.shape[1] // 128):
        lanes = slice(pair * 128, pair * 128 + 128)
        for start in range(first, last, block):
            stop = start + block if causal else keys
            halves = []
            for half in range(2):
                query = q_ref[start : start + block, lanes]
                query = jnp.where(half_mask(block, half), query, jnp.zeros_like(query))
                scores = nt(k_ref[:stop, lanes], query) * SCALE
                scores = jnp.where(valid(start, stop), scores, NEG)
                top = jnp.max(scores, axis=0, keepdims=True)
                grown = jnp.exp(scores - top)
                probs = (grown * (1.0 / jnp.sum(grown, axis=0, keepdims=True))).astype(BF)
                p_ref[2 * pair + half, :stop, start : start + block] = probs
                mixed = tn(v_ref[:stop, lanes], probs)
                halves.append(mixed[half * HEAD_DIM : (half + 1) * HEAD_DIM])
            mix_ref[start : start + block, lanes] = jnp.concatenate(halves, axis=0).T.astype(BF)
        if pair == 0:
            pump()


def attend_back(
    q_ref, k_ref, v_ref, p_ref, grad_ref, dq_ref, dk_ref, dv_ref, causal, block, first, last,
    pump,
):
    keys = k_ref.shape[0]
    for pair in range(q_ref.shape[1] // 128):
        lanes = slice(pair * 128, pair * 128 + 128)
        for start in range(first, last, block):
            stop = start + block if causal else keys
            halves = []
            sum_k, sum_v = None, None
            for half in range(2):
                mask = half_mask(block, half)
                query = q_ref[start : start + block, lanes]
                query = jnp.where(mask, query, jnp.zeros_like(query))
                grad = grad_ref[start : start + block, lanes]
                grad = jnp.where(mask, grad, jnp.zeros_like(grad))
                low = p_ref[2 * pair + half, :stop, start : start + block]
                probs = low.astype(F32)
                grad_probs = nt(v_ref[:stop, lanes], grad)
                delta = jnp.sum(probs * grad_probs, axis=0, keepdims=True)
                grad_scores = (probs * (grad_probs - delta)).astype(BF)
                turned = tn(k_ref[:stop, lanes], grad_scores) * SCALE
                halves.append(turned[half * HEAD_DIM : (half + 1) * HEAD_DIM])
                new_k, new_v = nn(grad_scores, query), nn(low, grad)
                sum_k = new_k if sum_k is None else sum_k + new_k
                sum_v = new_v if sum_v is None else sum_v + new_v
            old = start if causal else (keys if start else 0)
            for ref, value in ((dk_ref, sum_k), (dv_ref, sum_v)):
                if old:
                    ref[:old, lanes] = ref[:old, lanes] + value[:old]
                if old < stop:
                    ref[old:stop, lanes] = value[old:]
            dq_ref[start : start + block, lanes] = jnp.concatenate(halves, axis=0).T.astype(BF)
        if pair == 0:
            pump()


class Box:
    def __init__(self, names, refs):
        for name, ref in zip(names, refs):
            setattr(self, name, ref)


class Quarters:
    def __init__(self, link, place, grad, box_names, box):
        self.link, self.place, self.grad = link, place, grad
        self.recv, self.sums, self.last, self.lines, self.total, self.moved, self.done, self.out = (
            getattr(box, name) if name else None for name in box_names
        )

    def send(self):
        place, piece, link = self.place, self.piece, self.link
        self.steps = []
        for i, near in enumerate((place.tx, place.ty)):
            copies = [
                (self.grad.at[piece(near, i)], self.recv.at[i, 0], place.line(near)),
                (self.grad.at[piece(place.txy, i)], self.recv.at[i, 1], place.line(near)),
            ]
            self.steps.append(link.batch(copies, self.recv.at[i]))
        self.flying = list(self.steps)

    def turn(self):
        place, piece, link = self.place, self.piece, self.link
        steps = []
        for i, far in enumerate((place.ty, place.tx)):
            self.steps[i].wait_recv()
            value = self.grad[piece(far, i)].astype(F32) + self.recv[i, 1].astype(F32)
            self.sums[i] = value.astype(BF)
            steps.append(link.send(self.sums.at[i], self.last.at[i], place.line(far)))
        self.steps = steps
        self.flying += steps

    def add(self):
        place = self.place
        for i in range(2):
            self.steps[i].wait_recv()
            value = self.grad[self.piece(place.t, i)].astype(F32)
            value = value + self.recv[i, 0].astype(F32) + self.last[i].astype(F32)
            self.total[self.halves(i)] = value.astype(BF)
        if self.lines is not None:
            share, items = place.dims["share"], place.dims["items"]
            copies = []
            for a in range(1, items // share):
                target = {"items": lax.rem(place.it + a * share, items)}
                copies.append((self.total, self.lines.at[a - 1], target))
            step = self.link.batch(copies, self.lines)
            step.wait()
            self.link.open.pop()
            value = self.total[...].astype(F32)
            for a in range(1, items // share):
                value = value + self.lines[a - 1].astype(F32)
            self.total[...] = value.astype(BF)
        self.along()

    def gather(self):
        self.close()
        place, out = self.place, self.out
        self.own = self.link.local(self.done, out.at[place.t])
        self.near = [
            self.link.send(self.done, out.at[place.t], place.line(near))
            for near in (place.tx, place.ty)
        ]

    def forward(self):
        place, out, link = self.place, self.out, self.link
        self.steps = []
        for i, (source, near) in enumerate(((place.ty, place.tx), (place.tx, place.ty))):
            self.near[1 - i].wait_recv()
            part = out.at[self.cut(source, i)]
            self.steps.append(link.send(part, part, place.line(near)))

    def finish(self):
        arrive(self.steps)
        self.own.wait()


class Hidden(Quarters):
    def piece(self, t, i):
        rows = self.grad.shape[2] // 2
        return slice(None), t, slice(i * rows, (i + 1) * rows)

    def halves(self, i):
        rows = self.grad.shape[2] // 2
        return slice(None), slice(i * rows, (i + 1) * rows)

    def cut(self, t, i):
        rows = self.out.shape[1] // 2
        return t, slice(i * rows, (i + 1) * rows)

    def along(self):
        self.steps = [self.link.send(self.total.at[1], self.moved, self.place.partner())]

    def close(self):
        arrive(self.steps)
        self.done[...] = (self.total[0].astype(F32) + self.moved[...].astype(F32)).astype(BF)


class Columns(Quarters):
    def piece(self, t, i):
        blocks = self.grad.shape[1] // 2
        return slice(None), slice(i * blocks, (i + 1) * blocks), t

    def halves(self, i):
        blocks = self.grad.shape[1] // 2
        return slice(None), slice(i * blocks, (i + 1) * blocks)

    def cut(self, t, i):
        cols = self.out.shape[3] // 2
        return t, slice(None), slice(None), slice(i * cols, (i + 1) * cols)

    def along(self):
        place = self.place
        copies = []
        for d in range(1, place.dims["seq"]):
            target = place.seq_shift(d)
            copies.append((self.total.at[:, target], self.moved.at[place.me], {"seq": target}))
        self.steps = [self.link.batch(copies, self.moved.at[0 : place.dims["seq"] - 1])]
        self.own = self.link.local(self.total.at[:, place.me], self.moved.at[place.me])

    def close(self):
        arrive(self.steps)
        self.own.wait()
        dims = self.place.dims
        group, width = dims["group"], dims["width"]
        for index in range(3):
            for q in range(group):
                value = self.moved[q, index].astype(F32)
                for half in range(1, dims["items_dev"]):
                    value = value + self.moved[half * group + q, index].astype(F32)
                self.done[index, :, q * width : (q + 1) * width] = value.astype(BF)


class Rows(Quarters):
    def piece(self, t, i):
        return i, t

    def halves(self, i):
        return i

    def cut(self, t, i):
        cols = self.out.shape[2] // 2
        return t, slice(None), slice(i * cols, (i + 1) * cols)

    def along(self):
        self.moved_done = rows_back(self.link, self.place, self.total, self.moved)

    def close(self):
        self.moved_done()
        value = self.moved[0].astype(F32)
        for half in range(1, self.place.dims["items_dev"]):
            value = value + self.moved[half].astype(F32)
        self.done[...] = value.astype(BF)


class Stage:
    def __init__(self, sems, place, part, bufs, mid, spread, before):
        self.link, self.place, self.mid, self.spread = Link(*sems), place, mid, spread
        self.before = before
        self.reduce = Reduce(self.link, place, part, bufs)
        self.started, self.waits = {}, {}

    def start(self, k):
        self.reduce.start(k, k)

    def middle(self, k):
        self.reduce.middle(k, k)

    def end(self, k):
        place, spread = self.place, self.spread
        spread[k, place.c, place.b1, place.b0] = self.mid(k, self.reduce.end(k))
        self.started[k] = spread_start(self.link, place, spread, k)

    def forward(self, k):
        self.waits[k] = spread_end(self.link, self.place, self.spread, k, self.started[k])

    def arrive(self, k):
        arrive(self.waits[k])

    def release(self, k):
        done = (self.reduce.zero[k], self.reduce.one[k])
        for copy in done:
            copy.wait_send()
        late = {id(copy) for copy in done}
        self.link.open = [copy for copy in self.link.open if id(copy) not in late]


def stage_steps(stage, compute, flight=None, ended=None, after=None):
    before = stage.before
    compute(0, (lambda: before.forward(1)) if before else (lambda: None))
    stage.start(0)
    compute(1, lambda: None)
    stage.start(1)
    if before:
        before.link.finish()
    stage.middle(0)
    stage.middle(1)
    if flight:
        flight()
    stage.end(0)
    stage.end(1)
    if ended:
        ended()
    stage.forward(0)
    if after:
        after()


def layer_kernel(dims, names, *refs):
    b = Box(names, refs)
    b.grad_third, b.grad_r2, b.grad_r1, b.gc1_all = b.first, b.second, b.first, b.gy_all
    place = Place(dims)
    sems = b.send_sems, b.recv_sems
    link = Link(*sems, dims["chain"])
    width, block, items_dev = dims["width"], dims["block"], dims["items_dev"]
    h, t, q_place = place.h, place.t, place.q
    c, b1, b0 = place.c, place.b1, place.b0
    partner = place.partner()
    wr = b.w_sq.shape[0] // dims["share"]
    model = dims["model"]
    total_dec, total_mem = dims["total_dec"], dims["total_mem"]
    rb = b.dec.shape[1]

    def rows_of(ref, cols=model):
        return ref[...].reshape(-1, ref.shape[-1])[:, :cols]

    def chunk(ref, k):
        return ref[k].reshape(-1, model)

    half_rows = total_dec // 2

    def span(k):
        return slice(k * half_rows, (k + 1) * half_rows)

    def put(k, value, before=None):
        if before:
            before.release(k)
        b.part[k] = value.astype(BF).reshape(b.part.shape[1:])

    def weight(ref, index):
        return ref[index].reshape(model, width)

    weights = (b.w_sq, b.w_sk, b.w_sv, b.w_so, b.w_ck, b.w_cv, b.w_cq, b.w_co)
    rows_t = pl.ds(pl.multiple_of(t * wr, wr), wr)
    index = link.index()
    for i, w in enumerate(weights):
        pltpu.make_async_copy(w.at[rows_t], b.staged.at[i], b.send_sems.at[index]).start()
    staged = pltpu.make_async_copy(b.staged, b.staged, b.send_sems.at[index])
    own_fin = link.local(b.f_in, b.own_fin)
    own_fout = link.local(b.f_out, b.own_fout)
    greet(place.seq_peers() + place.items_peers())

    def share_columns(dst):
        blocks = dims["seq"] // 2
        return Share(
            link, place, lambda t: dst.at[:, t],
            lambda t, i: dst.at[i * blocks : (i + 1) * blocks, t],
        )

    def share_rows(dst):
        return Share(link, place, lambda t: dst.at[:, t], lambda t, i: dst.at[i, t])

    def share_hidden(dst):
        rows = dst.shape[1] // 2
        return Share(
            link, place, lambda t: dst.at[t], lambda t, i: dst.at[t, i * rows : (i + 1) * rows]
        )

    def join_cells():
        mb = b.cells.shape[1]
        same = lax.broadcasted_iota(jnp.int32, (mb, mb), 0) == lax.broadcasted_iota(
            jnp.int32, (mb, mb), 1
        )
        for k in range(items_dev):
            flags = (b.cells[k : k + 1] == 1).astype(F32)
            column = jnp.sum(jnp.where(same, flags, 0.0), axis=1, keepdims=True)
            b.mem_cells[k, :, :model] = b.mem[k]
            b.mem_cells[k, :, model:] = jnp.broadcast_to(column, (mb, 128)).astype(BF)

    staged.wait()
    steps, own_self = columns_out(link, place, b.staged.at[0:3], b.o_self, width)
    b.x_all[h, c, b1, b0] = b.dec[h]
    join_cells()
    b.m_all[h, c, b1, b0] = b.mem_cells[h]
    link.settle(steps)
    swap_x = link.send(b.dec.at[1 - h], b.x_all.at[h, c, b1, b0], partner)
    first_x = spread_start(link, place, b.x_all, h)
    so_arrived, so_sent = rows_out(link, place, b.staged.at[3], b.o_so)
    steps.wait_recv()
    own_self.wait()
    self_share = [share_columns(b.o_self.at[i]) for i in range(3)]
    waits = spread_end(link, place, b.x_all, h, first_x)
    swap_x.wait_recv()
    second_x = spread_start(link, place, b.x_all, 1 - h)
    waits += spread_end(link, place, b.x_all, 1 - h, second_x)
    cross_steps, own_cross = columns_out(link, place, b.staged.at[4:7], b.o_cross, width)
    co_arrived, co_sent = rows_out(link, place, b.staged.at[7], b.o_co)
    swap_m = link.send(b.mem_cells.at[1 - h], b.m_all.at[h, c, b1, b0], partner)
    first_m = spread_start(link, place, b.m_all, h)
    for share in self_share:
        share.forward()
    so_arrived()
    so_share = share_rows(b.o_so)

    arrive(waits)
    rows = rows_of(b.x_all)
    for index, dst in enumerate((b.sq, b.sk, b.sv)):
        self_share[index].wait()
        dst[...] = nn(rows, weight(b.o_self, index)).astype(BF)
    so_share.forward()
    cross_steps.wait_recv()
    own_cross.wait()
    cross_share = [share_columns(b.o_cross.at[i]) for i in range(3)]
    co_arrived()
    co_share = share_rows(b.o_co)
    mem_waits = spread_end(link, place, b.m_all, h, first_m)
    swap_m.wait_recv()
    second_m = spread_start(link, place, b.m_all, 1 - h)
    own_fin.wait()
    own_fout.wait()
    fr, gr = b.o_fin.shape[1], b.o_fout.shape[1]
    step_fin = link.send(b.own_fin.at[pl.ds(pl.multiple_of(t * fr, fr), fr)], b.o_fin.at[t], partner)
    length, mem_length = b.dec_len[h], b.mem_len[h]

    def self_ok(start, stop):
        keys = lax.broadcasted_iota(jnp.int32, (stop, block), 0)
        spots = lax.broadcasted_iota(jnp.int32, (stop, block), 1) + start
        return (keys <= spots) & (keys < length)

    bufs = [b.recv0, b.send1, b.recv1, b.keep1]
    if dims["bits"] == 3:
        bufs += [b.send2, b.recv2]

    def forward(index, res, summed, out):
        def mid(k, total):
            value = res(k) + total
            summed[k] = value
            normed, _ = moments(value)
            result = normed * b.gain[index : index + 1] + b.bias[index : index + 1]
            out[k] = result
            return result.astype(BF)

        return mid

    def self_part(k, pump):
        attend(
            b.sq, b.sk, b.sv, self_ok, b.sp, b.smix, True, block,
            k * half_rows, (k + 1) * half_rows, pump,
        )
        if k == 0:
            so_share.wait()
        put(k, nn(b.smix[span(k)], rows_of(b.o_so)))

    def memory_part():
        arrive(mem_waits)
        mems = rows_of(b.m_all)
        cross_share[0].wait()
        b.ck[...] = nn(mems, weight(b.o_cross, 0)).astype(BF)
        cross_share[1].wait()
        b.cv[...] = nn(mems, weight(b.o_cross, 1)).astype(BF)
        spots = lax.broadcasted_iota(jnp.int32, (total_mem, 128), 0)
        cells = b.m_all[...].reshape(-1, b.m_all.shape[-1])[:, model:].astype(F32)
        b.keep[...] = ((spots < mem_length) & ((cells > 0.5) | (spots == 0))).astype(F32)

    stage = Stage(
        sems, place, b.part, bufs,
        forward(0, lambda k: b.x_all[k, c, b1, b0].astype(F32), b.sum_one, b.first), b.first_all, None,
    )
    def cross_weights():
        rows = pl.ds(pl.multiple_of(t * gr, gr), gr)
        steps_fout.append(link.send(b.own_fout.at[rows], b.o_fout.at[t], partner))
        mem_waits.extend(spread_end(link, place, b.m_all, 1 - h, second_m))
        for share in cross_share + [co_share]:
            share.forward()
        step_fin.wait_recv()
        ffn_share.append(share_hidden(b.o_fin))

    ffn_share, steps_fout = [], []
    stage_steps(stage, self_part, after=cross_weights)
    memory_part()
    b.c_own[h] = b.cot[h]

    def cross_part(k, pump):
        last.arrive(k)
        if k == 0:
            cross_share[2].wait()
        b.cq[span(k)] = nn(chunk(b.first_all, k), weight(b.o_cross, 2)).astype(BF)
        attend(
            b.cq, b.ck, b.cv, lambda start, stop: b.keep[:, 0:1] > 0.5, b.cp, b.cmix, False, block,
            k * half_rows, (k + 1) * half_rows, pump,
        )
        if k == 0:
            co_share.wait()
        put(k, nn(b.cmix[span(k)], rows_of(b.o_co)), last)

    last = stage
    stage = Stage(
        sems, place, b.part, bufs, forward(1, lambda k: b.first[k], b.sum_two, b.second),
        b.second_all, last,
    )
    def ffn_weights():
        ffn_share[0].forward()
        arrive(steps_fout)
        ffn_share.append(share_hidden(b.o_fout))

    stage_steps(stage, cross_part, ffn_weights)
    swap_c = link.send(b.cot.at[1 - h], b.c_own.at[h], partner)

    w_ins = (lambda: b.own_fin[...], lambda: b.o_fin[...].reshape(model, -1))
    w_outs = (lambda: b.own_fout[...], lambda: b.o_fout[...].reshape(-1, model))
    hidden = b.own_fin.shape[1]
    last_second = stage

    def ffn_part(k, pump):
        last_second.arrive(k)
        if k == 0:
            ffn_share[0].wait()
        rows = chunk(b.second_all, k)
        for index in range(2):
            if index:
                pump()
                if k == 0:
                    ffn_share[1].forward()
            pre = nn(rows, w_ins[index]())
            cdf = 0.5 * (1.0 + lax.erf(pre * (0.5**0.5)))
            cols = slice(index * hidden, (index + 1) * hidden)
            b.act[span(k), cols] = (pre * cdf).astype(BF)
            b.slope[span(k), cols] = (
                cdf + pre * (jnp.exp(-0.5 * pre * pre) * 0.3989422804014327)
            ).astype(BF)
        if k == 0:
            ffn_share[1].wait()
        total = nn(b.act[span(k), :hidden], w_outs[0]())
        put(k, total + nn(b.act[span(k), hidden:], w_outs[1]()), last_second)

    swap_c.wait_recv()

    def add_sums(index, k, normed, grad):
        new = (jnp.sum(grad * normed, axis=0, keepdims=True), jnp.sum(grad, axis=0, keepdims=True))
        for row, value in zip((index, 3 + index), new):
            b.sums[row : row + 1] = value if k == 0 else b.sums[row : row + 1] + value

    def turn(k, total):
        gain = b.gain[2:3]
        normed, inv = moments(b.second[k] + total)
        spots = lax.broadcasted_iota(jnp.int32, (rb, model), 0) + (k * dims["group"] + q_place) * rb
        kept = spots < length
        b.layer[k] = jnp.where(kept, normed * gain + b.bias[2:3], 0.0).astype(BF)
        grad = jnp.where(kept, b.c_own[k].astype(F32), 0.0)
        add_sums(2, k, normed, grad)
        result = norm_back(normed, inv, gain, grad)
        b.grad_third[k] = result
        return result.astype(BF)

    stage = Stage(sems, place, b.part, bufs, turn, b.gy_all, last_second)
    stage_steps(stage, ffn_part)

    last_turn = stage

    way_fout = Hidden(
        link, place, b.g_fout, ("q_fout", "t_fout", "u_fout", dims["lines"] and "l_fout", "s_fout", "z_fout", "d_fout", "r_fout"), b
    )
    def out_grads():
        grad = rows_of(b.gy_all)
        for index in range(2):
            cols = slice(index * hidden, (index + 1) * hidden)
            value = tn(b.act[:, cols], grad)
            b.g_fout[index] = value.astype(BF).reshape(b.g_fout.shape[1:])
        way_fout.send()

    def ffn_back(k, pump):
        last_turn.arrive(k)
        if k == 1:
            out_grads()
        grad = chunk(b.gy_all, k)
        total = None
        for index in range(2):
            if index:
                pump()
            cols = slice(index * hidden, (index + 1) * hidden)
            grad_pre = (nt(grad, w_outs[index]()) * b.slope[span(k), cols].astype(F32)).astype(BF)
            b.slope[span(k), cols] = grad_pre
            term = nt(grad_pre, w_ins[index]())
            total = term if total is None else total + term
        put(k, total, last_turn)

    way_fin = Hidden(
        link, place, b.g_fin, ("q_fin", "t_fin", "u_fin", dims["lines"] and "l_fin", "s_fin", "z_fin", "d_fin", "r_fin"), b
    )
    way_cross = Columns(
        link, place, b.g_cross, ("q_cross", "t_cross", "u_cross", dims["lines"] and "l_cross", "s_cross", "z_cross", "d_cross", "r_cross"), b
    )
    way_self = Columns(
        link, place, b.g_self, ("q_self", "t_self", "u_self", dims["lines"] and "l_self", "s_self", "z_self", "d_self", "r_self"), b
    )
    way_co = Rows(
        link, place, b.g_co, ("q_co", "t_co", "u_co", dims["lines"] and "l_co", "s_co", "z_co", "d_co", "r_co"), b
    )
    way_so = Rows(
        link, place, b.g_so, ("q_so", "t_so", "u_so", dims["lines"] and "l_so", "s_so", "z_so", "d_so", "r_so"), b
    )

    def backward(index, res, summed, out):
        def mid(k, total):
            normed, inv = moments(summed[k])
            grad = res[k] + total
            add_sums(index, k, normed, grad)
            result = norm_back(normed, inv, b.gain[index : index + 1], grad)
            out[k] = result
            return result.astype(BF)

        return mid

    def in_grads():
        rows = rows_of(b.second_all)
        for index in range(2):
            cols = slice(index * hidden, (index + 1) * hidden)
            value = tn(rows, b.slope[:, cols])
            b.g_fin[index] = value.astype(BF).reshape(b.g_fin.shape[1:])
        way_fin.send()

    stage = Stage(
        sems, place, b.part, bufs, backward(1, b.grad_third, b.sum_two, b.grad_r2), b.gc2_all,
        last_turn,
    )
    stage_steps(stage, ffn_back, in_grads)

    last_back = stage

    def cross_back(k, pump):
        last_back.arrive(k)
        b.dmix[span(k)] = nt(chunk(b.gc2_all, k), rows_of(b.o_co)).astype(BF)
        attend_back(
            b.cq, b.ck, b.cv, b.cp, b.dmix, b.dq, b.sum_dk, b.sum_dv, False, block,
            k * half_rows, (k + 1) * half_rows, pump,
        )
        put(k, nt(b.dq[span(k)], weight(b.o_cross, 2)), last_back)
        if k == 1:
            way_fout.turn()

    def cross_grads():
        mems = rows_of(b.m_all)
        shape = b.g_cross.shape[1:]
        b.dck[...] = (b.sum_dk[:total_mem] * SCALE).astype(BF)
        b.dcv[...] = b.sum_dv[:total_mem].astype(BF)
        b.g_cross[0] = tn(rows_of(b.first_all), b.dq[...]).astype(BF).reshape(shape)
        b.g_cross[1] = tn(mems, b.dck[...]).astype(BF).reshape(shape)
        b.g_cross[2] = tn(mems, b.dcv[...]).astype(BF).reshape(shape)
        way_cross.send()
        b.g_co[...] = tn(b.cmix[...], rows_of(b.gc2_all)).astype(BF).reshape(b.g_co.shape)
        way_co.send()
        way_fin.turn()

    def part_mem():
        value = nt(b.dck[...], weight(b.o_cross, 0)) + nt(b.dcv[...], weight(b.o_cross, 1))
        b.part_m[...] = value.astype(BF).reshape(b.part_m.shape)
        for index in range(2):
            red_m.start(index, ks[index])

    stage = Stage(
        sems, place, b.part, bufs, backward(0, b.grad_r2, b.sum_one, b.grad_r1), b.gc1_all,
        last_back,
    )
    ks = (1 - h, h)
    mem_bufs = [b.recv0_m, b.send1_m, b.recv1_m, b.keep1_m]
    if dims["bits"] == 3:
        mem_bufs += [b.send2_m, b.recv2_m]
    red_m = Reduce(link, place, b.part_m, mem_bufs)
    stage_steps(stage, cross_back, cross_grads, part_mem)

    swap_l = link.send(b.layer.at[1 - h], b.layer_out.at[h], partner)
    b.layer_out[h] = b.layer[h]
    way_fout.add()
    for k in range(2):
        stage.arrive(k)
        pump = (lambda: stage.forward(1)) if k == 0 else (lambda: None)
        b.dmix[span(k)] = nt(chunk(b.gc1_all, k), rows_of(b.o_so)).astype(BF)
        attend_back(
            b.sq, b.sk, b.sv, b.sp, b.dmix, b.dq, b.sum_dk, b.sum_dv, True, block,
            k * half_rows, (k + 1) * half_rows, pump,
        )
        red_m.middle(k, ks[k])
    b.dsk[...] = (b.sum_dk[...] * SCALE).astype(BF)
    b.dsv[...] = b.sum_dv[...].astype(BF)
    for k in range(2):
        total = nt(b.dq[span(k)], weight(b.o_self, 0)) + nt(b.dsk[span(k)], weight(b.o_self, 1))
        put(k, total + nt(b.dsv[span(k)], weight(b.o_self, 2)), stage)
    stage.link.finish()
    chain = Link(*sems)
    red_x = Reduce(chain, place, b.part, bufs)
    for index in range(2):
        red_x.start(index, ks[index])
    way_cross.turn()
    way_co.turn()
    way_fin.add()
    rows = rows_of(b.x_all)
    shape = b.g_self.shape[1:]
    b.g_self[0] = tn(rows, b.dq[...]).astype(BF).reshape(shape)
    b.g_self[1] = tn(rows, b.dsk[...]).astype(BF).reshape(shape)
    b.g_self[2] = tn(rows, b.dsv[...]).astype(BF).reshape(shape)
    way_self.send()
    b.g_so[...] = tn(b.smix[...], rows_of(b.gc1_all)).astype(BF).reshape(b.g_so.shape)
    way_so.send()
    for index in range(2):
        red_x.middle(index, ks[index])
    b.send_m[...] = red_m.end(0).astype(BF)
    swap_m = link.send(b.send_m, b.recv_m, partner)
    b.grad_mem[h] = red_m.end(1)
    copies = []
    for d in range(1, dims["seq"]):
        copies.append((b.sums, b.sums_seq.at[d - 1], {"seq": place.seq_shift(d)}))
    seq_sums = link.batch(copies, b.sums_seq)
    way_cross.add()
    way_co.add()
    b.send_x[...] = (red_x.end(0) + b.grad_r1[1 - h]).astype(BF)
    swap_x = link.send(b.send_x, b.recv_x, partner)
    b.grad_dec[h] = red_x.end(1) + b.grad_r1[h]
    way_fout.gather()
    way_self.turn()
    way_so.turn()
    way_fin.gather()
    way_fout.forward()
    way_self.add()
    way_so.add()
    way_cross.gather()
    way_co.gather()
    way_fin.forward()
    seq_sums.wait_recv()
    value = b.sums[...]
    for d in range(1, dims["seq"]):
        value = value + b.sums_seq[d - 1]
    b.sums_line[...] = value
    copies = []
    for e in range(1, dims["items"]):
        target = {"items": lax.rem(place.it + e, dims["items"])}
        copies.append((b.sums_line, b.sums_items.at[e - 1], target))
    item_sums = link.batch(copies, b.sums_items)
    swap_x.wait_recv()
    b.grad_dec[1 - h] = b.recv_x[...].astype(F32)
    swap_m.wait_recv()
    b.grad_mem[1 - h] = b.recv_m[...].astype(F32)
    swap_l.wait_recv()
    way_self.gather()
    way_so.gather()
    way_cross.forward()
    way_co.forward()
    item_sums.wait_recv()
    value = b.sums_line[...]
    for e in range(1, dims["items"]):
        value = value + b.sums_items[e - 1]
    b.sums_out[...] = value
    way_self.forward()
    way_so.forward()
    for way in (way_fout, way_fin, way_cross, way_co, way_self, way_so):
        way.finish()
    so_sent()
    co_sent()
    chain.finish()
    link.finish()


def shape(dims, dtype):
    return jax.ShapeDtypeStruct(tuple(dims), dtype)


def outputs_kernel(layer, dec, mem, cross, own, co, so, fin, fout, sums, *outs):
    o_layer, o_dec, o_mem = outs[:3]
    o_layer[...] = layer[...]
    o_dec[...] = dec[...]
    o_mem[...] = mem[...]
    for index in range(3):
        outs[3 + index][...] = own[0, index].astype(F32)
        outs[7 + index][...] = cross[0, index].astype(F32)
    outs[6][...] = so[0].astype(F32)
    outs[10][...] = co[0].astype(F32)
    outs[11][...] = fin[0].astype(F32)
    outs[12][...] = fout[0].astype(F32)
    outs[13][...] = sums[0:3]
    outs[14][...] = sums[3:6]


def shards(
    mesh, dec_in, memory, dec_len, mem_len, cell_mask, self_query, self_key, self_value, self_out,
    cross_query, cross_key, cross_value, cross_out, ffn_in, ffn_out, norm_gain, norm_bias, cotangent,
):
    items_dev, rb, model = dec_in.shape
    mb = memory.shape[1]
    seq, items = mesh.shape["seq"], mesh.shape["items"]
    group = seq // items_dev
    share = 4
    bits = group.bit_length() - 1
    chips = group // 4
    width = model // group
    total_dec, total_mem = rb * seq, mb * seq
    heads = width // HEAD_DIM
    hidden = ffn_in.shape[1]
    wr = self_query.shape[0] // share
    fr, gr = model // share, hidden // share
    lines = items // share - 1
    dims = {
        "items_dev": items_dev, "items": items, "seq": seq, "group": group, "share": share,
        "bits": bits, "chips": chips, "width": width, "model": model, "block": 256,
        "total_dec": total_dec, "total_mem": total_mem, "lines": lines,
        "chain": 12 + 2 * (bits - 2),
    }
    ins = [
        ("dec", dec_in, VM), ("mem", memory, VM), ("cells", cell_mask, VM), ("cot", cotangent, VM),
        ("dec_len", dec_len, SM), ("mem_len", mem_len, SM),
        ("w_sq", self_query, HBM), ("w_sk", self_key, HBM), ("w_sv", self_value, HBM),
        ("w_so", self_out, HBM), ("w_cq", cross_query, HBM), ("w_ck", cross_key, HBM),
        ("w_cv", cross_value, HBM), ("w_co", cross_out, HBM), ("f_in", ffn_in, HBM),
        ("f_out", ffn_out, HBM), ("gain", norm_gain, VM), ("bias", norm_bias, VM),
    ]
    own, own_m = (items_dev, rb, model), (items_dev, mb, model)
    grid = (items_dev, chips, 2, 2)
    outs = [
        ("layer_out", own, BF, VM), ("grad_dec", own, F32, VM), ("grad_mem", own_m, F32, VM),
        ("sums_out", (8, model), F32, VM),
        ("r_cross", (share, 3, wr, model), BF, HBM), ("r_self", (share, 3, wr, model), BF, HBM),
        ("r_co", (share, wr, model), BF, HBM), ("r_so", (share, wr, model), BF, HBM),
        ("r_fin", (share, fr, hidden), BF, HBM), ("r_fout", (share, gr, model), BF, HBM),
    ]
    cols = (3, seq, share, wr, width)
    scratch = [
        ("x_all", grid + (rb, model), BF), ("m_all", grid + (mb, model + 128), BF),
        ("mem_cells", (items_dev, mb, model + 128), BF), ("c_own", own, BF), ("staged", (8, wr, model), BF),
        ("own_fin", (model, hidden), BF), ("own_fout", (hidden, model), BF),
        ("o_self", cols, BF), ("o_cross", cols, BF),
        ("o_so", (items_dev, share, wr, model), BF), ("o_co", (items_dev, share, wr, model), BF),
        ("o_fin", (share, fr, hidden), BF), ("o_fout", (share, gr, model), BF),
        ("sq", (total_dec, width), BF), ("sk", (total_dec, width), BF), ("sv", (total_dec, width), BF),
        ("cq", (total_dec, width), BF), ("ck", (total_mem, width), BF), ("cv", (total_mem, width), BF),
        ("sp", (heads, total_dec, total_dec), BF), ("cp", (heads, total_mem, total_dec), BF),
        ("smix", (total_dec, width), BF), ("cmix", (total_dec, width), BF),
        ("keep", (total_mem, 128), F32),
        ("part", grid + (rb, model), BF), ("part_m", grid + (mb, model), BF),
        ("first_all", grid + (rb, model), BF), ("second_all", grid + (rb, model), BF),
        ("gy_all", grid + (rb, model), BF), ("gc2_all", grid + (rb, model), BF),
        ("sum_one", own, F32), ("sum_two", own, F32), ("first", own, F32), ("second", own, F32),
        ("layer", own, BF), ("sum_dk", (total_dec, width), F32), ("sum_dv", (total_dec, width), F32),
        ("act", (total_dec, 2 * hidden), BF), ("slope", (total_dec, 2 * hidden), BF),
        ("dmix", (total_dec, width), BF), ("dq", (total_dec, width), BF),
        ("dsk", (total_dec, width), BF), ("dsv", (total_dec, width), BF),
        ("dck", (total_mem, width), BF), ("dcv", (total_mem, width), BF),
        ("send_x", (rb, model), BF), ("recv_x", (rb, model), BF),
        ("send_m", (mb, model), BF), ("recv_m", (mb, model), BF),
        ("sums", (8, model), F32), ("sums_line", (8, model), F32),
        ("sums_seq", (seq - 1, 8, model), F32), ("sums_items", (items - 1, 8, model), F32),
    ]
    for name, rows in (("", rb), ("_m", mb)):
        scratch += [
            ("recv0" + name, (items_dev, chips, 2, rows, model), BF),
            ("send1" + name, (items_dev, chips, rows, model), BF),
            ("recv1" + name, (items_dev, chips, rows, model), BF),
            ("keep1" + name, (items_dev, chips, rows, model), F32),
        ]
        if bits == 3:
            scratch += [
                ("send2" + name, (items_dev, rows, model), BF),
                ("recv2" + name, (items_dev, rows, model), BF),
            ]
    for name, grad, quarter, piece, moved, done in (
        ("fin", (2, share, fr, hidden), (2, fr, hidden), (2, fr // 2, hidden), (fr, hidden),
         (fr, hidden)),
        ("fout", (2, share, gr, model), (2, gr, model), (2, gr // 2, model), (gr, model), (gr, model)),
        ("cross", cols, (3, seq, wr, width), (3, seq // 2, wr, width), (seq, 3, wr, width),
         (3, wr, model)),
        ("self", cols, (3, seq, wr, width), (3, seq // 2, wr, width), (seq, 3, wr, width),
         (3, wr, model)),
        ("co", (items_dev, share, wr, model), (items_dev, wr, model), (wr, model),
         (items_dev, wr, model), (wr, model)),
        ("so", (items_dev, share, wr, model), (items_dev, wr, model), (wr, model),
         (items_dev, wr, model), (wr, model)),
    ):
        scratch += [
            ("g_" + name, grad, BF), ("q_" + name, (2, 2) + piece, BF), ("t_" + name, (2,) + piece, BF),
            ("u_" + name, (2,) + piece, BF), ("s_" + name, quarter, BF), ("z_" + name, moved, BF),
            ("d_" + name, done, BF),
        ]
        if lines:
            scratch.append(("l_" + name, (lines,) + quarter, BF))
    copies = dims["chain"] + 145 + 12 * (bits - 2)
    names = [x[0] for x in ins + outs + scratch] + ["send_sems", "recv_sems"]
    results = pl.pallas_call(
        functools.partial(layer_kernel, dims, names),
        name="layer",
        out_shape=[shape(x[1], x[2]) for x in outs],
        in_specs=[x[2] for x in ins],
        out_specs=[x[3] for x in outs],
        scratch_shapes=[pltpu.VMEM(x[1], x[2]) for x in scratch]
        + [pltpu.SemaphoreType.DMA((copies,)), pltpu.SemaphoreType.DMA((copies,))],
        compiler_params=pltpu.CompilerParams(
            collective_id=0, has_side_effects=True, vmem_limit_bytes=VMEM_BYTES
        ),
    )(*[x[1] for x in ins])
    layer_out, grad_dec, grad_memory, sums, r_cross, r_self, r_co, r_so, r_fin, r_fout = results
    tok, mem_rows = items_dev * rb, items_dev * mb
    pieces = (
        ((tok, model), (tok // share, model), BF), ((tok, model), (tok // share, model), F32),
        ((mem_rows, model), (mem_rows // share, model), F32),
    )
    heads_in = [
        pl.BlockSpec((1, 3, wr, model), lambda i: (i, 0, 0, 0)),
        pl.BlockSpec((1, 3, wr, model), lambda i: (i, 0, 0, 0)),
        pl.BlockSpec((1, wr, model), lambda i: (i, 0, 0)),
        pl.BlockSpec((1, wr, model), lambda i: (i, 0, 0)),
        pl.BlockSpec((1, fr, hidden), lambda i: (i, 0, 0)),
        pl.BlockSpec((1, gr, model), lambda i: (i, 0, 0)),
        pl.BlockSpec((8, model), lambda i: (0, 0)),
    ]
    row_specs = [pl.BlockSpec(x[1], lambda i: (i, 0)) for x in pieces]
    square = (share * wr, model)
    outs = pl.pallas_call(
        outputs_kernel,
        name="outputs",
        grid=(share,),
        in_specs=row_specs + heads_in,
        out_specs=row_specs
        + [pl.BlockSpec((wr, model), lambda i: (i, 0))] * 8
        + [pl.BlockSpec((fr, hidden), lambda i: (i, 0)), pl.BlockSpec((gr, model), lambda i: (i, 0))]
        + [pl.BlockSpec((3, model), lambda i: (0, 0))] * 2,
        out_shape=[shape(x[0], x[2]) for x in pieces]
        + [shape(square, F32)] * 8
        + [shape((model, hidden), F32), shape((hidden, model), F32)]
        + [shape((3, model), F32)] * 2,
        compiler_params=pltpu.CompilerParams(vmem_limit_bytes=VMEM_BYTES),
    )(
        layer_out.reshape(tok, model), grad_dec.reshape(tok, model),
        grad_memory.reshape(mem_rows, model), r_cross, r_self, r_co, r_so, r_fin, r_fout, sums,
    )
    return (
        outs[0].reshape(own), outs[1].reshape(own), outs[2].reshape(own_m), *outs[3:],
    )


def solution(mesh):
    rows = P("seq", None)
    tokens = P("items", "seq", None)
    placed = (
        (tokens, tokens, P("items"), P("items"), P("items", "seq"))
        + (rows,) * 8
        + (P(None, "seq"), rows, P(), P(), tokens)
    )
    return jax.shard_map(
        functools.partial(shards, mesh),
        mesh=mesh,
        in_specs=placed,
        out_specs=(tokens,) * 3 + (rows,) * 8 + (P(None, "seq"), rows, P(), P()),
        check_vma=False,
    )
```

```python
import functools

import jax
import jax.numpy as jnp
from jax import lax
from jax.experimental import pallas as pl
from jax.experimental.pallas import tpu as pltpu
from jax.sharding import PartitionSpec as P

HEAD_DIM = 64
EPS = 1e-05
NEG = -1e30
SCALE = HEAD_DIM ** (-0.5)
BF = jnp.bfloat16
F32 = jnp.float32
VMEM_BYTES = 63 * 1024 * 1024
MESH = pl.DeviceIdType.MESH
VM = pl.BlockSpec(memory_space=pltpu.VMEM)
HBM = pl.BlockSpec(memory_space=pl.ANY)
SM = pl.BlockSpec(memory_space=pltpu.SMEM)


def nn(left, right):
    return lax.dot_general(left, right, (((1,), (0,)), ((), ())), preferred_element_type=F32)


def nt(left, right):
    return lax.dot_general(left, right, (((1,), (1,)), ((), ())), preferred_element_type=F32)


def tn(left, right):
    return lax.dot_general(left, right, (((0,), (0,)), ((), ())), preferred_element_type=F32)


class Link:
    def __init__(self, send_sems, recv_sems, first=0):
        self.send_sems, self.recv_sems, self.count, self.open = send_sems, recv_sems, first, []

    def index(self):
        self.count += 1
        return self.count - 1

    def make(self, src, dst, device, index):
        return pltpu.make_async_remote_copy(
            src_ref=src,
            dst_ref=dst,
            send_sem=self.send_sems.at[index],
            recv_sem=self.recv_sems.at[index],
            device_id=device,
            device_id_type=MESH,
        )

    def send(self, src, dst, device):
        copy = self.make(src, dst, device, self.index())
        copy.start()
        self.open.append(copy)
        return copy

    def batch(self, copies, whole):
        index = self.index()
        for copy in copies:
            self.make(*copy, index).start()
        wait = self.make(whole, whole, copies[0][2], index)
        self.open.append(wait)
        return wait

    def settle(self, copy):
        copy.wait_send()
        self.open = [other for other in self.open if other is not copy]

    def local(self, src, dst):
        copy = pltpu.make_async_copy(src, dst, self.send_sems.at[self.index()])
        copy.start()
        return copy

    def finish(self, kept=()):
        late = {id(copy) for copy in kept}
        for copy in self.open:
            if id(copy) not in late:
                copy.wait_send()
        self.open = [copy for copy in self.open if id(copy) in late]


def greet(devices):
    barrier = pltpu.get_barrier_semaphore()
    for device in devices:
        pl.semaphore_signal(barrier, inc=1, device_id=device, device_id_type=MESH)
    pl.semaphore_wait(barrier, len(devices))


class Place:
    def __init__(self, dims):
        self.dims = dims
        group, share = dims["group"], dims["share"]
        self.me = lax.axis_index("seq")
        self.h = self.me // group
        self.q = self.me % group
        self.b0 = self.q % 2
        self.b1 = (self.q // 2) % 2
        self.c = self.q // 4
        self.it = lax.axis_index("items")
        self.base = (self.it // share) * share
        self.t = self.it % share
        x, y = self.t % 2, self.t // 2
        self.tx, self.ty, self.txy = y * 2 + 1 - x, (1 - y) * 2 + x, (1 - y) * 2 + 1 - x

    def across(self, bit):
        value = (self.q // (1 << bit)) % 2
        return {"seq": self.me + (1 - 2 * value) * (1 << bit)}

    def partner(self):
        return {"seq": (1 - self.h) * self.dims["group"] + self.q}

    def seq_shift(self, d):
        return lax.rem(self.me + d, self.dims["seq"])

    def line(self, t):
        return {"items": self.base + t}

    def seq_peers(self):
        return [{"seq": self.seq_shift(d)} for d in range(1, self.dims["seq"])]

    def items_peers(self):
        count = self.dims["items"]
        return [{"items": lax.rem(self.it + e, count)} for e in range(1, count)]


def spread_start(link, place, out, k):
    bits = place.dims["bits"]
    c, b1, b0 = place.c, place.b1, place.b0
    if bits == 3:
        step = link.send(out.at[k, c, b1, b0], out.at[k, c, b1, b0], place.across(2))
        step.wait_recv()
    waits = []
    high = link.send(out.at[k, :, b1, b0], out.at[k, :, b1, b0], place.across(1))
    waits.append(link.send(out.at[k, :, b1, b0], out.at[k, :, b1, b0], place.across(0)))
    return high, waits


def spread_end(link, place, out, k, started):
    high, waits = started
    b1, b0 = place.b1, place.b0
    high.wait_recv()
    waits.append(link.send(out.at[k, :, 1 - b1, b0], out.at[k, :, 1 - b1, b0], place.across(0)))
    return waits


def columns_out(link, place, src, dst, width):
    seq, group = place.dims["seq"], place.dims["group"]
    copies = []
    for d in range(1, seq):
        target = place.seq_shift(d)
        cols = pl.ds(pl.multiple_of(lax.rem(target, group) * width, width), width)
        copies.append((src.at[:, :, cols], dst.at[:, place.me, place.t], {"seq": target}))
    steps = link.batch(copies, dst.at[:, 0 : seq - 1, place.t])
    cols = pl.ds(pl.multiple_of(place.q * width, width), width)
    return steps, link.local(src.at[:, :, cols], dst.at[:, place.me, place.t])


def rows_out(link, place, src, dst):
    dims, me = place.dims, place.me
    slot = lax.rem(me, dims["items_dev"])
    base = link.count
    link.count += dims["items_dev"] + 1
    copies = []
    for half in range(dims["items_dev"]):
        target = half * dims["group"] + me // dims["items_dev"]
        copy = pltpu.make_async_remote_copy(
            src_ref=src,
            dst_ref=dst.at[slot, place.t],
            send_sem=link.send_sems.at[base + half],
            recv_sem=link.recv_sems.at[base + slot],
            device_id={"seq": target},
            device_id_type=MESH,
        )
        copies.append((target != me, copy))
        pl.when(target != me)(copy.start)
    own = pltpu.make_async_copy(
        src, dst.at[slot, place.t], link.send_sems.at[base + dims["items_dev"]]
    )
    mine = me // dims["items_dev"] == place.q
    pl.when(mine)(own.start)

    def arrived():
        pl.when(mine)(own.wait)
        for block in range(dims["items_dev"]):
            copy = pltpu.make_async_remote_copy(
                src_ref=src,
                dst_ref=dst.at[block, place.t],
                send_sem=link.send_sems.at[base],
                recv_sem=link.recv_sems.at[base + block],
                device_id={"seq": me},
                device_id_type=MESH,
            )
            pl.when(place.q * dims["items_dev"] + block != me)(copy.wait_recv)

    def sent():
        for other, copy in copies:
            pl.when(other)(copy.wait_send)

    return arrived, sent


class Share:
    def __init__(self, link, place, slab, half):
        self.link, self.place, self.half = link, place, half
        t = place.t
        self.from_x = link.send(slab(t), slab(t), place.line(place.tx))
        self.from_y = link.send(slab(t), slab(t), place.line(place.ty))

    def forward(self):
        link, place, half = self.link, self.place, self.half
        self.from_y.wait_recv()
        part = half(place.ty, 0)
        self.steps = [link.send(part, part, place.line(place.tx))]
        self.from_x.wait_recv()
        part = half(place.tx, 1)
        self.steps.append(link.send(part, part, place.line(place.ty)))

    def wait(self):
        arrive(self.steps)


class Direct(Share):
    def __init__(self, link, place, slab):
        lines = (place.tx, place.ty, place.txy)
        self.steps = [link.send(slab(place.t), slab(place.t), place.line(line)) for line in lines]

    def forward(self):
        pass


def arrive(steps):
    for step in steps:
        step.wait_recv()


class Reduce:
    def __init__(self, link, place, part, bufs):
        self.link, self.place, self.part, self.bufs = link, place, part, bufs
        self.zero, self.one = {}, {}

    def start(self, index, k):
        place = self.place
        self.zero[index] = self.link.send(
            self.part.at[k, :, :, 1 - place.b0], self.bufs[0].at[index], place.across(0)
        )

    def middle(self, index, k):
        place, part = self.place, self.part
        recv0, send1, recv1, keep1 = self.bufs[:4]
        self.zero[index].wait_recv()
        b1, b0 = place.b1, place.b0
        for c in range(part.shape[1]):
            value = part[k, c, 1 - b1, b0].astype(F32) + recv0[index, c, 1 - b1].astype(F32)
            send1[index, c] = value.astype(BF)
        self.one[index] = self.link.send(send1.at[index], recv1.at[index], place.across(1))
        for c in range(part.shape[1]):
            keep1[index, c] = part[k, c, b1, b0].astype(F32) + recv0[index, c, b1].astype(F32)

    def end(self, index):
        place = self.place
        recv1, keep1 = self.bufs[2:4]
        self.one[index].wait_recv()
        if place.dims["bits"] == 2:
            return keep1[index, 0] + recv1[index, 0].astype(F32)
        send2, recv2 = self.bufs[4:6]
        c = place.c
        send2[index] = (keep1[index, 1 - c] + recv1[index, 1 - c].astype(F32)).astype(BF)
        step = self.link.send(send2.at[index], recv2.at[index], place.across(2))
        kept = keep1[index, c] + recv1[index, c].astype(F32)
        step.wait_recv()
        return kept + recv2[index].astype(F32)


def reduce_bufs(dims, rows):
    items_dev, width, chips = dims["items_dev"], dims["model"], dims["chips"]
    bufs = [
        pltpu.VMEM((items_dev, chips, 2, rows, width), BF),
        pltpu.VMEM((items_dev, chips, rows, width), BF),
        pltpu.VMEM((items_dev, chips, rows, width), BF),
        pltpu.VMEM((items_dev, chips, rows, width), F32),
    ]
    if dims["bits"] == 3:
        bufs += [pltpu.VMEM((items_dev, rows, width), BF) for _ in range(2)]
    return bufs


def moments(value):
    mean = jnp.mean(value, axis=-1, keepdims=True)
    centered = value - mean
    inv = lax.rsqrt(jnp.mean(centered * centered, axis=-1, keepdims=True) + EPS)
    return centered * inv, inv


def norm_back(normed, inv, gain, grad):
    scaled = grad * gain
    mean = jnp.mean(scaled, axis=-1, keepdims=True)
    cross = jnp.mean(scaled * normed, axis=-1, keepdims=True)
    return inv * (scaled - mean - normed * cross)


def rows_back(link, place, src, dst):
    dims, me, h = place.dims, place.me, place.h
    count = dims["items_dev"]
    base = link.count
    link.count += count + 1
    copies = []
    for k in range(count):
        target = place.q * count + k
        copy = pltpu.make_async_remote_copy(
            src_ref=src.at[k],
            dst_ref=dst.at[h],
            send_sem=link.send_sems.at[base + k],
            recv_sem=link.recv_sems.at[base + h],
            device_id={"seq": target},
            device_id_type=MESH,
        )
        copies.append((target != me, copy))
        pl.when(target != me)(copy.start)
    own = pltpu.make_async_copy(
        src.at[lax.rem(me, count)], dst.at[h], link.send_sems.at[base + count]
    )
    mine = me // count == place.q
    pl.when(mine)(own.start)

    def done():
        pl.when(mine)(own.wait)
        for half in range(count):
            copy = pltpu.make_async_remote_copy(
                src_ref=src.at[0],
                dst_ref=dst.at[half],
                send_sem=link.send_sems.at[base],
                recv_sem=link.recv_sems.at[base + half],
                device_id={"seq": me},
                device_id_type=MESH,
            )
            pl.when(half * dims["group"] + me // count != me)(copy.wait_recv)
        for other, copy in copies:
            pl.when(other)(copy.wait_send)

    return done


def half_mask(rows, half):
    return (lax.broadcasted_iota(jnp.int32, (rows, 128), 1) // HEAD_DIM) == half


def attend(q_ref, k_ref, v_ref, valid, p_ref, mix_ref, causal, block, first, last, pump):
    keys = k_ref.shape[0]
    for pair in range(q_ref.shape[1] // 128):
        lanes = slice(pair * 128, pair * 128 + 128)
        for start in range(first, last, block):
            stop = start + block if causal else keys
            halves = []
            for half in range(2):
                query = q_ref[start : start + block, lanes]
                query = jnp.where(half_mask(block, half), query, jnp.zeros_like(query))
                scores = nt(k_ref[:stop, lanes], query) * SCALE
                scores = jnp.where(valid(start, stop), scores, NEG)
                top = jnp.max(scores, axis=0, keepdims=True)
                grown = jnp.exp(scores - top)
                probs = (grown * (1.0 / jnp.sum(grown, axis=0, keepdims=True))).astype(BF)
                p_ref[2 * pair + half, :stop, start : start + block] = probs
                mixed = tn(v_ref[:stop, lanes], probs)
                halves.append(mixed[half * HEAD_DIM : (half + 1) * HEAD_DIM])
            mix_ref[start : start + block, lanes] = jnp.concatenate(halves, axis=0).T.astype(BF)
        if pair == 0:
            pump()


def attend_back(
    q_ref, k_ref, v_ref, p_ref, grad_ref, dq_ref, dk_ref, dv_ref, causal, block, first, last,
    pump,
):
    keys = k_ref.shape[0]
    for pair in range(q_ref.shape[1] // 128):
        lanes = slice(pair * 128, pair * 128 + 128)
        for start in range(first, last, block):
            stop = start + block if causal else keys
            halves = []
            sum_k, sum_v = None, None
            for half in range(2):
                mask = half_mask(block, half)
                query = q_ref[start : start + block, lanes]
                query = jnp.where(mask, query, jnp.zeros_like(query))
                grad = grad_ref[start : start + block, lanes]
                grad = jnp.where(mask, grad, jnp.zeros_like(grad))
                low = p_ref[2 * pair + half, :stop, start : start + block]
                probs = low.astype(F32)
                grad_probs = nt(v_ref[:stop, lanes], grad)
                delta = jnp.sum(probs * grad_probs, axis=0, keepdims=True)
                grad_scores = (probs * (grad_probs - delta)).astype(BF)
                turned = tn(k_ref[:stop, lanes], grad_scores) * SCALE
                halves.append(turned[half * HEAD_DIM : (half + 1) * HEAD_DIM])
                new_k, new_v = nn(grad_scores, query), nn(low, grad)
                sum_k = new_k if sum_k is None else sum_k + new_k
                sum_v = new_v if sum_v is None else sum_v + new_v
            old = start if causal else (keys if start else 0)
            for ref, value in ((dk_ref, sum_k), (dv_ref, sum_v)):
                if old:
                    ref[:old, lanes] = ref[:old, lanes] + value[:old]
                if old < stop:
                    ref[old:stop, lanes] = value[old:]
            dq_ref[start : start + block, lanes] = jnp.concatenate(halves, axis=0).T.astype(BF)
        if pair == 0:
            pump()


class Box:
    def __init__(self, names, refs):
        for name, ref in zip(names, refs):
            setattr(self, name, ref)


class Quarters:
    def __init__(self, link, place, grad, box_names, box):
        self.link, self.place, self.grad = link, place, grad
        self.recv, self.sums, self.last, self.lines, self.total, self.moved, self.done, self.out = (
            getattr(box, name) if name else None for name in box_names
        )

    def send(self):
        place, piece, link = self.place, self.piece, self.link
        self.steps = []
        for i, near in enumerate((place.tx, place.ty)):
            copies = [
                (self.grad.at[piece(near, i)], self.recv.at[i, 0], place.line(near)),
                (self.grad.at[piece(place.txy, i)], self.recv.at[i, 1], place.line(near)),
            ]
            self.steps.append(link.batch(copies, self.recv.at[i]))
        self.flying = list(self.steps)

    def turn(self):
        place, piece, link = self.place, self.piece, self.link
        steps = []
        for i, far in enumerate((place.ty, place.tx)):
            self.steps[i].wait_recv()
            value = self.grad[piece(far, i)].astype(F32) + self.recv[i, 1].astype(F32)
            self.sums[i] = value.astype(BF)
            steps.append(link.send(self.sums.at[i], self.last.at[i], place.line(far)))
        self.steps = steps
        self.flying += steps

    def add(self):
        place = self.place
        for i in range(2):
            self.steps[i].wait_recv()
            value = self.grad[self.piece(place.t, i)].astype(F32)
            value = value + self.recv[i, 0].astype(F32) + self.last[i].astype(F32)
            self.total[self.halves(i)] = value.astype(BF)
        if self.lines is not None:
            share, items = place.dims["share"], place.dims["items"]
            copies = []
            for a in range(1, items // share):
                target = {"items": lax.rem(place.it + a * share, items)}
                copies.append((self.total, self.lines.at[a - 1], target))
            step = self.link.batch(copies, self.lines)
            step.wait()
            self.link.open.pop()
            value = self.total[...].astype(F32)
            for a in range(1, items // share):
                value = value + self.lines[a - 1].astype(F32)
            self.total[...] = value.astype(BF)
        self.along()

    def gather(self):
        self.close()
        place, out = self.place, self.out
        self.own = self.link.local(self.done, out.at[place.t])
        self.near = [
            self.link.send(self.done, out.at[place.t], place.line(near))
            for near in (place.tx, place.ty)
        ]

    def forward(self):
        place, out, link = self.place, self.out, self.link
        self.steps = []
        for i, (source, near) in enumerate(((place.ty, place.tx), (place.tx, place.ty))):
            self.near[1 - i].wait_recv()
            part = out.at[self.cut(source, i)]
            self.steps.append(link.send(part, part, place.line(near)))

    def finish(self):
        arrive(self.steps)
        self.own.wait()


class Hidden(Quarters):
    def piece(self, t, i):
        rows = self.grad.shape[2] // 2
        return slice(None), t, slice(i * rows, (i + 1) * rows)

    def halves(self, i):
        rows = self.grad.shape[2] // 2
        return slice(None), slice(i * rows, (i + 1) * rows)

    def cut(self, t, i):
        rows = self.out.shape[1] // 2
        return t, slice(i * rows, (i + 1) * rows)

    def along(self):
        self.steps = [self.link.send(self.total.at[1], self.moved, self.place.partner())]

    def close(self):
        arrive(self.steps)
        self.done[...] = (self.total[0].astype(F32) + self.moved[...].astype(F32)).astype(BF)


class Columns(Quarters):
    def piece(self, t, i):
        blocks = self.grad.shape[1] // 2
        return slice(None), slice(i * blocks, (i + 1) * blocks), t

    def halves(self, i):
        blocks = self.grad.shape[1] // 2
        return slice(None), slice(i * blocks, (i + 1) * blocks)

    def cut(self, t, i):
        cols = self.out.shape[3] // 2
        return t, slice(None), slice(None), slice(i * cols, (i + 1) * cols)

    def along(self):
        place = self.place
        copies = []
        for d in range(1, place.dims["seq"]):
            target = place.seq_shift(d)
            copies.append((self.total.at[:, target], self.moved.at[place.me], {"seq": target}))
        self.steps = [self.link.batch(copies, self.moved.at[0 : place.dims["seq"] - 1])]
        self.own = self.link.local(self.total.at[:, place.me], self.moved.at[place.me])

    def close(self):
        arrive(self.steps)
        self.own.wait()
        dims = self.place.dims
        group, width = dims["group"], dims["width"]
        for index in range(3):
            for q in range(group):
                value = self.moved[q, index].astype(F32)
                for half in range(1, dims["items_dev"]):
                    value = value + self.moved[half * group + q, index].astype(F32)
                self.done[index, :, q * width : (q + 1) * width] = value.astype(BF)


class Rows(Quarters):
    def piece(self, t, i):
        return i, t

    def halves(self, i):
        return i

    def cut(self, t, i):
        cols = self.out.shape[2] // 2
        return t, slice(None), slice(i * cols, (i + 1) * cols)

    def along(self):
        self.moved_done = rows_back(self.link, self.place, self.total, self.moved)

    def close(self):
        self.moved_done()
        value = self.moved[0].astype(F32)
        for half in range(1, self.place.dims["items_dev"]):
            value = value + self.moved[half].astype(F32)
        self.done[...] = value.astype(BF)


class Stage:
    def __init__(self, sems, place, part, bufs, mid, spread, before):
        self.link, self.place, self.mid, self.spread = Link(*sems), place, mid, spread
        self.before = before
        self.reduce = Reduce(self.link, place, part, bufs)
        self.started, self.waits = {}, {}

    def start(self, k):
        self.reduce.start(k, k)

    def middle(self, k):
        self.reduce.middle(k, k)

    def end(self, k):
        place, spread = self.place, self.spread
        spread[k, place.c, place.b1, place.b0] = self.mid(k, self.reduce.end(k))
        self.started[k] = spread_start(self.link, place, spread, k)

    def forward(self, k):
        self.waits[k] = spread_end(self.link, self.place, self.spread, k, self.started[k])

    def arrive(self, k):
        arrive(self.waits[k])

    def release(self, k):
        done = (self.reduce.zero[k], self.reduce.one[k])
        for copy in done:
            copy.wait_send()
        late = {id(copy) for copy in done}
        self.link.open = [copy for copy in self.link.open if id(copy) not in late]


def stage_steps(stage, compute, flight=None, ended=None, after=None):
    before = stage.before
    compute(0, (lambda: before.forward(1)) if before else (lambda: None))
    stage.start(0)
    compute(1, lambda: None)
    stage.start(1)
    if before:
        before.link.finish()
    stage.middle(0)
    stage.middle(1)
    if flight:
        flight()
    stage.end(0)
    stage.end(1)
    if ended:
        ended()
    stage.forward(0)
    if after:
        after()


def layer_kernel(dims, names, *refs):
    b = Box(names, refs)
    b.grad_third, b.grad_r2, b.grad_r1, b.gc1_all = b.first, b.second, b.first, b.gy_all
    place = Place(dims)
    sems = b.send_sems, b.recv_sems
    link = Link(*sems, dims["chain"])
    width, block, items_dev = dims["width"], dims["block"], dims["items_dev"]
    h, t, q_place = place.h, place.t, place.q
    c, b1, b0 = place.c, place.b1, place.b0
    partner = place.partner()
    wr = b.w_sq.shape[0] // dims["share"]
    model = dims["model"]
    total_dec, total_mem = dims["total_dec"], dims["total_mem"]
    rb = b.dec.shape[1]

    def rows_of(ref, cols=model):
        return ref[...].reshape(-1, ref.shape[-1])[:, :cols]

    def chunk(ref, k):
        return ref[k].reshape(-1, model)

    half_rows = total_dec // 2

    def span(k):
        return slice(k * half_rows, (k + 1) * half_rows)

    def put(k, value, before=None):
        if before:
            before.release(k)
        b.part[k] = value.astype(BF).reshape(b.part.shape[1:])

    def weight(ref, index):
        return ref[index].reshape(model, width)

    weights = (b.w_sq, b.w_sk, b.w_sv, b.w_so, b.w_ck, b.w_cv, b.w_cq, b.w_co)
    rows_t = pl.ds(pl.multiple_of(t * wr, wr), wr)
    index = link.index()
    for i, w in enumerate(weights):
        pltpu.make_async_copy(w.at[rows_t], b.staged.at[i], b.send_sems.at[index]).start()
    staged = pltpu.make_async_copy(b.staged, b.staged, b.send_sems.at[index])
    own_fin = link.local(b.f_in, b.own_fin)
    own_fout = link.local(b.f_out, b.own_fout)
    greet(place.seq_peers() + place.items_peers())

    def share_columns(dst):
        blocks = dims["seq"] // 2
        return Share(
            link, place, lambda t: dst.at[:, t],
            lambda t, i: dst.at[i * blocks : (i + 1) * blocks, t],
        )

    def share_rows(dst):
        return Share(link, place, lambda t: dst.at[:, t], lambda t, i: dst.at[i, t])

    def share_hidden(dst):
        rows = dst.shape[1] // 2
        return Share(
            link, place, lambda t: dst.at[t], lambda t, i: dst.at[t, i * rows : (i + 1) * rows]
        )

    def join_cells():
        mb = b.cells.shape[1]
        same = lax.broadcasted_iota(jnp.int32, (mb, mb), 0) == lax.broadcasted_iota(
            jnp.int32, (mb, mb), 1
        )
        for k in range(items_dev):
            flags = (b.cells[k : k + 1] == 1).astype(F32)
            column = jnp.sum(jnp.where(same, flags, 0.0), axis=1, keepdims=True)
            b.mem_cells[k, :, :model] = b.mem[k]
            b.mem_cells[k, :, model:] = jnp.broadcast_to(column, (mb, 128)).astype(BF)

    staged.wait()
    steps, own_self = columns_out(link, place, b.staged.at[0:3], b.o_self, width)
    b.x_all[h, c, b1, b0] = b.dec[h]
    join_cells()
    b.m_all[h, c, b1, b0] = b.mem_cells[h]
    link.settle(steps)
    swap_x = link.send(b.dec.at[1 - h], b.x_all.at[h, c, b1, b0], partner)
    first_x = spread_start(link, place, b.x_all, h)
    so_arrived, so_sent = rows_out(link, place, b.staged.at[3], b.o_so)
    steps.wait_recv()
    own_self.wait()
    self_share = [share_columns(b.o_self.at[i]) for i in range(3)]
    waits = spread_end(link, place, b.x_all, h, first_x)
    swap_x.wait_recv()
    second_x = spread_start(link, place, b.x_all, 1 - h)
    waits += spread_end(link, place, b.x_all, 1 - h, second_x)
    cross_steps, own_cross = columns_out(link, place, b.staged.at[4:7], b.o_cross, width)
    co_arrived, co_sent = rows_out(link, place, b.staged.at[7], b.o_co)
    swap_m = link.send(b.mem_cells.at[1 - h], b.m_all.at[h, c, b1, b0], partner)
    first_m = spread_start(link, place, b.m_all, h)
    for share in self_share:
        share.forward()
    so_arrived()
    so_share = share_rows(b.o_so)

    arrive(waits)
    rows = rows_of(b.x_all)
    for index, dst in enumerate((b.sq, b.sk, b.sv)):
        self_share[index].wait()
        dst[...] = nn(rows, weight(b.o_self, index)).astype(BF)
    so_share.forward()
    cross_steps.wait_recv()
    own_cross.wait()
    cross_share = [
        Direct(link, place, lambda _, dst=b.o_cross.at[i]: dst.at[:, t]) for i in range(3)
    ]
    co_arrived()
    co_share = Direct(link, place, lambda _: b.o_co.at[:, t])
    mem_waits = spread_end(link, place, b.m_all, h, first_m)
    swap_m.wait_recv()
    second_m = spread_start(link, place, b.m_all, 1 - h)
    own_fin.wait()
    own_fout.wait()
    fr, gr = b.o_fin.shape[1], b.o_fout.shape[1]
    step_fin = link.send(b.own_fin.at[pl.ds(pl.multiple_of(t * fr, fr), fr)], b.o_fin.at[t], partner)
    length, mem_length = b.dec_len[h], b.mem_len[h]

    def self_ok(start, stop):
        keys = lax.broadcasted_iota(jnp.int32, (stop, block), 0)
        spots = lax.broadcasted_iota(jnp.int32, (stop, block), 1) + start
        return (keys <= spots) & (keys < length)

    bufs = [b.recv0, b.send1, b.recv1, b.keep1]
    if dims["bits"] == 3:
        bufs += [b.send2, b.recv2]

    def forward(index, res, summed, out):
        def mid(k, total):
            value = res(k) + total
            summed[k] = value
            normed, _ = moments(value)
            result = normed * b.gain[index : index + 1] + b.bias[index : index + 1]
            out[k] = result
            return result.astype(BF)

        return mid

    def self_part(k, pump):
        attend(
            b.sq, b.sk, b.sv, self_ok, b.sp, b.smix, True, block,
            k * half_rows, (k + 1) * half_rows, pump,
        )
        if k == 0:
            so_share.wait()
        put(k, nn(b.smix[span(k)], rows_of(b.o_so)))

    def memory_part():
        arrive(mem_waits)
        mems = rows_of(b.m_all)
        cross_share[0].wait()
        b.ck[...] = nn(mems, weight(b.o_cross, 0)).astype(BF)
        cross_share[1].wait()
        b.cv[...] = nn(mems, weight(b.o_cross, 1)).astype(BF)
        spots = lax.broadcasted_iota(jnp.int32, (total_mem, 128), 0)
        cells = b.m_all[...].reshape(-1, b.m_all.shape[-1])[:, model:].astype(F32)
        b.keep[...] = ((spots < mem_length) & ((cells > 0.5) | (spots == 0))).astype(F32)

    stage = Stage(
        sems, place, b.part, bufs,
        forward(0, lambda k: b.x_all[k, c, b1, b0].astype(F32), b.sum_one, b.first), b.first_all, None,
    )
    def cross_weights():
        rows = pl.ds(pl.multiple_of(t * gr, gr), gr)
        steps_fout.append(link.send(b.own_fout.at[rows], b.o_fout.at[t], partner))
        mem_waits.extend(spread_end(link, place, b.m_all, 1 - h, second_m))
        step_fin.wait_recv()
        ffn_share.append(share_hidden(b.o_fin))

    ffn_share, steps_fout = [], []
    stage_steps(stage, self_part, after=cross_weights)
    memory_part()
    b.c_own[h] = b.cot[h]

    def cross_part(k, pump):
        last.arrive(k)
        if k == 0:
            cross_share[2].wait()
        b.cq[span(k)] = nn(chunk(b.first_all, k), weight(b.o_cross, 2)).astype(BF)
        attend(
            b.cq, b.ck, b.cv, lambda start, stop: b.keep[:, 0:1] > 0.5, b.cp, b.cmix, False, block,
            k * half_rows, (k + 1) * half_rows, pump,
        )
        if k == 0:
            co_share.wait()
        put(k, nn(b.cmix[span(k)], rows_of(b.o_co)), last)

    last = stage
    stage = Stage(
        sems, place, b.part, bufs, forward(1, lambda k: b.first[k], b.sum_two, b.second),
        b.second_all, last,
    )
    def ffn_weights():
        ffn_share[0].forward()
        arrive(steps_fout)
        ffn_share.append(Direct(link, place, lambda _: b.o_fout.at[t]))

    stage_steps(stage, cross_part, ffn_weights)
    swap_c = link.send(b.cot.at[1 - h], b.c_own.at[h], partner)

    w_ins = (lambda: b.own_fin[...], lambda: b.o_fin[...].reshape(model, -1))
    w_outs = (lambda: b.own_fout[...], lambda: b.o_fout[...].reshape(-1, model))
    hidden = b.own_fin.shape[1]
    last_second = stage

    def ffn_part(k, pump):
        last_second.arrive(k)
        if k == 0:
            ffn_share[0].wait()
        rows = chunk(b.second_all, k)
        for index in range(2):
            if index:
                pump()
            pre = nn(rows, w_ins[index]())
            cdf = 0.5 * (1.0 + lax.erf(pre * (0.5**0.5)))
            cols = slice(index * hidden, (index + 1) * hidden)
            b.act[span(k), cols] = (pre * cdf).astype(BF)
            b.slope[span(k), cols] = (
                cdf + pre * (jnp.exp(-0.5 * pre * pre) * 0.3989422804014327)
            ).astype(BF)
        if k == 0:
            ffn_share[1].wait()
        total = nn(b.act[span(k), :hidden], w_outs[0]())
        put(k, total + nn(b.act[span(k), hidden:], w_outs[1]()), last_second)

    swap_c.wait_recv()

    def add_sums(index, k, normed, grad):
        new = (jnp.sum(grad * normed, axis=0, keepdims=True), jnp.sum(grad, axis=0, keepdims=True))
        for row, value in zip((index, 3 + index), new):
            b.sums[row : row + 1] = value if k == 0 else b.sums[row : row + 1] + value

    def turn(k, total):
        gain = b.gain[2:3]
        normed, inv = moments(b.second[k] + total)
        spots = lax.broadcasted_iota(jnp.int32, (rb, model), 0) + (k * dims["group"] + q_place) * rb
        kept = spots < length
        b.layer[k] = jnp.where(kept, normed * gain + b.bias[2:3], 0.0).astype(BF)
        grad = jnp.where(kept, b.c_own[k].astype(F32), 0.0)
        add_sums(2, k, normed, grad)
        result = norm_back(normed, inv, gain, grad)
        b.grad_third[k] = result
        return result.astype(BF)

    stage = Stage(sems, place, b.part, bufs, turn, b.gy_all, last_second)
    stage_steps(stage, ffn_part)

    last_turn = stage

    way_fout = Hidden(
        link, place, b.g_fout, ("q_fout", "t_fout", "u_fout", dims["lines"] and "l_fout", "s_fout", "z_fout", "d_fout", "r_fout"), b
    )
    def out_grads():
        grad = rows_of(b.gy_all)
        for index in range(2):
            cols = slice(index * hidden, (index + 1) * hidden)
            value = tn(b.act[:, cols], grad)
            b.g_fout[index] = value.astype(BF).reshape(b.g_fout.shape[1:])
        way_fout.send()

    def ffn_back(k, pump):
        last_turn.arrive(k)
        if k == 1:
            out_grads()
        grad = chunk(b.gy_all, k)
        total = None
        for index in range(2):
            if index:
                pump()
            cols = slice(index * hidden, (index + 1) * hidden)
            grad_pre = (nt(grad, w_outs[index]()) * b.slope[span(k), cols].astype(F32)).astype(BF)
            b.slope[span(k), cols] = grad_pre
            term = nt(grad_pre, w_ins[index]())
            total = term if total is None else total + term
        put(k, total, last_turn)

    way_fin = Hidden(
        link, place, b.g_fin, ("q_fin", "t_fin", "u_fin", dims["lines"] and "l_fin", "s_fin", "z_fin", "d_fin", "r_fin"), b
    )
    way_cross = Columns(
        link, place, b.g_cross, ("q_cross", "t_cross", "u_cross", dims["lines"] and "l_cross", "s_cross", "z_cross", "d_cross", "r_cross"), b
    )
    way_self = Columns(
        link, place, b.g_self, ("q_self", "t_self", "u_self", dims["lines"] and "l_self", "s_self", "z_self", "d_self", "r_self"), b
    )
    way_co = Rows(
        link, place, b.g_co, ("q_co", "t_co", "u_co", dims["lines"] and "l_co", "s_co", "z_co", "d_co", "r_co"), b
    )
    way_so = Rows(
        link, place, b.g_so, ("q_so", "t_so", "u_so", dims["lines"] and "l_so", "s_so", "z_so", "d_so", "r_so"), b
    )

    def backward(index, res, summed, out):
        def mid(k, total):
            normed, inv = moments(summed[k])
            grad = res[k] + total
            add_sums(index, k, normed, grad)
            result = norm_back(normed, inv, b.gain[index : index + 1], grad)
            out[k] = result
            return result.astype(BF)

        return mid

    def in_grads():
        rows = rows_of(b.second_all)
        for index in range(2):
            cols = slice(index * hidden, (index + 1) * hidden)
            value = tn(rows, b.slope[:, cols])
            b.g_fin[index] = value.astype(BF).reshape(b.g_fin.shape[1:])
        way_fin.send()

    stage = Stage(
        sems, place, b.part, bufs, backward(1, b.grad_third, b.sum_two, b.grad_r2), b.gc2_all,
        last_turn,
    )
    stage_steps(stage, ffn_back, in_grads)

    last_back = stage

    def cross_back(k, pump):
        last_back.arrive(k)
        b.dmix[span(k)] = nt(chunk(b.gc2_all, k), rows_of(b.o_co)).astype(BF)
        attend_back(
            b.cq, b.ck, b.cv, b.cp, b.dmix, b.dq, b.sum_dk, b.sum_dv, False, block,
            k * half_rows, (k + 1) * half_rows, pump,
        )
        put(k, nt(b.dq[span(k)], weight(b.o_cross, 2)), last_back)
        if k == 1:
            way_fout.turn()

    def cross_grads():
        mems = rows_of(b.m_all)
        shape = b.g_cross.shape[1:]
        b.dck[...] = (b.sum_dk[:total_mem] * SCALE).astype(BF)
        b.dcv[...] = b.sum_dv[:total_mem].astype(BF)
        b.g_cross[0] = tn(rows_of(b.first_all), b.dq[...]).astype(BF).reshape(shape)
        b.g_cross[1] = tn(mems, b.dck[...]).astype(BF).reshape(shape)
        b.g_cross[2] = tn(mems, b.dcv[...]).astype(BF).reshape(shape)
        way_cross.send()
        b.g_co[...] = tn(b.cmix[...], rows_of(b.gc2_all)).astype(BF).reshape(b.g_co.shape)
        way_co.send()
        way_fin.turn()

    def part_mem():
        value = nt(b.dck[...], weight(b.o_cross, 0)) + nt(b.dcv[...], weight(b.o_cross, 1))
        b.part_m[...] = value.astype(BF).reshape(b.part_m.shape)
        for index in range(2):
            red_m.start(index, ks[index])

    stage = Stage(
        sems, place, b.part, bufs, backward(0, b.grad_r2, b.sum_one, b.grad_r1), b.gc1_all,
        last_back,
    )
    ks = (1 - h, h)
    mem_bufs = [b.recv0_m, b.send1_m, b.recv1_m, b.keep1_m]
    if dims["bits"] == 3:
        mem_bufs += [b.send2_m, b.recv2_m]
    red_m = Reduce(link, place, b.part_m, mem_bufs)
    stage_steps(stage, cross_back, cross_grads, part_mem)

    swap_l = link.send(b.layer.at[1 - h], b.layer_out.at[h], partner)
    b.layer_out[h] = b.layer[h]
    way_fout.add()
    for k in range(2):
        stage.arrive(k)
        pump = (lambda: stage.forward(1)) if k == 0 else (lambda: None)
        b.dmix[span(k)] = nt(chunk(b.gc1_all, k), rows_of(b.o_so)).astype(BF)
        attend_back(
            b.sq, b.sk, b.sv, b.sp, b.dmix, b.dq, b.sum_dk, b.sum_dv, True, block,
            k * half_rows, (k + 1) * half_rows, pump,
        )
        red_m.middle(k, ks[k])
    b.dsk[...] = (b.sum_dk[...] * SCALE).astype(BF)
    b.dsv[...] = b.sum_dv[...].astype(BF)
    for k in range(2):
        total = nt(b.dq[span(k)], weight(b.o_self, 0)) + nt(b.dsk[span(k)], weight(b.o_self, 1))
        put(k, total + nt(b.dsv[span(k)], weight(b.o_self, 2)), stage)
    stage.link.finish()
    chain = Link(*sems)
    red_x = Reduce(chain, place, b.part, bufs)
    for index in range(2):
        red_x.start(index, ks[index])
    way_cross.turn()
    way_co.turn()
    way_fin.add()
    rows = rows_of(b.x_all)
    shape = b.g_self.shape[1:]
    b.g_self[0] = tn(rows, b.dq[...]).astype(BF).reshape(shape)
    b.g_self[1] = tn(rows, b.dsk[...]).astype(BF).reshape(shape)
    b.g_self[2] = tn(rows, b.dsv[...]).astype(BF).reshape(shape)
    way_self.send()
    b.g_so[...] = tn(b.smix[...], rows_of(b.gc1_all)).astype(BF).reshape(b.g_so.shape)
    way_so.send()
    for index in range(2):
        red_x.middle(index, ks[index])
    b.send_m[...] = red_m.end(0).astype(BF)
    swap_m = link.send(b.send_m, b.recv_m, partner)
    b.grad_mem[h] = red_m.end(1)
    copies = []
    for d in range(1, dims["seq"]):
        copies.append((b.sums, b.sums_seq.at[d - 1], {"seq": place.seq_shift(d)}))
    seq_sums = link.batch(copies, b.sums_seq)
    way_cross.add()
    way_co.add()
    b.send_x[...] = (red_x.end(0) + b.grad_r1[1 - h]).astype(BF)
    swap_x = link.send(b.send_x, b.recv_x, partner)
    b.grad_dec[h] = red_x.end(1) + b.grad_r1[h]
    way_fout.gather()
    way_self.turn()
    way_so.turn()
    way_fin.gather()
    way_fout.forward()
    way_self.add()
    way_so.add()
    way_cross.gather()
    way_co.gather()
    way_fin.forward()
    seq_sums.wait_recv()
    value = b.sums[...]
    for d in range(1, dims["seq"]):
        value = value + b.sums_seq[d - 1]
    b.sums_line[...] = value
    copies = []
    for e in range(1, dims["items"]):
        target = {"items": lax.rem(place.it + e, dims["items"])}
        copies.append((b.sums_line, b.sums_items.at[e - 1], target))
    item_sums = link.batch(copies, b.sums_items)
    swap_x.wait_recv()
    b.grad_dec[1 - h] = b.recv_x[...].astype(F32)
    swap_m.wait_recv()
    b.grad_mem[1 - h] = b.recv_m[...].astype(F32)
    swap_l.wait_recv()
    way_self.gather()
    way_so.gather()
    way_cross.forward()
    way_co.forward()
    item_sums.wait_recv()
    value = b.sums_line[...]
    for e in range(1, dims["items"]):
        value = value + b.sums_items[e - 1]
    b.sums_out[...] = value
    way_self.forward()
    way_so.forward()
    for way in (way_fout, way_fin, way_cross, way_co, way_self, way_so):
        way.finish()
    so_sent()
    co_sent()
    chain.finish()
    link.finish()


def shape(dims, dtype):
    return jax.ShapeDtypeStruct(tuple(dims), dtype)


def outputs_kernel(layer, dec, mem, cross, own, co, so, fin, fout, sums, *outs):
    o_layer, o_dec, o_mem = outs[:3]
    o_layer[...] = layer[...]
    o_dec[...] = dec[...]
    o_mem[...] = mem[...]
    for index in range(3):
        outs[3 + index][...] = own[0, index].astype(F32)
        outs[7 + index][...] = cross[0, index].astype(F32)
    outs[6][...] = so[0].astype(F32)
    outs[10][...] = co[0].astype(F32)
    outs[11][...] = fin[0].astype(F32)
    outs[12][...] = fout[0].astype(F32)
    outs[13][...] = sums[0:3]
    outs[14][...] = sums[3:6]


def shards(
    mesh, dec_in, memory, dec_len, mem_len, cell_mask, self_query, self_key, self_value, self_out,
    cross_query, cross_key, cross_value, cross_out, ffn_in, ffn_out, norm_gain, norm_bias, cotangent,
):
    items_dev, rb, model = dec_in.shape
    mb = memory.shape[1]
    seq, items = mesh.shape["seq"], mesh.shape["items"]
    group = seq // items_dev
    share = 4
    bits = group.bit_length() - 1
    chips = group // 4
    width = model // group
    total_dec, total_mem = rb * seq, mb * seq
    heads = width // HEAD_DIM
    hidden = ffn_in.shape[1]
    wr = self_query.shape[0] // share
    fr, gr = model // share, hidden // share
    lines = items // share - 1
    dims = {
        "items_dev": items_dev, "items": items, "seq": seq, "group": group, "share": share,
        "bits": bits, "chips": chips, "width": width, "model": model, "block": 256,
        "total_dec": total_dec, "total_mem": total_mem, "lines": lines,
        "chain": 12 + 2 * (bits - 2),
    }
    ins = [
        ("dec", dec_in, VM), ("mem", memory, VM), ("cells", cell_mask, VM), ("cot", cotangent, VM),
        ("dec_len", dec_len, SM), ("mem_len", mem_len, SM),
        ("w_sq", self_query, HBM), ("w_sk", self_key, HBM), ("w_sv", self_value, HBM),
        ("w_so", self_out, HBM), ("w_cq", cross_query, HBM), ("w_ck", cross_key, HBM),
        ("w_cv", cross_value, HBM), ("w_co", cross_out, HBM), ("f_in", ffn_in, HBM),
        ("f_out", ffn_out, HBM), ("gain", norm_gain, VM), ("bias", norm_bias, VM),
    ]
    own, own_m = (items_dev, rb, model), (items_dev, mb, model)
    grid = (items_dev, chips, 2, 2)
    outs = [
        ("layer_out", own, BF, VM), ("grad_dec", own, F32, VM), ("grad_mem", own_m, F32, VM),
        ("sums_out", (8, model), F32, VM),
        ("r_cross", (share, 3, wr, model), BF, HBM), ("r_self", (share, 3, wr, model), BF, HBM),
        ("r_co", (share, wr, model), BF, HBM), ("r_so", (share, wr, model), BF, HBM),
        ("r_fin", (share, fr, hidden), BF, HBM), ("r_fout", (share, gr, model), BF, HBM),
    ]
    cols = (3, seq, share, wr, width)
    scratch = [
        ("x_all", grid + (rb, model), BF), ("m_all", grid + (mb, model + 128), BF),
        ("mem_cells", (items_dev, mb, model + 128), BF), ("c_own", own, BF), ("staged", (8, wr, model), BF),
        ("own_fin", (model, hidden), BF), ("own_fout", (hidden, model), BF),
        ("o_self", cols, BF), ("o_cross", cols, BF),
        ("o_so", (items_dev, share, wr, model), BF), ("o_co", (items_dev, share, wr, model), BF),
        ("o_fin", (share, fr, hidden), BF), ("o_fout", (share, gr, model), BF),
        ("sq", (total_dec, width), BF), ("sk", (total_dec, width), BF), ("sv", (total_dec, width), BF),
        ("cq", (total_dec, width), BF), ("ck", (total_mem, width), BF), ("cv", (total_mem, width), BF),
        ("sp", (heads, total_dec, total_dec), BF), ("cp", (heads, total_mem, total_dec), BF),
        ("smix", (total_dec, width), BF), ("cmix", (total_dec, width), BF),
        ("keep", (total_mem, 128), F32),
        ("part", grid + (rb, model), BF), ("part_m", grid + (mb, model), BF),
        ("first_all", grid + (rb, model), BF), ("second_all", grid + (rb, model), BF),
        ("gy_all", grid + (rb, model), BF), ("gc2_all", grid + (rb, model), BF),
        ("sum_one", own, F32), ("sum_two", own, F32), ("first", own, F32), ("second", own, F32),
        ("layer", own, BF), ("sum_dk", (total_dec, width), F32), ("sum_dv", (total_dec, width), F32),
        ("act", (total_dec, 2 * hidden), BF), ("slope", (total_dec, 2 * hidden), BF),
        ("dmix", (total_dec, width), BF), ("dq", (total_dec, width), BF),
        ("dsk", (total_dec, width), BF), ("dsv", (total_dec, width), BF),
        ("dck", (total_mem, width), BF), ("dcv", (total_mem, width), BF),
        ("send_x", (rb, model), BF), ("recv_x", (rb, model), BF),
        ("send_m", (mb, model), BF), ("recv_m", (mb, model), BF),
        ("sums", (8, model), F32), ("sums_line", (8, model), F32),
        ("sums_seq", (seq - 1, 8, model), F32), ("sums_items", (items - 1, 8, model), F32),
    ]
    for name, rows in (("", rb), ("_m", mb)):
        scratch += [
            ("recv0" + name, (items_dev, chips, 2, rows, model), BF),
            ("send1" + name, (items_dev, chips, rows, model), BF),
            ("recv1" + name, (items_dev, chips, rows, model), BF),
            ("keep1" + name, (items_dev, chips, rows, model), F32),
        ]
        if bits == 3:
            scratch += [
                ("send2" + name, (items_dev, rows, model), BF),
                ("recv2" + name, (items_dev, rows, model), BF),
            ]
    for name, grad, quarter, piece, moved, done in (
        ("fin", (2, share, fr, hidden), (2, fr, hidden), (2, fr // 2, hidden), (fr, hidden),
         (fr, hidden)),
        ("fout", (2, share, gr, model), (2, gr, model), (2, gr // 2, model), (gr, model), (gr, model)),
        ("cross", cols, (3, seq, wr, width), (3, seq // 2, wr, width), (seq, 3, wr, width),
         (3, wr, model)),
        ("self", cols, (3, seq, wr, width), (3, seq // 2, wr, width), (seq, 3, wr, width),
         (3, wr, model)),
        ("co", (items_dev, share, wr, model), (items_dev, wr, model), (wr, model),
         (items_dev, wr, model), (wr, model)),
        ("so", (items_dev, share, wr, model), (items_dev, wr, model), (wr, model),
         (items_dev, wr, model), (wr, model)),
    ):
        scratch += [
            ("g_" + name, grad, BF), ("q_" + name, (2, 2) + piece, BF), ("t_" + name, (2,) + piece, BF),
            ("u_" + name, (2,) + piece, BF), ("s_" + name, quarter, BF), ("z_" + name, moved, BF),
            ("d_" + name, done, BF),
        ]
        if lines:
            scratch.append(("l_" + name, (lines,) + quarter, BF))
    copies = dims["chain"] + 140 + 12 * (bits - 2)
    names = [x[0] for x in ins + outs + scratch] + ["send_sems", "recv_sems"]
    results = pl.pallas_call(
        functools.partial(layer_kernel, dims, names),
        name="layer",
        out_shape=[shape(x[1], x[2]) for x in outs],
        in_specs=[x[2] for x in ins],
        out_specs=[x[3] for x in outs],
        scratch_shapes=[pltpu.VMEM(x[1], x[2]) for x in scratch]
        + [pltpu.SemaphoreType.DMA((copies,)), pltpu.SemaphoreType.DMA((copies,))],
        compiler_params=pltpu.CompilerParams(
            collective_id=0, has_side_effects=True, vmem_limit_bytes=VMEM_BYTES
        ),
    )(*[x[1] for x in ins])
    layer_out, grad_dec, grad_memory, sums, r_cross, r_self, r_co, r_so, r_fin, r_fout = results
    tok, mem_rows = items_dev * rb, items_dev * mb
    pieces = (
        ((tok, model), (tok // share, model), BF), ((tok, model), (tok // share, model), F32),
        ((mem_rows, model), (mem_rows // share, model), F32),
    )
    heads_in = [
        pl.BlockSpec((1, 3, wr, model), lambda i: (i, 0, 0, 0)),
        pl.BlockSpec((1, 3, wr, model), lambda i: (i, 0, 0, 0)),
        pl.BlockSpec((1, wr, model), lambda i: (i, 0, 0)),
        pl.BlockSpec((1, wr, model), lambda i: (i, 0, 0)),
        pl.BlockSpec((1, fr, hidden), lambda i: (i, 0, 0)),
        pl.BlockSpec((1, gr, model), lambda i: (i, 0, 0)),
        pl.BlockSpec((8, model), lambda i: (0, 0)),
    ]
    row_specs = [pl.BlockSpec(x[1], lambda i: (i, 0)) for x in pieces]
    square = (share * wr, model)
    outs = pl.pallas_call(
        outputs_kernel,
        name="outputs",
        grid=(share,),
        in_specs=row_specs + heads_in,
        out_specs=row_specs
        + [pl.BlockSpec((wr, model), lambda i: (i, 0))] * 8
        + [pl.BlockSpec((fr, hidden), lambda i: (i, 0)), pl.BlockSpec((gr, model), lambda i: (i, 0))]
        + [pl.BlockSpec((3, model), lambda i: (0, 0))] * 2,
        out_shape=[shape(x[0], x[2]) for x in pieces]
        + [shape(square, F32)] * 8
        + [shape((model, hidden), F32), shape((hidden, model), F32)]
        + [shape((3, model), F32)] * 2,
        compiler_params=pltpu.CompilerParams(vmem_limit_bytes=VMEM_BYTES),
    )(
        layer_out.reshape(tok, model), grad_dec.reshape(tok, model),
        grad_memory.reshape(mem_rows, model), r_cross, r_self, r_co, r_so, r_fin, r_fout, sums,
    )
    return (
        outs[0].reshape(own), outs[1].reshape(own), outs[2].reshape(own_m), *outs[3:],
    )


def solution(mesh):
    rows = P("seq", None)
    tokens = P("items", "seq", None)
    placed = (
        (tokens, tokens, P("items"), P("items"), P("items", "seq"))
        + (rows,) * 8
        + (P(None, "seq"), rows, P(), P(), tokens)
    )
    return jax.shard_map(
        functools.partial(shards, mesh),
        mesh=mesh,
        in_specs=placed,
        out_specs=(tokens,) * 3 + (rows,) * 8 + (P(None, "seq"), rows, P(), P()),
        check_vma=False,
    )
```

```python
import functools

import jax
import jax.numpy as jnp
from jax import lax
from jax.experimental import pallas as pl
from jax.experimental.pallas import tpu as pltpu
from jax.sharding import PartitionSpec as P

HEAD_DIM = 64
EPS = 1e-05
NEG = -1e30
SCALE = HEAD_DIM ** (-0.5)
BF = jnp.bfloat16
F32 = jnp.float32
VMEM_BYTES = 63 * 1024 * 1024
MESH = pl.DeviceIdType.MESH
VM = pl.BlockSpec(memory_space=pltpu.VMEM)
HBM = pl.BlockSpec(memory_space=pl.ANY)
SM = pl.BlockSpec(memory_space=pltpu.SMEM)


def nn(left, right):
    return lax.dot_general(left, right, (((1,), (0,)), ((), ())), preferred_element_type=F32)


def nt(left, right):
    return lax.dot_general(left, right, (((1,), (1,)), ((), ())), preferred_element_type=F32)


def tn(left, right):
    return lax.dot_general(left, right, (((0,), (0,)), ((), ())), preferred_element_type=F32)


class Link:
    def __init__(self, send_sems, recv_sems, first=0):
        self.send_sems, self.recv_sems, self.count, self.open = send_sems, recv_sems, first, []

    def index(self):
        self.count += 1
        return self.count - 1

    def make(self, src, dst, device, index):
        return pltpu.make_async_remote_copy(
            src_ref=src,
            dst_ref=dst,
            send_sem=self.send_sems.at[index],
            recv_sem=self.recv_sems.at[index],
            device_id=device,
            device_id_type=MESH,
        )

    def send(self, src, dst, device):
        copy = self.make(src, dst, device, self.index())
        copy.start()
        self.open.append(copy)
        return copy

    def batch(self, copies, whole):
        index = self.index()
        for copy in copies:
            self.make(*copy, index).start()
        wait = self.make(whole, whole, copies[0][2], index)
        self.open.append(wait)
        return wait

    def settle(self, copy):
        copy.wait_send()
        self.open = [other for other in self.open if other is not copy]

    def local(self, src, dst):
        copy = pltpu.make_async_copy(src, dst, self.send_sems.at[self.index()])
        copy.start()
        return copy

    def finish(self, kept=()):
        late = {id(copy) for copy in kept}
        for copy in self.open:
            if id(copy) not in late:
                copy.wait_send()
        self.open = [copy for copy in self.open if id(copy) in late]


def greet(devices):
    barrier = pltpu.get_barrier_semaphore()
    for device in devices:
        pl.semaphore_signal(barrier, inc=1, device_id=device, device_id_type=MESH)
    pl.semaphore_wait(barrier, len(devices))


class Place:
    def __init__(self, dims):
        self.dims = dims
        group, share = dims["group"], dims["share"]
        self.me = lax.axis_index("seq")
        self.h = self.me // group
        self.q = self.me % group
        self.b0 = self.q % 2
        self.b1 = (self.q // 2) % 2
        self.c = self.q // 4
        self.it = lax.axis_index("items")
        self.base = (self.it // share) * share
        self.t = self.it % share
        x, y = self.t % 2, self.t // 2
        self.tx, self.ty, self.txy = y * 2 + 1 - x, (1 - y) * 2 + x, (1 - y) * 2 + 1 - x

    def across(self, bit):
        value = (self.q // (1 << bit)) % 2
        return {"seq": self.me + (1 - 2 * value) * (1 << bit)}

    def partner(self):
        return {"seq": (1 - self.h) * self.dims["group"] + self.q}

    def seq_shift(self, d):
        return lax.rem(self.me + d, self.dims["seq"])

    def line(self, t):
        return {"items": self.base + t}

    def seq_peers(self):
        return [{"seq": self.seq_shift(d)} for d in range(1, self.dims["seq"])]

    def items_peers(self):
        count = self.dims["items"]
        return [{"items": lax.rem(self.it + e, count)} for e in range(1, count)]


def spread_start(link, place, out, k):
    bits = place.dims["bits"]
    c, b1, b0 = place.c, place.b1, place.b0
    if bits == 3:
        step = link.send(out.at[k, c, b1, b0], out.at[k, c, b1, b0], place.across(2))
        step.wait_recv()
    waits = []
    high = link.send(out.at[k, :, b1, b0], out.at[k, :, b1, b0], place.across(1))
    waits.append(link.send(out.at[k, :, b1, b0], out.at[k, :, b1, b0], place.across(0)))
    return high, waits


def spread_end(link, place, out, k, started):
    high, waits = started
    b1, b0 = place.b1, place.b0
    high.wait_recv()
    waits.append(link.send(out.at[k, :, 1 - b1, b0], out.at[k, :, 1 - b1, b0], place.across(0)))
    return waits


def columns_out(link, place, src, dst, width):
    seq, group = place.dims["seq"], place.dims["group"]
    copies = []
    for d in range(1, seq):
        target = place.seq_shift(d)
        cols = pl.ds(pl.multiple_of(lax.rem(target, group) * width, width), width)
        copies.append((src.at[:, :, cols], dst.at[:, place.me, place.t], {"seq": target}))
    steps = link.batch(copies, dst.at[:, 0 : seq - 1, place.t])
    cols = pl.ds(pl.multiple_of(place.q * width, width), width)
    return steps, link.local(src.at[:, :, cols], dst.at[:, place.me, place.t])


def rows_out(link, place, src, dst):
    dims, me = place.dims, place.me
    slot = lax.rem(me, dims["items_dev"])
    base = link.count
    link.count += dims["items_dev"] + 1
    copies = []
    for half in range(dims["items_dev"]):
        target = half * dims["group"] + me // dims["items_dev"]
        copy = pltpu.make_async_remote_copy(
            src_ref=src,
            dst_ref=dst.at[slot, place.t],
            send_sem=link.send_sems.at[base + half],
            recv_sem=link.recv_sems.at[base + slot],
            device_id={"seq": target},
            device_id_type=MESH,
        )
        copies.append((target != me, copy))
        pl.when(target != me)(copy.start)
    own = pltpu.make_async_copy(
        src, dst.at[slot, place.t], link.send_sems.at[base + dims["items_dev"]]
    )
    mine = me // dims["items_dev"] == place.q
    pl.when(mine)(own.start)

    def arrived():
        pl.when(mine)(own.wait)
        for block in range(dims["items_dev"]):
            copy = pltpu.make_async_remote_copy(
                src_ref=src,
                dst_ref=dst.at[block, place.t],
                send_sem=link.send_sems.at[base],
                recv_sem=link.recv_sems.at[base + block],
                device_id={"seq": me},
                device_id_type=MESH,
            )
            pl.when(place.q * dims["items_dev"] + block != me)(copy.wait_recv)

    def sent():
        for other, copy in copies:
            pl.when(other)(copy.wait_send)

    return arrived, sent


class Share:
    def __init__(self, link, place, slab, half):
        self.link, self.place, self.half = link, place, half
        t = place.t
        self.from_x = link.send(slab(t), slab(t), place.line(place.tx))
        self.from_y = link.send(slab(t), slab(t), place.line(place.ty))

    def forward(self):
        link, place, half = self.link, self.place, self.half
        self.from_y.wait_recv()
        part = half(place.ty, 0)
        self.steps = [link.send(part, part, place.line(place.tx))]
        self.from_x.wait_recv()
        part = half(place.tx, 1)
        self.steps.append(link.send(part, part, place.line(place.ty)))

    def wait(self):
        arrive(self.steps)


class Direct(Share):
    def __init__(self, link, place, slab):
        lines = (place.tx, place.ty, place.txy)
        self.steps = [link.send(slab(place.t), slab(place.t), place.line(line)) for line in lines]

    def forward(self):
        pass


def arrive(steps):
    for step in steps:
        step.wait_recv()


class Reduce:
    def __init__(self, link, place, part, bufs):
        self.link, self.place, self.part, self.bufs = link, place, part, bufs
        self.zero, self.one = {}, {}

    def start(self, index, k):
        place = self.place
        self.zero[index] = self.link.send(
            self.part.at[k, :, :, 1 - place.b0], self.bufs[0].at[index], place.across(0)
        )

    def middle(self, index, k):
        place, part = self.place, self.part
        recv0, send1, recv1, keep1 = self.bufs[:4]
        self.zero[index].wait_recv()
        b1, b0 = place.b1, place.b0
        for c in range(part.shape[1]):
            value = part[k, c, 1 - b1, b0].astype(F32) + recv0[index, c, 1 - b1].astype(F32)
            send1[index, c] = value.astype(BF)
        self.one[index] = self.link.send(send1.at[index], recv1.at[index], place.across(1))
        for c in range(part.shape[1]):
            keep1[index, c] = part[k, c, b1, b0].astype(F32) + recv0[index, c, b1].astype(F32)

    def end(self, index):
        place = self.place
        recv1, keep1 = self.bufs[2:4]
        self.one[index].wait_recv()
        if place.dims["bits"] == 2:
            return keep1[index, 0] + recv1[index, 0].astype(F32)
        send2, recv2 = self.bufs[4:6]
        c = place.c
        send2[index] = (keep1[index, 1 - c] + recv1[index, 1 - c].astype(F32)).astype(BF)
        step = self.link.send(send2.at[index], recv2.at[index], place.across(2))
        kept = keep1[index, c] + recv1[index, c].astype(F32)
        step.wait_recv()
        return kept + recv2[index].astype(F32)


def reduce_bufs(dims, rows):
    items_dev, width, chips = dims["items_dev"], dims["model"], dims["chips"]
    bufs = [
        pltpu.VMEM((items_dev, chips, 2, rows, width), BF),
        pltpu.VMEM((items_dev, chips, rows, width), BF),
        pltpu.VMEM((items_dev, chips, rows, width), BF),
        pltpu.VMEM((items_dev, chips, rows, width), F32),
    ]
    if dims["bits"] == 3:
        bufs += [pltpu.VMEM((items_dev, rows, width), BF) for _ in range(2)]
    return bufs


def moments(value):
    mean = jnp.mean(value, axis=-1, keepdims=True)
    centered = value - mean
    inv = lax.rsqrt(jnp.mean(centered * centered, axis=-1, keepdims=True) + EPS)
    return centered * inv, inv


def norm_back(normed, inv, gain, grad):
    scaled = grad * gain
    mean = jnp.mean(scaled, axis=-1, keepdims=True)
    cross = jnp.mean(scaled * normed, axis=-1, keepdims=True)
    return inv * (scaled - mean - normed * cross)


def rows_back(link, place, src, dst):
    dims, me, h = place.dims, place.me, place.h
    count = dims["items_dev"]
    base = link.count
    link.count += count + 1
    copies = []
    for k in range(count):
        target = place.q * count + k
        copy = pltpu.make_async_remote_copy(
            src_ref=src.at[k],
            dst_ref=dst.at[h],
            send_sem=link.send_sems.at[base + k],
            recv_sem=link.recv_sems.at[base + h],
            device_id={"seq": target},
            device_id_type=MESH,
        )
        copies.append((target != me, copy))
        pl.when(target != me)(copy.start)
    own = pltpu.make_async_copy(
        src.at[lax.rem(me, count)], dst.at[h], link.send_sems.at[base + count]
    )
    mine = me // count == place.q
    pl.when(mine)(own.start)

    def done():
        pl.when(mine)(own.wait)
        for half in range(count):
            copy = pltpu.make_async_remote_copy(
                src_ref=src.at[0],
                dst_ref=dst.at[half],
                send_sem=link.send_sems.at[base],
                recv_sem=link.recv_sems.at[base + half],
                device_id={"seq": me},
                device_id_type=MESH,
            )
            pl.when(half * dims["group"] + me // count != me)(copy.wait_recv)
        for other, copy in copies:
            pl.when(other)(copy.wait_send)

    return done


def half_mask(rows, half):
    return (lax.broadcasted_iota(jnp.int32, (rows, 128), 1) // HEAD_DIM) == half


def attend(q_ref, k_ref, v_ref, valid, p_ref, mix_ref, causal, block, first, last, pump):
    keys = k_ref.shape[0]
    for pair in range(q_ref.shape[1] // 128):
        lanes = slice(pair * 128, pair * 128 + 128)
        for start in range(first, last, block):
            stop = start + block if causal else keys
            halves = []
            for half in range(2):
                query = q_ref[start : start + block, lanes]
                query = jnp.where(half_mask(block, half), query, jnp.zeros_like(query))
                scores = nt(k_ref[:stop, lanes], query) * SCALE
                scores = jnp.where(valid(start, stop), scores, NEG)
                top = jnp.max(scores, axis=0, keepdims=True)
                grown = jnp.exp(scores - top)
                probs = (grown * (1.0 / jnp.sum(grown, axis=0, keepdims=True))).astype(BF)
                p_ref[2 * pair + half, :stop, start : start + block] = probs
                mixed = tn(v_ref[:stop, lanes], probs)
                halves.append(mixed[half * HEAD_DIM : (half + 1) * HEAD_DIM])
            mix_ref[start : start + block, lanes] = jnp.concatenate(halves, axis=0).T.astype(BF)
        if pair == 0:
            pump()


def attend_back(
    q_ref, k_ref, v_ref, p_ref, grad_ref, dq_ref, dk_ref, dv_ref, causal, block, first, last,
    pump,
):
    keys = k_ref.shape[0]
    for pair in range(q_ref.shape[1] // 128):
        lanes = slice(pair * 128, pair * 128 + 128)
        for start in range(first, last, block):
            stop = start + block if causal else keys
            halves = []
            sum_k, sum_v = None, None
            for half in range(2):
                mask = half_mask(block, half)
                query = q_ref[start : start + block, lanes]
                query = jnp.where(mask, query, jnp.zeros_like(query))
                grad = grad_ref[start : start + block, lanes]
                grad = jnp.where(mask, grad, jnp.zeros_like(grad))
                low = p_ref[2 * pair + half, :stop, start : start + block]
                probs = low.astype(F32)
                grad_probs = nt(v_ref[:stop, lanes], grad)
                delta = jnp.sum(probs * grad_probs, axis=0, keepdims=True)
                grad_scores = (probs * (grad_probs - delta)).astype(BF)
                turned = tn(k_ref[:stop, lanes], grad_scores) * SCALE
                halves.append(turned[half * HEAD_DIM : (half + 1) * HEAD_DIM])
                new_k, new_v = nn(grad_scores, query), nn(low, grad)
                sum_k = new_k if sum_k is None else sum_k + new_k
                sum_v = new_v if sum_v is None else sum_v + new_v
            old = start if causal else (keys if start else 0)
            for ref, value in ((dk_ref, sum_k), (dv_ref, sum_v)):
                if old:
                    ref[:old, lanes] = ref[:old, lanes] + value[:old]
                if old < stop:
                    ref[old:stop, lanes] = value[old:]
            dq_ref[start : start + block, lanes] = jnp.concatenate(halves, axis=0).T.astype(BF)
        if pair == 0:
            pump()


class Box:
    def __init__(self, names, refs):
        for name, ref in zip(names, refs):
            setattr(self, name, ref)


class Quarters:
    def __init__(self, link, place, grad, box_names, box):
        self.link, self.place, self.grad = link, place, grad
        self.recv, self.sums, self.last, self.lines, self.total, self.moved, self.done, self.out = (
            getattr(box, name) if name else None for name in box_names
        )

    def send(self):
        place, piece, link = self.place, self.piece, self.link
        self.steps = []
        for i, near in enumerate((place.tx, place.ty)):
            copies = [
                (self.grad.at[piece(near, i)], self.recv.at[i, 0], place.line(near)),
                (self.grad.at[piece(place.txy, i)], self.recv.at[i, 1], place.line(near)),
            ]
            self.steps.append(link.batch(copies, self.recv.at[i]))
        self.flying = list(self.steps)

    def turn(self):
        place, piece, link = self.place, self.piece, self.link
        steps = []
        for i, far in enumerate((place.ty, place.tx)):
            self.steps[i].wait_recv()
            value = self.grad[piece(far, i)].astype(F32) + self.recv[i, 1].astype(F32)
            self.sums[i] = value.astype(BF)
            steps.append(link.send(self.sums.at[i], self.last.at[i], place.line(far)))
        self.steps = steps
        self.flying += steps

    def add(self):
        place = self.place
        for i in range(2):
            self.steps[i].wait_recv()
            value = self.grad[self.piece(place.t, i)].astype(F32)
            value = value + self.recv[i, 0].astype(F32) + self.last[i].astype(F32)
            self.total[self.halves(i)] = value.astype(BF)
        if self.lines is not None:
            share, items = place.dims["share"], place.dims["items"]
            copies = []
            for a in range(1, items // share):
                target = {"items": lax.rem(place.it + a * share, items)}
                copies.append((self.total, self.lines.at[a - 1], target))
            step = self.link.batch(copies, self.lines)
            step.wait()
            self.link.open.pop()
            value = self.total[...].astype(F32)
            for a in range(1, items // share):
                value = value + self.lines[a - 1].astype(F32)
            self.total[...] = value.astype(BF)
        self.along()

    def gather(self):
        self.close()
        place, out = self.place, self.out
        self.own = self.link.local(self.done, out.at[place.t])
        self.near = [
            self.link.send(self.done, out.at[place.t], place.line(near))
            for near in (place.tx, place.ty)
        ]

    def forward(self):
        place, out, link = self.place, self.out, self.link
        self.steps = []
        for i, (source, near) in enumerate(((place.ty, place.tx), (place.tx, place.ty))):
            self.near[1 - i].wait_recv()
            part = out.at[self.cut(source, i)]
            self.steps.append(link.send(part, part, place.line(near)))

    def finish(self):
        arrive(self.steps)
        self.own.wait()


class Hidden(Quarters):
    def piece(self, t, i):
        rows = self.grad.shape[2] // 2
        return slice(None), t, slice(i * rows, (i + 1) * rows)

    def halves(self, i):
        rows = self.grad.shape[2] // 2
        return slice(None), slice(i * rows, (i + 1) * rows)

    def cut(self, t, i):
        rows = self.out.shape[1] // 2
        return t, slice(i * rows, (i + 1) * rows)

    def along(self):
        self.steps = [self.link.send(self.total.at[1], self.moved, self.place.partner())]

    def close(self):
        arrive(self.steps)
        self.done[...] = (self.total[0].astype(F32) + self.moved[...].astype(F32)).astype(BF)


class Columns(Quarters):
    def piece(self, t, i):
        blocks = self.grad.shape[1] // 2
        return slice(None), slice(i * blocks, (i + 1) * blocks), t

    def halves(self, i):
        blocks = self.grad.shape[1] // 2
        return slice(None), slice(i * blocks, (i + 1) * blocks)

    def cut(self, t, i):
        cols = self.out.shape[3] // 2
        return t, slice(None), slice(None), slice(i * cols, (i + 1) * cols)

    def along(self):
        place = self.place
        copies = []
        for d in range(1, place.dims["seq"]):
            target = place.seq_shift(d)
            copies.append((self.total.at[:, target], self.moved.at[place.me], {"seq": target}))
        self.steps = [self.link.batch(copies, self.moved.at[0 : place.dims["seq"] - 1])]
        self.own = self.link.local(self.total.at[:, place.me], self.moved.at[place.me])

    def close(self):
        arrive(self.steps)
        self.own.wait()
        dims = self.place.dims
        group, width = dims["group"], dims["width"]
        for index in range(3):
            for q in range(group):
                value = self.moved[q, index].astype(F32)
                for half in range(1, dims["items_dev"]):
                    value = value + self.moved[half * group + q, index].astype(F32)
                self.done[index, :, q * width : (q + 1) * width] = value.astype(BF)


class Rows(Quarters):
    def piece(self, t, i):
        return i, t

    def halves(self, i):
        return i

    def cut(self, t, i):
        cols = self.out.shape[2] // 2
        return t, slice(None), slice(i * cols, (i + 1) * cols)

    def along(self):
        self.moved_done = rows_back(self.link, self.place, self.total, self.moved)

    def close(self):
        self.moved_done()
        value = self.moved[0].astype(F32)
        for half in range(1, self.place.dims["items_dev"]):
            value = value + self.moved[half].astype(F32)
        self.done[...] = value.astype(BF)


class Stage:
    def __init__(self, sems, place, part, bufs, mid, spread, before):
        self.link, self.place, self.mid, self.spread = Link(*sems), place, mid, spread
        self.before = before
        self.reduce = Reduce(self.link, place, part, bufs)
        self.started, self.waits = {}, {}

    def start(self, k):
        self.reduce.start(k, k)

    def middle(self, k):
        self.reduce.middle(k, k)

    def end(self, k):
        place, spread = self.place, self.spread
        spread[k, place.c, place.b1, place.b0] = self.mid(k, self.reduce.end(k))
        self.started[k] = spread_start(self.link, place, spread, k)

    def forward(self, k):
        self.waits[k] = spread_end(self.link, self.place, self.spread, k, self.started[k])

    def arrive(self, k):
        arrive(self.waits[k])

    def release(self, k):
        done = (self.reduce.zero[k], self.reduce.one[k])
        for copy in done:
            copy.wait_send()
        late = {id(copy) for copy in done}
        self.link.open = [copy for copy in self.link.open if id(copy) not in late]


def stage_steps(stage, compute, flight=None, ended=None, after=None):
    before = stage.before
    compute(0, (lambda: before.forward(1)) if before else (lambda: None))
    stage.start(0)
    compute(1, lambda: None)
    stage.start(1)
    if before:
        before.link.finish()
    stage.middle(0)
    stage.middle(1)
    if flight:
        flight()
    stage.end(0)
    stage.end(1)
    if ended:
        ended()
    stage.forward(0)
    if after:
        after()


def layer_kernel(dims, names, *refs):
    b = Box(names, refs)
    b.grad_third, b.grad_r2, b.grad_r1, b.gc1_all = b.first, b.second, b.first, b.gy_all
    place = Place(dims)
    sems = b.send_sems, b.recv_sems
    link = Link(*sems, dims["chain"])
    width, block, items_dev = dims["width"], dims["block"], dims["items_dev"]
    h, t, q_place = place.h, place.t, place.q
    c, b1, b0 = place.c, place.b1, place.b0
    partner = place.partner()
    wr = b.w_sq.shape[0] // dims["share"]
    model = dims["model"]
    total_dec, total_mem = dims["total_dec"], dims["total_mem"]
    rb = b.dec.shape[1]

    def rows_of(ref, cols=model):
        return ref[...].reshape(-1, ref.shape[-1])[:, :cols]

    def chunk(ref, k):
        return ref[k].reshape(-1, model)

    half_rows = total_dec // 2

    def span(k):
        return slice(k * half_rows, (k + 1) * half_rows)

    def put(k, value, before=None):
        if before:
            before.release(k)
        b.part[k] = value.astype(BF).reshape(b.part.shape[1:])

    def weight(ref, index):
        return ref[index].reshape(model, width)

    weights = (b.w_sq, b.w_sk, b.w_sv, b.w_so, b.w_ck, b.w_cv, b.w_cq, b.w_co)
    rows_t = pl.ds(pl.multiple_of(t * wr, wr), wr)
    index = link.index()
    for i, w in enumerate(weights):
        pltpu.make_async_copy(w.at[rows_t], b.staged.at[i], b.send_sems.at[index]).start()
    staged = pltpu.make_async_copy(b.staged, b.staged, b.send_sems.at[index])
    own_fin = link.local(b.f_in, b.own_fin)
    own_fout = link.local(b.f_out, b.own_fout)
    greet(place.seq_peers() + place.items_peers())

    def share_columns(dst):
        blocks = dims["seq"] // 2
        return Share(
            link, place, lambda t: dst.at[:, t],
            lambda t, i: dst.at[i * blocks : (i + 1) * blocks, t],
        )

    def share_hidden(dst):
        rows = dst.shape[1] // 2
        return Share(
            link, place, lambda t: dst.at[t], lambda t, i: dst.at[t, i * rows : (i + 1) * rows]
        )

    def join_cells():
        mb = b.cells.shape[1]
        same = lax.broadcasted_iota(jnp.int32, (mb, mb), 0) == lax.broadcasted_iota(
            jnp.int32, (mb, mb), 1
        )
        for k in range(items_dev):
            flags = (b.cells[k : k + 1] == 1).astype(F32)
            column = jnp.sum(jnp.where(same, flags, 0.0), axis=1, keepdims=True)
            b.mem_cells[k, :, :model] = b.mem[k]
            b.mem_cells[k, :, model:] = jnp.broadcast_to(column, (mb, 128)).astype(BF)

    staged.wait()
    steps, own_self = columns_out(link, place, b.staged.at[0:3], b.o_self, width)
    b.x_all[h, c, b1, b0] = b.dec[h]
    join_cells()
    b.m_all[h, c, b1, b0] = b.mem_cells[h]
    link.settle(steps)
    swap_x = link.send(b.dec.at[1 - h], b.x_all.at[h, c, b1, b0], partner)
    first_x = spread_start(link, place, b.x_all, h)
    so_arrived, so_sent = rows_out(link, place, b.staged.at[3], b.o_so)
    steps.wait_recv()
    own_self.wait()
    self_share = [share_columns(b.o_self.at[i]) for i in range(3)]
    waits = spread_end(link, place, b.x_all, h, first_x)
    swap_x.wait_recv()
    second_x = spread_start(link, place, b.x_all, 1 - h)
    waits += spread_end(link, place, b.x_all, 1 - h, second_x)
    cross_steps, own_cross = columns_out(link, place, b.staged.at[4:7], b.o_cross, width)
    co_arrived, co_sent = rows_out(link, place, b.staged.at[7], b.o_co)
    swap_m = link.send(b.mem_cells.at[1 - h], b.m_all.at[h, c, b1, b0], partner)
    first_m = spread_start(link, place, b.m_all, h)
    for share in self_share:
        share.forward()
    so_arrived()
    so_share = Direct(link, place, lambda _: b.o_so.at[:, t])

    arrive(waits)
    rows = rows_of(b.x_all)
    for index, dst in enumerate((b.sq, b.sk, b.sv)):
        self_share[index].wait()
        dst[...] = nn(rows, weight(b.o_self, index)).astype(BF)
    cross_steps.wait_recv()
    own_cross.wait()
    cross_share = [
        Direct(link, place, lambda _, dst=b.o_cross.at[i]: dst.at[:, t]) for i in range(3)
    ]
    co_arrived()
    co_share = Direct(link, place, lambda _: b.o_co.at[:, t])
    mem_waits = spread_end(link, place, b.m_all, h, first_m)
    swap_m.wait_recv()
    second_m = spread_start(link, place, b.m_all, 1 - h)
    own_fin.wait()
    own_fout.wait()
    fr, gr = b.o_fin.shape[1], b.o_fout.shape[1]
    step_fin = link.send(b.own_fin.at[pl.ds(pl.multiple_of(t * fr, fr), fr)], b.o_fin.at[t], partner)
    length, mem_length = b.dec_len[h], b.mem_len[h]

    def self_ok(start, stop):
        keys = lax.broadcasted_iota(jnp.int32, (stop, block), 0)
        spots = lax.broadcasted_iota(jnp.int32, (stop, block), 1) + start
        return (keys <= spots) & (keys < length)

    bufs = [b.recv0, b.send1, b.recv1, b.keep1]
    if dims["bits"] == 3:
        bufs += [b.send2, b.recv2]

    def forward(index, res, summed, out):
        def mid(k, total):
            value = res(k) + total
            summed[k] = value
            normed, _ = moments(value)
            result = normed * b.gain[index : index + 1] + b.bias[index : index + 1]
            out[k] = result
            return result.astype(BF)

        return mid

    def self_part(k, pump):
        attend(
            b.sq, b.sk, b.sv, self_ok, b.sp, b.smix, True, block,
            k * half_rows, (k + 1) * half_rows, pump,
        )
        if k == 0:
            so_share.wait()
        put(k, nn(b.smix[span(k)], rows_of(b.o_so)))

    def memory_part():
        arrive(mem_waits)
        mems = rows_of(b.m_all)
        cross_share[0].wait()
        b.ck[...] = nn(mems, weight(b.o_cross, 0)).astype(BF)
        cross_share[1].wait()
        b.cv[...] = nn(mems, weight(b.o_cross, 1)).astype(BF)
        spots = lax.broadcasted_iota(jnp.int32, (total_mem, 128), 0)
        cells = b.m_all[...].reshape(-1, b.m_all.shape[-1])[:, model:].astype(F32)
        b.keep[...] = ((spots < mem_length) & ((cells > 0.5) | (spots == 0))).astype(F32)

    stage = Stage(
        sems, place, b.part, bufs,
        forward(0, lambda k: b.x_all[k, c, b1, b0].astype(F32), b.sum_one, b.first), b.first_all, None,
    )
    def cross_weights():
        rows = pl.ds(pl.multiple_of(t * gr, gr), gr)
        steps_fout.append(link.send(b.own_fout.at[rows], b.o_fout.at[t], partner))
        mem_waits.extend(spread_end(link, place, b.m_all, 1 - h, second_m))

    ffn_share, steps_fout = [], []
    stage_steps(stage, self_part, after=cross_weights)
    memory_part()
    step_fin.wait_recv()
    ffn_share.append(share_hidden(b.o_fin))
    b.c_own[h] = b.cot[h]

    def cross_part(k, pump):
        last.arrive(k)
        if k == 0:
            cross_share[2].wait()
        b.cq[span(k)] = nn(chunk(b.first_all, k), weight(b.o_cross, 2)).astype(BF)
        attend(
            b.cq, b.ck, b.cv, lambda start, stop: b.keep[:, 0:1] > 0.5, b.cp, b.cmix, False, block,
            k * half_rows, (k + 1) * half_rows, pump,
        )
        if k == 0:
            co_share.wait()
        put(k, nn(b.cmix[span(k)], rows_of(b.o_co)), last)

    last = stage
    stage = Stage(
        sems, place, b.part, bufs, forward(1, lambda k: b.first[k], b.sum_two, b.second),
        b.second_all, last,
    )
    def ffn_weights():
        ffn_share[0].forward()
        arrive(steps_fout)
        ffn_share.append(Direct(link, place, lambda _: b.o_fout.at[t]))

    stage_steps(stage, cross_part, ffn_weights)
    swap_c = link.send(b.cot.at[1 - h], b.c_own.at[h], partner)

    w_ins = (lambda: b.own_fin[...], lambda: b.o_fin[...].reshape(model, -1))
    w_outs = (lambda: b.own_fout[...], lambda: b.o_fout[...].reshape(-1, model))
    hidden = b.own_fin.shape[1]
    last_second = stage

    def ffn_part(k, pump):
        last_second.arrive(k)
        if k == 0:
            ffn_share[0].wait()
        rows = chunk(b.second_all, k)
        for index in range(2):
            if index:
                pump()
            pre = nn(rows, w_ins[index]())
            cdf = 0.5 * (1.0 + lax.erf(pre * (0.5**0.5)))
            cols = slice(index * hidden, (index + 1) * hidden)
            b.act[span(k), cols] = (pre * cdf).astype(BF)
            b.slope[span(k), cols] = (
                cdf + pre * (jnp.exp(-0.5 * pre * pre) * 0.3989422804014327)
            ).astype(BF)
        if k == 0:
            ffn_share[1].wait()
        total = nn(b.act[span(k), :hidden], w_outs[0]())
        put(k, total + nn(b.act[span(k), hidden:], w_outs[1]()), last_second)

    swap_c.wait_recv()

    def add_sums(index, k, normed, grad):
        new = (jnp.sum(grad * normed, axis=0, keepdims=True), jnp.sum(grad, axis=0, keepdims=True))
        for row, value in zip((index, 3 + index), new):
            b.sums[row : row + 1] = value if k == 0 else b.sums[row : row + 1] + value

    def turn(k, total):
        gain = b.gain[2:3]
        normed, inv = moments(b.second[k] + total)
        spots = lax.broadcasted_iota(jnp.int32, (rb, model), 0) + (k * dims["group"] + q_place) * rb
        kept = spots < length
        b.layer[k] = jnp.where(kept, normed * gain + b.bias[2:3], 0.0).astype(BF)
        grad = jnp.where(kept, b.c_own[k].astype(F32), 0.0)
        add_sums(2, k, normed, grad)
        result = norm_back(normed, inv, gain, grad)
        b.grad_third[k] = result
        return result.astype(BF)

    stage = Stage(sems, place, b.part, bufs, turn, b.gy_all, last_second)
    stage_steps(stage, ffn_part)

    last_turn = stage

    way_fout = Hidden(
        link, place, b.g_fout, ("q_fout", "t_fout", "u_fout", dims["lines"] and "l_fout", "s_fout", "z_fout", "d_fout", "r_fout"), b
    )
    def out_grads():
        grad = rows_of(b.gy_all)
        for index in range(2):
            cols = slice(index * hidden, (index + 1) * hidden)
            value = tn(b.act[:, cols], grad)
            b.g_fout[index] = value.astype(BF).reshape(b.g_fout.shape[1:])
        way_fout.send()

    def ffn_back(k, pump):
        last_turn.arrive(k)
        if k == 1:
            out_grads()
        grad = chunk(b.gy_all, k)
        total = None
        for index in range(2):
            if index:
                pump()
            cols = slice(index * hidden, (index + 1) * hidden)
            grad_pre = (nt(grad, w_outs[index]()) * b.slope[span(k), cols].astype(F32)).astype(BF)
            b.slope[span(k), cols] = grad_pre
            term = nt(grad_pre, w_ins[index]())
            total = term if total is None else total + term
        put(k, total, last_turn)

    way_fin = Hidden(
        link, place, b.g_fin, ("q_fin", "t_fin", "u_fin", dims["lines"] and "l_fin", "s_fin", "z_fin", "d_fin", "r_fin"), b
    )
    way_cross = Columns(
        link, place, b.g_cross, ("q_cross", "t_cross", "u_cross", dims["lines"] and "l_cross", "s_cross", "z_cross", "d_cross", "r_cross"), b
    )
    way_self = Columns(
        link, place, b.g_self, ("q_self", "t_self", "u_self", dims["lines"] and "l_self", "s_self", "z_self", "d_self", "r_self"), b
    )
    way_co = Rows(
        link, place, b.g_co, ("q_co", "t_co", "u_co", dims["lines"] and "l_co", "s_co", "z_co", "d_co", "r_co"), b
    )
    way_so = Rows(
        link, place, b.g_so, ("q_so", "t_so", "u_so", dims["lines"] and "l_so", "s_so", "z_so", "d_so", "r_so"), b
    )

    def backward(index, res, summed, out):
        def mid(k, total):
            normed, inv = moments(summed[k])
            grad = res[k] + total
            add_sums(index, k, normed, grad)
            result = norm_back(normed, inv, b.gain[index : index + 1], grad)
            out[k] = result
            return result.astype(BF)

        return mid

    def in_grads():
        rows = rows_of(b.second_all)
        for index in range(2):
            cols = slice(index * hidden, (index + 1) * hidden)
            value = tn(rows, b.slope[:, cols])
            b.g_fin[index] = value.astype(BF).reshape(b.g_fin.shape[1:])
        way_fin.send()

    stage = Stage(
        sems, place, b.part, bufs, backward(1, b.grad_third, b.sum_two, b.grad_r2), b.gc2_all,
        last_turn,
    )
    stage_steps(stage, ffn_back, in_grads)

    last_back = stage

    def cross_back(k, pump):
        last_back.arrive(k)
        b.dmix[span(k)] = nt(chunk(b.gc2_all, k), rows_of(b.o_co)).astype(BF)
        attend_back(
            b.cq, b.ck, b.cv, b.cp, b.dmix, b.dq, b.sum_dk, b.sum_dv, False, block,
            k * half_rows, (k + 1) * half_rows, pump,
        )
        put(k, nt(b.dq[span(k)], weight(b.o_cross, 2)), last_back)
        if k == 1:
            way_fout.turn()

    def cross_grads():
        mems = rows_of(b.m_all)
        shape = b.g_cross.shape[1:]
        b.dck[...] = (b.sum_dk[:total_mem] * SCALE).astype(BF)
        b.dcv[...] = b.sum_dv[:total_mem].astype(BF)
        b.g_cross[0] = tn(rows_of(b.first_all), b.dq[...]).astype(BF).reshape(shape)
        b.g_cross[1] = tn(mems, b.dck[...]).astype(BF).reshape(shape)
        b.g_cross[2] = tn(mems, b.dcv[...]).astype(BF).reshape(shape)
        way_cross.send()
        b.g_co[...] = tn(b.cmix[...], rows_of(b.gc2_all)).astype(BF).reshape(b.g_co.shape)
        way_co.send()
        way_fin.turn()

    def part_mem():
        value = nt(b.dck[...], weight(b.o_cross, 0)) + nt(b.dcv[...], weight(b.o_cross, 1))
        b.part_m[...] = value.astype(BF).reshape(b.part_m.shape)
        for index in range(2):
            red_m.start(index, ks[index])

    stage = Stage(
        sems, place, b.part, bufs, backward(0, b.grad_r2, b.sum_one, b.grad_r1), b.gc1_all,
        last_back,
    )
    ks = (1 - h, h)
    mem_bufs = [b.recv0_m, b.send1_m, b.recv1_m, b.keep1_m]
    if dims["bits"] == 3:
        mem_bufs += [b.send2_m, b.recv2_m]
    red_m = Reduce(link, place, b.part_m, mem_bufs)
    stage_steps(stage, cross_back, cross_grads, part_mem)

    swap_l = link.send(b.layer.at[1 - h], b.layer_out.at[h], partner)
    b.layer_out[h] = b.layer[h]
    way_fout.add()
    for k in range(2):
        stage.arrive(k)
        pump = (lambda: stage.forward(1)) if k == 0 else (lambda: None)
        b.dmix[span(k)] = nt(chunk(b.gc1_all, k), rows_of(b.o_so)).astype(BF)
        attend_back(
            b.sq, b.sk, b.sv, b.sp, b.dmix, b.dq, b.sum_dk, b.sum_dv, True, block,
            k * half_rows, (k + 1) * half_rows, pump,
        )
        red_m.middle(k, ks[k])
    b.dsk[...] = (b.sum_dk[...] * SCALE).astype(BF)
    b.dsv[...] = b.sum_dv[...].astype(BF)
    for k in range(2):
        total = nt(b.dq[span(k)], weight(b.o_self, 0)) + nt(b.dsk[span(k)], weight(b.o_self, 1))
        put(k, total + nt(b.dsv[span(k)], weight(b.o_self, 2)), stage)
    stage.link.finish()
    chain = Link(*sems)
    red_x = Reduce(chain, place, b.part, bufs)
    for index in range(2):
        red_x.start(index, ks[index])
    way_cross.turn()
    way_co.turn()
    way_fin.add()
    rows = rows_of(b.x_all)
    shape = b.g_self.shape[1:]
    b.g_self[0] = tn(rows, b.dq[...]).astype(BF).reshape(shape)
    b.g_self[1] = tn(rows, b.dsk[...]).astype(BF).reshape(shape)
    b.g_self[2] = tn(rows, b.dsv[...]).astype(BF).reshape(shape)
    way_self.send()
    b.g_so[...] = tn(b.smix[...], rows_of(b.gc1_all)).astype(BF).reshape(b.g_so.shape)
    way_so.send()
    for index in range(2):
        red_x.middle(index, ks[index])
    b.send_m[...] = red_m.end(0).astype(BF)
    swap_m = link.send(b.send_m, b.recv_m, partner)
    b.grad_mem[h] = red_m.end(1)
    copies = []
    for d in range(1, dims["seq"]):
        copies.append((b.sums, b.sums_seq.at[d - 1], {"seq": place.seq_shift(d)}))
    seq_sums = link.batch(copies, b.sums_seq)
    way_cross.add()
    way_co.add()
    b.send_x[...] = (red_x.end(0) + b.grad_r1[1 - h]).astype(BF)
    swap_x = link.send(b.send_x, b.recv_x, partner)
    b.grad_dec[h] = red_x.end(1) + b.grad_r1[h]
    way_fout.gather()
    way_self.turn()
    way_so.turn()
    way_fin.gather()
    way_fout.forward()
    way_self.add()
    way_so.add()
    way_cross.gather()
    way_co.gather()
    way_fin.forward()
    seq_sums.wait_recv()
    value = b.sums[...]
    for d in range(1, dims["seq"]):
        value = value + b.sums_seq[d - 1]
    b.sums_line[...] = value
    copies = []
    for e in range(1, dims["items"]):
        target = {"items": lax.rem(place.it + e, dims["items"])}
        copies.append((b.sums_line, b.sums_items.at[e - 1], target))
    item_sums = link.batch(copies, b.sums_items)
    swap_x.wait_recv()
    b.grad_dec[1 - h] = b.recv_x[...].astype(F32)
    swap_m.wait_recv()
    b.grad_mem[1 - h] = b.recv_m[...].astype(F32)
    swap_l.wait_recv()
    way_self.gather()
    way_so.gather()
    way_cross.forward()
    way_co.forward()
    item_sums.wait_recv()
    value = b.sums_line[...]
    for e in range(1, dims["items"]):
        value = value + b.sums_items[e - 1]
    b.sums_out[...] = value
    way_self.forward()
    way_so.forward()
    for way in (way_fout, way_fin, way_cross, way_co, way_self, way_so):
        way.finish()
    so_sent()
    co_sent()
    chain.finish()
    link.finish()


def shape(dims, dtype):
    return jax.ShapeDtypeStruct(tuple(dims), dtype)


def outputs_kernel(layer, dec, mem, cross, own, co, so, fin, fout, sums, *outs):
    o_layer, o_dec, o_mem = outs[:3]
    o_layer[...] = layer[...]
    o_dec[...] = dec[...]
    o_mem[...] = mem[...]
    for index in range(3):
        outs[3 + index][...] = own[0, index].astype(F32)
        outs[7 + index][...] = cross[0, index].astype(F32)
    outs[6][...] = so[0].astype(F32)
    outs[10][...] = co[0].astype(F32)
    outs[11][...] = fin[0].astype(F32)
    outs[12][...] = fout[0].astype(F32)
    outs[13][...] = sums[0:3]
    outs[14][...] = sums[3:6]


def shards(
    mesh, dec_in, memory, dec_len, mem_len, cell_mask, self_query, self_key, self_value, self_out,
    cross_query, cross_key, cross_value, cross_out, ffn_in, ffn_out, norm_gain, norm_bias, cotangent,
):
    items_dev, rb, model = dec_in.shape
    mb = memory.shape[1]
    seq, items = mesh.shape["seq"], mesh.shape["items"]
    group = seq // items_dev
    share = 4
    bits = group.bit_length() - 1
    chips = group // 4
    width = model // group
    total_dec, total_mem = rb * seq, mb * seq
    heads = width // HEAD_DIM
    hidden = ffn_in.shape[1]
    wr = self_query.shape[0] // share
    fr, gr = model // share, hidden // share
    lines = items // share - 1
    dims = {
        "items_dev": items_dev, "items": items, "seq": seq, "group": group, "share": share,
        "bits": bits, "chips": chips, "width": width, "model": model, "block": 256,
        "total_dec": total_dec, "total_mem": total_mem, "lines": lines,
        "chain": 12 + 2 * (bits - 2),
    }
    ins = [
        ("dec", dec_in, VM), ("mem", memory, VM), ("cells", cell_mask, VM), ("cot", cotangent, VM),
        ("dec_len", dec_len, SM), ("mem_len", mem_len, SM),
        ("w_sq", self_query, HBM), ("w_sk", self_key, HBM), ("w_sv", self_value, HBM),
        ("w_so", self_out, HBM), ("w_cq", cross_query, HBM), ("w_ck", cross_key, HBM),
        ("w_cv", cross_value, HBM), ("w_co", cross_out, HBM), ("f_in", ffn_in, HBM),
        ("f_out", ffn_out, HBM), ("gain", norm_gain, VM), ("bias", norm_bias, VM),
    ]
    own, own_m = (items_dev, rb, model), (items_dev, mb, model)
    grid = (items_dev, chips, 2, 2)
    outs = [
        ("layer_out", own, BF, VM), ("grad_dec", own, F32, VM), ("grad_mem", own_m, F32, VM),
        ("sums_out", (8, model), F32, VM),
        ("r_cross", (share, 3, wr, model), BF, HBM), ("r_self", (share, 3, wr, model), BF, HBM),
        ("r_co", (share, wr, model), BF, HBM), ("r_so", (share, wr, model), BF, HBM),
        ("r_fin", (share, fr, hidden), BF, HBM), ("r_fout", (share, gr, model), BF, HBM),
    ]
    cols = (3, seq, share, wr, width)
    scratch = [
        ("x_all", grid + (rb, model), BF), ("m_all", grid + (mb, model + 128), BF),
        ("mem_cells", (items_dev, mb, model + 128), BF), ("c_own", own, BF), ("staged", (8, wr, model), BF),
        ("own_fin", (model, hidden), BF), ("own_fout", (hidden, model), BF),
        ("o_self", cols, BF), ("o_cross", cols, BF),
        ("o_so", (items_dev, share, wr, model), BF), ("o_co", (items_dev, share, wr, model), BF),
        ("o_fin", (share, fr, hidden), BF), ("o_fout", (share, gr, model), BF),
        ("sq", (total_dec, width), BF), ("sk", (total_dec, width), BF), ("sv", (total_dec, width), BF),
        ("cq", (total_dec, width), BF), ("ck", (total_mem, width), BF), ("cv", (total_mem, width), BF),
        ("sp", (heads, total_dec, total_dec), BF), ("cp", (heads, total_mem, total_dec), BF),
        ("smix", (total_dec, width), BF), ("cmix", (total_dec, width), BF),
        ("keep", (total_mem, 128), F32),
        ("part", grid + (rb, model), BF), ("part_m", grid + (mb, model), BF),
        ("first_all", grid + (rb, model), BF), ("second_all", grid + (rb, model), BF),
        ("gy_all", grid + (rb, model), BF), ("gc2_all", grid + (rb, model), BF),
        ("sum_one", own, F32), ("sum_two", own, F32), ("first", own, F32), ("second", own, F32),
        ("layer", own, BF), ("sum_dk", (total_dec, width), F32), ("sum_dv", (total_dec, width), F32),
        ("act", (total_dec, 2 * hidden), BF), ("slope", (total_dec, 2 * hidden), BF),
        ("dmix", (total_dec, width), BF), ("dq", (total_dec, width), BF),
        ("dsk", (total_dec, width), BF), ("dsv", (total_dec, width), BF),
        ("dck", (total_mem, width), BF), ("dcv", (total_mem, width), BF),
        ("send_x", (rb, model), BF), ("recv_x", (rb, model), BF),
        ("send_m", (mb, model), BF), ("recv_m", (mb, model), BF),
        ("sums", (8, model), F32), ("sums_line", (8, model), F32),
        ("sums_seq", (seq - 1, 8, model), F32), ("sums_items", (items - 1, 8, model), F32),
    ]
    for name, rows in (("", rb), ("_m", mb)):
        scratch += [
            ("recv0" + name, (items_dev, chips, 2, rows, model), BF),
            ("send1" + name, (items_dev, chips, rows, model), BF),
            ("recv1" + name, (items_dev, chips, rows, model), BF),
            ("keep1" + name, (items_dev, chips, rows, model), F32),
        ]
        if bits == 3:
            scratch += [
                ("send2" + name, (items_dev, rows, model), BF),
                ("recv2" + name, (items_dev, rows, model), BF),
            ]
    for name, grad, quarter, piece, moved, done in (
        ("fin", (2, share, fr, hidden), (2, fr, hidden), (2, fr // 2, hidden), (fr, hidden),
         (fr, hidden)),
        ("fout", (2, share, gr, model), (2, gr, model), (2, gr // 2, model), (gr, model), (gr, model)),
        ("cross", cols, (3, seq, wr, width), (3, seq // 2, wr, width), (seq, 3, wr, width),
         (3, wr, model)),
        ("self", cols, (3, seq, wr, width), (3, seq // 2, wr, width), (seq, 3, wr, width),
         (3, wr, model)),
        ("co", (items_dev, share, wr, model), (items_dev, wr, model), (wr, model),
         (items_dev, wr, model), (wr, model)),
        ("so", (items_dev, share, wr, model), (items_dev, wr, model), (wr, model),
         (items_dev, wr, model), (wr, model)),
    ):
        scratch += [
            ("g_" + name, grad, BF), ("q_" + name, (2, 2) + piece, BF), ("t_" + name, (2,) + piece, BF),
            ("u_" + name, (2,) + piece, BF), ("s_" + name, quarter, BF), ("z_" + name, moved, BF),
            ("d_" + name, done, BF),
        ]
        if lines:
            scratch.append(("l_" + name, (lines,) + quarter, BF))
    copies = dims["chain"] + 140 + 12 * (bits - 2)
    names = [x[0] for x in ins + outs + scratch] + ["send_sems", "recv_sems"]
    results = pl.pallas_call(
        functools.partial(layer_kernel, dims, names),
        name="layer",
        out_shape=[shape(x[1], x[2]) for x in outs],
        in_specs=[x[2] for x in ins],
        out_specs=[x[3] for x in outs],
        scratch_shapes=[pltpu.VMEM(x[1], x[2]) for x in scratch]
        + [pltpu.SemaphoreType.DMA((copies,)), pltpu.SemaphoreType.DMA((copies,))],
        compiler_params=pltpu.CompilerParams(
            collective_id=0, has_side_effects=True, vmem_limit_bytes=VMEM_BYTES
        ),
    )(*[x[1] for x in ins])
    layer_out, grad_dec, grad_memory, sums, r_cross, r_self, r_co, r_so, r_fin, r_fout = results
    tok, mem_rows = items_dev * rb, items_dev * mb
    pieces = (
        ((tok, model), (tok // share, model), BF), ((tok, model), (tok // share, model), F32),
        ((mem_rows, model), (mem_rows // share, model), F32),
    )
    heads_in = [
        pl.BlockSpec((1, 3, wr, model), lambda i: (i, 0, 0, 0)),
        pl.BlockSpec((1, 3, wr, model), lambda i: (i, 0, 0, 0)),
        pl.BlockSpec((1, wr, model), lambda i: (i, 0, 0)),
        pl.BlockSpec((1, wr, model), lambda i: (i, 0, 0)),
        pl.BlockSpec((1, fr, hidden), lambda i: (i, 0, 0)),
        pl.BlockSpec((1, gr, model), lambda i: (i, 0, 0)),
        pl.BlockSpec((8, model), lambda i: (0, 0)),
    ]
    row_specs = [pl.BlockSpec(x[1], lambda i: (i, 0)) for x in pieces]
    square = (share * wr, model)
    outs = pl.pallas_call(
        outputs_kernel,
        name="outputs",
        grid=(share,),
        in_specs=row_specs + heads_in,
        out_specs=row_specs
        + [pl.BlockSpec((wr, model), lambda i: (i, 0))] * 8
        + [pl.BlockSpec((fr, hidden), lambda i: (i, 0)), pl.BlockSpec((gr, model), lambda i: (i, 0))]
        + [pl.BlockSpec((3, model), lambda i: (0, 0))] * 2,
        out_shape=[shape(x[0], x[2]) for x in pieces]
        + [shape(square, F32)] * 8
        + [shape((model, hidden), F32), shape((hidden, model), F32)]
        + [shape((3, model), F32)] * 2,
        compiler_params=pltpu.CompilerParams(vmem_limit_bytes=VMEM_BYTES),
    )(
        layer_out.reshape(tok, model), grad_dec.reshape(tok, model),
        grad_memory.reshape(mem_rows, model), r_cross, r_self, r_co, r_so, r_fin, r_fout, sums,
    )
    return (
        outs[0].reshape(own), outs[1].reshape(own), outs[2].reshape(own_m), *outs[3:],
    )


def solution(mesh):
    rows = P("seq", None)
    tokens = P("items", "seq", None)
    placed = (
        (tokens, tokens, P("items"), P("items"), P("items", "seq"))
        + (rows,) * 8
        + (P(None, "seq"), rows, P(), P(), tokens)
    )
    return jax.shard_map(
        functools.partial(shards, mesh),
        mesh=mesh,
        in_specs=placed,
        out_specs=(tokens,) * 3 + (rows,) * 8 + (P(None, "seq"), rows, P(), P()),
        check_vma=False,
    )
```

```python
import functools

import jax
import jax.numpy as jnp
from jax import lax
from jax.experimental import pallas as pl
from jax.experimental.pallas import tpu as pltpu
from jax.sharding import PartitionSpec as P

HEAD_DIM = 64
EPS = 1e-05
NEG = -1e30
SCALE = HEAD_DIM ** (-0.5)
BF = jnp.bfloat16
F32 = jnp.float32
VMEM_BYTES = 63 * 1024 * 1024
MESH = pl.DeviceIdType.MESH
VM = pl.BlockSpec(memory_space=pltpu.VMEM)
HBM = pl.BlockSpec(memory_space=pl.ANY)
SM = pl.BlockSpec(memory_space=pltpu.SMEM)


def nn(left, right):
    return lax.dot_general(left, right, (((1,), (0,)), ((), ())), preferred_element_type=F32)


def nt(left, right):
    return lax.dot_general(left, right, (((1,), (1,)), ((), ())), preferred_element_type=F32)


def tn(left, right):
    return lax.dot_general(left, right, (((0,), (0,)), ((), ())), preferred_element_type=F32)


class Link:
    def __init__(self, send_sems, recv_sems, first=0):
        self.send_sems, self.recv_sems, self.count, self.open = send_sems, recv_sems, first, []

    def index(self):
        self.count += 1
        return self.count - 1

    def make(self, src, dst, device, index):
        return pltpu.make_async_remote_copy(
            src_ref=src,
            dst_ref=dst,
            send_sem=self.send_sems.at[index],
            recv_sem=self.recv_sems.at[index],
            device_id=device,
            device_id_type=MESH,
        )

    def send(self, src, dst, device):
        copy = self.make(src, dst, device, self.index())
        copy.start()
        self.open.append(copy)
        return copy

    def batch(self, copies, whole):
        index = self.index()
        for copy in copies:
            self.make(*copy, index).start()
        wait = self.make(whole, whole, copies[0][2], index)
        self.open.append(wait)
        return wait

    def settle(self, copy):
        copy.wait_send()
        self.open = [other for other in self.open if other is not copy]

    def local(self, src, dst):
        copy = pltpu.make_async_copy(src, dst, self.send_sems.at[self.index()])
        copy.start()
        return copy

    def finish(self, kept=()):
        late = {id(copy) for copy in kept}
        for copy in self.open:
            if id(copy) not in late:
                copy.wait_send()
        self.open = [copy for copy in self.open if id(copy) in late]


def greet(devices):
    barrier = pltpu.get_barrier_semaphore()
    for device in devices:
        pl.semaphore_signal(barrier, inc=1, device_id=device, device_id_type=MESH)
    pl.semaphore_wait(barrier, len(devices))


class Place:
    def __init__(self, dims):
        self.dims = dims
        group, share = dims["group"], dims["share"]
        self.me = lax.axis_index("seq")
        self.h = self.me // group
        self.q = self.me % group
        self.b0 = self.q % 2
        self.b1 = (self.q // 2) % 2
        self.c = self.q // 4
        self.it = lax.axis_index("items")
        self.base = (self.it // share) * share
        self.t = self.it % share
        x, y = self.t % 2, self.t // 2
        self.tx, self.ty, self.txy = y * 2 + 1 - x, (1 - y) * 2 + x, (1 - y) * 2 + 1 - x

    def across(self, bit):
        value = (self.q // (1 << bit)) % 2
        return {"seq": self.me + (1 - 2 * value) * (1 << bit)}

    def partner(self):
        return {"seq": (1 - self.h) * self.dims["group"] + self.q}

    def seq_shift(self, d):
        return lax.rem(self.me + d, self.dims["seq"])

    def line(self, t):
        return {"items": self.base + t}

    def seq_peers(self):
        return [{"seq": self.seq_shift(d)} for d in range(1, self.dims["seq"])]

    def items_peers(self):
        count = self.dims["items"]
        return [{"items": lax.rem(self.it + e, count)} for e in range(1, count)]


def spread_start(link, place, out, k):
    bits = place.dims["bits"]
    c, b1, b0 = place.c, place.b1, place.b0
    if bits == 3:
        step = link.send(out.at[k, c, b1, b0], out.at[k, c, b1, b0], place.across(2))
        step.wait_recv()
    waits = []
    high = link.send(out.at[k, :, b1, b0], out.at[k, :, b1, b0], place.across(1))
    waits.append(link.send(out.at[k, :, b1, b0], out.at[k, :, b1, b0], place.across(0)))
    return high, waits


def spread_end(link, place, out, k, started):
    high, waits = started
    b1, b0 = place.b1, place.b0
    high.wait_recv()
    waits.append(link.send(out.at[k, :, 1 - b1, b0], out.at[k, :, 1 - b1, b0], place.across(0)))
    return waits


def columns_out(link, place, src, dst, width):
    seq, group = place.dims["seq"], place.dims["group"]
    copies = []
    for d in range(1, seq):
        target = place.seq_shift(d)
        cols = pl.ds(pl.multiple_of(lax.rem(target, group) * width, width), width)
        copies.append((src.at[:, :, cols], dst.at[:, place.me, place.t], {"seq": target}))
    steps = link.batch(copies, dst.at[:, 0 : seq - 1, place.t])
    cols = pl.ds(pl.multiple_of(place.q * width, width), width)
    return steps, link.local(src.at[:, :, cols], dst.at[:, place.me, place.t])


def rows_out(link, place, src, dst):
    dims, me = place.dims, place.me
    slot = lax.rem(me, dims["items_dev"])
    base = link.count
    link.count += dims["items_dev"] + 1
    copies = []
    for half in range(dims["items_dev"]):
        target = half * dims["group"] + me // dims["items_dev"]
        copy = pltpu.make_async_remote_copy(
            src_ref=src,
            dst_ref=dst.at[slot, place.t],
            send_sem=link.send_sems.at[base + half],
            recv_sem=link.recv_sems.at[base + slot],
            device_id={"seq": target},
            device_id_type=MESH,
        )
        copies.append((target != me, copy))
        pl.when(target != me)(copy.start)
    own = pltpu.make_async_copy(
        src, dst.at[slot, place.t], link.send_sems.at[base + dims["items_dev"]]
    )
    mine = me // dims["items_dev"] == place.q
    pl.when(mine)(own.start)

    def arrived():
        pl.when(mine)(own.wait)
        for block in range(dims["items_dev"]):
            copy = pltpu.make_async_remote_copy(
                src_ref=src,
                dst_ref=dst.at[block, place.t],
                send_sem=link.send_sems.at[base],
                recv_sem=link.recv_sems.at[base + block],
                device_id={"seq": me},
                device_id_type=MESH,
            )
            pl.when(place.q * dims["items_dev"] + block != me)(copy.wait_recv)

    def sent():
        for other, copy in copies:
            pl.when(other)(copy.wait_send)

    return arrived, sent


class Share:
    def __init__(self, link, place, slab, half):
        self.link, self.place, self.half = link, place, half
        t = place.t
        self.from_x = link.send(slab(t), slab(t), place.line(place.tx))
        self.from_y = link.send(slab(t), slab(t), place.line(place.ty))

    def forward(self):
        link, place, half = self.link, self.place, self.half
        self.from_y.wait_recv()
        part = half(place.ty, 0)
        self.steps = [link.send(part, part, place.line(place.tx))]
        self.from_x.wait_recv()
        part = half(place.tx, 1)
        self.steps.append(link.send(part, part, place.line(place.ty)))

    def wait(self):
        arrive(self.steps)


class Direct(Share):
    def __init__(self, link, place, slab):
        lines = (place.tx, place.ty, place.txy)
        self.steps = [link.send(slab(place.t), slab(place.t), place.line(line)) for line in lines]

    def forward(self):
        pass


def arrive(steps):
    for step in steps:
        step.wait_recv()


class Reduce:
    def __init__(self, link, place, part, bufs):
        self.link, self.place, self.part, self.bufs = link, place, part, bufs
        self.zero, self.one = {}, {}

    def start(self, index, k):
        place = self.place
        self.zero[index] = self.link.send(
            self.part.at[k, :, :, 1 - place.b0], self.bufs[0].at[index], place.across(0)
        )

    def middle(self, index, k):
        place, part = self.place, self.part
        recv0, send1, recv1, keep1 = self.bufs[:4]
        self.zero[index].wait_recv()
        b1, b0 = place.b1, place.b0
        for c in range(part.shape[1]):
            value = part[k, c, 1 - b1, b0].astype(F32) + recv0[index, c, 1 - b1].astype(F32)
            send1[index, c] = value.astype(BF)
        self.one[index] = self.link.send(send1.at[index], recv1.at[index], place.across(1))
        for c in range(part.shape[1]):
            keep1[index, c] = part[k, c, b1, b0].astype(F32) + recv0[index, c, b1].astype(F32)

    def end(self, index):
        place = self.place
        recv1, keep1 = self.bufs[2:4]
        self.one[index].wait_recv()
        if place.dims["bits"] == 2:
            return keep1[index, 0] + recv1[index, 0].astype(F32)
        send2, recv2 = self.bufs[4:6]
        c = place.c
        send2[index] = (keep1[index, 1 - c] + recv1[index, 1 - c].astype(F32)).astype(BF)
        step = self.link.send(send2.at[index], recv2.at[index], place.across(2))
        kept = keep1[index, c] + recv1[index, c].astype(F32)
        step.wait_recv()
        return kept + recv2[index].astype(F32)


def reduce_bufs(dims, rows):
    items_dev, width, chips = dims["items_dev"], dims["model"], dims["chips"]
    bufs = [
        pltpu.VMEM((items_dev, chips, 2, rows, width), BF),
        pltpu.VMEM((items_dev, chips, rows, width), BF),
        pltpu.VMEM((items_dev, chips, rows, width), BF),
        pltpu.VMEM((items_dev, chips, rows, width), F32),
    ]
    if dims["bits"] == 3:
        bufs += [pltpu.VMEM((items_dev, rows, width), BF) for _ in range(2)]
    return bufs


def moments(value):
    mean = jnp.mean(value, axis=-1, keepdims=True)
    centered = value - mean
    inv = lax.rsqrt(jnp.mean(centered * centered, axis=-1, keepdims=True) + EPS)
    return centered * inv, inv


def norm_back(normed, inv, gain, grad):
    scaled = grad * gain
    mean = jnp.mean(scaled, axis=-1, keepdims=True)
    cross = jnp.mean(scaled * normed, axis=-1, keepdims=True)
    return inv * (scaled - mean - normed * cross)


def rows_back(link, place, src, dst):
    dims, me, h = place.dims, place.me, place.h
    count = dims["items_dev"]
    base = link.count
    link.count += count + 1
    copies = []
    for k in range(count):
        target = place.q * count + k
        copy = pltpu.make_async_remote_copy(
            src_ref=src.at[k],
            dst_ref=dst.at[h],
            send_sem=link.send_sems.at[base + k],
            recv_sem=link.recv_sems.at[base + h],
            device_id={"seq": target},
            device_id_type=MESH,
        )
        copies.append((target != me, copy))
        pl.when(target != me)(copy.start)
    own = pltpu.make_async_copy(
        src.at[lax.rem(me, count)], dst.at[h], link.send_sems.at[base + count]
    )
    mine = me // count == place.q
    pl.when(mine)(own.start)

    def done():
        pl.when(mine)(own.wait)
        for half in range(count):
            copy = pltpu.make_async_remote_copy(
                src_ref=src.at[0],
                dst_ref=dst.at[half],
                send_sem=link.send_sems.at[base],
                recv_sem=link.recv_sems.at[base + half],
                device_id={"seq": me},
                device_id_type=MESH,
            )
            pl.when(half * dims["group"] + me // count != me)(copy.wait_recv)
        for other, copy in copies:
            pl.when(other)(copy.wait_send)

    return done


def half_mask(rows, half):
    return (lax.broadcasted_iota(jnp.int32, (rows, 128), 1) // HEAD_DIM) == half


def attend(q_ref, k_ref, v_ref, valid, p_ref, mix_ref, causal, block, first, last, pump):
    keys = k_ref.shape[0]
    for pair in range(q_ref.shape[1] // 128):
        lanes = slice(pair * 128, pair * 128 + 128)
        for start in range(first, last, block):
            stop = start + block if causal else keys
            halves = []
            for half in range(2):
                query = q_ref[start : start + block, lanes]
                query = jnp.where(half_mask(block, half), query, jnp.zeros_like(query))
                scores = nt(k_ref[:stop, lanes], query) * SCALE
                scores = jnp.where(valid(start, stop), scores, NEG)
                top = jnp.max(scores, axis=0, keepdims=True)
                grown = jnp.exp(scores - top)
                probs = (grown * (1.0 / jnp.sum(grown, axis=0, keepdims=True))).astype(BF)
                p_ref[2 * pair + half, :stop, start : start + block] = probs
                mixed = tn(v_ref[:stop, lanes], probs)
                halves.append(mixed[half * HEAD_DIM : (half + 1) * HEAD_DIM])
            mix_ref[start : start + block, lanes] = jnp.concatenate(halves, axis=0).T.astype(BF)
        if pair == 0:
            pump()


def attend_back(
    q_ref, k_ref, v_ref, p_ref, grad_ref, dq_ref, dk_ref, dv_ref, causal, block, first, last,
    pump,
):
    keys = k_ref.shape[0]
    for pair in range(q_ref.shape[1] // 128):
        lanes = slice(pair * 128, pair * 128 + 128)
        for start in range(first, last, block):
            stop = start + block if causal else keys
            halves = []
            sum_k, sum_v = None, None
            for half in range(2):
                mask = half_mask(block, half)
                query = q_ref[start : start + block, lanes]
                query = jnp.where(mask, query, jnp.zeros_like(query))
                grad = grad_ref[start : start + block, lanes]
                grad = jnp.where(mask, grad, jnp.zeros_like(grad))
                low = p_ref[2 * pair + half, :stop, start : start + block]
                probs = low.astype(F32)
                grad_probs = nt(v_ref[:stop, lanes], grad)
                delta = jnp.sum(probs * grad_probs, axis=0, keepdims=True)
                grad_scores = (probs * (grad_probs - delta)).astype(BF)
                turned = tn(k_ref[:stop, lanes], grad_scores) * SCALE
                halves.append(turned[half * HEAD_DIM : (half + 1) * HEAD_DIM])
                new_k, new_v = nn(grad_scores, query), nn(low, grad)
                sum_k = new_k if sum_k is None else sum_k + new_k
                sum_v = new_v if sum_v is None else sum_v + new_v
            old = start if causal else (keys if start else 0)
            for ref, value in ((dk_ref, sum_k), (dv_ref, sum_v)):
                if old:
                    ref[:old, lanes] = ref[:old, lanes] + value[:old]
                if old < stop:
                    ref[old:stop, lanes] = value[old:]
            dq_ref[start : start + block, lanes] = jnp.concatenate(halves, axis=0).T.astype(BF)
        if pair == 0:
            pump()


class Box:
    def __init__(self, names, refs):
        for name, ref in zip(names, refs):
            setattr(self, name, ref)


class Quarters:
    def __init__(self, link, place, grad, box_names, box):
        self.link, self.place, self.grad = link, place, grad
        self.recv, self.sums, self.last, self.lines, self.total, self.moved, self.done, self.out = (
            getattr(box, name) if name else None for name in box_names
        )

    def send(self):
        place, piece, link = self.place, self.piece, self.link
        self.steps = []
        for i, near in enumerate((place.tx, place.ty)):
            copies = [
                (self.grad.at[piece(near, i)], self.recv.at[i, 0], place.line(near)),
                (self.grad.at[piece(place.txy, i)], self.recv.at[i, 1], place.line(near)),
            ]
            self.steps.append(link.batch(copies, self.recv.at[i]))
        self.flying = list(self.steps)

    def turn(self):
        place, piece, link = self.place, self.piece, self.link
        steps = []
        for i, far in enumerate((place.ty, place.tx)):
            self.steps[i].wait_recv()
            value = self.grad[piece(far, i)].astype(F32) + self.recv[i, 1].astype(F32)
            self.sums[i] = value.astype(BF)
            steps.append(link.send(self.sums.at[i], self.last.at[i], place.line(far)))
        self.steps = steps
        self.flying += steps

    def add(self):
        place = self.place
        for i in range(2):
            self.steps[i].wait_recv()
            value = self.grad[self.piece(place.t, i)].astype(F32)
            value = value + self.recv[i, 0].astype(F32) + self.last[i].astype(F32)
            self.total[self.halves(i)] = value.astype(BF)
        if self.lines is not None:
            share, items = place.dims["share"], place.dims["items"]
            copies = []
            for a in range(1, items // share):
                target = {"items": lax.rem(place.it + a * share, items)}
                copies.append((self.total, self.lines.at[a - 1], target))
            step = self.link.batch(copies, self.lines)
            step.wait()
            self.link.open.pop()
            value = self.total[...].astype(F32)
            for a in range(1, items // share):
                value = value + self.lines[a - 1].astype(F32)
            self.total[...] = value.astype(BF)
        self.along()

    def gather(self):
        self.close()
        place, out = self.place, self.out
        self.own = self.link.local(self.done, out.at[place.t])
        self.near = [
            self.link.send(self.done, out.at[place.t], place.line(near))
            for near in (place.tx, place.ty)
        ]

    def forward(self):
        place, out, link = self.place, self.out, self.link
        self.steps = []
        for i, (source, near) in enumerate(((place.ty, place.tx), (place.tx, place.ty))):
            self.near[1 - i].wait_recv()
            part = out.at[self.cut(source, i)]
            self.steps.append(link.send(part, part, place.line(near)))

    def finish(self):
        arrive(self.steps)
        self.own.wait()


class Hidden(Quarters):
    def piece(self, t, i):
        rows = self.grad.shape[2] // 2
        return slice(None), t, slice(i * rows, (i + 1) * rows)

    def halves(self, i):
        rows = self.grad.shape[2] // 2
        return slice(None), slice(i * rows, (i + 1) * rows)

    def cut(self, t, i):
        rows = self.out.shape[1] // 2
        return t, slice(i * rows, (i + 1) * rows)

    def along(self):
        self.steps = [self.link.send(self.total.at[1], self.moved, self.place.partner())]

    def close(self):
        arrive(self.steps)
        self.done[...] = (self.total[0].astype(F32) + self.moved[...].astype(F32)).astype(BF)


class Columns(Quarters):
    def piece(self, t, i):
        blocks = self.grad.shape[1] // 2
        return slice(None), slice(i * blocks, (i + 1) * blocks), t

    def halves(self, i):
        blocks = self.grad.shape[1] // 2
        return slice(None), slice(i * blocks, (i + 1) * blocks)

    def cut(self, t, i):
        cols = self.out.shape[3] // 2
        return t, slice(None), slice(None), slice(i * cols, (i + 1) * cols)

    def along(self):
        place = self.place
        copies = []
        for d in range(1, place.dims["seq"]):
            target = place.seq_shift(d)
            copies.append((self.total.at[:, target], self.moved.at[place.me], {"seq": target}))
        self.steps = [self.link.batch(copies, self.moved.at[0 : place.dims["seq"] - 1])]
        self.own = self.link.local(self.total.at[:, place.me], self.moved.at[place.me])

    def close(self):
        arrive(self.steps)
        self.own.wait()
        dims = self.place.dims
        group, width = dims["group"], dims["width"]
        for index in range(3):
            for q in range(group):
                value = self.moved[q, index].astype(F32)
                for half in range(1, dims["items_dev"]):
                    value = value + self.moved[half * group + q, index].astype(F32)
                self.done[index, :, q * width : (q + 1) * width] = value.astype(BF)


class Rows(Quarters):
    def piece(self, t, i):
        return i, t

    def halves(self, i):
        return i

    def cut(self, t, i):
        cols = self.out.shape[2] // 2
        return t, slice(None), slice(i * cols, (i + 1) * cols)

    def along(self):
        self.moved_done = rows_back(self.link, self.place, self.total, self.moved)

    def close(self):
        self.moved_done()
        value = self.moved[0].astype(F32)
        for half in range(1, self.place.dims["items_dev"]):
            value = value + self.moved[half].astype(F32)
        self.done[...] = value.astype(BF)


class Stage:
    def __init__(self, sems, place, part, bufs, mid, spread, before):
        self.link, self.place, self.mid, self.spread = Link(*sems), place, mid, spread
        self.before = before
        self.reduce = Reduce(self.link, place, part, bufs)
        self.started, self.waits = {}, {}

    def start(self, k):
        self.reduce.start(k, k)

    def middle(self, k):
        self.reduce.middle(k, k)

    def end(self, k):
        place, spread = self.place, self.spread
        spread[k, place.c, place.b1, place.b0] = self.mid(k, self.reduce.end(k))
        self.started[k] = spread_start(self.link, place, spread, k)

    def forward(self, k):
        self.waits[k] = spread_end(self.link, self.place, self.spread, k, self.started[k])

    def arrive(self, k):
        arrive(self.waits[k])

    def release(self, k):
        done = (self.reduce.zero[k], self.reduce.one[k])
        for copy in done:
            copy.wait_send()
        late = {id(copy) for copy in done}
        self.link.open = [copy for copy in self.link.open if id(copy) not in late]


def stage_steps(stage, compute, flight=None, ended=None, after=None):
    before = stage.before
    compute(0, (lambda: before.forward(1)) if before else (lambda: None))
    stage.start(0)
    compute(1, lambda: None)
    stage.start(1)
    if before:
        before.link.finish()
    stage.middle(0)
    stage.middle(1)
    if flight:
        flight()
    stage.end(0)
    stage.end(1)
    if ended:
        ended()
    stage.forward(0)
    if after:
        after()


def layer_kernel(dims, names, *refs):
    b = Box(names, refs)
    b.grad_third, b.grad_r2, b.grad_r1, b.gc1_all = b.first, b.second, b.first, b.gy_all
    place = Place(dims)
    sems = b.send_sems, b.recv_sems
    link = Link(*sems, dims["chain"])
    width, block, items_dev = dims["width"], dims["block"], dims["items_dev"]
    h, t, q_place = place.h, place.t, place.q
    c, b1, b0 = place.c, place.b1, place.b0
    partner = place.partner()
    wr = b.w_sq.shape[0] // dims["share"]
    model = dims["model"]
    total_dec, total_mem = dims["total_dec"], dims["total_mem"]
    rb = b.dec.shape[1]

    def rows_of(ref, cols=model):
        return ref[...].reshape(-1, ref.shape[-1])[:, :cols]

    def chunk(ref, k):
        return ref[k].reshape(-1, model)

    half_rows = total_dec // 2

    def span(k):
        return slice(k * half_rows, (k + 1) * half_rows)

    def put(k, value, before=None):
        if before:
            before.release(k)
        b.part[k] = value.astype(BF).reshape(b.part.shape[1:])

    def weight(ref, index):
        return ref[index].reshape(model, width)

    weights = (b.w_sq, b.w_sk, b.w_sv, b.w_so, b.w_ck, b.w_cv, b.w_cq, b.w_co)
    rows_t = pl.ds(pl.multiple_of(t * wr, wr), wr)
    index = link.index()
    for i, w in enumerate(weights):
        pltpu.make_async_copy(w.at[rows_t], b.staged.at[i], b.send_sems.at[index]).start()
    staged = pltpu.make_async_copy(b.staged, b.staged, b.send_sems.at[index])
    own_fin = link.local(b.f_in, b.own_fin)
    own_fout = link.local(b.f_out, b.own_fout)
    greet(place.seq_peers() + place.items_peers())

    def share_columns(dst):
        blocks = dims["seq"] // 2
        return Share(
            link, place, lambda t: dst.at[:, t],
            lambda t, i: dst.at[i * blocks : (i + 1) * blocks, t],
        )

    def share_hidden(dst):
        rows = dst.shape[1] // 2
        return Share(
            link, place, lambda t: dst.at[t], lambda t, i: dst.at[t, i * rows : (i + 1) * rows]
        )

    def join_cells():
        mb = b.cells.shape[1]
        same = lax.broadcasted_iota(jnp.int32, (mb, mb), 0) == lax.broadcasted_iota(
            jnp.int32, (mb, mb), 1
        )
        for k in range(items_dev):
            flags = (b.cells[k : k + 1] == 1).astype(F32)
            column = jnp.sum(jnp.where(same, flags, 0.0), axis=1, keepdims=True)
            b.mem_cells[k, :, :model] = b.mem[k]
            b.mem_cells[k, :, model:] = jnp.broadcast_to(column, (mb, 128)).astype(BF)

    staged.wait()
    steps, own_self = columns_out(link, place, b.staged.at[0:3], b.o_self, width)
    b.x_all[h, c, b1, b0] = b.dec[h]
    join_cells()
    b.m_all[h, c, b1, b0] = b.mem_cells[h]
    link.settle(steps)
    swap_x = link.send(b.dec.at[1 - h], b.x_all.at[h, c, b1, b0], partner)
    first_x = spread_start(link, place, b.x_all, h)
    so_arrived, so_sent = rows_out(link, place, b.staged.at[3], b.o_so)
    steps.wait_recv()
    own_self.wait()
    self_share = [share_columns(b.o_self.at[i]) for i in range(3)]
    waits = spread_end(link, place, b.x_all, h, first_x)
    swap_x.wait_recv()
    second_x = spread_start(link, place, b.x_all, 1 - h)
    waits += spread_end(link, place, b.x_all, 1 - h, second_x)
    cross_steps, own_cross = columns_out(link, place, b.staged.at[4:7], b.o_cross, width)
    co_arrived, co_sent = rows_out(link, place, b.staged.at[7], b.o_co)
    swap_m = link.send(b.mem_cells.at[1 - h], b.m_all.at[h, c, b1, b0], partner)
    first_m = spread_start(link, place, b.m_all, h)
    for share in self_share:
        share.forward()
    so_arrived()
    so_share = Direct(link, place, lambda _: b.o_so.at[:, t])

    arrive(waits)
    rows = rows_of(b.x_all)
    for index, dst in enumerate((b.sq, b.sk, b.sv)):
        self_share[index].wait()
        dst[...] = nn(rows, weight(b.o_self, index)).astype(BF)
    cross_steps.wait_recv()
    own_cross.wait()
    cross_share = [
        Direct(link, place, lambda _, dst=b.o_cross.at[i]: dst.at[:, t]) for i in range(3)
    ]
    co_arrived()
    co_share = Direct(link, place, lambda _: b.o_co.at[:, t])
    mem_waits = spread_end(link, place, b.m_all, h, first_m)
    swap_m.wait_recv()
    second_m = spread_start(link, place, b.m_all, 1 - h)
    own_fin.wait()
    own_fout.wait()
    fr, gr = b.o_fin.shape[1], b.o_fout.shape[1]
    step_fin = link.send(b.own_fin.at[pl.ds(pl.multiple_of(t * fr, fr), fr)], b.o_fin.at[t], partner)
    length, mem_length = b.dec_len[h], b.mem_len[h]

    def self_ok(start, stop):
        keys = lax.broadcasted_iota(jnp.int32, (stop, block), 0)
        spots = lax.broadcasted_iota(jnp.int32, (stop, block), 1) + start
        return (keys <= spots) & (keys < length)

    bufs = [b.recv0, b.send1, b.recv1, b.keep1]
    if dims["bits"] == 3:
        bufs += [b.send2, b.recv2]

    def forward(index, res, summed, out):
        def mid(k, total):
            value = res(k) + total
            summed[k] = value
            normed, _ = moments(value)
            result = normed * b.gain[index : index + 1] + b.bias[index : index + 1]
            out[k] = result
            return result.astype(BF)

        return mid

    def self_part(k, pump):
        attend(
            b.sq, b.sk, b.sv, self_ok, b.sp, b.smix, True, block,
            k * half_rows, (k + 1) * half_rows, pump,
        )
        if k == 0:
            so_share.wait()
        put(k, nn(b.smix[span(k)], rows_of(b.o_so)))

    def memory_part():
        arrive(mem_waits)
        mems = rows_of(b.m_all)
        cross_share[0].wait()
        b.ck[...] = nn(mems, weight(b.o_cross, 0)).astype(BF)
        cross_share[1].wait()
        b.cv[...] = nn(mems, weight(b.o_cross, 1)).astype(BF)
        spots = lax.broadcasted_iota(jnp.int32, (total_mem, 128), 0)
        cells = b.m_all[...].reshape(-1, b.m_all.shape[-1])[:, model:].astype(F32)
        b.keep[...] = ((spots < mem_length) & ((cells > 0.5) | (spots == 0))).astype(F32)

    stage = Stage(
        sems, place, b.part, bufs,
        forward(0, lambda k: b.x_all[k, c, b1, b0].astype(F32), b.sum_one, b.first), b.first_all, None,
    )
    def cross_weights():
        for i in range(2):
            rows = pl.ds(pl.multiple_of(t * gr + i * (gr // 2), gr // 2), gr // 2)
            steps_fout.append(link.send(b.own_fout.at[rows], out_rows(i), partner))
        mem_waits.extend(spread_end(link, place, b.m_all, 1 - h, second_m))

    ffn_share, steps_fout = [], []

    def out_rows(i):
        return b.o_fout.at[t, i * (gr // 2) : (i + 1) * (gr // 2)]

    def share_out(i):
        steps_fout[i].wait_recv()
        ffn_share.append(Direct(link, place, lambda _: out_rows(i)))

    stage_steps(stage, self_part, after=cross_weights)
    memory_part()
    step_fin.wait_recv()
    ffn_share.append(share_hidden(b.o_fin))
    b.c_own[h] = b.cot[h]

    def cross_part(k, pump):
        last.arrive(k)
        if k == 0:
            cross_share[2].wait()
        b.cq[span(k)] = nn(chunk(b.first_all, k), weight(b.o_cross, 2)).astype(BF)
        attend(
            b.cq, b.ck, b.cv, lambda start, stop: b.keep[:, 0:1] > 0.5, b.cp, b.cmix, False, block,
            k * half_rows, (k + 1) * half_rows, pump,
        )
        if k == 0:
            co_share.wait()
        put(k, nn(b.cmix[span(k)], rows_of(b.o_co)), last)
        if k == 1:
            share_out(0)

    last = stage
    stage = Stage(
        sems, place, b.part, bufs, forward(1, lambda k: b.first[k], b.sum_two, b.second),
        b.second_all, last,
    )
    def ffn_weights():
        ffn_share[0].forward()
        share_out(1)

    stage_steps(stage, cross_part, ffn_weights)
    swap_c = link.send(b.cot.at[1 - h], b.c_own.at[h], partner)

    w_ins = (lambda: b.own_fin[...], lambda: b.o_fin[...].reshape(model, -1))
    w_outs = (lambda: b.own_fout[...], lambda: b.o_fout[...].reshape(-1, model))
    hidden = b.own_fin.shape[1]
    last_second = stage

    def ffn_part(k, pump):
        last_second.arrive(k)
        if k == 0:
            ffn_share[0].wait()
        rows = chunk(b.second_all, k)
        for index in range(2):
            if index:
                pump()
            pre = nn(rows, w_ins[index]())
            cdf = 0.5 * (1.0 + lax.erf(pre * (0.5**0.5)))
            cols = slice(index * hidden, (index + 1) * hidden)
            b.act[span(k), cols] = (pre * cdf).astype(BF)
            b.slope[span(k), cols] = (
                cdf + pre * (jnp.exp(-0.5 * pre * pre) * 0.3989422804014327)
            ).astype(BF)
        if k == 0:
            ffn_share[1].wait()
            ffn_share[2].wait()
        total = nn(b.act[span(k), :hidden], w_outs[0]())
        put(k, total + nn(b.act[span(k), hidden:], w_outs[1]()), last_second)

    swap_c.wait_recv()

    def add_sums(index, k, normed, grad):
        new = (jnp.sum(grad * normed, axis=0, keepdims=True), jnp.sum(grad, axis=0, keepdims=True))
        for row, value in zip((index, 3 + index), new):
            b.sums[row : row + 1] = value if k == 0 else b.sums[row : row + 1] + value

    def turn(k, total):
        gain = b.gain[2:3]
        normed, inv = moments(b.second[k] + total)
        spots = lax.broadcasted_iota(jnp.int32, (rb, model), 0) + (k * dims["group"] + q_place) * rb
        kept = spots < length
        b.layer[k] = jnp.where(kept, normed * gain + b.bias[2:3], 0.0).astype(BF)
        grad = jnp.where(kept, b.c_own[k].astype(F32), 0.0)
        add_sums(2, k, normed, grad)
        result = norm_back(normed, inv, gain, grad)
        b.grad_third[k] = result
        return result.astype(BF)

    stage = Stage(sems, place, b.part, bufs, turn, b.gy_all, last_second)
    stage_steps(stage, ffn_part)

    last_turn = stage

    way_fout = Hidden(
        link, place, b.g_fout, ("q_fout", "t_fout", "u_fout", dims["lines"] and "l_fout", "s_fout", "z_fout", "d_fout", "r_fout"), b
    )
    def out_grads():
        grad = rows_of(b.gy_all)
        for index in range(2):
            cols = slice(index * hidden, (index + 1) * hidden)
            value = tn(b.act[:, cols], grad)
            b.g_fout[index] = value.astype(BF).reshape(b.g_fout.shape[1:])
        way_fout.send()

    def ffn_back(k, pump):
        last_turn.arrive(k)
        if k == 1:
            out_grads()
        grad = chunk(b.gy_all, k)
        total = None
        for index in range(2):
            if index:
                pump()
            cols = slice(index * hidden, (index + 1) * hidden)
            grad_pre = (nt(grad, w_outs[index]()) * b.slope[span(k), cols].astype(F32)).astype(BF)
            b.slope[span(k), cols] = grad_pre
            term = nt(grad_pre, w_ins[index]())
            total = term if total is None else total + term
        put(k, total, last_turn)

    way_fin = Hidden(
        link, place, b.g_fin, ("q_fin", "t_fin", "u_fin", dims["lines"] and "l_fin", "s_fin", "z_fin", "d_fin", "r_fin"), b
    )
    way_cross = Columns(
        link, place, b.g_cross, ("q_cross", "t_cross", "u_cross", dims["lines"] and "l_cross", "s_cross", "z_cross", "d_cross", "r_cross"), b
    )
    way_self = Columns(
        link, place, b.g_self, ("q_self", "t_self", "u_self", dims["lines"] and "l_self", "s_self", "z_self", "d_self", "r_self"), b
    )
    way_co = Rows(
        link, place, b.g_co, ("q_co", "t_co", "u_co", dims["lines"] and "l_co", "s_co", "z_co", "d_co", "r_co"), b
    )
    way_so = Rows(
        link, place, b.g_so, ("q_so", "t_so", "u_so", dims["lines"] and "l_so", "s_so", "z_so", "d_so", "r_so"), b
    )

    def backward(index, res, summed, out):
        def mid(k, total):
            normed, inv = moments(summed[k])
            grad = res[k] + total
            add_sums(index, k, normed, grad)
            result = norm_back(normed, inv, b.gain[index : index + 1], grad)
            out[k] = result
            return result.astype(BF)

        return mid

    def in_grads():
        rows = rows_of(b.second_all)
        for index in range(2):
            cols = slice(index * hidden, (index + 1) * hidden)
            value = tn(rows, b.slope[:, cols])
            b.g_fin[index] = value.astype(BF).reshape(b.g_fin.shape[1:])
        way_fin.send()

    stage = Stage(
        sems, place, b.part, bufs, backward(1, b.grad_third, b.sum_two, b.grad_r2), b.gc2_all,
        last_turn,
    )
    stage_steps(stage, ffn_back, in_grads)

    last_back = stage

    def cross_back(k, pump):
        last_back.arrive(k)
        b.dmix[span(k)] = nt(chunk(b.gc2_all, k), rows_of(b.o_co)).astype(BF)
        attend_back(
            b.cq, b.ck, b.cv, b.cp, b.dmix, b.dq, b.sum_dk, b.sum_dv, False, block,
            k * half_rows, (k + 1) * half_rows, pump,
        )
        put(k, nt(b.dq[span(k)], weight(b.o_cross, 2)), last_back)
        if k == 1:
            way_fout.turn()

    def cross_grads():
        mems = rows_of(b.m_all)
        shape = b.g_cross.shape[1:]
        b.dck[...] = (b.sum_dk[:total_mem] * SCALE).astype(BF)
        b.dcv[...] = b.sum_dv[:total_mem].astype(BF)
        b.g_cross[0] = tn(rows_of(b.first_all), b.dq[...]).astype(BF).reshape(shape)
        b.g_cross[1] = tn(mems, b.dck[...]).astype(BF).reshape(shape)
        b.g_cross[2] = tn(mems, b.dcv[...]).astype(BF).reshape(shape)
        way_cross.send()
        b.g_co[...] = tn(b.cmix[...], rows_of(b.gc2_all)).astype(BF).reshape(b.g_co.shape)
        way_co.send()
        way_fin.turn()

    def part_mem():
        value = nt(b.dck[...], weight(b.o_cross, 0)) + nt(b.dcv[...], weight(b.o_cross, 1))
        b.part_m[...] = value.astype(BF).reshape(b.part_m.shape)
        for index in range(2):
            red_m.start(index, ks[index])

    stage = Stage(
        sems, place, b.part, bufs, backward(0, b.grad_r2, b.sum_one, b.grad_r1), b.gc1_all,
        last_back,
    )
    ks = (1 - h, h)
    mem_bufs = [b.recv0_m, b.send1_m, b.recv1_m, b.keep1_m]
    if dims["bits"] == 3:
        mem_bufs += [b.send2_m, b.recv2_m]
    red_m = Reduce(link, place, b.part_m, mem_bufs)
    stage_steps(stage, cross_back, cross_grads, part_mem)

    swap_l = link.send(b.layer.at[1 - h], b.layer_out.at[h], partner)
    b.layer_out[h] = b.layer[h]
    way_fout.add()
    for k in range(2):
        stage.arrive(k)
        pump = (lambda: stage.forward(1)) if k == 0 else (lambda: None)
        b.dmix[span(k)] = nt(chunk(b.gc1_all, k), rows_of(b.o_so)).astype(BF)
        attend_back(
            b.sq, b.sk, b.sv, b.sp, b.dmix, b.dq, b.sum_dk, b.sum_dv, True, block,
            k * half_rows, (k + 1) * half_rows, pump,
        )
        red_m.middle(k, ks[k])
    b.dsk[...] = (b.sum_dk[...] * SCALE).astype(BF)
    b.dsv[...] = b.sum_dv[...].astype(BF)
    for k in range(2):
        total = nt(b.dq[span(k)], weight(b.o_self, 0)) + nt(b.dsk[span(k)], weight(b.o_self, 1))
        put(k, total + nt(b.dsv[span(k)], weight(b.o_self, 2)), stage)
    stage.link.finish()
    chain = Link(*sems)
    red_x = Reduce(chain, place, b.part, bufs)
    for index in range(2):
        red_x.start(index, ks[index])
    way_cross.turn()
    way_co.turn()
    way_fin.add()
    rows = rows_of(b.x_all)
    shape = b.g_self.shape[1:]
    b.g_self[0] = tn(rows, b.dq[...]).astype(BF).reshape(shape)
    b.g_self[1] = tn(rows, b.dsk[...]).astype(BF).reshape(shape)
    b.g_self[2] = tn(rows, b.dsv[...]).astype(BF).reshape(shape)
    way_self.send()
    b.g_so[...] = tn(b.smix[...], rows_of(b.gc1_all)).astype(BF).reshape(b.g_so.shape)
    way_so.send()
    for index in range(2):
        red_x.middle(index, ks[index])
    b.send_m[...] = red_m.end(0).astype(BF)
    swap_m = link.send(b.send_m, b.recv_m, partner)
    b.grad_mem[h] = red_m.end(1)
    copies = []
    for d in range(1, dims["seq"]):
        copies.append((b.sums, b.sums_seq.at[d - 1], {"seq": place.seq_shift(d)}))
    seq_sums = link.batch(copies, b.sums_seq)
    way_cross.add()
    way_co.add()
    b.send_x[...] = (red_x.end(0) + b.grad_r1[1 - h]).astype(BF)
    swap_x = link.send(b.send_x, b.recv_x, partner)
    b.grad_dec[h] = red_x.end(1) + b.grad_r1[h]
    way_fout.gather()
    way_self.turn()
    way_so.turn()
    way_fin.gather()
    way_fout.forward()
    way_self.add()
    way_so.add()
    way_cross.gather()
    way_co.gather()
    way_fin.forward()
    seq_sums.wait_recv()
    value = b.sums[...]
    for d in range(1, dims["seq"]):
        value = value + b.sums_seq[d - 1]
    b.sums_line[...] = value
    copies = []
    for e in range(1, dims["items"]):
        target = {"items": lax.rem(place.it + e, dims["items"])}
        copies.append((b.sums_line, b.sums_items.at[e - 1], target))
    item_sums = link.batch(copies, b.sums_items)
    swap_x.wait_recv()
    b.grad_dec[1 - h] = b.recv_x[...].astype(F32)
    swap_m.wait_recv()
    b.grad_mem[1 - h] = b.recv_m[...].astype(F32)
    swap_l.wait_recv()
    way_self.gather()
    way_so.gather()
    way_cross.forward()
    way_co.forward()
    item_sums.wait_recv()
    value = b.sums_line[...]
    for e in range(1, dims["items"]):
        value = value + b.sums_items[e - 1]
    b.sums_out[...] = value
    way_self.forward()
    way_so.forward()
    for way in (way_fout, way_fin, way_cross, way_co, way_self, way_so):
        way.finish()
    so_sent()
    co_sent()
    chain.finish()
    link.finish()


def shape(dims, dtype):
    return jax.ShapeDtypeStruct(tuple(dims), dtype)


def outputs_kernel(layer, dec, mem, cross, own, co, so, fin, fout, sums, *outs):
    o_layer, o_dec, o_mem = outs[:3]
    o_layer[...] = layer[...]
    o_dec[...] = dec[...]
    o_mem[...] = mem[...]
    for index in range(3):
        outs[3 + index][...] = own[0, index].astype(F32)
        outs[7 + index][...] = cross[0, index].astype(F32)
    outs[6][...] = so[0].astype(F32)
    outs[10][...] = co[0].astype(F32)
    outs[11][...] = fin[0].astype(F32)
    outs[12][...] = fout[0].astype(F32)
    outs[13][...] = sums[0:3]
    outs[14][...] = sums[3:6]


def shards(
    mesh, dec_in, memory, dec_len, mem_len, cell_mask, self_query, self_key, self_value, self_out,
    cross_query, cross_key, cross_value, cross_out, ffn_in, ffn_out, norm_gain, norm_bias, cotangent,
):
    items_dev, rb, model = dec_in.shape
    mb = memory.shape[1]
    seq, items = mesh.shape["seq"], mesh.shape["items"]
    group = seq // items_dev
    share = 4
    bits = group.bit_length() - 1
    chips = group // 4
    width = model // group
    total_dec, total_mem = rb * seq, mb * seq
    heads = width // HEAD_DIM
    hidden = ffn_in.shape[1]
    wr = self_query.shape[0] // share
    fr, gr = model // share, hidden // share
    lines = items // share - 1
    dims = {
        "items_dev": items_dev, "items": items, "seq": seq, "group": group, "share": share,
        "bits": bits, "chips": chips, "width": width, "model": model, "block": 256,
        "total_dec": total_dec, "total_mem": total_mem, "lines": lines,
        "chain": 12 + 2 * (bits - 2),
    }
    ins = [
        ("dec", dec_in, VM), ("mem", memory, VM), ("cells", cell_mask, VM), ("cot", cotangent, VM),
        ("dec_len", dec_len, SM), ("mem_len", mem_len, SM),
        ("w_sq", self_query, HBM), ("w_sk", self_key, HBM), ("w_sv", self_value, HBM),
        ("w_so", self_out, HBM), ("w_cq", cross_query, HBM), ("w_ck", cross_key, HBM),
        ("w_cv", cross_value, HBM), ("w_co", cross_out, HBM), ("f_in", ffn_in, HBM),
        ("f_out", ffn_out, HBM), ("gain", norm_gain, VM), ("bias", norm_bias, VM),
    ]
    own, own_m = (items_dev, rb, model), (items_dev, mb, model)
    grid = (items_dev, chips, 2, 2)
    outs = [
        ("layer_out", own, BF, VM), ("grad_dec", own, F32, VM), ("grad_mem", own_m, F32, VM),
        ("sums_out", (8, model), F32, VM),
        ("r_cross", (share, 3, wr, model), BF, HBM), ("r_self", (share, 3, wr, model), BF, HBM),
        ("r_co", (share, wr, model), BF, HBM), ("r_so", (share, wr, model), BF, HBM),
        ("r_fin", (share, fr, hidden), BF, HBM), ("r_fout", (share, gr, model), BF, HBM),
    ]
    cols = (3, seq, share, wr, width)
    scratch = [
        ("x_all", grid + (rb, model), BF), ("m_all", grid + (mb, model + 128), BF),
        ("mem_cells", (items_dev, mb, model + 128), BF), ("c_own", own, BF), ("staged", (8, wr, model), BF),
        ("own_fin", (model, hidden), BF), ("own_fout", (hidden, model), BF),
        ("o_self", cols, BF), ("o_cross", cols, BF),
        ("o_so", (items_dev, share, wr, model), BF), ("o_co", (items_dev, share, wr, model), BF),
        ("o_fin", (share, fr, hidden), BF), ("o_fout", (share, gr, model), BF),
        ("sq", (total_dec, width), BF), ("sk", (total_dec, width), BF), ("sv", (total_dec, width), BF),
        ("cq", (total_dec, width), BF), ("ck", (total_mem, width), BF), ("cv", (total_mem, width), BF),
        ("sp", (heads, total_dec, total_dec), BF), ("cp", (heads, total_mem, total_dec), BF),
        ("smix", (total_dec, width), BF), ("cmix", (total_dec, width), BF),
        ("keep", (total_mem, 128), F32),
        ("part", grid + (rb, model), BF), ("part_m", grid + (mb, model), BF),
        ("first_all", grid + (rb, model), BF), ("second_all", grid + (rb, model), BF),
        ("gy_all", grid + (rb, model), BF), ("gc2_all", grid + (rb, model), BF),
        ("sum_one", own, F32), ("sum_two", own, F32), ("first", own, F32), ("second", own, F32),
        ("layer", own, BF), ("sum_dk", (total_dec, width), F32), ("sum_dv", (total_dec, width), F32),
        ("act", (total_dec, 2 * hidden), BF), ("slope", (total_dec, 2 * hidden), BF),
        ("dmix", (total_dec, width), BF), ("dq", (total_dec, width), BF),
        ("dsk", (total_dec, width), BF), ("dsv", (total_dec, width), BF),
        ("dck", (total_mem, width), BF), ("dcv", (total_mem, width), BF),
        ("send_x", (rb, model), BF), ("recv_x", (rb, model), BF),
        ("send_m", (mb, model), BF), ("recv_m", (mb, model), BF),
        ("sums", (8, model), F32), ("sums_line", (8, model), F32),
        ("sums_seq", (seq - 1, 8, model), F32), ("sums_items", (items - 1, 8, model), F32),
    ]
    for name, rows in (("", rb), ("_m", mb)):
        scratch += [
            ("recv0" + name, (items_dev, chips, 2, rows, model), BF),
            ("send1" + name, (items_dev, chips, rows, model), BF),
            ("recv1" + name, (items_dev, chips, rows, model), BF),
            ("keep1" + name, (items_dev, chips, rows, model), F32),
        ]
        if bits == 3:
            scratch += [
                ("send2" + name, (items_dev, rows, model), BF),
                ("recv2" + name, (items_dev, rows, model), BF),
            ]
    for name, grad, quarter, piece, moved, done in (
        ("fin", (2, share, fr, hidden), (2, fr, hidden), (2, fr // 2, hidden), (fr, hidden),
         (fr, hidden)),
        ("fout", (2, share, gr, model), (2, gr, model), (2, gr // 2, model), (gr, model), (gr, model)),
        ("cross", cols, (3, seq, wr, width), (3, seq // 2, wr, width), (seq, 3, wr, width),
         (3, wr, model)),
        ("self", cols, (3, seq, wr, width), (3, seq // 2, wr, width), (seq, 3, wr, width),
         (3, wr, model)),
        ("co", (items_dev, share, wr, model), (items_dev, wr, model), (wr, model),
         (items_dev, wr, model), (wr, model)),
        ("so", (items_dev, share, wr, model), (items_dev, wr, model), (wr, model),
         (items_dev, wr, model), (wr, model)),
    ):
        scratch += [
            ("g_" + name, grad, BF), ("q_" + name, (2, 2) + piece, BF), ("t_" + name, (2,) + piece, BF),
            ("u_" + name, (2,) + piece, BF), ("s_" + name, quarter, BF), ("z_" + name, moved, BF),
            ("d_" + name, done, BF),
        ]
        if lines:
            scratch.append(("l_" + name, (lines,) + quarter, BF))
    copies = dims["chain"] + 144 + 12 * (bits - 2)
    names = [x[0] for x in ins + outs + scratch] + ["send_sems", "recv_sems"]
    results = pl.pallas_call(
        functools.partial(layer_kernel, dims, names),
        name="layer",
        out_shape=[shape(x[1], x[2]) for x in outs],
        in_specs=[x[2] for x in ins],
        out_specs=[x[3] for x in outs],
        scratch_shapes=[pltpu.VMEM(x[1], x[2]) for x in scratch]
        + [pltpu.SemaphoreType.DMA((copies,)), pltpu.SemaphoreType.DMA((copies,))],
        compiler_params=pltpu.CompilerParams(
            collective_id=0, has_side_effects=True, vmem_limit_bytes=VMEM_BYTES
        ),
    )(*[x[1] for x in ins])
    layer_out, grad_dec, grad_memory, sums, r_cross, r_self, r_co, r_so, r_fin, r_fout = results
    tok, mem_rows = items_dev * rb, items_dev * mb
    pieces = (
        ((tok, model), (tok // share, model), BF), ((tok, model), (tok // share, model), F32),
        ((mem_rows, model), (mem_rows // share, model), F32),
    )
    heads_in = [
        pl.BlockSpec((1, 3, wr, model), lambda i: (i, 0, 0, 0)),
        pl.BlockSpec((1, 3, wr, model), lambda i: (i, 0, 0, 0)),
        pl.BlockSpec((1, wr, model), lambda i: (i, 0, 0)),
        pl.BlockSpec((1, wr, model), lambda i: (i, 0, 0)),
        pl.BlockSpec((1, fr, hidden), lambda i: (i, 0, 0)),
        pl.BlockSpec((1, gr, model), lambda i: (i, 0, 0)),
        pl.BlockSpec((8, model), lambda i: (0, 0)),
    ]
    row_specs = [pl.BlockSpec(x[1], lambda i: (i, 0)) for x in pieces]
    square = (share * wr, model)
    outs = pl.pallas_call(
        outputs_kernel,
        name="outputs",
        grid=(share,),
        in_specs=row_specs + heads_in,
        out_specs=row_specs
        + [pl.BlockSpec((wr, model), lambda i: (i, 0))] * 8
        + [pl.BlockSpec((fr, hidden), lambda i: (i, 0)), pl.BlockSpec((gr, model), lambda i: (i, 0))]
        + [pl.BlockSpec((3, model), lambda i: (0, 0))] * 2,
        out_shape=[shape(x[0], x[2]) for x in pieces]
        + [shape(square, F32)] * 8
        + [shape((model, hidden), F32), shape((hidden, model), F32)]
        + [shape((3, model), F32)] * 2,
        compiler_params=pltpu.CompilerParams(vmem_limit_bytes=VMEM_BYTES),
    )(
        layer_out.reshape(tok, model), grad_dec.reshape(tok, model),
        grad_memory.reshape(mem_rows, model), r_cross, r_self, r_co, r_so, r_fin, r_fout, sums,
    )
    return (
        outs[0].reshape(own), outs[1].reshape(own), outs[2].reshape(own_m), *outs[3:],
    )


def solution(mesh):
    rows = P("seq", None)
    tokens = P("items", "seq", None)
    placed = (
        (tokens, tokens, P("items"), P("items"), P("items", "seq"))
        + (rows,) * 8
        + (P(None, "seq"), rows, P(), P(), tokens)
    )
    return jax.shard_map(
        functools.partial(shards, mesh),
        mesh=mesh,
        in_specs=placed,
        out_specs=(tokens,) * 3 + (rows,) * 8 + (P(None, "seq"), rows, P(), P()),
        check_vma=False,
    )
```
